32 devices in a mesh: section: 2 (over core), seq: 4 (over z), fsdp: 4 (over y, x).
Axes of the slice: x: 2, y: 2, z: 4, core: 2. Of those that a mesh axis runs over, the one named last changes fastest.
Arguments:
- inputs: bfloat16 [2, 4, 512, 2048], P(None, 'fsdp', 'seq'), may hold values from -6 to 6
- cotangent: bfloat16 [2, 4, 512, 2048], P(None, 'fsdp', 'seq'), may hold values from -6 to 6
- lengths: int32 [2, 4], P(None, 'fsdp'), may hold values from 257 to 512, as said below
- gain_in: bfloat16 [2, 2048], P('section', 'fsdp'), may hold values from 0.25 to 1.75
- w_in: bfloat16 [2, 2048, 8512], P('section', 'fsdp'), may hold values from -0.125 to 0.125
- conv_w: bfloat16 [2, 4, 4352], P('section', None, 'fsdp'), may hold values from -3 to 3
- conv_b: bfloat16 [2, 4352], P('section', 'fsdp'), may hold values from -3 to 3
- dt_bias: bfloat16 [2, 64], P('section', 'fsdp'), may hold values from -6 to -2
- a_log: bfloat16 [2, 64], P('section', 'fsdp'), may hold values from -6 to -1
- d_skip: bfloat16 [2, 64], P('section', 'fsdp'), may hold values from -3 to 3
- gain_out: bfloat16 [2, 4096], P('section', 'fsdp'), may hold values from 0.25 to 1.75
- w_out: bfloat16 [2, 4096, 2048], P('section', 'fsdp'), may hold values from -0.09375 to 0.09375
Outputs:
- layer_outputs: bfloat16 [2, 2, 4, 512, 2048], P('section', None, 'fsdp', 'seq')
- input_grads: float32 [2, 2, 4, 512, 2048], P('section', None, 'fsdp', 'seq')
- grad_gain_in: float32 [2, 2048], P('section', 'fsdp')
- grad_w_in: float32 [2, 2048, 8512], P('section', 'fsdp')
- grad_conv_w: float32 [2, 4, 4352], P('section', None, 'fsdp')
- grad_conv_b: float32 [2, 4352], P('section', 'fsdp')
- grad_dt_bias: float32 [2, 64], P('section', 'fsdp')
- grad_a_log: float32 [2, 64], P('section', 'fsdp')
- grad_d_skip: float32 [2, 64], P('section', 'fsdp')
- grad_gain_out: float32 [2, 4096], P('section', 'fsdp')
- grad_w_out: float32 [2, 4096, 2048], P('section', 'fsdp')
- act_rms: float32 [2, 2], P('section')
The draws below stay inside these ranges and needn't reach their ends.
Inputs may be any that keep to these rules, and one draw needn't show every extreme that they name: `lengths`: each slot holds one sequence from position 0 and padding after it; in every slot column some micro-batch is full, 512 long.
All inputs are finite; a program needn't handle non-finite values.
Results may differ from the reference program's by a relative error of at most 0.008.
The reference program's roundings to bfloat16 on the way count: a program that leaves them out, or rounds other values in their place, can miss the bound.
Values may be sent and summed in bfloat16 or wider, within the bound.
No kernel may reach another device: no remote copies, remote signals or barrier semaphores. Data moves between devices by JAX's collectives and lax.ppermute only.
A program may use at most 512 MiB of HBM per device.

```python
import jax
import jax.numpy as jnp
from jax import lax

D = 2048
INNER = 4096
HEADS = 64
HEAD_DIM = 64
STATE = 128
KERNEL = 4
TOK_SEQ = 128
MICRO = 2
SLOTS = 4
SEQLEN = 512
CHANNELS = 4352
PROJ = 8512
N_SECTION = 2


def draw_lengths(key, part):
    key = jax.random.fold_in(key, 7)
    key_lengths, key_longest = jax.random.split(key)
    drawn_lengths = jax.random.randint(key_lengths, (MICRO, SLOTS), SEQLEN // 2 + 1, SEQLEN + 1)
    longest_row = jax.random.randint(key_longest, (SLOTS,), 0, MICRO)
    return jnp.where(jnp.arange(MICRO)[:, None] == longest_row[None, :], SEQLEN, drawn_lengths).astype(jnp.int32)


def level_of(key, shape, pieces, least, largest):
    factor_of = 1.0
    for dim, shards_of in pieces:
        steps = jax.random.uniform(jax.random.fold_in(jax.random.fold_in(key, 6), dim), (shards_of,), jnp.float32, least / len(pieces), largest / len(pieces))
        factor_of = factor_of * jnp.repeat(jnp.exp(steps), shape[dim] // shards_of).reshape((-1,) + (1,) * (len(shape) - 1 - dim))
    return factor_of


def centred(own_key, shape, scale, reach, shards=(), kind=jnp.bfloat16):
    level = level_of(own_key, shape, shards, -0.22, 0.18) if shards else 1.0
    values = jax.random.normal(own_key, shape, jnp.float32) * scale * level
    return jnp.minimum(jnp.maximum(values, -reach), reach).astype(kind)


def setup_inputs(seed: int = 0) -> dict:
    key_list = jax.random.split(jax.random.key(seed), 13)
    return {
        "inputs": centred(key_list[0], (MICRO, SLOTS, SEQLEN, D), 1.0, 6.0, ((1, 4), (2, 4))),
        "cotangent": centred(key_list[1], (MICRO, SLOTS, SEQLEN, D), 1.0, 6.0, ((1, 4), (2, 4))),
        "lengths": draw_lengths(jax.random.fold_in(key_list[12], 71), 0),
        "gain_in": jnp.clip(1.0 + 0.15 * jax.random.normal(key_list[3], (N_SECTION, D), jnp.float32), 0.25, 1.75).astype(jnp.bfloat16),
        "w_in": centred(key_list[4], (N_SECTION, D, PROJ), D ** -0.5, 0.125, ((0, 2), (1, 4))),
        "conv_w": centred(key_list[5], (N_SECTION, KERNEL, CHANNELS), 0.5, 3.0, ((0, 2), (2, 4))),
        "conv_b": centred(key_list[6], (N_SECTION, CHANNELS), 0.5, 3.0, ((0, 2), (1, 4))),
        "dt_bias": jnp.clip(-6.0 + 4.0 * jax.random.uniform(key_list[7], (N_SECTION, HEADS), jnp.float32) ** level_of(key_list[7], (N_SECTION, HEADS), ((0, 2), (1, 4)), -0.2, 0.2), -6.0, -2.0).astype(jnp.bfloat16),
        "a_log": jnp.clip(-6.0 + 5.0 * jax.random.uniform(key_list[8], (N_SECTION, HEADS), jnp.float32) ** level_of(key_list[8], (N_SECTION, HEADS), ((0, 2), (1, 4)), -0.2, 0.2), -6.0, -1.0).astype(jnp.bfloat16),
        "d_skip": centred(key_list[9], (N_SECTION, HEADS), 1.0, 3.0, ((0, 2), (1, 4))),
        "gain_out": jnp.clip(1.0 + 0.15 * jax.random.normal(key_list[10], (N_SECTION, INNER), jnp.float32), 0.25, 1.75).astype(jnp.bfloat16),
        "w_out": centred(key_list[11], (N_SECTION, INNER, D), INNER ** -0.5, 0.09375, ((0, 2), (1, 4))),
    }


norm_eps = 1e-05
highest = lax.Precision.HIGHEST

@jax.custom_vjp
def low(v):
    return lax.optimization_barrier(v.astype(jnp.bfloat16)).astype(jnp.float32)

@jax.custom_vjp
def low_back(v):
    return v

def low_keep(v):
    return (low(v), None)

def low_pass(kept, grad):
    return (grad,)

def back_keep(v):
    return (v, None)

def back_low(kept, grad):
    return (low(grad),)
low.defvjp(low_keep, low_pass)
low_back.defvjp(back_keep, back_low)

def rms_part(hidden, gain_vec):
    return hidden * lax.rsqrt(lax.optimization_barrier(jnp.mean(hidden * hidden, axis=-1, keepdims=True)) + norm_eps) * gain_vec

def conv_part(projected, edge_rows, conv_taps, conv_shift, dt_shift, decay_param):
    tokens_here = projected.shape[0]
    gate_z = projected[:, :INNER]
    conv_input = projected[:, INNER:INNER + CHANNELS]
    dt_input = projected[:, INNER + CHANNELS:]
    padded = jnp.concatenate([edge_rows, conv_input], axis=0)
    filtered = conv_shift[None, :] + sum((conv_taps[tap_index][None, :] * padded[tap_index:tap_index + tokens_here] for tap_index in range(KERNEL)))
    activated = jax.nn.silu(filtered)
    x_values = activated[:, :INNER]
    b_coeffs = activated[:, INNER:INNER + STATE]
    c_coeffs = activated[:, INNER + STATE:]
    dt_values = jax.nn.softplus(dt_input + dt_shift[None, :])
    decay_cum = jnp.cumsum(dt_values * (-jnp.exp(decay_param))[None, :], axis=0)
    return (gate_z, x_values, b_coeffs, c_coeffs, dt_values, decay_cum)

def mix_part(gate_z, x_values, b_coeffs, c_coeffs, dt_values, decay_cum, state_in, skip_gain, out_gain):
    tokens_here = x_values.shape[0]
    match_scores = jnp.dot(c_coeffs, b_coeffs.T, precision=highest)
    causal_mask = (jnp.arange(tokens_here)[:, None] >= jnp.arange(tokens_here)[None, :])[None]
    cum_heads = decay_cum.T
    log_gaps = cum_heads[:, :, None] - cum_heads[:, None, :]
    decay_matrix = jnp.where(causal_mask, jnp.exp(jnp.where(causal_mask, log_gaps, 0.0)), 0.0) * match_scores[None]
    head_values = x_values.reshape(tokens_here, HEADS, HEAD_DIM)
    scaled_values = head_values * dt_values[:, :, None]
    within = jnp.einsum('hts,shp->thp', decay_matrix, scaled_values, precision=highest)
    carried = jnp.einsum('tn,hpn->thp', c_coeffs, state_in, precision=highest) * jnp.exp(decay_cum)[:, :, None]
    ssm_out = within + carried + skip_gain[None, :, None] * head_values
    gated_out = ssm_out.reshape(tokens_here, INNER) * jax.nn.silu(gate_z)
    return rms_part(gated_out, out_gain)

def state_part(x_values, b_coeffs, dt_values, decay_cum):
    final_log = decay_cum[-1]
    weighting = jnp.exp(final_log[None, :] - decay_cum) * dt_values
    head_values = x_values.reshape(-1, HEADS, HEAD_DIM) * weighting[:, :, None]
    return (jnp.exp(final_log), jnp.einsum('thp,tn->hpn', head_values, b_coeffs, precision=highest))

def layer(hidden, valid, params):
    gain_in, w_in, conv_w, conv_b, dt_bias, a_log, d_skip, gain_out, w_out = params
    seq_count, seq_length = (hidden.shape[0], hidden.shape[1])
    normed_in = low(rms_part(hidden, gain_in))
    projected = low_back(jnp.einsum('bsd,dp->bsp', normed_in, w_in, precision=highest))
    blocks_all = projected.reshape(seq_count, seq_length // TOK_SEQ, TOK_SEQ, PROJ).transpose(1, 0, 2, 3)

    def advance(carry_pair, block_rows):
        edge_rows, state_now = carry_pair
        features = jax.vmap(conv_part, in_axes=(0, 0, None, None, None, None))(block_rows, edge_rows, conv_w, conv_b, dt_bias, a_log)
        normed_rows = jax.vmap(mix_part, in_axes=(0, 0, 0, 0, 0, 0, 0, None, None))(*features, state_now, d_skip, gain_out)
        decay_total, state_local = jax.vmap(state_part)(features[1], features[2], features[4], features[5])
        state_next = decay_total[:, :, None, None] * state_now + state_local
        edge_next = block_rows[:, TOK_SEQ - (KERNEL - 1):, INNER:INNER + CHANNELS]
        return ((edge_next, state_next), normed_rows)
    initial = (jnp.zeros((seq_count, KERNEL - 1, CHANNELS), jnp.float32), jnp.zeros((seq_count, HEADS, HEAD_DIM, STATE), jnp.float32))
    _, normed_blocks = lax.scan(jax.checkpoint(advance), initial, blocks_all)
    normed = low(normed_blocks.transpose(1, 0, 2, 3).reshape(seq_count, seq_length, INNER))
    mixed = low_back(jnp.einsum('bse,ed->bsd', normed, w_out, precision=highest))
    return (valid * (hidden + mixed), mixed)

def reference(inputs, cotangent, lengths, gain_in, w_in, conv_w, conv_b, dt_bias, a_log, d_skip, gain_out, w_out):
    seq_count = MICRO * SLOTS
    hidden = inputs.astype(jnp.float32).reshape(seq_count, SEQLEN, D)
    positions = jnp.arange(SEQLEN, dtype=jnp.int32)
    valid = (positions[None, :] < lengths.reshape(seq_count, 1).astype(jnp.int32)).astype(jnp.float32)[:, :, None]
    stacked = tuple((weight.astype(jnp.float32) for weight in (gain_in, w_in, conv_w, conv_b, dt_bias, a_log, d_skip, gain_out, w_out)))
    pulls = []
    outputs = []
    statistics = []
    for section_id in range(N_SECTION):
        params = tuple((weight[section_id] for weight in stacked))
        result, pull_fn, mixed = jax.vjp(lambda act, par: layer(act, valid, par), hidden, params, has_aux=True)
        pulls.append(pull_fn)
        outputs.append(result.astype(jnp.bfloat16).reshape(MICRO, SLOTS, SEQLEN, D))
        counted = jnp.sum(valid) * D
        statistics.append(jnp.stack([jnp.sqrt(jnp.sum(result * result) / counted), jnp.sqrt(jnp.sum((valid * mixed) ** 2) / counted)]))
        hidden = low(result)
    incoming = cotangent.astype(jnp.float32).reshape(seq_count, SEQLEN, D)
    in_grads = [None] * N_SECTION
    weight_grads = [None] * N_SECTION
    for section_id in reversed(range(N_SECTION)):
        grad_hidden, grad_params = pulls[section_id](incoming)
        in_grads[section_id] = grad_hidden.reshape(MICRO, SLOTS, SEQLEN, D)
        weight_grads[section_id] = grad_params
        incoming = low(grad_hidden)
    grads = [jnp.stack([weight_grads[section_id][which] for section_id in range(N_SECTION)]) for which in range(9)]
    return (jnp.stack(outputs), jnp.stack(in_grads), grads[0], grads[1], grads[2], grads[3], grads[4], grads[5], grads[6], grads[7], grads[8], jnp.stack(statistics))
```

```python
import functools

import jax
import jax.numpy as jnp
from jax import lax
from jax.experimental import pallas as pl
from jax.experimental.pallas import tpu as pltpu
from jax.sharding import PartitionSpec as P

D = 2048
INNER = 4096
HEADS = 64
HEAD_DIM = 64
STATE = 128
KERNEL = 4
GROUP = 2 * STATE
CHANNELS = INNER + GROUP
LANES = 128
EPS = 1e-05
F32 = jnp.float32
BF16 = jnp.bfloat16
VMEM_BYTES = 48 * 1024 * 1024


def dot32(a, b, ca, cb):
    return lax.dot_general(
        a,
        b,
        (((ca,), (cb,)), ((), ())),
        precision=lax.Precision.HIGHEST,
        preferred_element_type=F32,
    )


def step_sizes(raw, hp, rows):
    shifted = raw + hp[0:1, :]
    dt = jnp.maximum(shifted, 0.0) + jnp.log1p(jnp.exp(-jnp.abs(shifted)))
    decay = dt * hp[1:2, :]
    row = lax.broadcasted_iota(jnp.int32, (rows, rows), 0)
    col = lax.broadcasted_iota(jnp.int32, (rows, rows), 1)
    lower = (row >= col).astype(F32)
    cum = dot32(lower, decay, 1, 0)
    cum_t = dot32(decay, lower, 0, 1)
    return shifted, dt, cum, cum_t, row, col, lower


def spread(v, table):
    hi = v.astype(BF16)
    rest = v - hi.astype(F32)
    mid = rest.astype(BF16)
    low = (rest - mid.astype(F32)).astype(BF16)
    one = lambda p: jnp.dot(p, table, preferred_element_type=F32)
    return one(hi) + one(mid) + one(low)


def forward_kernel(f_ref, pz, px, pbd, cw, hp, table, s0, e0, *rest, second):
    if second:
        dn, gain, y_ref, filt_ref, st_ref, fin_ref, stat_ref, state, xp, xw_s = rest
    else:
        y_ref, filt_ref, st_ref, fin_ref, stat_ref, state, xp, xw_s = rest
    i = pl.program_id(0)
    rows, width = px.shape

    @pl.when(i == 0)
    def _():
        state[...] = s0[...]
        xp[0:8, :] = e0[...]

    xp[8 : 8 + rows, :width] = px[...]
    xp[8 : 8 + rows, width:] = pbd[:, :GROUP]

    def conv_tile(lo):
        acc = cw[4:5, lo : lo + LANES]
        for k in range(KERNEL):
            acc = acc + cw[k : k + 1, lo : lo + LANES] * xp[5 + k : 5 + k + rows, lo : lo + LANES]
        filt_ref[:, lo : lo + LANES] = acc
        return acc * jax.nn.sigmoid(acc)

    b_c = conv_tile(width)
    c_c = conv_tile(width + STATE)
    _, dt, cum, cum_t, row, col, _ = step_sizes(pbd[:, GROUP:], hp, rows)
    last = cum[rows - 1 : rows, :]
    dt_e = spread(dt, table[...])
    ecum_e = spread(jnp.exp(cum), table[...])
    w_e = spread(jnp.exp(last - cum) * dt, table[...])
    last_e = spread(jnp.broadcast_to(jnp.exp(last), (8, last.shape[1])), table[...])
    skip_e = spread(jnp.broadcast_to(hp[2:3, :], (8, last.shape[1])), table[...])
    st_ref[0] = state[...]
    carried = dot32(c_c, state[...], 1, 0)
    scores = dot32(c_c, b_c, 1, 1)
    causal = row >= col
    lane = lax.broadcasted_iota(jnp.int32, (rows, LANES), 1)
    first = lane < HEAD_DIM
    ss = jnp.zeros((rows, LANES), F32)
    s2 = jnp.zeros((rows, LANES), F32)
    for j in range(width // LANES):
        lo = j * LANES
        here = slice(lo, lo + LANES)
        x = conv_tile(lo)
        xd = x * dt_e[:, here]
        parts = []
        for h in (2 * j, 2 * j + 1):
            gap = cum[:, h : h + 1] - cum_t[h : h + 1, :]
            m = jnp.exp(jnp.where(causal, gap, -1e30)) * scores
            parts.append(dot32(m, xd, 1, 0))
        y = (
            jnp.where(first, parts[0], parts[1])
            + carried[:, here] * ecum_e[:, here]
            + skip_e[0:1, here] * x
        )
        y_ref[:, here] = y
        xw_s[:, here] = x * w_e[:, here]
        z = pz[:, here]
        g = y * z * jax.nn.sigmoid(z)
        ss = ss + g * g
        if second:
            s2 = s2 + g * dn[:, here] * gain[0:1, here]
    state[...] = state[...] * last_e[0:1, :] + dot32(b_c, xw_s[...], 0, 0)
    fin_ref[...] = state[...]
    xp[0:8, :] = xp[rows : rows + 8, :]
    stat_ref[:, 0:1] = jnp.sum(ss, axis=1, keepdims=True)
    stat_ref[:, 1:2] = jnp.sum(s2, axis=1, keepdims=True)


def backward_kernel(
    f_ref,
    pz,
    px,
    pbd,
    y_ref,
    filt,
    dn,
    rc,
    st_in,
    st_out,
    cw,
    hp,
    table,
    gain,
    g0,
    e0,
    dz_ref,
    dx_ref,
    dbc_ref,
    ddt_ref,
    dgain_ref,
    dconv_ref,
    dhp_ref,
    gfin_ref,
    efin_ref,
    grad,
    dfp,
    both,
    xw_s,
    dyc_s,
    rowv,
):
    i = pl.program_id(0)
    rows, width = px.shape
    heads = hp.shape[1]

    @pl.when(i == 0)
    def _():
        grad[...] = g0[...]
        dfp[rows : rows + 8, :] = e0[...]
        dgain_ref[...] = jnp.zeros_like(dgain_ref)
        dconv_ref[...] = jnp.zeros_like(dconv_ref)
        dhp_ref[...] = jnp.zeros_like(dhp_ref)

    def silu_pair(v):
        s = jax.nn.sigmoid(v)
        a = v * s
        return a, s * (1.0 + v - a)

    b_c, b_d = silu_pair(filt[:, width : width + STATE])
    c_c, c_d = silu_pair(filt[:, width + STATE :])
    shifted, dt, cum, cum_t, row, col, lower = step_sizes(pbd[:, GROUP:], hp, rows)
    last = cum[rows - 1 : rows, :]
    tail = jnp.exp(last - cum)
    dt_e = spread(dt, table[...])
    ecum_e = spread(jnp.exp(cum), table[...])
    tail_e = spread(tail, table[...])
    last_e = spread(jnp.broadcast_to(jnp.exp(last), (8, heads)), table[...])
    skip_e = spread(jnp.broadcast_to(hp[2:3, :], (8, heads)), table[...])
    k_all = dot32(b_c, grad[...], 1, 0)
    scores_t = dot32(b_c, c_c, 1, 1)
    causal_t = row <= col
    lane = lax.broadcasted_iota(jnp.int32, (rows, LANES), 1)
    first = lane < HEAD_DIM
    dcb_t = jnp.zeros((rows, rows), F32)
    r = rc[:, 0:1]
    coef = rc[:, 1:2]
    rowv[0:1, :] = jnp.sum(grad[...] * st_out[0], axis=0, keepdims=True)
    for j in range(width // LANES):
        lo = j * LANES
        here = slice(lo, lo + LANES)
        z = pz[:, here]
        y = y_ref[:, here]
        sz, dsz = silu_pair(z)
        g = y * sz
        dnt = dn[:, here]
        dg = dnt * gain[0:1, here] * r - g * coef
        dgain_ref[0:1, here] += jnp.sum(dnt * g * r, axis=0, keepdims=True)
        dy = dg * sz
        dz_ref[:, here] = (dg * y * dsz).astype(BF16)
        x, xder = silu_pair(filt[:, here])
        xd = x * dt_e[:, here]
        parts = []
        for n, h in enumerate((2 * j, 2 * j + 1)):
            gap = cum_t[h : h + 1, :] - cum[:, h : h + 1]
            decay_t = jnp.exp(jnp.where(causal_t, gap, -1e30))
            parts.append(dot32(decay_t * scores_t, dy, 1, 0))
            keep = first if n == 0 else jnp.logical_not(first)
            dcb_t = dcb_t + decay_t * dot32(jnp.where(keep, xd, 0.0), dy, 1, 1)
        v = jnp.where(first, parts[0], parts[1]) + k_all[:, here] * tail_e[:, here]
        skip = skip_e[0:1, here]
        dx = dt_e[:, here] * v + skip * dy
        both[0:rows, here] = x * v
        both[rows : 2 * rows, here] = dy * (y - skip * x)
        rowv[1:2, here] = jnp.sum(dy * x, axis=0, keepdims=True)
        xw_s[:, here] = xd * tail_e[:, here]
        dyc_s[:, here] = dy * ecum_e[:, here]
        dfp[0:rows, here] = dx * xder
    dc = dot32(dcb_t, b_c, 0, 0) + dot32(dyc_s[...], st_in[0], 1, 1)
    db = dot32(dcb_t, c_c, 1, 0) + dot32(xw_s[...], grad[...], 1, 1)
    dfp[0:rows, width : width + STATE] = db * b_d
    dfp[0:rows, width + STATE :] = dc * c_d
    grad[...] = grad[...] * last_e[0:1, :] + dot32(c_c, dyc_s[...], 0, 0)
    gfin_ref[...] = grad[...]

    table32 = table[...].astype(F32)
    sums = dot32(both[...], table32, 1, 1)
    rsums = dot32(rowv[...], table32, 1, 1)
    ddt_x = sums[0:rows]
    dcum = sums[rows : 2 * rows] - dt * ddt_x
    upto = lax.broadcasted_iota(jnp.int32, (rows, heads), 0)
    dcum = dcum + jnp.where(upto == rows - 1, rsums[0:1, :], 0.0)
    ddecay = dot32(lower, dcum, 0, 0)
    ddt = ddt_x + hp[1:2, :] * ddecay
    draw = ddt * jax.nn.sigmoid(shifted)
    ddt_ref[...] = draw
    dhp_ref[0:1, :] += jnp.sum(draw, axis=0, keepdims=True)
    dhp_ref[1:2, :] += jnp.sum(ddecay * dt, axis=0, keepdims=True) * hp[1:2, :]
    dhp_ref[2:3, :] += rsums[1:2, :]

    for lo in range(0, width + GROUP, LANES):
        here = slice(lo, lo + LANES)
        src = px[:, here] if lo < width else pbd[:, lo - width : lo - width + LANES]
        total = jnp.zeros((rows, LANES), F32)
        for k in range(KERNEL):
            shift = KERNEL - 1 - k
            moved = dfp[shift : shift + rows, here]
            total = total + cw[k : k + 1, here] * moved
            dconv_ref[k : k + 1, here] += jnp.sum(src * moved, axis=0, keepdims=True)
        dconv_ref[4:5, here] += jnp.sum(dfp[0:rows, here], axis=0, keepdims=True)
        if lo < width:
            dx_ref[:, here] = total.astype(BF16)
        else:
            dbc_ref[:, lo - width : lo - width + LANES] = total
    dfp[rows : rows + 8, :] = dfp[0:8, :]
    efin_ref[...] = dfp[0:8, :]


def whole(shape):
    return pl.BlockSpec(shape, lambda i, f: (0,) * len(shape))


def run_forward(f, pz, px, pbd, cw, hp, table, s0, e0, extra, rows):
    total, width = px.shape
    heads = hp.shape[1]
    count = total // rows
    block = lambda w: pl.BlockSpec((rows, w), lambda i, f: (jnp.bitwise_xor(i, f[0]), 0))
    in_specs = [
        block(width),
        block(width),
        block(GROUP + heads),
        whole((8, width + GROUP)),
        whole((8, heads)),
        whole((heads, width)),
        whole((STATE, width)),
        whole((8, width + GROUP)),
    ]
    if extra:
        in_specs += [block(width), whole((1, width))]
    shape = jax.ShapeDtypeStruct
    return pl.pallas_call(
        functools.partial(forward_kernel, second=bool(extra)),
        grid_spec=pltpu.PrefetchScalarGridSpec(
            num_scalar_prefetch=1,
            grid=(count,),
            in_specs=in_specs,
            out_specs=[
                block(width),
                block(width + GROUP),
                pl.BlockSpec((1, STATE, width), lambda i, f: (i, 0, 0)),
                whole((STATE, width)),
                block(8),
            ],
            scratch_shapes=[
                pltpu.VMEM((STATE, width), F32),
                pltpu.VMEM((rows + 8, width + GROUP), F32),
                pltpu.VMEM((rows, width), F32),
            ],
        ),
        out_shape=[
            shape((total, width), F32),
            shape((total, width + GROUP), F32),
            shape((count, STATE, width), F32),
            shape((STATE, width), F32),
            shape((total, 8), F32),
        ],
        compiler_params=pltpu.CompilerParams(vmem_limit_bytes=VMEM_BYTES),
        name="scan_forward",
    )(f, pz, px, pbd, cw, hp, table, s0, e0, *extra)


def run_backward(f, pz, px, pbd, y, filt, dn, rc, states, cw, hp, table, gain, g0, e0, rows):
    total, width = px.shape
    heads = hp.shape[1]
    count = total // rows
    turn = lambda i: count - 1 - i
    block = lambda w: pl.BlockSpec((rows, w), lambda i, f: (jnp.bitwise_xor(turn(i), f[0]), 0))
    shape = jax.ShapeDtypeStruct
    return pl.pallas_call(
        backward_kernel,
        grid_spec=pltpu.PrefetchScalarGridSpec(
            num_scalar_prefetch=1,
            grid=(count,),
            in_specs=[
                block(width),
                block(width),
                block(GROUP + heads),
                block(width),
                block(width + GROUP),
                block(width),
                block(8),
                pl.BlockSpec((1, STATE, width), lambda i, f: (turn(i), 0, 0)),
                pl.BlockSpec((1, STATE, width), lambda i, f: (turn(i) + 1, 0, 0)),
                whole((8, width + GROUP)),
                whole((8, heads)),
                whole((heads, width)),
                whole((1, width)),
                whole((STATE, width)),
                whole((8, width + GROUP)),
            ],
            out_specs=[
                block(width),
                block(width),
                block(GROUP),
                block(heads),
                whole((8, width)),
                whole((8, width + GROUP)),
                whole((8, heads)),
                whole((STATE, width)),
                whole((8, width + GROUP)),
            ],
            scratch_shapes=[
                pltpu.VMEM((STATE, width), F32),
                pltpu.VMEM((rows + 8, width + GROUP), F32),
                pltpu.VMEM((2 * rows, width), F32),
                pltpu.VMEM((rows, width), F32),
                pltpu.VMEM((rows, width), F32),
                pltpu.VMEM((8, width), F32),
            ],
        ),
        out_shape=[
            shape((total, width), BF16),
            shape((total, width), BF16),
            shape((total, GROUP), F32),
            shape((total, heads), F32),
            shape((8, width), F32),
            shape((8, width + GROUP), F32),
            shape((8, heads), F32),
            shape((STATE, width), F32),
            shape((8, width + GROUP), F32),
        ],
        compiler_params=pltpu.CompilerParams(vmem_limit_bytes=VMEM_BYTES),
        name="scan_backward",
    )(f, pz, px, pbd, y, filt, dn, rc, states, states, cw, hp, table, gain, g0, e0)


def swap_section(v):
    return lax.ppermute(v, "section", [(0, 1), (1, 0)])


def move_fsdp(v, m):
    n = lax.axis_size("fsdp")
    return lax.ppermute(v, "fsdp", [(i, i ^ m) for i in range(n)])


def transpose_places(v):
    n, s = lax.axis_size("fsdp"), lax.axis_size("seq")
    pairs = [
        ((j * n + i) * n + k, (j * n + k) * n + i)
        for j in range(s // n)
        for i in range(n)
        for k in range(n)
    ]
    return lax.ppermute(v, ("seq", "fsdp"), pairs)


def gather_blocks(v):
    n = lax.axis_size("fsdp")
    return jnp.stack([v] + [move_fsdp(v, m) for m in range(1, n)])


def gather_in_order(v, f):
    n = lax.axis_size("fsdp")
    out = jnp.zeros((n,) + v.shape, v.dtype)
    for m in range(n):
        piece = v if m == 0 else move_fsdp(v, m)
        out = lax.dynamic_update_index_in_dim(out, piece, f ^ m, 0)
    return out


def scatter_sum(partial):
    n = lax.axis_size("fsdp")
    total = partial[0]
    for m in range(1, n):
        total = total + move_fsdp(partial[m].astype(BF16), m).astype(F32)
    return total


def sum_rows(v):
    n = lax.axis_size("fsdp")
    total = v
    for m in range(1, n):
        got = move_fsdp(v, m)
        total = total + jnp.stack([got[j ^ m] for j in range(n)])
    return total


def relay(total, local, reverse):
    n, s = lax.axis_size("fsdp"), lax.axis_size("seq")
    segments = s // n
    place = lax.axis_index("seq") // n
    own = lax.axis_index("seq") % n
    totals = lax.all_gather(total, "seq")
    locals_ = lax.all_gather(local, "seq")
    state = jnp.zeros_like(local)
    order = range(segments - 1, -1, -1) if reverse else range(segments)
    for j in order:
        use = (j > place) if reverse else (j < place)
        t = lax.dynamic_index_in_dim(totals, j * n + own, 0, False)
        v = lax.dynamic_index_in_dim(locals_, j * n + own, 0, False)
        state = jnp.where(use, t * state + v, state)
    return state


def next_segment(v, step):
    n, s = lax.axis_size("fsdp"), lax.axis_size("seq")
    pairs = [(k, k + step * n) for k in range(s) if 0 <= k + step * n < s]
    return lax.ppermute(v, "seq", pairs)


def dot_rows(a, b):
    return lax.dot_general(a, b, (((0,), (0,)), ((), ())), preferred_element_type=F32)


def dot_cols(a, b):
    return lax.dot_general(a, b, (((1,), (1,)), ((), ())), preferred_element_type=F32)


def normalised(h, gain):
    return h * lax.rsqrt(jnp.mean(h * h, axis=-1, keepdims=True) + EPS) * gain


def per_device(
    inputs,
    cotangent,
    lengths,
    gain_in,
    w_in,
    conv_w,
    conv_b,
    dt_bias,
    a_log,
    d_skip,
    gain_out,
    w_out,
):
    n = lax.axis_size("fsdp")
    nz = lax.axis_size("seq")
    segments = nz // n
    c = lax.axis_index("section")
    f = lax.axis_index("fsdp")
    place = lax.axis_index("seq")
    upper = c == 0
    rows = inputs.shape[2]
    width = INNER // n
    heads = HEADS // n
    share = D // n
    group = GROUP // n
    f1 = f.reshape(1).astype(jnp.int32)

    def pick(a, b):
        return jnp.where(upper, a, b)

    own_in = lax.dynamic_index_in_dim(inputs, c, 0, False)[0]
    own_ct = lax.dynamic_index_in_dim(cotangent, c, 0, False)[0]
    own_len = lax.dynamic_index_in_dim(lengths, c, 0, False)
    length = transpose_places(own_len)
    start = ((place // n) * n + f) * rows
    valid = (start + jnp.arange(rows, dtype=jnp.int32) < length[0]).astype(F32)[:, None]
    h0 = transpose_places(own_in)
    dout1 = transpose_places(own_ct).astype(F32)
    all_h0 = gather_blocks(h0).reshape(n * rows, D)

    pack = jnp.concatenate(
        [
            gain_in[0],
            conv_w[0].reshape(-1),
            conv_b[0],
            dt_bias[0],
            a_log[0],
            d_skip[0],
            gain_out[0],
        ]
    )
    mine = gather_in_order(pack, f)
    theirs = swap_section(mine)
    small = []
    for full in (pick(mine, theirs), pick(theirs, mine)):
        full = full.astype(F32)
        at = 0

        def take(size):
            nonlocal at
            at += size
            return full[:, at - size : at]

        per = CHANNELS // n
        gain = take(share).reshape(1, D)
        taps = take(KERNEL * per).reshape(n, KERNEL, per).transpose(1, 0, 2).reshape(KERNEL, -1)
        bias = take(per).reshape(1, CHANNELS)
        table = jnp.concatenate([taps, bias, jnp.zeros((3, CHANNELS), F32)])
        cw = jnp.concatenate(
            [lax.dynamic_slice_in_dim(table, f * width, width, 1), table[:, INNER:]], axis=1
        )
        own_heads = [
            lax.dynamic_index_in_dim(take(heads), f, 0, True) for _ in range(3)
        ]
        hp = jnp.concatenate(
            [own_heads[0], -jnp.exp(own_heads[1]), own_heads[2], jnp.zeros((5, heads), F32)]
        )
        gout = lax.dynamic_index_in_dim(take(width), f, 0, True)
        small.append((gain, cw, hp, gout))

    w = w_in[0]

    def columns(k):
        cut = lambda at, size: lax.dynamic_slice_in_dim(w, at, size, 1)
        return (
            cut(k * width, width),
            cut(INNER + k * width, width),
            jnp.concatenate(
                [w[:, 2 * INNER : 2 * INNER + GROUP], cut(2 * INNER + GROUP + k * heads, heads)],
                axis=1,
            ),
        )

    blocks = [columns(f ^ m) for m in range(n)]

    def fetch(layer, blocks):
        full = [jnp.zeros((n,) + b.shape, BF16) for b in blocks[0]]
        for m in range(n):
            for q in range(3):
                piece = blocks[m][q]
                if m:
                    pairs = [(layer * n + i, layer * n + (i ^ m)) for i in range(n)]
                    piece = lax.ppermute(piece, ("section", "fsdp"), pairs)
                other = lax.ppermute(piece, "section", [(layer, 1 - layer)])
                got = jnp.where(c == layer, piece, other)
                full[q] = lax.dynamic_update_index_in_dim(full[q], got, f ^ m, 0)
        return [v.reshape(D, v.shape[-1]) for v in full]

    w0 = fetch(0, blocks)
    blocks, _ = lax.optimization_barrier((blocks, w0))
    w1 = fetch(1, blocks)
    wo_mine = w_out[0]
    wo_other = swap_section(wo_mine)
    wo = (pick(wo_mine, wo_other), pick(wo_other, wo_mine))
    win = (w0, w1)

    expand = (
        jnp.arange(heads)[:, None] == jnp.arange(width)[None, :] // HEAD_DIM
    ).astype(BF16)
    zero_state = jnp.zeros((STATE, width), F32)
    zero_edge = jnp.zeros((8, width + GROUP), F32)

    def project(normed, layer):
        return [
            jnp.dot(normed, part, preferred_element_type=F32) for part in win[layer]
        ]

    def scan(proj, layer, extra):
        pz, px, pbd = proj
        _, cw, hp, _ = small[layer]
        args = (f1, pz, px, pbd, cw, hp, expand)
        if segments == 1:
            return run_forward(*args, zero_state, zero_edge, extra, rows)
        rear = lax.dynamic_slice_in_dim(
            jnp.concatenate([px, pbd[:, :GROUP]], axis=1), ((n - 1) ^ f) * rows + rows - 8, 8, 0
        )
        edge = next_segment(rear, 1)
        local = run_forward(*args, zero_state, edge, extra, rows)[3]
        decay = jax.nn.softplus(pbd[:, GROUP:] + hp[0:1]) * hp[1:2]
        total = jnp.repeat(jnp.exp(jnp.sum(decay, axis=0)), HEAD_DIM)[None, :]
        state = relay(total, local, False)
        return run_forward(*args, state, edge, extra, rows)

    def unscan(proj, fwd, dn, rc, layer):
        pz, px, pbd = proj
        y, filt, states, final = fwd[:4]
        _, cw, hp, gout = small[layer]
        states = jnp.concatenate([states, final[None]])
        args = (f1, pz, px, pbd, y, filt, dn, rc, states, cw, hp, expand, gout)
        if segments == 1:
            return run_backward(*args, zero_state, zero_edge, rows)
        local = run_backward(*args, zero_state, zero_edge, rows)[7]
        decay = jax.nn.softplus(pbd[:, GROUP:] + hp[0:1]) * hp[1:2]
        total = jnp.repeat(jnp.exp(jnp.sum(decay, axis=0)), HEAD_DIM)[None, :]
        grad = relay(total, local, True)
        edge = next_segment(run_backward(*args, grad, zero_edge, rows)[8], -1)
        return run_backward(*args, grad, edge, rows)

    def gated(pz, y, r, layer):
        g = y * jax.nn.silu(pz)
        return (g * r * small[layer][3]).astype(BF16)

    blockwise = lambda v: v.reshape(n, rows, v.shape[-1])

    normed_in0 = normalised(all_h0.astype(F32), small[0][0]).astype(BF16)
    proj0 = project(normed_in0, 0)
    fwd0 = scan(proj0, 0, ())
    stat0 = sum_rows(blockwise(fwd0[4][:, 0:1])).reshape(n * rows, 1)
    r0 = lax.rsqrt(stat0 / INNER + EPS)
    normed0 = gated(proj0[0], fwd0[0], r0, 0)
    mixed0 = scatter_sum(blockwise(jnp.dot(normed0, wo[0], preferred_element_type=F32)))
    out0 = valid * (h0.astype(F32) + mixed0)
    h1 = out0.astype(BF16)

    part1 = normalised(h1.astype(F32), small[1][0]).astype(BF16)
    normed_in1 = gather_blocks(part1).reshape(n * rows, D)
    proj1 = project(normed_in1, 1)
    dmixed1 = gather_blocks((valid * dout1).astype(BF16)).reshape(n * rows, D)
    dn1 = dot_cols(dmixed1, wo[1])
    fwd1 = scan(proj1, 1, (dn1, small[1][3]))
    stat1 = sum_rows(blockwise(fwd1[4][:, 0:2])).reshape(n * rows, 2)
    r1 = lax.rsqrt(stat1[:, 0:1] / INNER + EPS)
    normed1 = gated(proj1[0], fwd1[0], r1, 1)
    mixed1 = scatter_sum(blockwise(jnp.dot(normed1, wo[1], preferred_element_type=F32)))
    out1 = valid * (h1.astype(F32) + mixed1)
    last1 = out1.astype(BF16)

    def half_sums(a, b, parts):
        view = a.reshape(a.shape[0], parts, 2, -1)
        cut = lambda k: lax.dynamic_index_in_dim(view, k, 2, False).reshape(a.shape[0], -1)
        away = swap_section(dot_rows(cut(1 - c), b).astype(BF16))
        return (dot_rows(cut(c), b) + away.astype(F32)).astype(BF16)

    def over_seq(v, dim):
        piece = lax.psum_scatter(v, "seq", scatter_dimension=dim, tiled=True)
        return piece

    def back_layer(layer, dn, dmixed, rc, proj, fwd, normed, normed_in):
        gw_out = half_sums(normed, dmixed, 1)
        dz, dx, dbc, ddt, dgain, dconv, dhp, _, _ = unscan(proj, fwd, dn, rc, layer)
        wz, wx, wbd = win[layer]
        shares = blockwise(dbc)
        own_cols = lambda k: lax.dynamic_slice_in_dim(shares, k * group, group, 2)
        total = own_cols(f)
        for m in range(1, n):
            got = move_fsdp(own_cols(f ^ m), m)
            total = total + jnp.stack([got[j ^ m] for j in range(n)])
        dsmall = jnp.concatenate([total.reshape(n * rows, group), ddt], axis=1).astype(BF16)
        wsmall = jnp.concatenate(
            [lax.dynamic_slice_in_dim(wbd, f * group, group, 1), wbd[:, GROUP:]], axis=1
        )
        back = dot_cols(dz, wz) + dot_cols(dx, wx) + dot_cols(dsmall, wsmall)
        dnormed_in = scatter_sum(blockwise(back))
        dproj = jnp.concatenate([dz, dx, dsmall], axis=1)
        gw_in = half_sums(normed_in, dproj, n)
        return dnormed_in, gw_in, gw_out, (dgain[0], dconv[:5], dhp[:3])

    def back_norm(dout, dnormed_in, h, gain):
        h = h.astype(F32)
        r = lax.rsqrt(jnp.mean(h * h, axis=-1, keepdims=True) + EPS)
        u = dnormed_in * gain
        mean = jnp.mean(u * h, axis=-1, keepdims=True)
        dgain = jnp.sum(dnormed_in * h * r, axis=0)
        return valid * dout + r * u - h * (r * r * r) * mean, dgain

    def combine(layer, gw_in, gw_out):
        a = over_seq(gw_in.reshape(n, share // 2, -1), 1)
        b = over_seq(gw_out, 0)
        full = jnp.zeros_like(a)
        for m in range(n):
            piece = lax.dynamic_index_in_dim(a, f ^ m, 0, False)
            if m:
                piece = move_fsdp(piece, m)
            full = lax.dynamic_update_index_in_dim(full, piece, f ^ m, 0)
        return (
            lax.all_gather(full, "seq", axis=1, tiled=True),
            lax.all_gather(b, "seq", axis=0, tiled=True),
        )

    rc1 = jnp.concatenate(
        [r1, (r1 * r1 * r1 / INNER) * stat1[:, 1:2], jnp.zeros((n * rows, 6), F32)], axis=1
    )
    dnin1, gwi1, gwo1, smalls1 = back_layer(
        1, dn1, dmixed1, rc1, proj1, fwd1, normed1, normed_in1
    )
    grad1, dgin1 = back_norm(dout1, dnin1, h1, small[1][0])
    full1 = combine(1, gwi1, gwo1)

    dout0 = grad1.astype(BF16).astype(F32)
    dmixed0_own = (valid * dout0).astype(BF16)
    dmixed0 = gather_blocks(dmixed0_own).reshape(n * rows, D)
    along = jnp.sum(dmixed0_own.astype(F32) * mixed0, axis=-1, keepdims=True)
    along0 = gather_blocks(along).reshape(n * rows, 1)
    dn0 = dot_cols(dmixed0, wo[0])
    rc0 = jnp.concatenate(
        [r0, (r0 * r0 / INNER) * along0, jnp.zeros((n * rows, 6), F32)], axis=1
    )
    dnin0, gwi0, gwo0, smalls0 = back_layer(
        0, dn0, dmixed0, rc0, proj0, fwd0, normed0, normed_in0
    )
    grad0, dgin0 = back_norm(dout0, dnin0, h0, small[0][0])
    full0 = combine(0, gwi0, gwo0)

    def packed(dgin, smalls, out, mixed):
        dgain, dconv, dhp = smalls
        put = lambda v, size, at: lax.dynamic_update_slice(
            jnp.zeros(v.shape[:-1] + (size,), F32), v, (0,) * (v.ndim - 1) + (at,)
        )
        conv = put(dconv[:, :width], CHANNELS, f * width)
        conv = conv.at[:, INNER:].set(dconv[:, width:])
        sums = jnp.stack(
            [jnp.sum(out * out), jnp.sum((valid * mixed) ** 2), jnp.sum(valid)]
        )
        return jnp.concatenate(
            [
                dgin,
                conv.reshape(-1),
                put(dhp, HEADS, f * heads).reshape(-1),
                put(dgain, INNER, f * width),
                sums,
            ]
        )

    everyone = ("section", "seq", "fsdp")
    p1 = lax.psum(packed(dgin1, smalls1, out1, mixed1), everyone)
    p0 = lax.psum(packed(dgin0, smalls0, out0, mixed0), everyone)
    p = pick(p0, p1)
    at = 0

    def take(size):
        nonlocal at
        at += size
        return p[at - size : at]

    mine_of = lambda v, size: lax.dynamic_slice_in_dim(v, f * size, size, v.ndim - 1)
    o_gain_in = mine_of(take(D), share)
    o_conv = mine_of(take(5 * CHANNELS).reshape(5, CHANNELS), CHANNELS // n)
    o_heads = mine_of(take(3 * HEADS).reshape(3, HEADS), heads)
    o_gain_out = mine_of(take(INNER), width)
    sums = take(3)
    act_rms = jnp.sqrt(sums[:2] / (sums[2] * D))[None]

    def owned(a, b):
        own, away = pick(a, b), swap_section(pick(b, a))
        return pick(own, away), pick(away, own)

    lo_in, hi_in = owned(full0[0], full1[0])
    cols = jnp.concatenate([lo_in, hi_in], axis=1).astype(F32)
    side = lambda v: v.transpose(1, 0, 2).reshape(share, -1)
    g_w_in = jnp.concatenate(
        [
            side(cols[:, :, :width]),
            side(cols[:, :, width : 2 * width]),
            side(cols[:, :, 2 * width : 2 * width + group]),
            side(cols[:, :, 2 * width + group :]),
        ],
        axis=1,
    )
    lo_out, hi_out = owned(full0[1], full1[1])
    g_w_out = jnp.concatenate([lo_out, hi_out], axis=0).astype(F32)

    def returned(a, b):
        own, away = pick(a, b), pick(b, a)
        own = transpose_places(own)
        away = swap_section(transpose_places(away))
        return jnp.stack([pick(own, away), pick(away, own)])

    layer_out = returned(h1, last1)
    in_grads = returned(grad0, grad1)
    return (
        layer_out[None, :, None],
        in_grads[None, :, None],
        o_gain_in[None],
        g_w_in[None],
        o_conv[None, :4],
        o_conv[None, 4],
        o_heads[None, 0],
        o_heads[None, 1],
        o_heads[None, 2],
        o_gain_out[None],
        g_w_out[None],
        act_rms,
    )


def solution(mesh):
    in_specs = (
        P(None, "fsdp", "seq", None),
        P(None, "fsdp", "seq", None),
        P(None, "fsdp"),
        P("section", "fsdp"),
        P("section", "fsdp", None),
        P("section", None, "fsdp"),
        P("section", "fsdp"),
        P("section", "fsdp"),
        P("section", "fsdp"),
        P("section", "fsdp"),
        P("section", "fsdp"),
        P("section", "fsdp", None),
    )
    out_specs = (
        P("section", None, "fsdp", "seq", None),
        P("section", None, "fsdp", "seq", None),
        P("section", "fsdp"),
        P("section", "fsdp", None),
        P("section", None, "fsdp"),
        P("section", "fsdp"),
        P("section", "fsdp"),
        P("section", "fsdp"),
        P("section", "fsdp"),
        P("section", "fsdp"),
        P("section", "fsdp", None),
        P("section", None),
    )
    return jax.shard_map(
        per_device, mesh=mesh, in_specs=in_specs, out_specs=out_specs, check_vma=False
    )
```

```python
import functools

import jax
import jax.numpy as jnp
from jax import lax
from jax.experimental import pallas as pl
from jax.experimental.pallas import tpu as pltpu
from jax.sharding import PartitionSpec as P

D = 2048
INNER = 4096
HEADS = 64
HEAD_DIM = 64
STATE = 128
KERNEL = 4
GROUP = 2 * STATE
CHANNELS = INNER + GROUP
LANES = 128
EPS = 1e-05
F32 = jnp.float32
BF16 = jnp.bfloat16
VMEM_BYTES = 48 * 1024 * 1024


def dot32(a, b, ca, cb):
    return lax.dot_general(
        a,
        b,
        (((ca,), (cb,)), ((), ())),
        precision=lax.Precision.HIGHEST,
        preferred_element_type=F32,
    )


def step_sizes(raw, hp, rows):
    shifted = raw + hp[0:1, :]
    dt = jnp.maximum(shifted, 0.0) + jnp.log1p(jnp.exp(-jnp.abs(shifted)))
    decay = dt * hp[1:2, :]
    row = lax.broadcasted_iota(jnp.int32, (rows, rows), 0)
    col = lax.broadcasted_iota(jnp.int32, (rows, rows), 1)
    lower = (row >= col).astype(F32)
    cum = dot32(lower, decay, 1, 0)
    cum_t = dot32(decay, lower, 0, 1)
    return shifted, dt, cum, cum_t, row, col, lower


def spread(v, table):
    hi = v.astype(BF16)
    rest = v - hi.astype(F32)
    mid = rest.astype(BF16)
    low = (rest - mid.astype(F32)).astype(BF16)
    one = lambda p: jnp.dot(p, table, preferred_element_type=F32)
    return one(hi) + one(mid) + one(low)


def forward_kernel(f_ref, pzx, pbd, cw, hp, table, s0, e0, *rest, second):
    if second:
        dn, gain, y_ref, filt_ref, st_ref, fin_ref, stat_ref, state, xp, xw_s = rest
    else:
        y_ref, filt_ref, st_ref, fin_ref, stat_ref, state, xp, xw_s = rest
    i = pl.program_id(0)
    rows, width = y_ref.shape

    @pl.when(i == 0)
    def _():
        state[...] = s0[...]
        xp[0:8, :] = e0[...]

    xp[8 : 8 + rows, :width] = pzx[:, width:]
    xp[8 : 8 + rows, width:] = pbd[:, :GROUP]

    def conv_tile(lo):
        acc = cw[4:5, lo : lo + LANES]
        for k in range(KERNEL):
            acc = acc + cw[k : k + 1, lo : lo + LANES] * xp[5 + k : 5 + k + rows, lo : lo + LANES]
        filt_ref[:, lo : lo + LANES] = acc
        return acc * jax.nn.sigmoid(acc)

    b_c = conv_tile(width)
    c_c = conv_tile(width + STATE)
    _, dt, cum, cum_t, row, col, _ = step_sizes(pbd[:, GROUP:], hp, rows)
    last = cum[rows - 1 : rows, :]
    dt_e = spread(dt, table[...])
    ecum_e = spread(jnp.exp(cum), table[...])
    w_e = spread(jnp.exp(last - cum) * dt, table[...])
    last_e = spread(jnp.broadcast_to(jnp.exp(last), (8, last.shape[1])), table[...])
    skip_e = spread(jnp.broadcast_to(hp[2:3, :], (8, last.shape[1])), table[...])
    st_ref[0] = state[...]
    carried = dot32(c_c, state[...], 1, 0)
    scores = dot32(c_c, b_c, 1, 1)
    causal = row >= col
    lane = lax.broadcasted_iota(jnp.int32, (rows, LANES), 1)
    first = lane < HEAD_DIM
    ss = jnp.zeros((rows, LANES), F32)
    s2 = jnp.zeros((rows, LANES), F32)
    for j in range(width // LANES):
        lo = j * LANES
        here = slice(lo, lo + LANES)
        x = conv_tile(lo)
        xd = x * dt_e[:, here]
        parts = []
        for h in (2 * j, 2 * j + 1):
            gap = cum[:, h : h + 1] - cum_t[h : h + 1, :]
            m = jnp.exp(jnp.where(causal, gap, -1e30)) * scores
            parts.append(dot32(m, xd, 1, 0))
        y = (
            jnp.where(first, parts[0], parts[1])
            + carried[:, here] * ecum_e[:, here]
            + skip_e[0:1, here] * x
        )
        y_ref[:, here] = y
        xw_s[:, here] = x * w_e[:, here]
        z = pzx[:, here]
        g = y * z * jax.nn.sigmoid(z)
        ss = ss + g * g
        if second:
            s2 = s2 + g * dn[:, here] * gain[0:1, here]
    state[...] = state[...] * last_e[0:1, :] + dot32(b_c, xw_s[...], 0, 0)
    fin_ref[...] = state[...]
    xp[0:8, :] = xp[rows : rows + 8, :]
    ones = jnp.ones((8, LANES), F32)
    stat_ref[0, 0:1, :] = dot32(ones, ss, 1, 1)[0:1]
    stat_ref[0, 1:2, :] = dot32(ones, s2, 1, 1)[0:1]


def backward_kernel(
    f_ref,
    pzx,
    pbd,
    y_ref,
    filt,
    dn,
    rc,
    st_in,
    st_out,
    cw,
    hp,
    table,
    gain,
    g0,
    e0,
    dzx_ref,
    dbc_ref,
    ddt_ref,
    dgain_ref,
    dconv_ref,
    dhp_ref,
    gfin_ref,
    efin_ref,
    grad,
    dfp,
    both,
    xw_s,
    dyc_s,
    rowv,
):
    i = pl.program_id(0)
    rows, width = y_ref.shape
    heads = hp.shape[1]

    @pl.when(i == 0)
    def _():
        grad[...] = g0[...]
        dfp[rows : rows + 8, :] = e0[...]
        dgain_ref[...] = jnp.zeros_like(dgain_ref)
        dconv_ref[...] = jnp.zeros_like(dconv_ref)
        dhp_ref[...] = jnp.zeros_like(dhp_ref)

    def silu_pair(v):
        s = jax.nn.sigmoid(v)
        a = v * s
        return a, s * (1.0 + v - a)

    b_c, b_d = silu_pair(filt[:, width : width + STATE])
    c_c, c_d = silu_pair(filt[:, width + STATE :])
    shifted, dt, cum, cum_t, row, col, lower = step_sizes(pbd[:, GROUP:], hp, rows)
    last = cum[rows - 1 : rows, :]
    tail = jnp.exp(last - cum)
    dt_e = spread(dt, table[...])
    ecum_e = spread(jnp.exp(cum), table[...])
    tail_e = spread(tail, table[...])
    last_e = spread(jnp.broadcast_to(jnp.exp(last), (8, heads)), table[...])
    skip_e = spread(jnp.broadcast_to(hp[2:3, :], (8, heads)), table[...])
    k_all = dot32(b_c, grad[...], 1, 0)
    scores_t = dot32(b_c, c_c, 1, 1)
    causal_t = row <= col
    lane = lax.broadcasted_iota(jnp.int32, (rows, LANES), 1)
    first = lane < HEAD_DIM
    dcb_t = jnp.zeros((rows, rows), F32)
    rc_t = dot32((row == col).astype(F32), rc[0], 1, 1)
    r = rc_t[:, 0:1]
    coef = rc_t[:, 1:2]
    rowv[0:1, :] = jnp.sum(grad[...] * st_out[0], axis=0, keepdims=True)
    for j in range(width // LANES):
        lo = j * LANES
        here = slice(lo, lo + LANES)
        z = pzx[:, here]
        y = y_ref[:, here]
        sz, dsz = silu_pair(z)
        g = y * sz
        dnt = dn[:, here]
        dg = dnt * gain[0:1, here] * r - g * coef
        dgain_ref[0:1, here] += jnp.sum(dnt * g * r, axis=0, keepdims=True)
        dy = dg * sz
        dzx_ref[:, here] = (dg * y * dsz).astype(BF16)
        x, xder = silu_pair(filt[:, here])
        xd = x * dt_e[:, here]
        parts = []
        for n, h in enumerate((2 * j, 2 * j + 1)):
            gap = cum_t[h : h + 1, :] - cum[:, h : h + 1]
            decay_t = jnp.exp(jnp.where(causal_t, gap, -1e30))
            parts.append(dot32(decay_t * scores_t, dy, 1, 0))
            keep = first if n == 0 else jnp.logical_not(first)
            dcb_t = dcb_t + decay_t * dot32(jnp.where(keep, xd, 0.0), dy, 1, 1)
        v = jnp.where(first, parts[0], parts[1]) + k_all[:, here] * tail_e[:, here]
        skip = skip_e[0:1, here]
        dx = dt_e[:, here] * v + skip * dy
        both[0:rows, here] = x * v
        both[rows : 2 * rows, here] = dy * (y - skip * x)
        rowv[1:2, here] = jnp.sum(dy * x, axis=0, keepdims=True)
        xw_s[:, here] = xd * tail_e[:, here]
        dyc_s[:, here] = dy * ecum_e[:, here]
        dfp[0:rows, here] = dx * xder
    dc = dot32(dcb_t, b_c, 0, 0) + dot32(dyc_s[...], st_in[0], 1, 1)
    db = dot32(dcb_t, c_c, 1, 0) + dot32(xw_s[...], grad[...], 1, 1)
    dfp[0:rows, width : width + STATE] = db * b_d
    dfp[0:rows, width + STATE :] = dc * c_d
    grad[...] = grad[...] * last_e[0:1, :] + dot32(c_c, dyc_s[...], 0, 0)
    gfin_ref[...] = grad[...]

    table32 = table[...].astype(F32)
    sums = dot32(both[...], table32, 1, 1)
    rsums = dot32(rowv[...], table32, 1, 1)
    ddt_x = sums[0:rows]
    dcum = sums[rows : 2 * rows] - dt * ddt_x
    upto = lax.broadcasted_iota(jnp.int32, (rows, heads), 0)
    dcum = dcum + jnp.where(upto == rows - 1, rsums[0:1, :], 0.0)
    ddecay = dot32(lower, dcum, 0, 0)
    ddt = ddt_x + hp[1:2, :] * ddecay
    draw = ddt * jax.nn.sigmoid(shifted)
    ddt_ref[...] = draw
    dhp_ref[0:1, :] += jnp.sum(draw, axis=0, keepdims=True)
    dhp_ref[1:2, :] += jnp.sum(ddecay * dt, axis=0, keepdims=True) * hp[1:2, :]
    dhp_ref[2:3, :] += rsums[1:2, :]

    for lo in range(0, width + GROUP, LANES):
        here = slice(lo, lo + LANES)
        src = pzx[:, width + lo : width + lo + LANES] if lo < width else pbd[:, lo - width : lo - width + LANES]
        total = jnp.zeros((rows, LANES), F32)
        for k in range(KERNEL):
            shift = KERNEL - 1 - k
            moved = dfp[shift : shift + rows, here]
            total = total + cw[k : k + 1, here] * moved
            dconv_ref[k : k + 1, here] += jnp.sum(src * moved, axis=0, keepdims=True)
        dconv_ref[4:5, here] += jnp.sum(dfp[0:rows, here], axis=0, keepdims=True)
        if lo < width:
            dzx_ref[:, width + lo : width + lo + LANES] = total.astype(BF16)
        else:
            dbc_ref[:, lo - width : lo - width + LANES] = total
    dfp[rows : rows + 8, :] = dfp[0:8, :]
    efin_ref[...] = dfp[0:8, :]


def whole(shape):
    return pl.BlockSpec(shape, lambda i, f: (0,) * len(shape))


def run_forward(f, pzx, pbd, cw, hp, table, s0, e0, extra, rows):
    total, width = pzx.shape[0], pzx.shape[1] // 2
    heads = hp.shape[1]
    count = total // rows
    block = lambda w: pl.BlockSpec((rows, w), lambda i, f: (jnp.bitwise_xor(i, f[0]), 0))
    in_specs = [
        block(2 * width),
        block(GROUP + heads),
        whole((8, width + GROUP)),
        whole((8, heads)),
        whole((heads, width)),
        whole((STATE, width)),
        whole((8, width + GROUP)),
    ]
    if extra:
        in_specs += [block(width), whole((1, width))]
    shape = jax.ShapeDtypeStruct
    return pl.pallas_call(
        functools.partial(forward_kernel, second=bool(extra)),
        grid_spec=pltpu.PrefetchScalarGridSpec(
            num_scalar_prefetch=1,
            grid=(count,),
            in_specs=in_specs,
            out_specs=[
                block(width),
                block(width + GROUP),
                pl.BlockSpec((1, STATE, width), lambda i, f: (i, 0, 0)),
                whole((STATE, width)),
                pl.BlockSpec((1, 8, rows), lambda i, f: (jnp.bitwise_xor(i, f[0]), 0, 0)),
            ],
            scratch_shapes=[
                pltpu.VMEM((STATE, width), F32),
                pltpu.VMEM((rows + 8, width + GROUP), F32),
                pltpu.VMEM((rows, width), F32),
            ],
        ),
        out_shape=[
            shape((total, width), F32),
            shape((total, width + GROUP), F32),
            shape((count, STATE, width), F32),
            shape((STATE, width), F32),
            shape((count, 8, rows), F32),
        ],
        compiler_params=pltpu.CompilerParams(vmem_limit_bytes=VMEM_BYTES),
        name="scan_forward",
    )(f, pzx, pbd, cw, hp, table, s0, e0, *extra)


def run_backward(f, pzx, pbd, y, filt, dn, rc, states, cw, hp, table, gain, g0, e0, rows):
    total, width = pzx.shape[0], pzx.shape[1] // 2
    heads = hp.shape[1]
    count = total // rows
    turn = lambda i: count - 1 - i
    block = lambda w: pl.BlockSpec((rows, w), lambda i, f: (jnp.bitwise_xor(turn(i), f[0]), 0))
    shape = jax.ShapeDtypeStruct
    return pl.pallas_call(
        backward_kernel,
        grid_spec=pltpu.PrefetchScalarGridSpec(
            num_scalar_prefetch=1,
            grid=(count,),
            in_specs=[
                block(2 * width),
                block(GROUP + heads),
                block(width),
                block(width + GROUP),
                block(width),
                pl.BlockSpec((1, 8, rows), lambda i, f: (jnp.bitwise_xor(turn(i), f[0]), 0, 0)),
                pl.BlockSpec((1, STATE, width), lambda i, f: (turn(i), 0, 0)),
                pl.BlockSpec((1, STATE, width), lambda i, f: (turn(i) + 1, 0, 0)),
                whole((8, width + GROUP)),
                whole((8, heads)),
                whole((heads, width)),
                whole((1, width)),
                whole((STATE, width)),
                whole((8, width + GROUP)),
            ],
            out_specs=[
                block(2 * width),
                block(GROUP),
                block(heads),
                whole((8, width)),
                whole((8, width + GROUP)),
                whole((8, heads)),
                whole((STATE, width)),
                whole((8, width + GROUP)),
            ],
            scratch_shapes=[
                pltpu.VMEM((STATE, width), F32),
                pltpu.VMEM((rows + 8, width + GROUP), F32),
                pltpu.VMEM((2 * rows, width), F32),
                pltpu.VMEM((rows, width), F32),
                pltpu.VMEM((rows, width), F32),
                pltpu.VMEM((8, width), F32),
            ],
        ),
        out_shape=[
            shape((total, 2 * width), BF16),
            shape((total, GROUP), F32),
            shape((total, heads), F32),
            shape((8, width), F32),
            shape((8, width + GROUP), F32),
            shape((8, heads), F32),
            shape((STATE, width), F32),
            shape((8, width + GROUP), F32),
        ],
        compiler_params=pltpu.CompilerParams(vmem_limit_bytes=VMEM_BYTES),
        name="scan_backward",
    )(f, pzx, pbd, y, filt, dn, rc, states, states, cw, hp, table, gain, g0, e0)


def place_kernel(ids, *refs, plan, small):
    out = refs[-1]
    h, j = pl.program_id(0), pl.program_id(1)
    core = ids[1]
    for ref, (side, layer, first, size) in zip(refs, plan):

        @pl.when((h == side) & (core == layer) & (j >= first) & (j < first + size))
        def _():
            v = ref[...]
            out[...] = v.reshape(out.shape).astype(F32)

    if small:

        @pl.when(j == pl.num_programs(1) - 1)
        def _():
            v = refs[len(plan)]
            out[:, : v.shape[2]] = v[0]


def place_blocks(ids, chunks, small, out_shape, block, out_index, steps):
    def step_of(side, layer, first, size, index):
        def where(h, j, ids):
            used = jnp.logical_and(h == side, ids[1] == layer)
            return index(jnp.where(used, jnp.clip(j - first, 0, size - 1), 0))

        return where

    in_specs = [
        pl.BlockSpec(shape, step_of(side, layer, first, size, index))
        for _, side, layer, first, size, shape, index in chunks
    ]
    args = [c[0] for c in chunks]
    if small is not None:
        in_specs.append(pl.BlockSpec((1,) + small.shape[1:], lambda h, j, ids: (h, 0, 0)))
        args.append(small)
    return pl.pallas_call(
        functools.partial(
            place_kernel, plan=tuple(c[1:5] for c in chunks), small=small is not None
        ),
        grid_spec=pltpu.PrefetchScalarGridSpec(
            num_scalar_prefetch=1,
            grid=(2, steps),
            in_specs=in_specs,
            out_specs=pl.BlockSpec(block, out_index),
        ),
        out_shape=jax.ShapeDtypeStruct(out_shape, F32),
        compiler_params=pltpu.CompilerParams(vmem_limit_bytes=VMEM_BYTES),
        name="place_gradient",
    )(ids, *args)


def swap_section(v):
    return lax.ppermute(v, "section", [(0, 1), (1, 0)])


def move_fsdp(v, m):
    n = lax.axis_size("fsdp")
    return lax.ppermute(v, "fsdp", [(i, i ^ m) for i in range(n)])


def transpose_places(v):
    n, s = lax.axis_size("fsdp"), lax.axis_size("seq")
    pairs = [
        ((j * n + i) * n + k, (j * n + k) * n + i)
        for j in range(s // n)
        for i in range(n)
        for k in range(n)
    ]
    return lax.ppermute(v, ("seq", "fsdp"), pairs)


def to_local(v):
    n, f, c = lax.axis_size("fsdp"), lax.axis_index("fsdp"), lax.axis_index("section")
    size = v.shape[-1] // (2 * n)
    return jnp.concatenate(
        [
            lax.dynamic_slice_in_dim(v, ((f ^ m) * 2 + (c ^ t)) * size, size, v.ndim - 1)
            for t in range(2)
            for m in range(n)
        ],
        axis=-1,
    )


def to_natural(v):
    n, f, c = lax.axis_size("fsdp"), lax.axis_index("fsdp"), lax.axis_index("section")
    size = v.shape[-1] // (2 * n)
    return jnp.concatenate(
        [
            lax.dynamic_slice_in_dim(v, ((c ^ h) * n + (f ^ k)) * size, size, v.ndim - 1)
            for k in range(n)
            for h in range(2)
        ],
        axis=-1,
    )


def reorder(v, m):
    n = lax.axis_size("fsdp")
    size = v.shape[-1] // (2 * n)
    return jnp.concatenate(
        [
            v[..., (t * n + (j ^ m)) * size : (t * n + (j ^ m) + 1) * size]
            for t in range(2)
            for j in range(n)
        ],
        axis=-1,
    )


def gather_plain(v):
    n = lax.axis_size("fsdp")
    return jnp.stack([v] + [move_fsdp(v, m) for m in range(1, n)])


def gather_rows(v):
    n = lax.axis_size("fsdp")
    return jnp.concatenate([v] + [reorder(move_fsdp(v, m), m) for m in range(1, n)])


def scatter_sum(partial):
    n = lax.axis_size("fsdp")
    total = partial[0]
    for m in range(1, n):
        total = total + reorder(move_fsdp(partial[m].astype(BF16), m), m).astype(F32)
    return total


def sum_rows(v):
    n = lax.axis_size("fsdp")
    total = v
    for m in range(1, n):
        got = move_fsdp(v, m)
        total = total + jnp.stack([got[j ^ m] for j in range(n)])
    return total


def seq_sum(v):
    s = lax.axis_size("seq")
    place = lax.axis_index("seq")
    half = s // 2
    add = lambda a, b: (a.astype(F32) + b.astype(F32)).astype(BF16)
    total = v
    for j in range(half - 1):
        pairs = [(j, j + 1), (s - 1 - j, s - 2 - j)]
        total = add(total, lax.ppermute(total, "seq", pairs))
    total = add(total, lax.ppermute(total, "seq", [(half - 1, half), (half, half - 1)]))
    for j in reversed(range(half - 1)):
        got = lax.ppermute(total, "seq", [(j + 1, j), (s - 2 - j, s - 1 - j)])
        total = jnp.where((place == j) | (place == s - 1 - j), got, total)
    return total


def relay(total, local, reverse):
    n, s = lax.axis_size("fsdp"), lax.axis_size("seq")
    segments = s // n
    place = lax.axis_index("seq") // n
    own = lax.axis_index("seq") % n
    totals = lax.all_gather(total, "seq")
    locals_ = lax.all_gather(local, "seq")
    state = jnp.zeros_like(local)
    order = range(segments - 1, -1, -1) if reverse else range(segments)
    for j in order:
        use = (j > place) if reverse else (j < place)
        t = lax.dynamic_index_in_dim(totals, j * n + own, 0, False)
        v = lax.dynamic_index_in_dim(locals_, j * n + own, 0, False)
        state = jnp.where(use, t * state + v, state)
    return state


def next_segment(v, step):
    n, s = lax.axis_size("fsdp"), lax.axis_size("seq")
    pairs = [(k, k + step * n) for k in range(s) if 0 <= k + step * n < s]
    return lax.ppermute(v, "seq", pairs)


def dot_rows(a, b):
    return lax.dot_general(a, b, (((0,), (0,)), ((), ())), preferred_element_type=F32)


def dot_cols(a, b):
    return lax.dot_general(a, b, (((1,), (1,)), ((), ())), preferred_element_type=F32)


def normalised(h, gain):
    return h * lax.rsqrt(jnp.mean(h * h, axis=-1, keepdims=True) + EPS) * gain


def per_device(
    inputs,
    cotangent,
    lengths,
    gain_in,
    w_in,
    conv_w,
    conv_b,
    dt_bias,
    a_log,
    d_skip,
    gain_out,
    w_out,
):
    n = lax.axis_size("fsdp")
    nz = lax.axis_size("seq")
    segments = nz // n
    c = lax.axis_index("section")
    f = lax.axis_index("fsdp")
    place = lax.axis_index("seq")
    upper = c == 0
    rows = inputs.shape[2]
    width = INNER // n
    heads = HEADS // n
    share = D // n
    half = share // 2
    group = GROUP // n
    pairs_of = n // 2
    f1 = f.reshape(1).astype(jnp.int32)
    ids = jnp.stack([f, c]).astype(jnp.int32)

    def pick(a, b):
        return jnp.where(upper, a, b)

    w = w_in[0]
    kept = lax.dynamic_slice_in_dim(w, c * half, half, 0)
    other = swap_section(lax.dynamic_slice_in_dim(w, (1 - c) * half, half, 0))

    def columns(v, k):
        cut = lambda at, size: lax.dynamic_slice_in_dim(v, at, size, 1)
        return (
            jnp.concatenate([cut(k * width, width), cut(INNER + k * width, width)], axis=1),
            jnp.concatenate(
                [v[:, 2 * INNER : 2 * INNER + GROUP], cut(2 * INNER + GROUP + k * heads, heads)],
                axis=1,
            ),
        )

    def cut_blocks(layer):
        return [
            [
                jnp.where(c == layer, a, b)
                for a, b in zip(columns(kept, f ^ m), columns(other, f ^ m))
            ]
            for m in range(n)
        ]

    def fetch(blocks):
        got = [
            [b if m == 0 else move_fsdp(b, m) for b in blocks[m]] for m in range(n)
        ]
        across = [[swap_section(b) for b in pieces] for pieces in got]
        full = [
            jnp.concatenate([p[q] for p in got] + [p[q] for p in across]) for q in range(2)
        ]
        return full, got

    own_in = lax.dynamic_index_in_dim(inputs, c, 0, False)[0]
    own_ct = lax.dynamic_index_in_dim(cotangent, c, 0, False)[0]
    own_len = lax.dynamic_index_in_dim(lengths, c, 0, False)
    h0 = to_local(transpose_places(own_in))
    length = transpose_places(own_len)
    start = ((place // n) * n + f) * rows
    valid = (start + jnp.arange(rows, dtype=jnp.int32) < length[0]).astype(F32)[:, None]
    all_h0 = gather_rows(h0)

    pack = jnp.concatenate(
        [
            gain_in[0],
            dt_bias[0],
            a_log[0],
            d_skip[0],
            gain_out[0],
            conv_w[0].reshape(-1),
            conv_b[0],
        ]
    )
    mine = gather_plain(pack)
    theirs = swap_section(mine)
    small = []
    for full in (pick(mine, theirs), pick(theirs, mine)):
        full = full.astype(F32)
        at = 0

        def take(size):
            nonlocal at
            at += size
            return full[:, at - size : at]

        halves = take(share).reshape(n, 2, half)
        gain = pick(halves, halves[:, ::-1]).transpose(1, 0, 2).reshape(1, D)
        hp = [take(heads)[0:1] for _ in range(3)]
        hp = jnp.concatenate([hp[0], -jnp.exp(hp[1]), hp[2], jnp.zeros((5, heads), F32)])
        gout = take(width)[0:1]
        rest = full[:, at:]
        rest = jnp.concatenate(
            [lax.dynamic_index_in_dim(rest, f ^ k, 0, True) for k in range(n)]
        )
        per = CHANNELS // n
        taps = rest[:, : KERNEL * per].reshape(n, KERNEL, per).transpose(1, 0, 2)
        bias = rest[:, KERNEL * per :].reshape(1, CHANNELS)
        table = jnp.concatenate(
            [taps.reshape(KERNEL, CHANNELS), bias, jnp.zeros((3, CHANNELS), F32)]
        )
        cw = jnp.concatenate(
            [lax.dynamic_slice_in_dim(table, f * width, width, 1), table[:, INNER:]], axis=1
        )
        small.append((gain, cw, hp, gout))

    w0, came = fetch(cut_blocks(0))
    blocks1, own_ct, wo_mine, _ = lax.optimization_barrier(
        (cut_blocks(1), own_ct, w_out[0], came)
    )
    wo_other = swap_section(wo_mine)
    wo = (to_local(pick(wo_mine, wo_other)), to_local(pick(wo_other, wo_mine)))
    w1, _ = fetch(blocks1)
    win = (w0, w1)
    dout1 = to_local(transpose_places(own_ct)).astype(F32)

    expand = (
        jnp.arange(heads)[:, None] == jnp.arange(width)[None, :] // HEAD_DIM
    ).astype(BF16)
    zero_state = jnp.zeros((STATE, width), F32)
    zero_edge = jnp.zeros((8, width + GROUP), F32)

    def project(normed, layer):
        return [jnp.dot(normed, part, preferred_element_type=F32) for part in win[layer]]

    def decay_of(pbd, hp):
        decay = jax.nn.softplus(pbd[:, GROUP:] + hp[0:1]) * hp[1:2]
        return jnp.repeat(jnp.exp(jnp.sum(decay, axis=0)), HEAD_DIM)[None, :]

    def scan(proj, layer, extra):
        pzx, pbd = proj
        _, cw, hp, _ = small[layer]
        args = (f1, pzx, pbd, cw, hp, expand)
        if segments == 1:
            return run_forward(*args, zero_state, zero_edge, extra, rows)
        rear = lax.dynamic_slice_in_dim(
            jnp.concatenate([pzx[:, width:], pbd[:, :GROUP]], axis=1),
            ((n - 1) ^ f) * rows + rows - 8,
            8,
            0,
        )
        edge = next_segment(rear, 1)
        local = run_forward(*args, zero_state, edge, extra, rows)[3]
        state = relay(decay_of(pbd, hp), local, False)
        return run_forward(*args, state, edge, extra, rows)

    def unscan(proj, fwd, dn, rc, layer):
        pzx, pbd = proj
        y, filt, states, final = fwd[:4]
        _, cw, hp, gout = small[layer]
        states = jnp.concatenate([states, final[None]])
        args = (f1, pzx, pbd, y, filt, dn, rc, states, cw, hp, expand, gout)
        if segments == 1:
            return run_backward(*args, zero_state, zero_edge, rows)
        local = run_backward(*args, zero_state, zero_edge, rows)[6]
        grad = relay(decay_of(pbd, hp), local, True)
        edge = next_segment(run_backward(*args, grad, zero_edge, rows)[7], -1)
        return run_backward(*args, grad, edge, rows)

    def gated(pzx, y, r, layer):
        g = y * jax.nn.silu(pzx[:, :width])
        return (g * r.reshape(-1, 1) * small[layer][3]).astype(BF16)

    blockwise = lambda v: v.reshape(n, rows, v.shape[-1])

    normed_in0 = normalised(all_h0.astype(F32), small[0][0]).astype(BF16)
    proj0 = project(normed_in0, 0)
    fwd0 = scan(proj0, 0, ())
    stat0 = sum_rows(fwd0[4])
    r0 = lax.rsqrt(stat0[:, 0] / INNER + EPS)
    normed0 = gated(proj0[0], fwd0[0], r0, 0)
    mixed0 = scatter_sum(blockwise(jnp.dot(normed0, wo[0], preferred_element_type=F32)))
    out0 = valid * (h0.astype(F32) + mixed0)
    h1 = out0.astype(BF16)

    part1 = normalised(h1.astype(F32), small[1][0]).astype(BF16)
    normed_in1 = gather_rows(part1)
    proj1 = project(normed_in1, 1)
    dmixed1 = gather_rows((valid * dout1).astype(BF16))
    dn1 = dot_cols(dmixed1, wo[1])
    fwd1 = scan(proj1, 1, (dn1, small[1][3]))
    stat1 = sum_rows(fwd1[4])
    r1 = lax.rsqrt(stat1[:, 0] / INNER + EPS)
    normed1 = gated(proj1[0], fwd1[0], r1, 1)
    mixed1 = scatter_sum(blockwise(jnp.dot(normed1, wo[1], preferred_element_type=F32)))
    out1 = valid * (h1.astype(F32) + mixed1)
    last1 = out1.astype(BF16)

    def half_sum(own, away):
        away = swap_section(dot_rows(*away).astype(BF16))
        return (dot_rows(*own) + away.astype(F32)).astype(BF16)

    def grads_in(normed_in, part):
        total = half_sum((normed_in[:, : D // 2], part), (normed_in[:, D // 2 :], part))
        total = total.reshape(n, half, -1)
        pieces = [total[0]] + [move_fsdp(total[m], m) for m in range(1, n)]
        return pieces

    def pair_up(pieces):
        return [
            seq_sum(jnp.stack(pieces[2 * k : 2 * k + 2])) for k in range(pairs_of)
        ]

    def grads_out(normed, dmixed):
        size = D // 2 // pairs_of
        result = []
        for k in range(pairs_of):
            own = dmixed[:, k * size : (k + 1) * size]
            away = dmixed[:, D // 2 + k * size : D // 2 + (k + 1) * size]
            result.append(seq_sum(half_sum((normed, own), (normed, away))))
        return result

    def back_layer(layer, dn, dmixed, rc, proj, fwd, normed, normed_in):
        gw_out = grads_out(normed, dmixed)
        dzx, dbc, ddt, dgain, dconv, dhp, _, _ = unscan(proj, fwd, dn, rc, layer)
        wzx, wbd = win[layer]
        shares = blockwise(dbc)
        own_cols = lambda k: lax.dynamic_slice_in_dim(shares, k * group, group, 2)
        total = own_cols(f)
        for m in range(1, n):
            got = move_fsdp(own_cols(f ^ m), m)
            total = total + jnp.stack([got[j ^ m] for j in range(n)])
        dsmall = jnp.concatenate([total.reshape(n * rows, group), ddt], axis=1).astype(BF16)
        wsmall = jnp.concatenate(
            [lax.dynamic_slice_in_dim(wbd, f * group, group, 1), wbd[:, GROUP:]], axis=1
        )
        back = dot_cols(dzx, wzx) + dot_cols(dsmall, wsmall)
        dnormed_in = scatter_sum(blockwise(back))
        gz = grads_in(normed_in, dzx[:, :width])
        gx = grads_in(normed_in, dzx[:, width:])
        gs = grads_in(normed_in, dsmall)
        gw_in = pair_up(gz) + pair_up(gx) + [seq_sum(jnp.stack(gs))]
        return dnormed_in, gw_in, gw_out, (dgain[0], dconv[:5], dhp[:3])

    def back_norm(dout, dnormed_in, h, gain):
        h = h.astype(F32)
        r = lax.rsqrt(jnp.mean(h * h, axis=-1, keepdims=True) + EPS)
        u = dnormed_in * gain
        mean = jnp.mean(u * h, axis=-1, keepdims=True)
        dgain = jnp.sum(dnormed_in * h * r, axis=0)
        return valid * dout + r * u - h * (r * r * r) * mean, dgain

    def scales(r, coef):
        rest = jnp.zeros((n, 6, rows), F32)
        return jnp.concatenate([r[:, None], coef[:, None], rest], axis=1)

    rc1 = scales(r1, (r1 * r1 * r1 / INNER) * stat1[:, 1])
    dnin1, gwi1, gwo1, smalls1 = back_layer(
        1, dn1, dmixed1, rc1, proj1, fwd1, normed1, normed_in1
    )
    grad1, dgin1 = back_norm(dout1, dnin1, h1, small[1][0])

    dout0 = grad1.astype(BF16).astype(F32)
    dmixed0_own = (valid * dout0).astype(BF16)
    dmixed0 = gather_rows(dmixed0_own)
    along0 = gather_plain(jnp.sum(dmixed0_own.astype(F32) * mixed0, axis=-1))
    dn0 = dot_cols(dmixed0, wo[0])
    rc0 = scales(r0, (r0 * r0 / INNER) * along0)
    dnin0, gwi0, gwo0, smalls0 = back_layer(
        0, dn0, dmixed0, rc0, proj0, fwd0, normed0, normed_in0
    )
    grad0, dgin0 = back_norm(dout0, dnin0, h0, small[0][0])

    def packed(dgin, smalls, out, mixed):
        dgain, dconv, dhp = smalls
        put = lambda v, size, at: lax.dynamic_update_slice(
            jnp.zeros(v.shape[:-1] + (size,), F32), v, (0,) * (v.ndim - 1) + (at,)
        )
        conv = put(dconv[:, :width], CHANNELS, f * width)
        conv = conv.at[:, INNER:].set(dconv[:, width:])
        sums = jnp.stack(
            [jnp.sum(out * out), jnp.sum((valid * mixed) ** 2), jnp.sum(valid)]
        )
        return jnp.concatenate(
            [
                to_natural(dgin),
                conv.reshape(-1),
                put(dhp, HEADS, f * heads).reshape(-1),
                put(dgain, INNER, f * width),
                sums,
            ]
        )

    everyone = ("section", "seq", "fsdp")
    p1 = packed(dgin1, smalls1, out1, mixed1)
    p0 = packed(dgin0, smalls0, out0, mixed0)
    p0, p1 = lax.psum((p0, p1), everyone)
    p = pick(p0, p1)
    at = 0

    def take(size):
        nonlocal at
        at += size
        return p[at - size : at]

    mine_of = lambda v, size: lax.dynamic_slice_in_dim(v, f * size, size, v.ndim - 1)
    o_gain_in = mine_of(take(D), share)
    o_conv = mine_of(take(5 * CHANNELS).reshape(5, CHANNELS), CHANNELS // n)
    o_heads = mine_of(take(3 * HEADS).reshape(3, HEADS), heads)
    o_gain_out = mine_of(take(INNER), width)
    sums = take(3)
    act_rms = jnp.sqrt(sums[:2] / (sums[2] * D))[None]

    def hand_over(v, layer):
        return lax.ppermute(v, "section", [(1 - layer, layer)])

    away1 = [hand_over(v, 1) for v in gwi1 + gwo1]
    away0 = [hand_over(v, 0) for v in gwi0 + gwo0]
    in_count = len(gwi1)
    own = (gwi0 + gwo0, gwi1 + gwo1)
    away = (away0, away1)

    def small_columns(v):
        v = v.astype(F32)
        by_place = [lax.dynamic_index_in_dim(v, f ^ k, 0, False) for k in range(n)]
        return jnp.concatenate(
            [b[:, :group] for b in by_place] + [b[:, group:] for b in by_place], axis=1
        )

    at_small = in_count - 1
    small_in = jnp.stack(
        [
            small_columns(pick(own[0][at_small], own[1][at_small])),
            small_columns(pick(away0[at_small], away1[at_small])),
        ]
    )
    side_row = lambda h, ids: jnp.where(h == 0, ids[1], 1 - ids[1])
    chunks_in = [
        (src[side][layer][k], side, layer, 2 * k, 2, (1, half, width), lambda i: (i, 0, 0))
        for src in ((own, away),)
        for side in range(2)
        for layer in range(2)
        for k in range(at_small)
    ]
    g_w_in = place_blocks(
        ids,
        chunks_in,
        small_in,
        (share, 2 * INNER + GROUP + HEADS),
        (half, width),
        lambda h, j, ids: (
            side_row(h, ids),
            jnp.where(
                j < 2 * n, (j // n) * n + jnp.bitwise_xor(j % n, ids[0]), 2 * n
            ),
        ),
        2 * n + 1,
    )
    chunks_out = [
        (src[side][layer][in_count + k], side, layer, 2 * k, 2, (width, half), lambda i: (0, i))
        for src in ((own, away),)
        for side in range(2)
        for layer in range(2)
        for k in range(pairs_of)
    ]
    g_w_out = place_blocks(
        ids,
        chunks_out,
        None,
        (width, D),
        (width, half),
        lambda h, j, ids: (0, jnp.bitwise_xor(j, ids[0]) * 2 + side_row(h, ids)),
        n,
    )

    def returned(a, b):
        own, away = pick(a, b), pick(b, a)
        own = transpose_places(to_natural(own))
        away = swap_section(transpose_places(to_natural(away)))
        return jnp.stack([pick(own, away), pick(away, own)])

    layer_out = returned(h1, last1)
    in_grads = returned(grad0, grad1)
    return (
        layer_out[None, :, None],
        in_grads[None, :, None],
        o_gain_in[None],
        g_w_in[None],
        o_conv[None, :4],
        o_conv[None, 4],
        o_heads[None, 0],
        o_heads[None, 1],
        o_heads[None, 2],
        o_gain_out[None],
        g_w_out[None],
        act_rms,
    )


def solution(mesh):
    in_specs = (
        P(None, "fsdp", "seq", None),
        P(None, "fsdp", "seq", None),
        P(None, "fsdp"),
        P("section", "fsdp"),
        P("section", "fsdp", None),
        P("section", None, "fsdp"),
        P("section", "fsdp"),
        P("section", "fsdp"),
        P("section", "fsdp"),
        P("section", "fsdp"),
        P("section", "fsdp"),
        P("section", "fsdp", None),
    )
    out_specs = (
        P("section", None, "fsdp", "seq", None),
        P("section", None, "fsdp", "seq", None),
        P("section", "fsdp"),
        P("section", "fsdp", None),
        P("section", None, "fsdp"),
        P("section", "fsdp"),
        P("section", "fsdp"),
        P("section", "fsdp"),
        P("section", "fsdp"),
        P("section", "fsdp"),
        P("section", "fsdp", None),
        P("section", None),
    )
    return jax.shard_map(
        per_device, mesh=mesh, in_specs=in_specs, out_specs=out_specs, check_vma=False
    )
```

```python
import functools

import jax
import jax.numpy as jnp
from jax import lax
from jax.experimental import pallas as pl
from jax.experimental.pallas import tpu as pltpu
from jax.sharding import PartitionSpec as P

D = 2048
INNER = 4096
HEADS = 64
HEAD_DIM = 64
STATE = 128
KERNEL = 4
GROUP = 2 * STATE
CHANNELS = INNER + GROUP
LANES = 128
EPS = 1e-05
F32 = jnp.float32
BF16 = jnp.bfloat16
VMEM_BYTES = 48 * 1024 * 1024


def split(v):
    hi = v.astype(BF16)
    return hi, (v - hi.astype(F32)).astype(BF16)


def dot32(a, b, ca, cb):
    (ah, al), (bh, bl) = (v if isinstance(v, tuple) else split(v) for v in (a, b))
    one = lambda p, q: lax.dot_general(
        p, q, (((ca,), (cb,)), ((), ())), preferred_element_type=F32
    )
    return one(ah, bh) + (one(ah, bl) + one(al, bh))


def step_sizes(raw, hp, rows):
    shifted = raw + hp[0:1, :]
    dt = jnp.maximum(shifted, 0.0) + jnp.log1p(jnp.exp(-jnp.abs(shifted)))
    decay = dt * hp[1:2, :]
    row = lax.broadcasted_iota(jnp.int32, (rows, rows), 0)
    col = lax.broadcasted_iota(jnp.int32, (rows, rows), 1)
    lower = (row >= col).astype(F32)
    cum = dot32(lower, decay, 1, 0)
    cum_t = dot32(decay, lower, 0, 1)
    return shifted, dt, cum, cum_t, row, col, lower


def pair_lanes(v, j, first):
    return jnp.where(first, v[:, 2 * j : 2 * j + 1], v[:, 2 * j + 1 : 2 * j + 2])


def head_sums(v, table):
    hi, low = split(v)
    one = lambda p: lax.dot_general(
        p, table, (((1,), (1,)), ((), ())), preferred_element_type=F32
    )
    return one(hi) + one(low)


def forward_kernel(f_ref, proj, cw, hp, table, s0, e0, *rest, second):
    if second:
        dn, gain, y_ref, filt_ref, st_ref, stat_ref, state, xp, xw_s, last_s = rest
    else:
        y_ref, filt_ref, st_ref, stat_ref, state, xp, xw_s, last_s = rest
    i = pl.program_id(0)
    rows, width = y_ref.shape

    @pl.when(i == 0)
    def _():
        state[...] = s0[...]
        xp[0:8, :] = e0[...]

    xp[8 : 8 + rows, :] = proj[:, width : 2 * width + GROUP]

    def conv_tile(lo):
        acc = cw[4:5, lo : lo + LANES]
        for k in range(KERNEL):
            acc = acc + cw[k : k + 1, lo : lo + LANES] * xp[5 + k : 5 + k + rows, lo : lo + LANES]
        filt_ref[:, lo : lo + LANES] = acc
        return acc * jax.nn.sigmoid(acc)

    b_c = conv_tile(width)
    c_c = conv_tile(width + STATE)
    _, dt, cum, cum_t, row, col, _ = step_sizes(proj[:, 2 * width + GROUP :], hp, rows)
    last = cum[rows - 1 : rows, :]
    ecum = jnp.exp(cum)
    weight = jnp.exp(last - cum) * dt
    elast = jnp.exp(last)
    b_c, c_c = split(b_c), split(c_c)
    carried = dot32(c_c, state[...], 1, 0)
    scores = dot32(c_c, b_c, 1, 1)
    causal = row >= col
    lane = lax.broadcasted_iota(jnp.int32, (rows, LANES), 1)
    first = lane < HEAD_DIM
    ss = jnp.zeros((rows, LANES), F32)
    s2 = jnp.zeros((rows, LANES), F32)
    for j in range(width // LANES):
        lo = j * LANES
        here = slice(lo, lo + LANES)
        x = conv_tile(lo)
        xd = x * pair_lanes(dt, j, first)
        m = []
        for h in (2 * j, 2 * j + 1):
            gap = cum[:, h : h + 1] - cum_t[h : h + 1, :]
            m.append(jnp.exp(jnp.where(causal, gap, -1e30)) * scores)
        xd2 = jnp.concatenate([jnp.where(first, xd, 0.0), jnp.where(first, 0.0, xd)])
        y = (
            dot32(jnp.concatenate(m, axis=1), xd2, 1, 0)
            + carried[:, here] * pair_lanes(ecum, j, first)
            + pair_lanes(hp[2:3, :], j, first[0:1]) * x
        )
        y_ref[:, here] = y
        xw_s[:, here] = x * pair_lanes(weight, j, first)
        last_s[0:1, here] = pair_lanes(elast, j, first[0:1])
        z = proj[:, here]
        g = y * z * jax.nn.sigmoid(z)
        ss = ss + g * g
        if second:
            s2 = s2 + g * dn[:, here] * gain[0:1, here]
    state[...] = state[...] * last_s[0:1, :] + dot32(b_c, xw_s[...], 0, 0)
    st_ref[0] = state[...]
    xp[0:8, :] = xp[rows : rows + 8, :]
    ones = jnp.ones((8, LANES), F32)
    stat_ref[0, 0:1, :] = dot32(ones, ss, 1, 1)[0:1]
    stat_ref[0, 1:2, :] = dot32(ones, s2, 1, 1)[0:1]


def backward_kernel(
    f_ref,
    proj,
    y_ref,
    filt,
    dn,
    rc,
    st_before,
    st_out,
    s0,
    cw,
    hp,
    table,
    gain,
    g0,
    e0,
    dproj,
    dbc_ref,
    dgain_ref,
    dconv_ref,
    dhp_ref,
    gfin_ref,
    efin_ref,
    grad,
    dfp,
    both,
    xw_s,
    dyc_s,
    rowv,
):
    i = pl.program_id(0)
    rows, width = y_ref.shape
    heads = hp.shape[1]

    @pl.when(i == 0)
    def _():
        grad[...] = g0[...]
        dfp[rows : rows + 8, :] = e0[...]
        dgain_ref[...] = jnp.zeros_like(dgain_ref)
        dconv_ref[...] = jnp.zeros_like(dconv_ref)
        dhp_ref[...] = jnp.zeros_like(dhp_ref)

    def silu_pair(v):
        s = jax.nn.sigmoid(v)
        a = v * s
        return a, s * (1.0 + v - a)

    b_c, b_d = silu_pair(filt[:, width : width + STATE])
    c_c, c_d = silu_pair(filt[:, width + STATE :])
    shifted, dt, cum, cum_t, row, col, lower = step_sizes(proj[:, 2 * width + GROUP :], hp, rows)
    last = cum[rows - 1 : rows, :]
    tail = jnp.exp(last - cum)
    ecum = jnp.exp(cum)
    elast = jnp.exp(last)
    b_c, c_c = split(b_c), split(c_c)
    grad_p = split(grad[...])
    k_all = dot32(b_c, grad_p, 1, 0)
    scores_t = dot32(b_c, c_c, 1, 1)
    causal_t = row <= col
    lane = lax.broadcasted_iota(jnp.int32, (rows, LANES), 1)
    first = lane < HEAD_DIM
    dcb_t = jnp.zeros((rows, rows), F32)
    rc_t = dot32((row == col).astype(F32), rc[0], 1, 1)
    r = rc_t[:, 0:1]
    coef = rc_t[:, 1:2]
    rowv[0:1, :] = jnp.sum(grad[...] * st_out[0], axis=0, keepdims=True)
    for j in range(width // LANES):
        lo = j * LANES
        here = slice(lo, lo + LANES)
        z = proj[:, here]
        y = y_ref[:, here]
        sz, dsz = silu_pair(z)
        g = y * sz
        dnt = dn[:, here]
        dg = dnt * gain[0:1, here] * r - g * coef
        dgain_ref[0:1, here] += jnp.sum(dnt * g * r, axis=0, keepdims=True)
        dy = dg * sz
        dproj[:, here] = (dg * y * dsz).astype(BF16)
        x, xder = silu_pair(filt[:, here])
        dt_e = pair_lanes(dt, j, first)
        tail_e = pair_lanes(tail, j, first)
        xd = x * dt_e
        dy2 = split(jnp.concatenate([jnp.where(first, dy, 0.0), jnp.where(first, 0.0, dy)]))
        decays = []
        for h in (2 * j, 2 * j + 1):
            gap = cum_t[h : h + 1, :] - cum[:, h : h + 1]
            decays.append(jnp.exp(jnp.where(causal_t, gap, -1e30)))
        m = jnp.concatenate([d * scores_t for d in decays], axis=1)
        dm = dot32(xd, dy2, 1, 1)
        dcb_t = dcb_t + (decays[0] * dm[:, :rows] + decays[1] * dm[:, rows:])
        v = dot32(m, dy2, 1, 0) + k_all[:, here] * tail_e
        skip = pair_lanes(hp[2:3, :], j, first[0:1])
        dx = dt_e * v + skip * dy
        both[0:rows, here] = x * v
        both[rows : 2 * rows, here] = dy * (y - skip * x)
        rowv[1:2, here] = jnp.sum(dy * x, axis=0, keepdims=True)
        rowv[2:3, here] = pair_lanes(elast, j, first[0:1])
        xw_s[:, here] = xd * tail_e
        dyc_s[:, here] = dy * pair_lanes(ecum, j, first)
        dfp[0:rows, here] = dx * xder
    dcb_t = split(dcb_t)
    dyc = split(dyc_s[...])
    st_in = jnp.where(i == pl.num_programs(0) - 1, s0[...], st_before[0])
    dc = dot32(dcb_t, b_c, 0, 0) + dot32(dyc, st_in, 1, 1)
    db = dot32(dcb_t, c_c, 1, 0) + dot32(xw_s[...], grad_p, 1, 1)
    dfp[0:rows, width : width + STATE] = db * b_d
    dfp[0:rows, width + STATE :] = dc * c_d
    grad[...] = grad[...] * rowv[2:3, :] + dot32(c_c, dyc, 0, 0)
    gfin_ref[...] = grad[...]

    sums = head_sums(both[...], table[...])
    rsums = head_sums(rowv[...], table[...])
    ddt_x = sums[0:rows]
    dcum = sums[rows : 2 * rows] - dt * ddt_x
    upto = lax.broadcasted_iota(jnp.int32, (rows, heads), 0)
    dcum = dcum + jnp.where(upto == rows - 1, rsums[0:1, :], 0.0)
    ddecay = dot32(lower, dcum, 0, 0)
    ddt = ddt_x + hp[1:2, :] * ddecay
    draw = ddt * jax.nn.sigmoid(shifted)
    dproj[:, 2 * width + GROUP :] = draw.astype(BF16)
    dhp_ref[0:1, :] += jnp.sum(draw, axis=0, keepdims=True)
    dhp_ref[1:2, :] += jnp.sum(ddecay * dt, axis=0, keepdims=True) * hp[1:2, :]
    dhp_ref[2:3, :] += rsums[1:2, :]

    for lo in range(0, width + GROUP, LANES):
        here = slice(lo, lo + LANES)
        src = proj[:, width + lo : width + lo + LANES]
        total = jnp.zeros((rows, LANES), F32)
        for k in range(KERNEL):
            shift = KERNEL - 1 - k
            moved = dfp[shift : shift + rows, here]
            total = total + cw[k : k + 1, here] * moved
            dconv_ref[k : k + 1, here] += jnp.sum(src * moved, axis=0, keepdims=True)
        dconv_ref[4:5, here] += jnp.sum(dfp[0:rows, here], axis=0, keepdims=True)
        out = slice(width + lo, width + lo + LANES)
        if lo < width:
            dproj[:, out] = total.astype(BF16)
        else:
            dproj[:, out] = jnp.zeros((rows, LANES), BF16)
            dbc_ref[:, lo - width : lo - width + LANES] = total
    dfp[rows : rows + 8, :] = dfp[0:8, :]
    efin_ref[...] = dfp[0:8, :]


def whole(shape):
    return pl.BlockSpec(shape, lambda i, f: (0,) * len(shape))


def run_forward(f, proj, cw, hp, table, s0, e0, extra, rows):
    total, (heads, width) = proj.shape[0], table.shape
    count = total // rows
    block = lambda w: pl.BlockSpec((rows, w), lambda i, f: (jnp.bitwise_xor(i, f[0]), 0))
    in_specs = [
        block(proj.shape[1]),
        whole((8, width + GROUP)),
        whole((8, heads)),
        whole((heads, width)),
        whole((STATE, width)),
        whole((8, width + GROUP)),
    ]
    if extra:
        in_specs += [block(width), whole((1, width))]
    shape = jax.ShapeDtypeStruct
    return pl.pallas_call(
        functools.partial(forward_kernel, second=bool(extra)),
        grid_spec=pltpu.PrefetchScalarGridSpec(
            num_scalar_prefetch=1,
            grid=(count,),
            in_specs=in_specs,
            out_specs=[
                block(width),
                block(width + GROUP),
                pl.BlockSpec((1, STATE, width), lambda i, f: (i, 0, 0)),
                pl.BlockSpec((1, 8, rows), lambda i, f: (jnp.bitwise_xor(i, f[0]), 0, 0)),
            ],
            scratch_shapes=[
                pltpu.VMEM((STATE, width), F32),
                pltpu.VMEM((rows + 8, width + GROUP), F32),
                pltpu.VMEM((rows, width), F32),
                pltpu.VMEM((8, width), F32),
            ],
        ),
        out_shape=[
            shape((total, width), F32),
            shape((total, width + GROUP), F32),
            shape((count, STATE, width), F32),
            shape((count, 8, rows), F32),
        ],
        compiler_params=pltpu.CompilerParams(vmem_limit_bytes=VMEM_BYTES),
        name="scan_forward",
    )(f, proj, cw, hp, table, s0, e0, *extra)


def run_backward(f, proj, y, filt, dn, rc, states, s0, cw, hp, table, gain, g0, e0, rows):
    total, (heads, width) = proj.shape[0], table.shape
    count = total // rows
    turn = lambda i: count - 1 - i
    block = lambda w: pl.BlockSpec((rows, w), lambda i, f: (jnp.bitwise_xor(turn(i), f[0]), 0))
    shape = jax.ShapeDtypeStruct
    return pl.pallas_call(
        backward_kernel,
        grid_spec=pltpu.PrefetchScalarGridSpec(
            num_scalar_prefetch=1,
            grid=(count,),
            in_specs=[
                block(proj.shape[1]),
                block(width),
                block(width + GROUP),
                block(width),
                pl.BlockSpec((1, 8, rows), lambda i, f: (jnp.bitwise_xor(turn(i), f[0]), 0, 0)),
                pl.BlockSpec((1, STATE, width), lambda i, f: (jnp.maximum(turn(i) - 1, 0), 0, 0)),
                pl.BlockSpec((1, STATE, width), lambda i, f: (turn(i), 0, 0)),
                whole((STATE, width)),
                whole((8, width + GROUP)),
                whole((8, heads)),
                whole((heads, width)),
                whole((1, width)),
                whole((STATE, width)),
                whole((8, width + GROUP)),
            ],
            out_specs=[
                block(proj.shape[1]),
                block(GROUP),
                whole((8, width)),
                whole((8, width + GROUP)),
                whole((8, heads)),
                whole((STATE, width)),
                whole((8, width + GROUP)),
            ],
            scratch_shapes=[
                pltpu.VMEM((STATE, width), F32),
                pltpu.VMEM((rows + 8, width + GROUP), F32),
                pltpu.VMEM((2 * rows, width), F32),
                pltpu.VMEM((rows, width), F32),
                pltpu.VMEM((rows, width), F32),
                pltpu.VMEM((8, width), F32),
            ],
        ),
        out_shape=[
            shape(proj.shape, BF16),
            shape((total, GROUP), F32),
            shape((8, width), F32),
            shape((8, width + GROUP), F32),
            shape((8, heads), F32),
            shape((STATE, width), F32),
            shape((8, width + GROUP), F32),
        ],
        compiler_params=pltpu.CompilerParams(vmem_limit_bytes=VMEM_BYTES),
        name="scan_backward",
    )(f, proj, y, filt, dn, rc, states, states, s0, cw, hp, table, gain, g0, e0)


def place_kernel(ids, *refs, plan, small):
    out = refs[-1]
    h, j = pl.program_id(0), pl.program_id(1)
    core = ids[1]
    for ref, (side, layer, first, size) in zip(refs, plan):

        @pl.when((h == side) & (core == layer) & (j >= first) & (j < first + size))
        def _():
            v = ref[...]
            out[...] = v.reshape(out.shape).astype(F32)

    if small:

        @pl.when(j == pl.num_programs(1) - 1)
        def _():
            v = refs[len(plan)]
            out[: v.shape[1], :] = v[0]


def place_blocks(ids, chunks, small, out_shape, block, out_index, steps):
    def step_of(side, layer, first, size, index):
        def where(h, j, ids):
            used = jnp.logical_and(h == side, ids[1] == layer)
            return index(jnp.where(used, jnp.clip(j - first, 0, size - 1), 0))

        return where

    in_specs = [
        pl.BlockSpec(shape, step_of(side, layer, first, size, index))
        for _, side, layer, first, size, shape, index in chunks
    ]
    args = [c[0] for c in chunks]
    if small is not None:
        in_specs.append(pl.BlockSpec((1,) + small.shape[1:], lambda h, j, ids: (h, 0, 0)))
        args.append(small)
    return pl.pallas_call(
        functools.partial(
            place_kernel, plan=tuple(c[1:5] for c in chunks), small=small is not None
        ),
        grid_spec=pltpu.PrefetchScalarGridSpec(
            num_scalar_prefetch=1,
            grid=(2, steps),
            in_specs=in_specs,
            out_specs=pl.BlockSpec(block, out_index),
        ),
        out_shape=jax.ShapeDtypeStruct(out_shape, F32),
        compiler_params=pltpu.CompilerParams(vmem_limit_bytes=VMEM_BYTES),
        name="place_gradient",
    )(ids, *args)


def swap_section(v):
    return lax.ppermute(v, "section", [(0, 1), (1, 0)])


def move_fsdp(v, m):
    n = lax.axis_size("fsdp")
    return lax.ppermute(v, "fsdp", [(i, i ^ m) for i in range(n)])


def move_in_group(v, m):
    n, s = lax.axis_size("fsdp"), lax.axis_size("seq")
    return lax.ppermute(v, "seq", [(k, k // n * n + (k % n ^ m)) for k in range(s)])


def at(v, k):
    return lax.dynamic_index_in_dim(v, k, 0, False)


def exchange(pieces, move):
    return jnp.stack([p if m == 0 else move(p, m) for m, p in enumerate(pieces)])


def trade_places(v):
    n, f = lax.axis_size("fsdp"), lax.axis_index("fsdp")
    i = lax.axis_index("seq") % n
    size = v.shape[-1] // n
    cut = lambda k: lax.dynamic_slice_in_dim(v, k * size, size, 1)
    v = exchange([cut(f ^ m) for m in range(n)], move_fsdp)
    v = exchange([at(v, f ^ i ^ m) for m in range(n)], move_in_group)
    v = exchange([at(v, f ^ i ^ m) for m in range(n)], move_fsdp)
    return jnp.concatenate([at(v, f ^ k) for k in range(n)], axis=1)


def to_local(v):
    n, f, c = lax.axis_size("fsdp"), lax.axis_index("fsdp"), lax.axis_index("section")
    size = v.shape[-1] // (2 * n)
    cut = lambda k: lax.dynamic_slice_in_dim(v, k * size, size, v.ndim - 1)
    return [
        jnp.concatenate([cut((f ^ m) * 2 + (c ^ t)) for m in range(n)], axis=-1)
        for t in range(2)
    ]


def to_natural(pair):
    n, f, c = lax.axis_size("fsdp"), lax.axis_index("fsdp"), lax.axis_index("section")
    v = jnp.concatenate(pair, axis=-1)
    size = v.shape[-1] // (2 * n)
    cut = lambda k: lax.dynamic_slice_in_dim(v, k * size, size, v.ndim - 1)
    return jnp.concatenate(
        [cut((c ^ h) * n + (f ^ k)) for k in range(n) for h in range(2)], axis=-1
    )


def reorder(v, m):
    n = lax.axis_size("fsdp")
    size = v.shape[-1] // n
    return jnp.concatenate(
        [v[..., (j ^ m) * size : ((j ^ m) + 1) * size] for j in range(n)], axis=-1
    )


def gather_rows(v):
    n = lax.axis_size("fsdp")
    return jnp.concatenate([v] + [move_fsdp(v, m) for m in range(1, n)])


def gather_local(pair):
    n = lax.axis_size("fsdp")
    joint = jnp.concatenate(pair, axis=-1)
    came = [joint] + [move_fsdp(joint, m) for m in range(1, n)]
    size = joint.shape[-1] // 2
    return [
        jnp.concatenate(
            [reorder(v[:, t * size : (t + 1) * size], m) for m, v in enumerate(came)]
        )
        for t in range(2)
    ]


def scatter_sum(partial, local):
    n = lax.axis_size("fsdp")
    size = partial.shape[-1] // 2
    total = partial[0]
    for m in range(1, n):
        got = move_fsdp(partial[m].astype(BF16), m)
        if local:
            got = jnp.concatenate([reorder(got[:, :size], m), reorder(got[:, size:], m)], axis=-1)
        total = total + got.astype(F32)
    return total


def sum_rows(v):
    n = lax.axis_size("fsdp")
    total = v
    for m in range(1, n):
        got = move_fsdp(v, m)
        total = total + jnp.stack([got[j ^ m] for j in range(n)])
    return total


def sum_everywhere(v):
    n, s = lax.axis_size("fsdp"), lax.axis_size("seq")
    v = v + swap_section(v)
    m = 1
    while m < n:
        v = v + move_fsdp(v, m)
        m *= 2
    m = 1
    while m < s:
        v = v + lax.ppermute(v, "seq", [(k, k ^ m) for k in range(s)])
        m *= 2
    return v


class SeqSums:
    def __init__(self):
        s = lax.axis_size("seq")
        half = s // 2
        self.pairs = [[(j, j + 1), (s - 1 - j, s - 2 - j)] for j in range(half - 1)]
        self.pairs.append([(half - 1, half), (half, half - 1)])
        self.inward = half
        self.pairs += [[(j + 1, j), (s - 2 - j, s - 1 - j)] for j in reversed(range(half - 1))]
        self.values, self.phase, self.moving = [], [], []

    def add(self, values):
        first = len(self.values)
        self.values += values
        self.phase += [0] * len(values)
        return list(range(first, len(self.values)))

    def begin(self, chosen=None):
        place = lax.axis_index("seq")
        for k in range(len(self.values)) if chosen is None else chosen:
            step = self.phase[k]
            if step == len(self.pairs):
                continue
            v = self.values[k]
            got = lax.ppermute(v, "seq", self.pairs[step])
            if step < self.inward:
                v = (v.astype(F32) + got.astype(F32)).astype(BF16)
            else:
                here = functools.reduce(
                    jnp.logical_or, [place == to for _, to in self.pairs[step]]
                )
                v = jnp.where(here, got, v)
            self.moving.append((k, v))
            self.phase[k] = step + 1

    def end(self, work):
        moved = [v for _, v in self.moving]
        work, moved, rest = lax.optimization_barrier(
            (work, moved, [v for v, p in zip(self.values, self.phase) if p == 0])
        )
        for (k, _), v in zip(self.moving, moved):
            self.values[k] = v
        fresh = [k for k, p in enumerate(self.phase) if p == 0]
        for k, v in zip(fresh, rest):
            self.values[k] = v
        self.moving = []
        return work

    def busy(self):
        return any(p < len(self.pairs) for p in self.phase)


def relay(total, local, reverse):
    n, s = lax.axis_size("fsdp"), lax.axis_size("seq")
    segments = s // n
    place = lax.axis_index("seq") // n
    own = lax.axis_index("seq") % n
    totals = lax.all_gather(total, "seq")
    locals_ = lax.all_gather(local, "seq")
    state = jnp.zeros_like(local)
    order = range(segments - 1, -1, -1) if reverse else range(segments)
    for j in order:
        use = (j > place) if reverse else (j < place)
        t = lax.dynamic_index_in_dim(totals, j * n + own, 0, False)
        v = lax.dynamic_index_in_dim(locals_, j * n + own, 0, False)
        state = jnp.where(use, t * state + v, state)
    return state


def next_segment(v, step):
    n, s = lax.axis_size("fsdp"), lax.axis_size("seq")
    pairs = [(k, k + step * n) for k in range(s) if 0 <= k + step * n < s]
    return lax.ppermute(v, "seq", pairs)


def dot_rows(a, b):
    return lax.dot_general(a, b, (((0,), (0,)), ((), ())), preferred_element_type=F32)


def dot_cols(a, b):
    return lax.dot_general(a, b, (((1,), (1,)), ((), ())), preferred_element_type=F32)


def normalised(h, gain):
    return h * lax.rsqrt(jnp.mean(h * h, axis=-1, keepdims=True) + EPS) * gain


def per_device(
    inputs,
    cotangent,
    lengths,
    gain_in,
    w_in,
    conv_w,
    conv_b,
    dt_bias,
    a_log,
    d_skip,
    gain_out,
    w_out,
):
    n = lax.axis_size("fsdp")
    nz = lax.axis_size("seq")
    segments = nz // n
    c = lax.axis_index("section")
    f = lax.axis_index("fsdp")
    place = lax.axis_index("seq")
    upper = c == 0
    even = place % 2 == 0
    rows = inputs.shape[2]
    width = INNER // n
    heads = HEADS // n
    share = D // n
    half = share // 2
    group = GROUP // n
    pairs_of = n // 2
    f1 = f.reshape(1).astype(jnp.int32)
    ids = jnp.stack([f, c]).astype(jnp.int32)
    tie = lax.optimization_barrier

    def pick(a, b):
        return jnp.where(upper, a, b)

    h0 = trade_places(at(inputs, c)[0])

    pack = jnp.concatenate(
        [
            gain_in[0],
            dt_bias[0],
            a_log[0],
            d_skip[0],
            gain_out[0],
            conv_w[0].reshape(-1),
            conv_b[0],
        ]
    )
    mine = exchange([pack] * n, move_fsdp)

    w = w_in[0].T

    def cut_pieces(side):
        cut = lambda at_row, size: lax.dynamic_slice(w, (at_row, side * half), (size, half))
        first = jnp.where(even, 0, INNER)
        return jnp.stack(
            [
                jnp.concatenate(
                    [
                        cut(first + (f ^ m) * width, width),
                        cut(2 * INNER, GROUP),
                        cut(2 * INNER + GROUP + (f ^ m) * heads, heads),
                    ]
                )
                for m in range(n)
            ]
        )

    kept = cut_pieces(c)
    other = swap_section(cut_pieces(1 - c))

    def neighbour(v):
        return lax.ppermute(v, "seq", [(k, k ^ 1) for k in range(nz)])

    def arrange(came, traded):
        zs = [jnp.where(even, a[:width], b) for a, b in zip(came, traded)]
        xs = [jnp.where(even, b, a[:width]) for a, b in zip(came, traded)]
        rest = [a[width:] for a in came]
        return jnp.concatenate([jnp.concatenate(v, axis=1) for v in (zs, xs, rest)])

    first = jnp.where(upper, kept, other)
    came = [first[0]] + [move_fsdp(first[m], m) for m in range(1, n)]
    traded = [neighbour(v[:width]) for v in came]
    h0_local = gather_local(to_local(h0))
    mine, came, traded, h0_local = tie((mine, came, traded, h0_local))
    w0_own = arrange(came, traded)
    w0 = (w0_own, swap_section(w0_own))

    second, own_ct, wo_mine, own_len, _ = tie(
        (jnp.where(upper, other, kept), at(cotangent, c)[0], w_out[0], at(lengths, c), w0_own)
    )
    wo_other = swap_section(wo_mine)
    wo = (pick(wo_mine, wo_other), pick(wo_other, wo_mine))
    came = [second[0]] + [move_fsdp(second[m], m) for m in range(1, n)]
    came_half = jnp.stack([v[:width] for v in came])
    w1_own = arrange(came, neighbour(came_half))
    w1 = (w1_own, swap_section(w1_own))
    win = (w0, w1)
    slot_pairs = [
        ((j * n + i) * n + k, (j * n + k) * n + i)
        for j in range(segments)
        for i in range(n)
        for k in range(n)
    ]
    length = lax.ppermute(own_len, ("seq", "fsdp"), slot_pairs)
    start = ((place // n) * n + f) * rows
    valid = (start + jnp.arange(rows, dtype=jnp.int32) < length[0]).astype(F32)[:, None]
    dout1 = trade_places(own_ct).astype(F32)

    theirs = swap_section(mine)
    small = []
    for full in (pick(mine, theirs), pick(theirs, mine)):
        full = full.astype(F32)
        used = 0

        def take(size):
            nonlocal used
            used += size
            return full[:, used - size : used]

        gain = take(share)
        hp = [take(heads)[0:1] for _ in range(3)]
        hp = jnp.concatenate([hp[0], -jnp.exp(hp[1]), hp[2], jnp.zeros((5, heads), F32)])
        gout = take(width)[0:1]
        rest = jnp.stack([at(full[:, used:], f ^ k) for k in range(n)])
        gain = jnp.concatenate([at(gain, f ^ k) for k in range(n)])[None]
        per = CHANNELS // n
        taps = rest[:, : KERNEL * per].reshape(n, KERNEL, per).transpose(1, 0, 2)
        bias = rest[:, KERNEL * per :].reshape(1, CHANNELS)
        table = jnp.concatenate(
            [taps.reshape(KERNEL, CHANNELS), bias, jnp.zeros((3, CHANNELS), F32)]
        )
        cw = jnp.concatenate(
            [lax.dynamic_slice_in_dim(table, f * width, width, 1), table[:, INNER:]], axis=1
        )
        small.append((gain, cw, hp, gout))

    expand = (
        jnp.arange(heads)[:, None] == jnp.arange(width)[None, :] // HEAD_DIM
    ).astype(BF16)
    zero_state = jnp.zeros((STATE, width), F32)
    zero_edge = jnp.zeros((8, width + GROUP), F32)

    def project(normed, layer):
        return dot_cols(normed[0], win[layer][0]) + dot_cols(normed[1], win[layer][1])

    def decay_of(proj, hp):
        decay = jax.nn.softplus(proj[:, 2 * width + GROUP :] + hp[0:1]) * hp[1:2]
        return jnp.repeat(jnp.exp(jnp.sum(decay, axis=0)), HEAD_DIM)[None, :]

    def scan(proj, layer, extra):
        _, cw, hp, _ = small[layer]
        args = (f1, proj, cw, hp, expand)
        if segments == 1:
            return run_forward(*args, zero_state, zero_edge, extra, rows), zero_state
        rear = lax.dynamic_slice_in_dim(
            proj[:, width : 2 * width + GROUP], ((n - 1) ^ f) * rows + rows - 8, 8, 0
        )
        edge = next_segment(rear, 1)
        local = run_forward(*args, zero_state, edge, extra, rows)[2][-1]
        state = relay(decay_of(proj, hp), local, False)
        return run_forward(*args, state, edge, extra, rows), state

    def unscan(proj, fwd, dn, rc, layer):
        (y, filt, states, _), state = fwd
        _, cw, hp, gout = small[layer]
        args = (f1, proj, y, filt, dn, rc, states, state, cw, hp, expand, gout)
        if segments == 1:
            return run_backward(*args, zero_state, zero_edge, rows)[:5]
        local = run_backward(*args, zero_state, zero_edge, rows)[5]
        grad = relay(decay_of(proj, hp), local, True)
        edge = next_segment(run_backward(*args, grad, zero_edge, rows)[6], -1)
        return run_backward(*args, grad, edge, rows)[:5]

    def gated(proj, y, r, layer):
        g = y * jax.nn.silu(proj[:, :width])
        return (g * r.reshape(-1, 1) * small[layer][3]).astype(BF16)

    blockwise = lambda v: v.reshape(n, rows, v.shape[-1])

    both = jnp.concatenate(h0_local, axis=1).astype(F32)
    gain0 = jnp.concatenate(to_local(small[0][0]), axis=1)
    normed_in0 = normalised(both, gain0).astype(BF16)
    normed_in0 = (normed_in0[:, : D // 2], normed_in0[:, D // 2 :])
    proj0 = project(normed_in0, 0)
    fwd0 = scan(proj0, 0, ())
    stat0 = sum_rows(fwd0[0][3])
    r0 = lax.rsqrt(stat0[:, 0] / INNER + EPS)
    normed0 = gated(proj0, fwd0[0][0], r0, 0)
    mixed0 = scatter_sum(
        blockwise(jnp.dot(normed0, wo[0], preferred_element_type=F32)), False
    )
    out0 = valid * (h0.astype(F32) + mixed0)
    h1 = out0.astype(BF16)

    part1 = normalised(h1.astype(F32), small[1][0]).astype(BF16)
    normed_in1 = gather_local(to_local(part1))
    dmixed1 = gather_rows((valid * dout1).astype(BF16))
    dn1 = dot_cols(dmixed1, wo[1])
    proj1 = project(normed_in1, 1)
    fwd1 = scan(proj1, 1, (dn1, small[1][3]))
    stat1 = sum_rows(fwd1[0][3])
    r1 = lax.rsqrt(stat1[:, 0] / INNER + EPS)
    normed1 = gated(proj1, fwd1[0][0], r1, 1)

    sums = SeqSums()

    def half_sum(own, away):
        away = swap_section(dot_rows(*away).astype(BF16))
        return (dot_rows(*own) + away.astype(F32)).astype(BF16)

    def grads_in(part, normed_in):
        total = half_sum((part, normed_in[0]), (part, normed_in[1]))
        pieces = [total[:, m * half : (m + 1) * half] for m in range(n)]
        return [pieces[0]] + [move_fsdp(pieces[m], m) for m in range(1, n)]

    def pair_up(pieces):
        return [jnp.stack(pieces[2 * k : 2 * k + 2]) for k in range(pairs_of)]

    def grads_out(normed, dmixed):
        size = D // 2
        cut = lambda k: lax.dynamic_slice_in_dim(normed, k * (width // 2), width // 2, 1)
        own, away = cut(c), cut(1 - c)
        parts = [dmixed[:, k * size : (k + 1) * size] for k in range(2)]
        return [half_sum((own, v), (away, v)) for v in parts]

    def group_sum(dbc):
        shares = blockwise(dbc)
        own_cols = lambda k: lax.dynamic_slice_in_dim(shares, k * group, group, 2)
        total = own_cols(f)
        for m in range(1, n):
            got = move_fsdp(own_cols(f ^ m), m)
            total = total + jnp.stack([got[j ^ m] for j in range(n)])
        return total.reshape(n * rows, group).astype(BF16)

    def back_in(dproj, dgroup, layer):
        out = []
        for part in win[layer]:
            mine = lax.dynamic_slice_in_dim(part, 2 * width + f * group, group, 0)
            out.append(
                jnp.dot(dproj, part, preferred_element_type=F32)
                + jnp.dot(dgroup, mine, preferred_element_type=F32)
            )
        return scatter_sum(blockwise(jnp.concatenate(out, axis=1)), True)

    def back_norm(dout, dnormed_in, h, gain):
        dnormed_in = to_natural([dnormed_in])
        h = h.astype(F32)
        r = lax.rsqrt(jnp.mean(h * h, axis=-1, keepdims=True) + EPS)
        u = dnormed_in * gain
        mean = jnp.mean(u * h, axis=-1, keepdims=True)
        dgain = jnp.sum(dnormed_in * h * r, axis=0)
        return valid * dout + r * u - h * (r * r * r) * mean, dgain

    def scales(r, coef):
        rest = jnp.zeros((n, 6, rows), F32)
        return jnp.concatenate([r[:, None], coef[:, None], rest], axis=1)

    rc1 = scales(r1, (r1 * r1 * r1 / INNER) * stat1[:, 1])
    go1 = sums.add(grads_out(normed1, dmixed1))
    rc1, normed1 = sums.end((rc1, normed1))

    sums.begin()
    d1 = unscan(proj1, fwd1, dn1, rc1, 1)
    d1 = sums.end(d1)

    sums.begin()
    dproj1, dbc1 = d1[:2]
    dgroup1 = group_sum(dbc1)
    dnin1 = back_in(dproj1, dgroup1, 1)
    gz = pair_up(grads_in(dproj1[:, :width], normed_in1))
    dnin1, dgroup1, gz, normed1 = sums.end((dnin1, dgroup1, gz, normed1))
    gz1 = sums.add(gz)

    sums.begin()
    grad1, dgin1 = back_norm(dout1, dnin1, h1, small[1][0])
    dout0 = grad1.astype(BF16).astype(F32)
    dmixed0_own = (valid * dout0).astype(BF16)
    dmixed0 = gather_rows(dmixed0_own)
    along0 = exchange([jnp.sum(dmixed0_own.astype(F32) * mixed0, axis=-1)] * n, move_fsdp)
    rc0 = scales(r0, (r0 * r0 / INNER) * along0)
    dn0 = dot_cols(dmixed0, wo[0])
    gx = pair_up(grads_in(dproj1[:, width : 2 * width], normed_in1))
    dsmall1 = jnp.concatenate([dgroup1, dproj1[:, 2 * width + GROUP :]], axis=1)
    gs = jnp.stack(grads_in(dsmall1, normed_in1))
    grad1, dgin1, dmixed0, rc0, dn0, gx, gs = sums.end(
        (grad1, dgin1, dmixed0, rc0, dn0, gx, gs)
    )
    gx1 = sums.add(gx)
    gs1 = sums.add([gs])

    sums.begin()
    d0 = unscan(proj0, fwd0, dn0, rc0, 0)
    go = grads_out(normed0, dmixed0)
    d0, go = sums.end((d0, go))
    go0 = sums.add(go)

    sums.begin()
    dproj0, dbc0 = d0[:2]
    gz = pair_up(grads_in(dproj0[:, :width], normed_in0))
    dgroup0 = group_sum(dbc0)
    dnin0 = back_in(dproj0, dgroup0, 0)
    gz, dgroup0, dnin0 = sums.end((gz, dgroup0, dnin0))
    gz0 = sums.add(gz)

    sums.begin()
    gx = pair_up(grads_in(dproj0[:, width : 2 * width], normed_in0))
    dsmall0 = jnp.concatenate([dgroup0, dproj0[:, 2 * width + GROUP :]], axis=1)
    gs = jnp.stack(grads_in(dsmall0, normed_in0))
    grad0, dgin0 = back_norm(dout0, dnin0, h0, small[0][0])
    gx, gs, grad0, dgin0 = sums.end((gx, gs, grad0, dgin0))
    gx0 = sums.add(gx)
    gs0 = sums.add([gs])

    sums.begin()
    mixed1 = scatter_sum(
        blockwise(jnp.dot(normed1, wo[1], preferred_element_type=F32)), False
    )
    out1 = valid * (h1.astype(F32) + mixed1)
    last1 = out1.astype(BF16)
    back = trade_places(jnp.concatenate([h1, last1, grad0.astype(BF16), grad1.astype(BF16)]))
    back, out1, mixed1 = sums.end((back, out1, mixed1))

    sums.begin()
    smalls1 = (d1[2][0], d1[3][:5], d1[4][:3])
    smalls0 = (d0[2][0], d0[3][:5], d0[4][:3])

    def packed(dgin, smalls, out, mixed):
        dgain, dconv, dhp = smalls
        put = lambda v, size, at_lane: lax.dynamic_update_slice(
            jnp.zeros(v.shape[:-1] + (size,), F32), v, (0,) * (v.ndim - 1) + (at_lane,)
        )
        conv = put(dconv[:, :width], CHANNELS, f * width)
        conv = conv.at[:, INNER:].set(dconv[:, width:])
        totals = jnp.stack(
            [jnp.sum(out * out), jnp.sum((valid * mixed) ** 2), jnp.sum(valid)]
        )
        return jnp.concatenate(
            [
                dgin,
                conv.reshape(-1),
                put(dhp, HEADS, f * heads).reshape(-1),
                put(dgain, INNER, f * width),
                totals,
            ]
        )

    p = sum_everywhere(
        jnp.stack([packed(dgin0, smalls0, out0, mixed0), packed(dgin1, smalls1, out1, mixed1)])
    )
    p = sums.end(pick(p[0], p[1]))
    while sums.busy():
        sums.begin()
        p = sums.end(p)

    used = 0

    def part(size):
        nonlocal used
        used += size
        return p[used - size : used]

    mine_of = lambda v, size: lax.dynamic_slice_in_dim(v, f * size, size, v.ndim - 1)
    o_gain_in = mine_of(part(D), share)
    o_conv = mine_of(part(5 * CHANNELS).reshape(5, CHANNELS), CHANNELS // n)
    o_heads = mine_of(part(3 * HEADS).reshape(3, HEADS), heads)
    o_gain_out = mine_of(part(INNER), width)
    totals = part(3)
    act_rms = jnp.sqrt(totals[:2] / (totals[2] * D))[None]

    def hand_over(v, layer):
        return lax.ppermute(v, "section", [(1 - layer, layer)])

    own = [[sums.values[k] for k in ks] for ks in (gz0 + gx0 + gs0 + go0, gz1 + gx1 + gs1 + go1)]
    away = [[hand_over(v, layer) for v in own[layer]] for layer in range(2)]
    held = (own, away)
    at_small = 2 * pairs_of

    def small_rows(v):
        v = v.astype(F32)
        by_place = [at(v, f ^ k) for k in range(n)]
        return jnp.concatenate([b[:group] for b in by_place] + [b[group:] for b in by_place])

    small_in = jnp.stack(
        [small_rows(pick(side[0][at_small], side[1][at_small])) for side in held]
    )
    turned = lambda h, ids: jnp.where(h == 0, ids[1], 1 - ids[1])
    chunks_in = [
        (held[side][layer][k], side, layer, 2 * k, 2, (1, width, half), lambda i: (i, 0, 0))
        for side in range(2)
        for layer in range(2)
        for k in range(at_small)
    ]
    g_w_in = place_blocks(
        ids,
        chunks_in,
        small_in,
        (2 * INNER + GROUP + HEADS, share),
        (width, half),
        lambda h, j, ids: (
            jnp.where(j < 2 * n, (j // n) * n + jnp.bitwise_xor(j % n, ids[0]), 2 * n),
            turned(h, ids),
        ),
        2 * n + 1,
    )
    chunks_out = [
        (
            held[side][layer][at_small + 1 + k],
            side,
            layer,
            k,
            1,
            (width // 2, D // 2),
            lambda i: (0, 0),
        )
        for side in range(2)
        for layer in range(2)
        for k in range(2)
    ]
    g_w_out = place_blocks(
        ids,
        chunks_out,
        None,
        (width, D),
        (width // 2, D // 2),
        lambda h, j, ids: (turned(h, ids), j),
        2,
    )

    back = back.reshape(2, 2, rows, D)
    kept_back = pick(back[:, 0], back[:, 1])
    other_back = swap_section(pick(back[:, 1], back[:, 0]))
    both_back = jnp.stack(
        [pick(kept_back, other_back), pick(other_back, kept_back)], axis=1
    )
    return (
        both_back[0][None, :, None],
        both_back[1].astype(F32)[None, :, None],
        o_gain_in[None],
        g_w_in.T[None],
        o_conv[None, :4],
        o_conv[None, 4],
        o_heads[None, 0],
        o_heads[None, 1],
        o_heads[None, 2],
        o_gain_out[None],
        g_w_out[None],
        act_rms,
    )


def solution(mesh):
    in_specs = (
        P(None, "fsdp", "seq", None),
        P(None, "fsdp", "seq", None),
        P(None, "fsdp"),
        P("section", "fsdp"),
        P("section", "fsdp", None),
        P("section", None, "fsdp"),
        P("section", "fsdp"),
        P("section", "fsdp"),
        P("section", "fsdp"),
        P("section", "fsdp"),
        P("section", "fsdp"),
        P("section", "fsdp", None),
    )
    out_specs = (
        P("section", None, "fsdp", "seq", None),
        P("section", None, "fsdp", "seq", None),
        P("section", "fsdp"),
        P("section", "fsdp", None),
        P("section", None, "fsdp"),
        P("section", "fsdp"),
        P("section", "fsdp"),
        P("section", "fsdp"),
        P("section", "fsdp"),
        P("section", "fsdp"),
        P("section", "fsdp", None),
        P("section", None),
    )
    return jax.shard_map(
        per_device, mesh=mesh, in_specs=in_specs, out_specs=out_specs, check_vma=False
    )
```

```python
import functools

import jax
import jax.numpy as jnp
from jax import lax
from jax.experimental import pallas as pl
from jax.experimental.pallas import tpu as pltpu
from jax.sharding import PartitionSpec as P

D = 2048
INNER = 4096
HEADS = 64
HEAD_DIM = 64
STATE = 128
KERNEL = 4
GROUP = 2 * STATE
CHANNELS = INNER + GROUP
LANES = 128
EPS = 1e-05
F32 = jnp.float32
BF16 = jnp.bfloat16
VMEM_BYTES = 48 * 1024 * 1024


def split(v):
    hi = v.astype(BF16)
    return hi, (v - hi.astype(F32)).astype(BF16)


def dot32(a, b, ca, cb):
    (ah, al), (bh, bl) = (v if isinstance(v, tuple) else split(v) for v in (a, b))
    one = lambda p, q: lax.dot_general(
        p, q, (((ca,), (cb,)), ((), ())), preferred_element_type=F32
    )
    return one(ah, bh) + (one(ah, bl) + one(al, bh))


def step_sizes(raw, hp, rows):
    shifted = raw + hp[0:1, :]
    dt = jnp.maximum(shifted, 0.0) + jnp.log1p(jnp.exp(-jnp.abs(shifted)))
    decay = dt * hp[1:2, :]
    row = lax.broadcasted_iota(jnp.int32, (rows, rows), 0)
    col = lax.broadcasted_iota(jnp.int32, (rows, rows), 1)
    lower = (row >= col).astype(F32)
    cum = dot32(lower, decay, 1, 0)
    cum_t = dot32(decay, lower, 0, 1)
    return shifted, dt, cum, cum_t, row, col, lower


def pair_lanes(v, j, first):
    return jnp.where(first, v[:, 2 * j : 2 * j + 1], v[:, 2 * j + 1 : 2 * j + 2])


def head_sums(v, table):
    hi, low = split(v)
    one = lambda p: lax.dot_general(
        p, table, (((1,), (1,)), ((), ())), preferred_element_type=F32
    )
    return one(hi) + one(low)


def forward_kernel(proj, cw, hp, s0, e0, y_ref, filt_ref, st_ref, state, xp, xw_s, last_s):
    i = pl.program_id(0)
    rows, width = y_ref.shape

    @pl.when(i == 0)
    def _():
        state[...] = s0[...]
        xp[0:8, :] = e0[...]

    xp[8 : 8 + rows, :] = proj[:, : width + GROUP]

    def conv_tile(lo):
        acc = cw[4:5, lo : lo + LANES]
        for k in range(KERNEL):
            acc = acc + cw[k : k + 1, lo : lo + LANES] * xp[5 + k : 5 + k + rows, lo : lo + LANES]
        filt_ref[:, lo : lo + LANES] = acc
        return acc * jax.nn.sigmoid(acc)

    b_c = conv_tile(width)
    c_c = conv_tile(width + STATE)
    _, dt, cum, cum_t, row, col, _ = step_sizes(proj[:, width + GROUP :], hp, rows)
    last = cum[rows - 1 : rows, :]
    ecum = jnp.exp(cum)
    weight = jnp.exp(last - cum) * dt
    elast = jnp.exp(last)
    b_c, c_c = split(b_c), split(c_c)
    carried = dot32(c_c, state[...], 1, 0)
    scores = dot32(c_c, b_c, 1, 1)
    causal = row >= col
    lane = lax.broadcasted_iota(jnp.int32, (rows, LANES), 1)
    first = lane < HEAD_DIM
    for j in range(width // LANES):
        lo = j * LANES
        here = slice(lo, lo + LANES)
        x = conv_tile(lo)
        xd = x * pair_lanes(dt, j, first)
        m = []
        for h in (2 * j, 2 * j + 1):
            gap = cum[:, h : h + 1] - cum_t[h : h + 1, :]
            m.append(jnp.exp(jnp.where(causal, gap, -1e30)) * scores)
        xd2 = jnp.concatenate([jnp.where(first, xd, 0.0), jnp.where(first, 0.0, xd)])
        y = (
            dot32(jnp.concatenate(m, axis=1), xd2, 1, 0)
            + carried[:, here] * pair_lanes(ecum, j, first)
            + pair_lanes(hp[2:3, :], j, first[0:1]) * x
        )
        y_ref[:, here] = y
        xw_s[:, here] = x * pair_lanes(weight, j, first)
        last_s[0:1, here] = pair_lanes(elast, j, first[0:1])
    state[...] = state[...] * last_s[0:1, :] + dot32(b_c, xw_s[...], 0, 0)
    st_ref[0] = state[...]
    xp[0:8, :] = xp[rows : rows + 8, :]


def backward_kernel(
    pz,
    proj,
    y_ref,
    filt,
    dn,
    rc,
    st_before,
    st_out,
    s0,
    cw,
    hp,
    table,
    gain,
    g0,
    e0,
    dz_ref,
    dproj,
    dbc_ref,
    dgain_ref,
    dconv_ref,
    dhp_ref,
    gfin_ref,
    efin_ref,
    grad,
    dfp,
    both,
    xw_s,
    dyc_s,
    rowv,
):
    i = pl.program_id(0)
    rows, width = y_ref.shape
    heads = hp.shape[1]

    @pl.when(i == 0)
    def _():
        grad[...] = g0[...]
        dfp[rows : rows + 8, :] = e0[...]
        dgain_ref[...] = jnp.zeros_like(dgain_ref)
        dconv_ref[...] = jnp.zeros_like(dconv_ref)
        dhp_ref[...] = jnp.zeros_like(dhp_ref)

    def silu_pair(v):
        s = jax.nn.sigmoid(v)
        a = v * s
        return a, s * (1.0 + v - a)

    b_c, b_d = silu_pair(filt[:, width : width + STATE])
    c_c, c_d = silu_pair(filt[:, width + STATE :])
    shifted, dt, cum, cum_t, row, col, lower = step_sizes(proj[:, width + GROUP :], hp, rows)
    last = cum[rows - 1 : rows, :]
    tail = jnp.exp(last - cum)
    ecum = jnp.exp(cum)
    elast = jnp.exp(last)
    b_c, c_c = split(b_c), split(c_c)
    grad_p = split(grad[...])
    k_all = dot32(b_c, grad_p, 1, 0)
    scores_t = dot32(b_c, c_c, 1, 1)
    causal_t = row <= col
    lane = lax.broadcasted_iota(jnp.int32, (rows, LANES), 1)
    first = lane < HEAD_DIM
    dcb_t = jnp.zeros((rows, rows), F32)
    rc_t = dot32((row == col).astype(F32), rc[0], 1, 1)
    r = rc_t[:, 0:1]
    coef = rc_t[:, 1:2]
    rowv[0:1, :] = jnp.sum(grad[...] * st_out[0], axis=0, keepdims=True)
    for j in range(width // LANES):
        lo = j * LANES
        here = slice(lo, lo + LANES)
        z = pz[:, here]
        y = y_ref[:, here]
        sz, dsz = silu_pair(z)
        g = y * sz
        dnt = dn[:, here]
        dg = dnt * gain[0:1, here] * r - g * coef
        dgain_ref[0:1, here] += jnp.sum(dnt * g * r, axis=0, keepdims=True)
        dy = dg * sz
        dz_ref[:, here] = (dg * y * dsz).astype(BF16)
        x, xder = silu_pair(filt[:, here])
        dt_e = pair_lanes(dt, j, first)
        tail_e = pair_lanes(tail, j, first)
        xd = x * dt_e
        dy2 = split(jnp.concatenate([jnp.where(first, dy, 0.0), jnp.where(first, 0.0, dy)]))
        decays = []
        for h in (2 * j, 2 * j + 1):
            gap = cum_t[h : h + 1, :] - cum[:, h : h + 1]
            decays.append(jnp.exp(jnp.where(causal_t, gap, -1e30)))
        m = jnp.concatenate([d * scores_t for d in decays], axis=1)
        dm = dot32(xd, dy2, 1, 1)
        dcb_t = dcb_t + (decays[0] * dm[:, :rows] + decays[1] * dm[:, rows:])
        v = dot32(m, dy2, 1, 0) + k_all[:, here] * tail_e
        skip = pair_lanes(hp[2:3, :], j, first[0:1])
        dx = dt_e * v + skip * dy
        both[0:rows, here] = x * v
        both[rows : 2 * rows, here] = dy * (y - skip * x)
        rowv[1:2, here] = jnp.sum(dy * x, axis=0, keepdims=True)
        rowv[2:3, here] = pair_lanes(elast, j, first[0:1])
        xw_s[:, here] = xd * tail_e
        dyc_s[:, here] = dy * pair_lanes(ecum, j, first)
        dfp[0:rows, here] = dx * xder
    dcb_t = split(dcb_t)
    dyc = split(dyc_s[...])
    st_in = jnp.where(i == pl.num_programs(0) - 1, s0[...], st_before[0])
    dc = dot32(dcb_t, b_c, 0, 0) + dot32(dyc, st_in, 1, 1)
    db = dot32(dcb_t, c_c, 1, 0) + dot32(xw_s[...], grad_p, 1, 1)
    dfp[0:rows, width : width + STATE] = db * b_d
    dfp[0:rows, width + STATE :] = dc * c_d
    grad[...] = grad[...] * rowv[2:3, :] + dot32(c_c, dyc, 0, 0)
    gfin_ref[...] = grad[...]

    sums = head_sums(both[...], table[...])
    rsums = head_sums(rowv[...], table[...])
    ddt_x = sums[0:rows]
    dcum = sums[rows : 2 * rows] - dt * ddt_x
    upto = lax.broadcasted_iota(jnp.int32, (rows, heads), 0)
    dcum = dcum + jnp.where(upto == rows - 1, rsums[0:1, :], 0.0)
    ddecay = dot32(lower, dcum, 0, 0)
    ddt = ddt_x + hp[1:2, :] * ddecay
    draw = ddt * jax.nn.sigmoid(shifted)
    dproj[:, width + GROUP :] = draw.astype(BF16)
    dhp_ref[0:1, :] += jnp.sum(draw, axis=0, keepdims=True)
    dhp_ref[1:2, :] += jnp.sum(ddecay * dt, axis=0, keepdims=True) * hp[1:2, :]
    dhp_ref[2:3, :] += rsums[1:2, :]

    for lo in range(0, width + GROUP, LANES):
        here = slice(lo, lo + LANES)
        src = proj[:, here]
        total = jnp.zeros((rows, LANES), F32)
        for k in range(KERNEL):
            shift = KERNEL - 1 - k
            moved = dfp[shift : shift + rows, here]
            total = total + cw[k : k + 1, here] * moved
            dconv_ref[k : k + 1, here] += jnp.sum(src * moved, axis=0, keepdims=True)
        dconv_ref[4:5, here] += jnp.sum(dfp[0:rows, here], axis=0, keepdims=True)
        if lo < width:
            dproj[:, here] = total.astype(BF16)
        else:
            dproj[:, here] = jnp.zeros((rows, LANES), BF16)
            share = dbc_ref.shape[2]
            for k in range(LANES // share):
                dbc_ref[(lo - width) // share + k] = total[:, k * share : (k + 1) * share]
    dfp[rows : rows + 8, :] = dfp[0:8, :]
    efin_ref[...] = dfp[0:8, :]


def whole(shape):
    return pl.BlockSpec(shape, lambda i: (0,) * len(shape))


def run_forward(proj, cw, hp, s0, e0, rows):
    total, width = proj.shape[0], s0.shape[1]
    count = total // rows
    block = lambda w: pl.BlockSpec((rows, w), lambda i: (i, 0))
    shape = jax.ShapeDtypeStruct
    return pl.pallas_call(
        forward_kernel,
        grid=(count,),
        in_specs=[block(proj.shape[1])] + [whole(v.shape) for v in (cw, hp, s0, e0)],
        out_specs=[
            block(width),
            block(width + GROUP),
            pl.BlockSpec((1, STATE, width), lambda i: (i, 0, 0)),
        ],
        scratch_shapes=[
            pltpu.VMEM((STATE, width), F32),
            pltpu.VMEM((rows + 8, width + GROUP), F32),
            pltpu.VMEM((rows, width), F32),
            pltpu.VMEM((8, width), F32),
        ],
        out_shape=[
            shape((total, width), F32),
            shape((total, width + GROUP), F32),
            shape((count, STATE, width), F32),
        ],
        compiler_params=pltpu.CompilerParams(vmem_limit_bytes=VMEM_BYTES),
        name="scan_forward",
    )(proj, cw, hp, s0, e0)


def run_backward(pz, proj, y, filt, dn, rc, states, s0, cw, hp, table, gain, g0, e0, rows, places):
    total, (heads, width) = proj.shape[0], table.shape
    count = total // rows
    turn = lambda i: count - 1 - i
    block = lambda w: pl.BlockSpec((rows, w), lambda i: (turn(i), 0))
    shape = jax.ShapeDtypeStruct
    share = GROUP // places
    return pl.pallas_call(
        backward_kernel,
        grid=(count,),
        in_specs=[
            block(width),
            block(proj.shape[1]),
            block(width),
            block(width + GROUP),
            block(width),
            pl.BlockSpec((1, 8, rows), lambda i: (turn(i), 0, 0)),
            pl.BlockSpec((1, STATE, width), lambda i: (jnp.maximum(turn(i) - 1, 0), 0, 0)),
            pl.BlockSpec((1, STATE, width), lambda i: (turn(i), 0, 0)),
        ]
        + [whole(v.shape) for v in (s0, cw, hp, table, gain, g0, e0)],
        out_specs=[
            block(width),
            block(proj.shape[1]),
            pl.BlockSpec((places, rows, share), lambda i: (0, turn(i), 0)),
            whole((8, width)),
            whole((8, width + GROUP)),
            whole((8, heads)),
            whole((STATE, width)),
            whole((8, width + GROUP)),
        ],
        scratch_shapes=[
            pltpu.VMEM((STATE, width), F32),
            pltpu.VMEM((rows + 8, width + GROUP), F32),
            pltpu.VMEM((2 * rows, width), F32),
            pltpu.VMEM((rows, width), F32),
            pltpu.VMEM((rows, width), F32),
            pltpu.VMEM((8, width), F32),
        ],
        out_shape=[
            shape((total, width), BF16),
            shape(proj.shape, BF16),
            shape((places, total, share), F32),
            shape((8, width), F32),
            shape((8, width + GROUP), F32),
            shape((8, heads), F32),
            shape((STATE, width), F32),
            shape((8, width + GROUP), F32),
        ],
        compiler_params=pltpu.CompilerParams(vmem_limit_bytes=VMEM_BYTES),
        name="scan_backward",
    )(pz, proj, y, filt, dn, rc, states, states, s0, cw, hp, table, gain, g0, e0)


def bring(step, pieces, buffers, sems, own):
    for near, far, buffer, sem in zip(*pieces, buffers, sems):
        to, done = buffer.at[step % 2], sem.at[step % 2]

        @pl.when(own)
        def _():
            pltpu.make_async_copy(near[step], to, done).start()

        @pl.when(jnp.logical_not(own))
        def _():
            pltpu.make_async_copy(far[step], to, done).start()


def arrived(step, pieces, buffers, sems):
    for near, buffer, sem in zip(pieces[0], buffers, sems):
        pltpu.make_async_copy(near[step], buffer.at[step % 2], sem.at[step % 2]).wait()
    return [buffer.at[step % 2] for buffer in buffers]


def project_kernel(ids, normed, *refs, layer, n):
    near, far = [refs[0:n]], [refs[n : 2 * n]]
    out, buffer, sem = refs[2 * n :]
    pieces = (near, far)
    own = ids[1] == layer
    columns = out.shape[1]
    share = buffer.shape[2]
    bring(0, pieces, [buffer], [sem], own)
    for m in range(n):
        if m + 1 < n:
            bring(m + 1, pieces, [buffer], [sem], own)
        (w,) = arrived(m, pieces, [buffer], [sem])
        from_place = pl.multiple_of(jnp.bitwise_xor(ids[0], m) * share, share)
        a = normed[:, pl.ds(from_place, share)]
        for lo in range(0, columns, 256):
            here = slice(lo, min(lo + 256, columns))
            v = lax.dot_general(
                a, w[here, :], (((1,), (1,)), ((), ())), preferred_element_type=F32
            )
            out[:, here] = v if m == 0 else out[:, here] + v


def project(ids, normed, near, far, layer):
    n = len(near)
    columns, share = near[0].shape
    rows = normed.shape[0]
    vmem = pl.BlockSpec(memory_space=pltpu.VMEM)
    return pl.pallas_call(
        functools.partial(project_kernel, layer=layer, n=n),
        in_specs=[pl.BlockSpec(memory_space=pltpu.SMEM), vmem]
        + [pl.BlockSpec(memory_space=pl.ANY)] * (2 * n),
        out_specs=vmem,
        scratch_shapes=[
            pltpu.VMEM((2, columns, share), BF16),
            pltpu.SemaphoreType.DMA((2,)),
        ],
        out_shape=jax.ShapeDtypeStruct((rows, columns), F32),
        compiler_params=pltpu.CompilerParams(vmem_limit_bytes=VMEM_BYTES),
        cost_estimate=pl.CostEstimate(
            flops=2 * rows * columns * share * n,
            bytes_accessed=columns * share * n * 2 + rows * columns * 4,
            transcendentals=0,
        ),
        name="project",
    )(ids, normed, *near, *far)


def back_kernel(ids, dz, dx, *refs, layer, n):
    near = (refs[0:n], refs[n : 2 * n])
    far = (refs[2 * n : 3 * n], refs[3 * n : 4 * n])
    out, zbuf, xbuf, zsem, xsem = refs[4 * n :]
    pieces = (near, far)
    own = ids[1] == layer
    share = zbuf.shape[2]
    args = ([zbuf, xbuf], [zsem, xsem])
    bring(0, pieces, *args, own)
    for m in range(n):
        if m + 1 < n:
            bring(m + 1, pieces, *args, own)
        wz, wx = arrived(m, pieces, *args)
        for lo in range(0, share, 256):
            here = slice(lo, lo + 256)
            v = jnp.dot(dz[...], wz[:, here], preferred_element_type=F32) + jnp.dot(
                dx[...], wx[:, here], preferred_element_type=F32
            )
            at_lane = pl.multiple_of(jnp.bitwise_xor(ids[0], m) * share + lo, 256)
            out[:, pl.ds(at_lane, 256)] = v.astype(BF16)


def project_back(ids, dz, dx, near, far, layer):
    n = len(near[0])
    share = near[0][0].shape[1]
    rows = dz.shape[0]
    columns = dz.shape[1] + dx.shape[1]
    vmem = pl.BlockSpec(memory_space=pltpu.VMEM)
    return pl.pallas_call(
        functools.partial(back_kernel, layer=layer, n=n),
        in_specs=[pl.BlockSpec(memory_space=pltpu.SMEM), vmem, vmem]
        + [pl.BlockSpec(memory_space=pl.ANY)] * (4 * n),
        out_specs=vmem,
        scratch_shapes=[
            pltpu.VMEM((2, dz.shape[1], share), BF16),
            pltpu.VMEM((2, dx.shape[1], share), BF16),
            pltpu.SemaphoreType.DMA((2,)),
            pltpu.SemaphoreType.DMA((2,)),
        ],
        out_shape=jax.ShapeDtypeStruct((rows, n * share), BF16),
        compiler_params=pltpu.CompilerParams(vmem_limit_bytes=VMEM_BYTES),
        cost_estimate=pl.CostEstimate(
            flops=2 * rows * columns * share * n,
            bytes_accessed=columns * share * n * 2 + rows * n * share * 2,
            transcendentals=0,
        ),
        name="project_back",
    )(ids, dz, dx, *near[0], *near[1], *far[0], *far[1])


def place_kernel(ids, *refs, plan, small):
    out = refs[-1]
    h, j = pl.program_id(0), pl.program_id(1)
    for ref, (side, layer, first, size, turned) in zip(refs, plan):

        @pl.when((h == side) & (ids[1] == layer) & (j >= first) & (j < first + size))
        def _():
            v = (ref[0] if turned else ref[...]).astype(F32)
            out[...] = v.T if turned else v

    if small:

        @pl.when(j == pl.num_programs(1) - 1)
        def _():
            v = refs[len(plan)]
            out[: v.shape[1], :] = v[0]


def place_blocks(ids, chunks, small, out_shape, block, out_index, steps):
    def step_of(side, layer, first, size, index):
        def where(h, j, ids):
            used = jnp.logical_and(h == side, ids[1] == layer)
            return index(jnp.where(used, jnp.clip(j - first, 0, size - 1), 0))

        return where

    in_specs = [
        pl.BlockSpec(shape, step_of(side, layer, first, size, index))
        for _, side, layer, first, size, _, shape, index in chunks
    ]
    args = [c[0] for c in chunks]
    if small is not None:
        in_specs.append(pl.BlockSpec((1,) + small.shape[1:], lambda h, j, ids: (h, 0, 0)))
        args.append(small)
    return pl.pallas_call(
        functools.partial(
            place_kernel, plan=tuple(c[1:6] for c in chunks), small=small is not None
        ),
        grid_spec=pltpu.PrefetchScalarGridSpec(
            num_scalar_prefetch=1,
            grid=(2, steps),
            in_specs=in_specs,
            out_specs=pl.BlockSpec(block, out_index),
        ),
        out_shape=jax.ShapeDtypeStruct(out_shape, F32),
        compiler_params=pltpu.CompilerParams(vmem_limit_bytes=VMEM_BYTES),
        name="place_gradient",
    )(ids, *args)


def swap_section(v):
    return lax.ppermute(v, "section", [(0, 1), (1, 0)])


def at(v, k):
    return lax.dynamic_index_in_dim(v, k, 0, False)


def exchange(v):
    return lax.all_to_all(v, "fsdp", 0, 0, tiled=True)


def to_all(v):
    n = lax.axis_size("fsdp")
    return exchange(jnp.broadcast_to(v[None], (n,) + v.shape))


def gather_rows(v):
    return to_all(v).reshape(-1, v.shape[-1])


def scatter_sum(partial):
    n = lax.axis_size("fsdp")
    got = exchange(partial.reshape(n, -1, partial.shape[-1]))
    return jnp.sum(got.astype(F32), axis=0)


def trade_places(v):
    n, s = lax.axis_size("fsdp"), lax.axis_size("seq")
    rows, size = v.shape[0], v.shape[1] // n
    groups = [[j * n + i for i in range(n)] for j in range(s // n)]
    v = v.reshape(rows, n, size).transpose(1, 0, 2)
    v = lax.all_to_all(exchange(v), "seq", 0, 0, axis_index_groups=groups, tiled=True)
    return exchange(v).transpose(1, 0, 2).reshape(rows, n * size)


def sum_everywhere(v):
    n, s = lax.axis_size("fsdp"), lax.axis_size("seq")
    v = v + swap_section(v)
    m = 1
    while m < n:
        v = v + lax.ppermute(v, "fsdp", [(k, k ^ m) for k in range(n)])
        m *= 2
    m = 1
    while m < s:
        v = v + lax.ppermute(v, "seq", [(k, k ^ m) for k in range(s)])
        m *= 2
    return v


class SeqSums:
    def __init__(self):
        s = lax.axis_size("seq")
        half = s // 2
        self.pairs = [[(j, j + 1), (s - 1 - j, s - 2 - j)] for j in range(half - 1)]
        self.pairs.append([(half - 1, half), (half, half - 1)])
        self.inward = half
        self.pairs += [[(j + 1, j), (s - 2 - j, s - 1 - j)] for j in reversed(range(half - 1))]
        self.values, self.phase, self.moving = [], [], []

    def add(self, values):
        first = len(self.values)
        self.values += values
        self.phase += [0] * len(values)
        return list(range(first, len(self.values)))

    def begin(self):
        place = lax.axis_index("seq")
        taken = set()
        for k, step in enumerate(self.phase):
            if step == len(self.pairs) or step in taken:
                continue
            taken.add(step)
            v = self.values[k]
            got = lax.ppermute(v, "seq", self.pairs[step])
            if step < self.inward:
                v = (v.astype(F32) + got.astype(F32)).astype(BF16)
            else:
                here = functools.reduce(
                    jnp.logical_or, [place == to for _, to in self.pairs[step]]
                )
                v = jnp.where(here, got, v)
            self.moving.append((k, v))
            self.phase[k] = step + 1

    def end(self, work):
        moved = [v for _, v in self.moving]
        still = [k for k, p in enumerate(self.phase) if p == 0]
        work, moved, rest = lax.optimization_barrier(
            (work, moved, [self.values[k] for k in still])
        )
        for (k, _), v in zip(self.moving, moved):
            self.values[k] = v
        for k, v in zip(still, rest):
            self.values[k] = v
        self.moving = []
        return work

    def done(self, ks):
        return all(self.phase[k] == len(self.pairs) for k in ks)


def relay(total, local, reverse):
    n, s = lax.axis_size("fsdp"), lax.axis_size("seq")
    segments = s // n
    place = lax.axis_index("seq") // n
    own = lax.axis_index("seq") % n
    totals = lax.all_gather(total, "seq")
    locals_ = lax.all_gather(local, "seq")
    state = jnp.zeros_like(local)
    order = range(segments - 1, -1, -1) if reverse else range(segments)
    for j in order:
        use = (j > place) if reverse else (j < place)
        t = lax.dynamic_index_in_dim(totals, j * n + own, 0, False)
        v = lax.dynamic_index_in_dim(locals_, j * n + own, 0, False)
        state = jnp.where(use, t * state + v, state)
    return state


def next_segment(v, step):
    n, s = lax.axis_size("fsdp"), lax.axis_size("seq")
    pairs = [(k, k + step * n) for k in range(s) if 0 <= k + step * n < s]
    return lax.ppermute(v, "seq", pairs)


def dot_rows(a, b):
    return lax.dot_general(a, b, (((0,), (0,)), ((), ())), preferred_element_type=F32)


def dot_cols(a, b):
    return lax.dot_general(a, b, (((1,), (1,)), ((), ())), preferred_element_type=F32)


def normalised(h, gain):
    return h * lax.rsqrt(jnp.mean(h * h, axis=-1, keepdims=True) + EPS) * gain


def per_device(
    inputs,
    cotangent,
    lengths,
    gain_in,
    w_in,
    conv_w,
    conv_b,
    dt_bias,
    a_log,
    d_skip,
    gain_out,
    w_out,
):
    n = lax.axis_size("fsdp")
    nz = lax.axis_size("seq")
    segments = nz // n
    c = lax.axis_index("section")
    f = lax.axis_index("fsdp")
    place = lax.axis_index("seq")
    upper = c == 0
    rows = inputs.shape[2]
    width = INNER // n
    heads = HEADS // n
    share = D // n
    half = share // 2
    group = GROUP // n
    ids = jnp.stack([f, c]).astype(jnp.int32)
    tie = lax.optimization_barrier

    def pick(a, b):
        return jnp.where(upper, a, b)

    h0 = trade_places(at(inputs, c)[0])

    w = w_in[0].T

    def cut(first, size):
        return lax.dynamic_slice_in_dim(w, first, size, 0)

    def piece_z(m):
        return cut((f ^ m) * width, width)

    def piece_x(m):
        return jnp.concatenate(
            [
                cut(INNER + (f ^ m) * width, width),
                w[2 * INNER : 2 * INNER + GROUP],
                cut(2 * INNER + GROUP + (f ^ m) * heads, heads),
            ]
        )

    def fetch(pieces, layer):
        pairs = lambda m: [(layer * n + i, layer * n + (i ^ m)) for i in range(n)]
        near = [
            v if m == 0 else lax.ppermute(v, ("section", "fsdp"), pairs(m))
            for m, v in enumerate(pieces)
        ]
        return near, [lax.ppermute(v, "section", [(layer, 1 - layer)]) for v in near]

    pieces_x = [piece_x(m) for m in range(n)]
    pieces_z = [piece_z(m) for m in range(n)]
    near_x0, far_x0 = fetch(pieces_x, 0)
    all_h0 = gather_rows(h0)
    pieces_z0, near_x0, all_h0 = tie((pieces_z, near_x0, all_h0))
    near_z0, far_z0 = fetch(pieces_z0, 0)

    pack = jnp.concatenate(
        [
            gain_in[0],
            dt_bias[0],
            a_log[0],
            d_skip[0],
            gain_out[0],
            conv_w[0].reshape(-1),
            conv_b[0],
        ]
    )
    mine = to_all(pack)
    theirs = swap_section(mine)
    small = []
    for full in (pick(mine, theirs), pick(theirs, mine)):
        full = full.astype(F32)
        used = 0

        def take(size):
            nonlocal used
            used += size
            return full[:, used - size : used]

        gain = take(share).reshape(1, D)
        hp = [at(take(heads), f)[None] for _ in range(3)]
        hp = jnp.concatenate([hp[0], -jnp.exp(hp[1]), hp[2], jnp.zeros((5, heads), F32)])
        gout = at(take(width), f)[None]
        per = CHANNELS // n
        taps = take(KERNEL * per).reshape(n, KERNEL, per).transpose(1, 0, 2)
        bias = take(per).reshape(1, CHANNELS)
        table = jnp.concatenate(
            [taps.reshape(KERNEL, CHANNELS), bias, jnp.zeros((3, CHANNELS), F32)]
        )
        cw = jnp.concatenate(
            [lax.dynamic_slice_in_dim(table, f * width, width, 1), table[:, INNER:]], axis=1
        )
        small.append((gain, cw, hp, gout))

    pieces_x1, pieces_z1, own_ct, wo_mine, own_len, near_z0 = tie(
        (pieces_x, pieces_z, at(cotangent, c)[0], w_out[0], at(lengths, c), near_z0)
    )
    wo_other = swap_section(wo_mine)
    wo = (pick(wo_mine, wo_other), pick(wo_other, wo_mine))
    near_x1, far_x1 = fetch(pieces_x1, 1)
    near_z1, far_z1 = fetch(pieces_z1, 1)
    win = ((near_z0, far_z0, near_x0, far_x0), (near_z1, far_z1, near_x1, far_x1))
    slot_pairs = [
        ((j * n + i) * n + k, (j * n + k) * n + i)
        for j in range(segments)
        for i in range(n)
        for k in range(n)
    ]
    length = lax.ppermute(own_len, ("seq", "fsdp"), slot_pairs)
    start = ((place // n) * n + f) * rows
    valid = (start + jnp.arange(rows, dtype=jnp.int32) < length[0]).astype(F32)[:, None]
    dout1 = trade_places(own_ct).astype(F32)

    expand = (
        jnp.arange(heads)[:, None] == jnp.arange(width)[None, :] // HEAD_DIM
    ).astype(BF16)
    zero_state = jnp.zeros((STATE, width), F32)
    zero_edge = jnp.zeros((8, width + GROUP), F32)

    def project_x(normed, layer):
        return project(ids, normed, win[layer][2], win[layer][3], layer)

    def project_z(normed, layer):
        return project(ids, normed, win[layer][0], win[layer][1], layer)

    def decay_of(px, hp):
        decay = jax.nn.softplus(px[:, width + GROUP :] + hp[0:1]) * hp[1:2]
        return jnp.repeat(jnp.exp(jnp.sum(decay, axis=0)), HEAD_DIM)[None, :]

    def scan(px, layer):
        _, cw, hp, _ = small[layer]
        args = (px, cw, hp)
        if segments == 1:
            return run_forward(*args, zero_state, zero_edge, rows), zero_state
        edge = next_segment(px[-8:, : width + GROUP], 1)
        local = run_forward(*args, zero_state, edge, rows)[2][-1]
        state = relay(decay_of(px, hp), local, False)
        return run_forward(*args, state, edge, rows), state

    def unscan(pz, px, fwd, dn, rc, layer):
        (y, filt, states), state = fwd
        _, cw, hp, gout = small[layer]
        args = (pz, px, y, filt, dn, rc, states, state, cw, hp, expand, gout)
        if segments == 1:
            return run_backward(*args, zero_state, zero_edge, rows, n)[:6]
        local = run_backward(*args, zero_state, zero_edge, rows, n)[6]
        grad = relay(decay_of(px, hp), local, True)
        edge = next_segment(run_backward(*args, grad, zero_edge, rows, n)[7], -1)
        return run_backward(*args, grad, edge, rows, n)[:6]

    def gate(pz, y):
        return y * jax.nn.silu(pz)

    def gated(pz, y, r, layer):
        return (gate(pz, y) * r[:, None] * small[layer][3]).astype(BF16)

    def sum_of_shares(v):
        return jnp.sum(to_all(v), axis=0)

    normed_in0 = normalised(all_h0.astype(F32), small[0][0]).astype(BF16)
    px0 = project_x(normed_in0, 0)
    fwd0 = scan(px0, 0)
    pz0 = project_z(normed_in0, 0)
    g0 = gate(pz0, fwd0[0][0])
    stat0 = sum_of_shares(jnp.sum(g0 * g0, axis=1).reshape(n, rows)).reshape(-1)
    r0 = lax.rsqrt(stat0 / INNER + EPS)
    normed0 = gated(pz0, fwd0[0][0], r0, 0)
    mixed0 = scatter_sum(jnp.dot(normed0, wo[0], preferred_element_type=F32).astype(BF16))
    out0 = valid * (h0.astype(F32) + mixed0)
    h1 = out0.astype(BF16)

    normed_in1 = gather_rows(normalised(h1.astype(F32), small[1][0]).astype(BF16))
    px1 = project_x(normed_in1, 1)
    dmixed1 = gather_rows((valid * dout1).astype(BF16))
    dn1 = dot_cols(dmixed1, wo[1])
    fwd1 = scan(px1, 1)
    pz1 = project_z(normed_in1, 1)
    g1 = gate(pz1, fwd1[0][0])
    stat1 = sum_of_shares(
        jnp.stack(
            [
                jnp.sum(g1 * g1, axis=1).reshape(n, rows),
                jnp.sum(g1 * dn1 * small[1][3], axis=1).reshape(n, rows),
            ]
        )
    ).reshape(2, -1)
    r1 = lax.rsqrt(stat1[0] / INNER + EPS)
    normed1 = gated(pz1, fwd1[0][0], r1, 1)

    sums = SeqSums()

    def halves(v):
        v = v.reshape(v.shape[0], n, 2, half)
        return [
            pick(v[:, :, t], v[:, :, 1 - t]).reshape(v.shape[0], n * half) for t in range(2)
        ]

    def half_sums(own, away, parts):
        sizes = [p.shape[1] for p in parts]
        other = swap_section(dot_rows(away, jnp.concatenate(parts, axis=1)).astype(BF16))
        result, first = [], 0
        for p, size in zip(parts, sizes):
            share_of = other[:, first : first + size].astype(F32)
            result.append((dot_rows(own, p) + share_of).astype(BF16))
            first += size
        return result

    def grads_in(kept, parts):
        return [v.reshape(n, half, -1) for v in half_sums(*kept, parts)]

    def grads_out(normed, dmixed):
        part = lambda k: lax.dynamic_slice_in_dim(normed, k * (width // 2), width // 2, 1)
        return half_sums(part(c), part(1 - c), [dmixed[:, : D // 2], dmixed[:, D // 2 :]])

    def with_group(dxs, dbc):
        total = jnp.sum(exchange(dbc), axis=0).astype(BF16)
        column = jnp.arange(GROUP)[None, :] // group
        own = jnp.where(column == f, jnp.concatenate([total] * n, axis=1), 0)
        full = lax.dynamic_update_slice(dxs, own.astype(BF16), (0, width))
        late = jnp.concatenate(
            [dxs[:, width // 2 : width], total, dxs[:, width + GROUP :]], axis=1
        )
        return full, late

    def back_in(dz, full, layer):
        near_z, far_z, near_x, far_x = win[layer]
        return project_back(ids, dz, full, (near_z, near_x), (far_z, far_x), layer)

    def back_norm(dout, dnormed_in, h, gain):
        h = h.astype(F32)
        r = lax.rsqrt(jnp.mean(h * h, axis=-1, keepdims=True) + EPS)
        u = dnormed_in * gain
        mean = jnp.mean(u * h, axis=-1, keepdims=True)
        dgain = jnp.sum(dnormed_in * h * r, axis=0)
        return valid * dout + r * u - h * (r * r * r) * mean, dgain

    def scales(r, coef):
        top = jnp.stack([r.reshape(n, rows), coef.reshape(n, rows)], axis=1)
        return jnp.concatenate([top, jnp.zeros((n, 6, rows), F32)], axis=1)

    rc1 = scales(r1, (r1 * r1 * r1 / INNER) * stat1[1])
    kept0, kept1 = halves(normed_in0), halves(normed_in1)
    go1 = sums.add(grads_out(normed1, dmixed1))
    rc1, normed1, h1 = sums.end((rc1, normed1, h1))

    sums.begin()
    mixed1 = scatter_sum(jnp.dot(normed1, wo[1], preferred_element_type=F32).astype(BF16))
    d1 = unscan(pz1, px1, fwd1, dn1, rc1, 1)
    out1 = valid * (h1.astype(F32) + mixed1)
    d1, out1, mixed1 = sums.end((d1, out1, mixed1))

    sums.begin()
    full1, late1 = with_group(d1[1], d1[2])
    back1 = back_in(d1[0], full1, 1)
    gz = grads_in(kept1, [d1[0][:, : width // 2], d1[0][:, width // 2 :]])
    back1, late1, gz = sums.end((back1, late1, gz))
    gz1 = sums.add(gz)

    sums.begin()
    dnin1 = scatter_sum(back1)
    gx = grads_in(kept1, [d1[1][:, : width // 2], late1])
    dnin1, gx = sums.end((dnin1, gx))
    gx1 = sums.add(gx)

    sums.begin()
    grad1, dgin1 = back_norm(dout1, dnin1, h1, small[1][0])
    dout0 = grad1.astype(BF16).astype(F32)
    dmixed0_own = (valid * dout0).astype(BF16)
    dmixed0 = gather_rows(dmixed0_own)
    along0 = to_all(jnp.sum(dmixed0_own.astype(F32) * mixed0, axis=-1)).reshape(-1)
    rc0 = scales(r0, (r0 * r0 / INNER) * along0)
    grad1, dgin1, dmixed0, rc0 = sums.end((grad1, dgin1, dmixed0, rc0))

    sums.begin()
    dn0 = dot_cols(dmixed0, wo[0])
    d0 = unscan(pz0, px0, fwd0, dn0, rc0, 0)
    d0 = sums.end(d0)

    sums.begin()
    go = grads_out(normed0, dmixed0)
    full0, late0 = with_group(d0[1], d0[2])
    gz = [exchange(v) for v in grads_in(kept0, [d0[0][:, : width // 2], d0[0][:, width // 2 :]])]
    go, full0, late0, gz = sums.end((go, full0, late0, gz))
    go0 = sums.add(go)
    gz0 = sums.add(gz)

    sums.begin()
    dnin0 = scatter_sum(back_in(d0[0], full0, 0))
    gx = grads_in(kept0, [d0[1][:, : width // 2], late0])
    dnin0, gx = sums.end((dnin0, gx))

    sums.begin()
    gx = [exchange(v) for v in gx]
    grad0, dgin0 = back_norm(dout0, dnin0, h0, small[0][0])
    gx, grad0, dgin0 = sums.end((gx, grad0, dgin0))
    gx0 = sums.add(gx)

    sums.begin()
    back = trade_places(
        jnp.concatenate([h1, out1.astype(BF16), grad0.astype(BF16), grad1.astype(BF16)])
    )
    back = sums.end(back)

    sums.begin()
    smalls1 = (d1[3][0], d1[4][:5], d1[5][:3])
    smalls0 = (d0[3][0], d0[4][:5], d0[5][:3])

    def packed(dgin, smalls, out, mixed):
        dgain, dconv, dhp = smalls
        put = lambda v, size, at_lane: lax.dynamic_update_slice(
            jnp.zeros(v.shape[:-1] + (size,), F32), v, (0,) * (v.ndim - 1) + (at_lane,)
        )
        conv = put(dconv[:, :width], CHANNELS, f * width)
        conv = conv.at[:, INNER:].set(dconv[:, width:])
        totals = jnp.stack(
            [jnp.sum(out * out), jnp.sum((valid * mixed) ** 2), jnp.sum(valid)]
        )
        return jnp.concatenate(
            [
                dgin,
                conv.reshape(-1),
                put(dhp, HEADS, f * heads).reshape(-1),
                put(dgain, INNER, f * width),
                totals,
            ]
        )

    p = sum_everywhere(
        jnp.stack([packed(dgin0, smalls0, out0, mixed0), packed(dgin1, smalls1, out1, mixed1)])
    )
    p = sums.end(pick(p[0], p[1]))

    def hand_over(v, layer):
        return lax.ppermute(v, "section", [(1 - layer, layer)])

    names = {"own": {}, "away": {}}
    order = [(k, 1, "in") for k in gz1 + gx1] + [(k, 1, "out") for k in go1]
    order += [(k, 0, "in") for k in gz0 + gx0] + [(k, 0, "out") for k in go0]
    while order:
        sums.begin()
        ready = [e for e in order if e[0] not in [k for k, _ in sums.moving]]
        ready = [e for e in ready if sums.done([e[0]])][:3]
        fresh = []
        for k, layer, kind in ready:
            v = sums.values[k]
            v = exchange(v) if (layer, kind) == (1, "in") else v
            fresh.append((v, hand_over(v, layer)))
        fresh, p = sums.end((fresh, p))
        for (k, layer, kind), (v, other) in zip(ready, fresh):
            names["own"][k], names["away"][k] = v, other
        order = [e for e in order if e not in ready]

    used = 0

    def part(size):
        nonlocal used
        used += size
        return p[used - size : used]

    mine_of = lambda v, size: lax.dynamic_slice_in_dim(v, f * size, size, v.ndim - 1)
    o_gain_in = mine_of(part(D), share)
    o_conv = mine_of(part(5 * CHANNELS).reshape(5, CHANNELS), CHANNELS // n)
    o_heads = mine_of(part(3 * HEADS).reshape(3, HEADS), heads)
    o_gain_out = mine_of(part(INNER), width)
    totals = part(3)
    act_rms = jnp.sqrt(totals[:2] / (totals[2] * D))[None]

    sides = ("own", "away")
    part_width = width // 2
    by_layer = (gz0 + gx0, gz1 + gx1)

    def small_rows(v):
        v = v[:, :, part_width:].astype(F32).transpose(0, 2, 1)
        return jnp.concatenate(
            [v[:, :group].reshape(GROUP, half), v[:, group:].reshape(HEADS, half)]
        )

    small_in = jnp.stack(
        [
            small_rows(pick(names[side][by_layer[0][3]], names[side][by_layer[1][3]]))
            for side in sides
        ]
    )
    turned = lambda h, ids: jnp.where(h == 0, ids[1], 1 - ids[1])
    chunks_in = [
        (
            names[side][by_layer[layer][k]],
            s,
            layer,
            n * k,
            n,
            True,
            (1, half, part_width),
            lambda i: (i, 0, 0),
        )
        for s, side in enumerate(sides)
        for layer in range(2)
        for k in range(4)
    ]
    g_w_in = place_blocks(
        ids,
        chunks_in,
        small_in,
        (2 * INNER + GROUP + HEADS, share),
        (part_width, half),
        lambda h, j, ids: (
            jnp.where(
                j < 4 * n, j // (2 * n) * 2 * n + (j % n) * 2 + j // n % 2, 4 * n
            ),
            turned(h, ids),
        ),
        4 * n + 1,
    )
    chunks_out = [
        (
            names[side][(go0, go1)[layer][k]],
            s,
            layer,
            k,
            1,
            False,
            (width // 2, D // 2),
            lambda i: (0, 0),
        )
        for s, side in enumerate(sides)
        for layer in range(2)
        for k in range(2)
    ]
    g_w_out = place_blocks(
        ids,
        chunks_out,
        None,
        (width, D),
        (width // 2, D // 2),
        lambda h, j, ids: (turned(h, ids), j),
        2,
    )

    back = back.reshape(2, 2, rows, D)
    kept_back = pick(back[:, 0], back[:, 1])
    other_back = swap_section(pick(back[:, 1], back[:, 0]))
    both_back = jnp.stack(
        [pick(kept_back, other_back), pick(other_back, kept_back)], axis=1
    )
    return (
        both_back[0][None, :, None],
        both_back[1].astype(F32)[None, :, None],
        o_gain_in[None],
        g_w_in.T[None],
        o_conv[None, :4],
        o_conv[None, 4],
        o_heads[None, 0],
        o_heads[None, 1],
        o_heads[None, 2],
        o_gain_out[None],
        g_w_out[None],
        act_rms,
    )


def solution(mesh):
    in_specs = (
        P(None, "fsdp", "seq", None),
        P(None, "fsdp", "seq", None),
        P(None, "fsdp"),
        P("section", "fsdp"),
        P("section", "fsdp", None),
        P("section", None, "fsdp"),
        P("section", "fsdp"),
        P("section", "fsdp"),
        P("section", "fsdp"),
        P("section", "fsdp"),
        P("section", "fsdp"),
        P("section", "fsdp", None),
    )
    out_specs = (
        P("section", None, "fsdp", "seq", None),
        P("section", None, "fsdp", "seq", None),
        P("section", "fsdp"),
        P("section", "fsdp", None),
        P("section", None, "fsdp"),
        P("section", "fsdp"),
        P("section", "fsdp"),
        P("section", "fsdp"),
        P("section", "fsdp"),
        P("section", "fsdp"),
        P("section", "fsdp", None),
        P("section", None),
    )
    return jax.shard_map(
        per_device, mesh=mesh, in_specs=in_specs, out_specs=out_specs, check_vma=False
    )
```

```python
import functools

import jax
import jax.numpy as jnp
from jax import lax
from jax.experimental import pallas as pl
from jax.experimental.pallas import tpu as pltpu
from jax.sharding import PartitionSpec as P

D = 2048
INNER = 4096
HEADS = 64
HEAD_DIM = 64
STATE = 128
KERNEL = 4
GROUP = 2 * STATE
CHANNELS = INNER + GROUP
LANES = 128
EPS = 1e-05
F32 = jnp.float32
BF16 = jnp.bfloat16
VMEM_BYTES = 48 * 1024 * 1024


def split(v):
    hi = v.astype(BF16)
    return hi, (v - hi.astype(F32)).astype(BF16)


def dot32(a, b, ca, cb):
    (ah, al), (bh, bl) = (v if isinstance(v, tuple) else split(v) for v in (a, b))
    one = lambda p, q: lax.dot_general(
        p, q, (((ca,), (cb,)), ((), ())), preferred_element_type=F32
    )
    return one(ah, bh) + (one(ah, bl) + one(al, bh))


def step_sizes(raw, hp, rows):
    shifted = raw + hp[0:1, :]
    dt = jnp.maximum(shifted, 0.0) + jnp.log1p(jnp.exp(-jnp.abs(shifted)))
    decay = dt * hp[1:2, :]
    row = lax.broadcasted_iota(jnp.int32, (rows, rows), 0)
    col = lax.broadcasted_iota(jnp.int32, (rows, rows), 1)
    lower = (row >= col).astype(F32)
    cum = dot32(lower, decay, 1, 0)
    cum_t = dot32(decay, lower, 0, 1)
    return shifted, dt, cum, cum_t, row, col, lower


def pair_lanes(v, j, first):
    return jnp.where(first, v[:, 2 * j : 2 * j + 1], v[:, 2 * j + 1 : 2 * j + 2])


def head_sums(v, table):
    hi, low = split(v)
    one = lambda p: lax.dot_general(
        p, table, (((1,), (1,)), ((), ())), preferred_element_type=F32
    )
    return one(hi) + one(low)


def forward_kernel(proj, cw, hp, s0, e0, y_ref, filt_ref, st_ref, state, xp, xw_s, last_s):
    i = pl.program_id(0)
    rows, width = y_ref.shape

    @pl.when(i == 0)
    def _():
        state[...] = s0[...]
        xp[0:8, :] = e0[...]

    xp[8 : 8 + rows, :] = proj[:, : width + GROUP]

    def conv_tile(lo):
        acc = cw[4:5, lo : lo + LANES]
        for k in range(KERNEL):
            acc = acc + cw[k : k + 1, lo : lo + LANES] * xp[5 + k : 5 + k + rows, lo : lo + LANES]
        filt_ref[:, lo : lo + LANES] = acc
        return acc * jax.nn.sigmoid(acc)

    b_c = conv_tile(width)
    c_c = conv_tile(width + STATE)
    _, dt, cum, cum_t, row, col, _ = step_sizes(proj[:, width + GROUP :], hp, rows)
    last = cum[rows - 1 : rows, :]
    ecum = jnp.exp(cum)
    weight = jnp.exp(last - cum) * dt
    elast = jnp.exp(last)
    b_c, c_c = split(b_c), split(c_c)
    carried = dot32(c_c, state[...], 1, 0)
    scores = dot32(c_c, b_c, 1, 1)
    causal = row >= col
    lane = lax.broadcasted_iota(jnp.int32, (rows, LANES), 1)
    first = lane < HEAD_DIM
    for j in range(width // LANES):
        lo = j * LANES
        here = slice(lo, lo + LANES)
        x = conv_tile(lo)
        xd = x * pair_lanes(dt, j, first)
        m = []
        for h in (2 * j, 2 * j + 1):
            gap = cum[:, h : h + 1] - cum_t[h : h + 1, :]
            m.append(jnp.exp(jnp.where(causal, gap, -1e30)) * scores)
        xd2 = jnp.concatenate([jnp.where(first, xd, 0.0), jnp.where(first, 0.0, xd)])
        y = (
            dot32(jnp.concatenate(m, axis=1), xd2, 1, 0)
            + carried[:, here] * pair_lanes(ecum, j, first)
            + pair_lanes(hp[2:3, :], j, first[0:1]) * x
        )
        y_ref[:, here] = y
        xw_s[:, here] = x * pair_lanes(weight, j, first)
        last_s[0:1, here] = pair_lanes(elast, j, first[0:1])
    state[...] = state[...] * last_s[0:1, :] + dot32(b_c, xw_s[...], 0, 0)
    st_ref[0] = state[...]
    xp[0:8, :] = xp[rows : rows + 8, :]


def backward_kernel(
    pz,
    proj,
    y_ref,
    filt,
    dn,
    rc,
    st_before,
    st_out,
    s0,
    cw,
    hp,
    table,
    gain,
    g0,
    e0,
    dz_ref,
    dproj,
    dbc_ref,
    dgain_ref,
    dconv_ref,
    dhp_ref,
    gfin_ref,
    efin_ref,
    grad,
    dfp,
    both,
    xw_s,
    dyc_s,
    rowv,
):
    i = pl.program_id(0)
    rows, width = y_ref.shape
    heads = hp.shape[1]

    @pl.when(i == 0)
    def _():
        grad[...] = g0[...]
        dfp[rows : rows + 8, :] = e0[...]
        dgain_ref[...] = jnp.zeros_like(dgain_ref)
        dconv_ref[...] = jnp.zeros_like(dconv_ref)
        dhp_ref[...] = jnp.zeros_like(dhp_ref)

    def silu_pair(v):
        s = jax.nn.sigmoid(v)
        a = v * s
        return a, s * (1.0 + v - a)

    b_c, b_d = silu_pair(filt[:, width : width + STATE])
    c_c, c_d = silu_pair(filt[:, width + STATE :])
    shifted, dt, cum, cum_t, row, col, lower = step_sizes(proj[:, width + GROUP :], hp, rows)
    last = cum[rows - 1 : rows, :]
    tail = jnp.exp(last - cum)
    ecum = jnp.exp(cum)
    elast = jnp.exp(last)
    b_c, c_c = split(b_c), split(c_c)
    grad_p = split(grad[...])
    k_all = dot32(b_c, grad_p, 1, 0)
    scores_t = dot32(b_c, c_c, 1, 1)
    causal_t = row <= col
    lane = lax.broadcasted_iota(jnp.int32, (rows, LANES), 1)
    first = lane < HEAD_DIM
    dcb_t = jnp.zeros((rows, rows), F32)
    rc_t = dot32((row == col).astype(F32), rc[0], 1, 1)
    r = rc_t[:, 0:1]
    coef = rc_t[:, 1:2]
    rowv[0:1, :] = jnp.sum(grad[...] * st_out[0], axis=0, keepdims=True)
    for j in range(width // LANES):
        lo = j * LANES
        here = slice(lo, lo + LANES)
        z = pz[:, here]
        y = y_ref[:, here]
        sz, dsz = silu_pair(z)
        g = y * sz
        dnt = dn[:, here]
        dg = dnt * gain[0:1, here] * r - g * coef
        dgain_ref[0:1, here] += jnp.sum(dnt * g * r, axis=0, keepdims=True)
        dy = dg * sz
        dz_ref[:, here] = (dg * y * dsz).astype(BF16)
        x, xder = silu_pair(filt[:, here])
        dt_e = pair_lanes(dt, j, first)
        tail_e = pair_lanes(tail, j, first)
        xd = x * dt_e
        dy2 = split(jnp.concatenate([jnp.where(first, dy, 0.0), jnp.where(first, 0.0, dy)]))
        decays = []
        for h in (2 * j, 2 * j + 1):
            gap = cum_t[h : h + 1, :] - cum[:, h : h + 1]
            decays.append(jnp.exp(jnp.where(causal_t, gap, -1e30)))
        m = jnp.concatenate([d * scores_t for d in decays], axis=1)
        dm = dot32(xd, dy2, 1, 1)
        dcb_t = dcb_t + (decays[0] * dm[:, :rows] + decays[1] * dm[:, rows:])
        v = dot32(m, dy2, 1, 0) + k_all[:, here] * tail_e
        skip = pair_lanes(hp[2:3, :], j, first[0:1])
        dx = dt_e * v + skip * dy
        both[0:rows, here] = x * v
        both[rows : 2 * rows, here] = dy * (y - skip * x)
        rowv[1:2, here] = jnp.sum(dy * x, axis=0, keepdims=True)
        rowv[2:3, here] = pair_lanes(elast, j, first[0:1])
        xw_s[:, here] = xd * tail_e
        dyc_s[:, here] = dy * pair_lanes(ecum, j, first)
        dfp[0:rows, here] = dx * xder
    dcb_t = split(dcb_t)
    dyc = split(dyc_s[...])
    st_in = jnp.where(i == pl.num_programs(0) - 1, s0[...], st_before[0])
    dc = dot32(dcb_t, b_c, 0, 0) + dot32(dyc, st_in, 1, 1)
    db = dot32(dcb_t, c_c, 1, 0) + dot32(xw_s[...], grad_p, 1, 1)
    dfp[0:rows, width : width + STATE] = db * b_d
    dfp[0:rows, width + STATE :] = dc * c_d
    grad[...] = grad[...] * rowv[2:3, :] + dot32(c_c, dyc, 0, 0)
    gfin_ref[...] = grad[...]

    sums = head_sums(both[...], table[...])
    rsums = head_sums(rowv[...], table[...])
    ddt_x = sums[0:rows]
    dcum = sums[rows : 2 * rows] - dt * ddt_x
    upto = lax.broadcasted_iota(jnp.int32, (rows, heads), 0)
    dcum = dcum + jnp.where(upto == rows - 1, rsums[0:1, :], 0.0)
    ddecay = dot32(lower, dcum, 0, 0)
    ddt = ddt_x + hp[1:2, :] * ddecay
    draw = ddt * jax.nn.sigmoid(shifted)
    dproj[:, width + GROUP :] = draw.astype(BF16)
    dhp_ref[0:1, :] += jnp.sum(draw, axis=0, keepdims=True)
    dhp_ref[1:2, :] += jnp.sum(ddecay * dt, axis=0, keepdims=True) * hp[1:2, :]
    dhp_ref[2:3, :] += rsums[1:2, :]

    for lo in range(0, width + GROUP, LANES):
        here = slice(lo, lo + LANES)
        src = proj[:, here]
        total = jnp.zeros((rows, LANES), F32)
        for k in range(KERNEL):
            shift = KERNEL - 1 - k
            moved = dfp[shift : shift + rows, here]
            total = total + cw[k : k + 1, here] * moved
            dconv_ref[k : k + 1, here] += jnp.sum(src * moved, axis=0, keepdims=True)
        dconv_ref[4:5, here] += jnp.sum(dfp[0:rows, here], axis=0, keepdims=True)
        if lo < width:
            dproj[:, here] = total.astype(BF16)
        else:
            dproj[:, here] = jnp.zeros((rows, LANES), BF16)
            share = dbc_ref.shape[2]
            for k in range(LANES // share):
                dbc_ref[(lo - width) // share + k] = total[:, k * share : (k + 1) * share]
    dfp[rows : rows + 8, :] = dfp[0:8, :]
    efin_ref[...] = dfp[0:8, :]


def whole(shape):
    return pl.BlockSpec(shape, lambda i: (0,) * len(shape))


def run_forward(proj, cw, hp, s0, e0, rows):
    total, width = proj.shape[0], s0.shape[1]
    count = total // rows
    block = lambda w: pl.BlockSpec((rows, w), lambda i: (i, 0))
    shape = jax.ShapeDtypeStruct
    return pl.pallas_call(
        forward_kernel,
        grid=(count,),
        in_specs=[block(proj.shape[1])] + [whole(v.shape) for v in (cw, hp, s0, e0)],
        out_specs=[
            block(width),
            block(width + GROUP),
            pl.BlockSpec((1, STATE, width), lambda i: (i, 0, 0)),
        ],
        scratch_shapes=[
            pltpu.VMEM((STATE, width), F32),
            pltpu.VMEM((rows + 8, width + GROUP), F32),
            pltpu.VMEM((rows, width), F32),
            pltpu.VMEM((8, width), F32),
        ],
        out_shape=[
            shape((total, width), F32),
            shape((total, width + GROUP), F32),
            shape((count, STATE, width), F32),
        ],
        compiler_params=pltpu.CompilerParams(vmem_limit_bytes=VMEM_BYTES),
        name="scan_forward",
    )(proj, cw, hp, s0, e0)


def run_backward(pz, proj, y, filt, dn, rc, states, s0, cw, hp, table, gain, g0, e0, rows, places):
    total, (heads, width) = proj.shape[0], table.shape
    count = total // rows
    turn = lambda i: count - 1 - i
    block = lambda w: pl.BlockSpec((rows, w), lambda i: (turn(i), 0))
    shape = jax.ShapeDtypeStruct
    share = GROUP // places
    return pl.pallas_call(
        backward_kernel,
        grid=(count,),
        in_specs=[
            block(width),
            block(proj.shape[1]),
            block(width),
            block(width + GROUP),
            block(width),
            pl.BlockSpec((1, 8, rows), lambda i: (turn(i), 0, 0)),
            pl.BlockSpec((1, STATE, width), lambda i: (jnp.maximum(turn(i) - 1, 0), 0, 0)),
            pl.BlockSpec((1, STATE, width), lambda i: (turn(i), 0, 0)),
        ]
        + [whole(v.shape) for v in (s0, cw, hp, table, gain, g0, e0)],
        out_specs=[
            block(width),
            block(proj.shape[1]),
            pl.BlockSpec((places, rows, share), lambda i: (0, turn(i), 0)),
            whole((8, width)),
            whole((8, width + GROUP)),
            whole((8, heads)),
            whole((STATE, width)),
            whole((8, width + GROUP)),
        ],
        scratch_shapes=[
            pltpu.VMEM((STATE, width), F32),
            pltpu.VMEM((rows + 8, width + GROUP), F32),
            pltpu.VMEM((2 * rows, width), F32),
            pltpu.VMEM((rows, width), F32),
            pltpu.VMEM((rows, width), F32),
            pltpu.VMEM((8, width), F32),
        ],
        out_shape=[
            shape((total, width), BF16),
            shape(proj.shape, BF16),
            shape((places, total, share), F32),
            shape((8, width), F32),
            shape((8, width + GROUP), F32),
            shape((8, heads), F32),
            shape((STATE, width), F32),
            shape((8, width + GROUP), F32),
        ],
        compiler_params=pltpu.CompilerParams(vmem_limit_bytes=VMEM_BYTES),
        name="scan_backward",
    )(pz, proj, y, filt, dn, rc, states, states, s0, cw, hp, table, gain, g0, e0)


def bring(step, pieces, buffers, sems, own):
    for near, far, buffer, sem in zip(*pieces, buffers, sems):
        to, done = buffer.at[step % 2], sem.at[step % 2]

        @pl.when(own)
        def _():
            pltpu.make_async_copy(near[step], to, done).start()

        @pl.when(jnp.logical_not(own))
        def _():
            pltpu.make_async_copy(far[step], to, done).start()


def arrived(step, pieces, buffers, sems):
    for near, buffer, sem in zip(pieces[0], buffers, sems):
        pltpu.make_async_copy(near[step], buffer.at[step % 2], sem.at[step % 2]).wait()
    return [buffer.at[step % 2] for buffer in buffers]


def project_kernel(ids, normed, *refs, layer, n):
    near, far = [refs[0:n]], [refs[n : 2 * n]]
    out, buffer, sem = refs[2 * n :]
    pieces = (near, far)
    own = ids[1] == layer
    columns = out.shape[1]
    share = buffer.shape[2]
    bring(0, pieces, [buffer], [sem], own)
    for m in range(n):
        if m + 1 < n:
            bring(m + 1, pieces, [buffer], [sem], own)
        (w,) = arrived(m, pieces, [buffer], [sem])
        from_place = pl.multiple_of(jnp.bitwise_xor(ids[0], m) * share, share)
        a = normed[:, pl.ds(from_place, share)]
        for lo in range(0, columns, 256):
            here = slice(lo, min(lo + 256, columns))
            v = lax.dot_general(
                a, w[here, :], (((1,), (1,)), ((), ())), preferred_element_type=F32
            )
            out[:, here] = v if m == 0 else out[:, here] + v


def project(ids, normed, near, far, layer):
    n = len(near)
    columns, share = near[0].shape
    rows = normed.shape[0]
    vmem = pl.BlockSpec(memory_space=pltpu.VMEM)
    return pl.pallas_call(
        functools.partial(project_kernel, layer=layer, n=n),
        in_specs=[pl.BlockSpec(memory_space=pltpu.SMEM), vmem]
        + [pl.BlockSpec(memory_space=pl.ANY)] * (2 * n),
        out_specs=vmem,
        scratch_shapes=[
            pltpu.VMEM((2, columns, share), BF16),
            pltpu.SemaphoreType.DMA((2,)),
        ],
        out_shape=jax.ShapeDtypeStruct((rows, columns), F32),
        compiler_params=pltpu.CompilerParams(vmem_limit_bytes=VMEM_BYTES),
        cost_estimate=pl.CostEstimate(
            flops=2 * rows * columns * share * n,
            bytes_accessed=columns * share * n * 2 + rows * columns * 4,
            transcendentals=0,
        ),
        name="project",
    )(ids, normed, *near, *far)


def back_kernel(ids, dz, dx, *refs, layer, n):
    near = (refs[0:n], refs[n : 2 * n])
    far = (refs[2 * n : 3 * n], refs[3 * n : 4 * n])
    out, zbuf, xbuf, zsem, xsem = refs[4 * n :]
    pieces = (near, far)
    own = ids[1] == layer
    share = zbuf.shape[2]
    args = ([zbuf, xbuf], [zsem, xsem])
    bring(0, pieces, *args, own)
    for m in range(n):
        if m + 1 < n:
            bring(m + 1, pieces, *args, own)
        wz, wx = arrived(m, pieces, *args)
        for lo in range(0, share, 256):
            here = slice(lo, lo + 256)
            v = jnp.dot(dz[...], wz[:, here], preferred_element_type=F32) + jnp.dot(
                dx[...], wx[:, here], preferred_element_type=F32
            )
            at_lane = pl.multiple_of(jnp.bitwise_xor(ids[0], m) * share + lo, 256)
            out[:, pl.ds(at_lane, 256)] = v.astype(BF16)


def project_back(ids, dz, dx, near, far, layer):
    n = len(near[0])
    share = near[0][0].shape[1]
    rows = dz.shape[0]
    columns = dz.shape[1] + dx.shape[1]
    vmem = pl.BlockSpec(memory_space=pltpu.VMEM)
    return pl.pallas_call(
        functools.partial(back_kernel, layer=layer, n=n),
        in_specs=[pl.BlockSpec(memory_space=pltpu.SMEM), vmem, vmem]
        + [pl.BlockSpec(memory_space=pl.ANY)] * (4 * n),
        out_specs=vmem,
        scratch_shapes=[
            pltpu.VMEM((2, dz.shape[1], share), BF16),
            pltpu.VMEM((2, dx.shape[1], share), BF16),
            pltpu.SemaphoreType.DMA((2,)),
            pltpu.SemaphoreType.DMA((2,)),
        ],
        out_shape=jax.ShapeDtypeStruct((rows, n * share), BF16),
        compiler_params=pltpu.CompilerParams(vmem_limit_bytes=VMEM_BYTES),
        cost_estimate=pl.CostEstimate(
            flops=2 * rows * columns * share * n,
            bytes_accessed=columns * share * n * 2 + rows * n * share * 2,
            transcendentals=0,
        ),
        name="project_back",
    )(ids, dz, dx, *near[0], *near[1], *far[0], *far[1])


def place_kernel(ids, *refs, plan, count, rows_of_small):
    small = refs[count]
    out, eye, pieces, blocks, in_sem, out_sem = refs[-6:]
    core = ids[1]
    size, share = blocks.shape[1:]

    def fetch(k):
        for layer in range(2):

            @pl.when(core == layer)
            def _():
                src = refs[plan[k][layer]]
                pltpu.make_async_copy(
                    src.at[:, :, pl.ds(0, size)], pieces.at[k % 2], in_sem.at[k % 2]
                ).start()

    def send(step, first, count):
        return pltpu.make_async_copy(
            blocks.at[step % 2, pl.ds(0, count)],
            out.at[pl.ds(first, count)],
            out_sem.at[step % 2],
        )

    eye[...] = (
        lax.broadcasted_iota(jnp.int32, eye.shape, 0)
        == lax.broadcasted_iota(jnp.int32, eye.shape, 1)
    ).astype(BF16)
    fetch(0)
    sent = []
    for k, (_, _, side, firsts) in enumerate(plan):
        if k + 1 < len(plan):
            fetch(k + 1)
        pltpu.make_async_copy(pieces.at[k % 2], pieces.at[k % 2], in_sem.at[k % 2]).wait()
        shift = jnp.where(side == 0, core, 1 - core) * (2 * size)
        for p, first in enumerate(firsts):
            step = len(sent)
            if step >= 2:
                sent[step - 2].wait()
            blocks[step % 2] = lax.dot_general(
                pieces[k % 2, p],
                eye[...],
                (((0,), (0,)), ((), ())),
                preferred_element_type=F32,
            )
            sent.append(send(step, pl.multiple_of(first + shift, 8), size))
            sent[-1].start()
    if rows_of_small:
        step = len(sent)
        sent[step - 2].wait()
        first, count = rows_of_small
        sent.append(
            pltpu.make_async_copy(small, out.at[pl.ds(first, count)], out_sem.at[step % 2])
        )
        sent[-1].start()
    sent[-2].wait()
    sent[-1].wait()


def place_in(ids, arrays, plan, small, rows_of_small, before, shape, size):
    places, share, _ = arrays[0].shape
    any_space = pl.BlockSpec(memory_space=pl.ANY)
    return pl.pallas_call(
        functools.partial(
            place_kernel, plan=plan, count=len(arrays), rows_of_small=rows_of_small
        ),
        in_specs=[pl.BlockSpec(memory_space=pltpu.SMEM)]
        + [any_space] * len(arrays)
        + [pl.BlockSpec(memory_space=pltpu.VMEM)]
        + [any_space] * len(before),
        out_specs=any_space,
        scratch_shapes=[
            pltpu.VMEM((share, share), BF16),
            pltpu.VMEM((2, places, share, size), BF16),
            pltpu.VMEM((2, size, share), F32),
            pltpu.SemaphoreType.DMA((2,)),
            pltpu.SemaphoreType.DMA((2,)),
        ],
        out_shape=jax.ShapeDtypeStruct(shape, F32),
        input_output_aliases={len(arrays) + 2: 0} if before else {},
        compiler_params=pltpu.CompilerParams(vmem_limit_bytes=VMEM_BYTES),
        name="place_in",
    )(ids, *arrays, small, *before)


def swap_section(v):
    return lax.ppermute(v, "section", [(0, 1), (1, 0)])


def at(v, k):
    return lax.dynamic_index_in_dim(v, k, 0, False)


def exchange(v):
    return lax.all_to_all(v, "fsdp", 0, 0, tiled=True)


def to_all(v):
    n = lax.axis_size("fsdp")
    return exchange(jnp.broadcast_to(v[None], (n,) + v.shape))


def gather_rows(v):
    return to_all(v).reshape(-1, v.shape[-1])


def scatter_sum(partial):
    n = lax.axis_size("fsdp")
    got = exchange(partial.reshape(n, -1, partial.shape[-1]))
    return jnp.sum(got.astype(F32), axis=0)


def in_group(v):
    n, s = lax.axis_size("fsdp"), lax.axis_size("seq")
    groups = [[j * n + i for i in range(n)] for j in range(s // n)]
    return lax.all_to_all(v, "seq", 0, 0, axis_index_groups=groups, tiled=True)


def quarters(v):
    n = lax.axis_size("fsdp")
    return v.reshape(v.shape[0], n, -1).transpose(1, 0, 2)


def joined(v):
    return v.transpose(1, 0, 2).reshape(v.shape[1], -1)


def move_fsdp(v, m):
    n = lax.axis_size("fsdp")
    return lax.ppermute(v, "fsdp", [(k, k ^ m) for k in range(n)])


def move_seq(v, m):
    s = lax.axis_size("seq")
    return lax.ppermute(v, "seq", [(k, k ^ m) for k in range(s)])


class SeqSums:
    def __init__(self):
        s = lax.axis_size("seq")
        half = s // 2
        self.pairs = [[(j, j + 1), (s - 1 - j, s - 2 - j)] for j in range(half - 1)]
        self.pairs.append([(half - 1, half), (half, half - 1)])
        self.inward = half
        self.pairs += [[(j + 1, j), (s - 2 - j, s - 1 - j)] for j in reversed(range(half - 1))]
        self.values, self.phase, self.moving = [], [], []

    def add(self, values):
        first = len(self.values)
        self.values += values
        self.phase += [0] * len(values)
        return list(range(first, len(self.values)))

    def begin(self):
        place = lax.axis_index("seq")
        taken = set()
        for k, step in enumerate(self.phase):
            if step == len(self.pairs) or step in taken:
                continue
            taken.add(step)
            v = self.values[k]
            got = lax.ppermute(v, "seq", self.pairs[step])
            if step < self.inward:
                v = (v.astype(F32) + got.astype(F32)).astype(BF16)
            else:
                here = functools.reduce(
                    jnp.logical_or, [place == to for _, to in self.pairs[step]]
                )
                v = jnp.where(here, got, v)
            self.moving.append((k, v))
            self.phase[k] = step + 1

    def end(self, work):
        moved = [v for _, v in self.moving]
        still = [k for k, p in enumerate(self.phase) if p == 0]
        work, moved, rest = lax.optimization_barrier(
            (work, moved, [self.values[k] for k in still])
        )
        for (k, _), v in zip(self.moving, moved):
            self.values[k] = v
        for k, v in zip(still, rest):
            self.values[k] = v
        self.moving = []
        return work

    def done(self, ks):
        return all(self.phase[k] == len(self.pairs) for k in ks)


def relay(total, local, reverse):
    n, s = lax.axis_size("fsdp"), lax.axis_size("seq")
    segments = s // n
    place = lax.axis_index("seq") // n
    own = lax.axis_index("seq") % n
    totals = lax.all_gather(total, "seq")
    locals_ = lax.all_gather(local, "seq")
    state = jnp.zeros_like(local)
    order = range(segments - 1, -1, -1) if reverse else range(segments)
    for j in order:
        use = (j > place) if reverse else (j < place)
        t = lax.dynamic_index_in_dim(totals, j * n + own, 0, False)
        v = lax.dynamic_index_in_dim(locals_, j * n + own, 0, False)
        state = jnp.where(use, t * state + v, state)
    return state


def next_segment(v, step):
    n, s = lax.axis_size("fsdp"), lax.axis_size("seq")
    pairs = [(k, k + step * n) for k in range(s) if 0 <= k + step * n < s]
    return lax.ppermute(v, "seq", pairs)


def dot_rows(a, b):
    return lax.dot_general(a, b, (((0,), (0,)), ((), ())), preferred_element_type=F32)


def dot_cols(a, b):
    return lax.dot_general(a, b, (((1,), (1,)), ((), ())), preferred_element_type=F32)


def normalised(h, gain):
    return h * lax.rsqrt(jnp.mean(h * h, axis=-1, keepdims=True) + EPS) * gain


def per_device(
    inputs,
    cotangent,
    lengths,
    gain_in,
    w_in,
    conv_w,
    conv_b,
    dt_bias,
    a_log,
    d_skip,
    gain_out,
    w_out,
):
    n = lax.axis_size("fsdp")
    nz = lax.axis_size("seq")
    segments = nz // n
    c = lax.axis_index("section")
    f = lax.axis_index("fsdp")
    place = lax.axis_index("seq")
    upper = c == 0
    rows = inputs.shape[2]
    width = INNER // n
    heads = HEADS // n
    share = D // n
    half = share // 2
    group = GROUP // n
    ids = jnp.stack([f, c]).astype(jnp.int32)
    tie = lax.optimization_barrier

    def pick(a, b):
        return jnp.where(upper, a, b)

    w = w_in[0].T

    def cut(first, size):
        return lax.dynamic_slice_in_dim(w, first, size, 0)

    def piece_z(m):
        return cut((f ^ m) * width, width)

    def piece_x(m):
        return jnp.concatenate(
            [
                cut(INNER + (f ^ m) * width, width),
                w[2 * INNER : 2 * INNER + GROUP],
                cut(2 * INNER + GROUP + (f ^ m) * heads, heads),
            ]
        )

    def fetch(pieces, layer):
        pairs = lambda m: [(layer * n + i, layer * n + (i ^ m)) for i in range(n)]
        near = [
            v if m == 0 else lax.ppermute(v, ("section", "fsdp"), pairs(m))
            for m, v in enumerate(pieces)
        ]
        return near, [lax.ppermute(v, "section", [(layer, 1 - layer)]) for v in near]

    def whole_slot(v):
        return joined(to_all(v.reshape(n * rows, share)))

    pieces_x = [piece_x(m) for m in range(n)]
    near_x0, far_x0 = fetch(pieces_x, 0)
    part_h0 = in_group(exchange(quarters(at(inputs, c)[0])))
    near_x0, part_h0 = tie((near_x0, part_h0))
    far_x0 = [lax.ppermute(v, "section", [(0, 1)]) for v in near_x0]
    all_h0 = whole_slot(part_h0)
    pieces_z, _ = tie(([piece_z(m) for m in range(n)], part_h0))
    near_z0, far_z0 = fetch(pieces_z, 0)

    pack = jnp.concatenate(
        [
            gain_in[0],
            dt_bias[0],
            a_log[0],
            d_skip[0],
            gain_out[0],
            conv_w[0].reshape(-1),
            conv_b[0],
        ]
    )
    mine = to_all(pack)
    theirs = swap_section(mine)
    small = []
    for full in (pick(mine, theirs), pick(theirs, mine)):
        full = full.astype(F32)
        used = 0

        def take(size):
            nonlocal used
            used += size
            return full[:, used - size : used]

        gain = take(share).reshape(1, D)
        hp = [at(take(heads), f)[None] for _ in range(3)]
        hp = jnp.concatenate([hp[0], -jnp.exp(hp[1]), hp[2], jnp.zeros((5, heads), F32)])
        gout = at(take(width), f)[None]
        per = CHANNELS // n
        taps = take(KERNEL * per).reshape(n, KERNEL, per).transpose(1, 0, 2)
        bias = take(per).reshape(1, CHANNELS)
        table = jnp.concatenate(
            [taps.reshape(KERNEL, CHANNELS), bias, jnp.zeros((3, CHANNELS), F32)]
        )
        cw = jnp.concatenate(
            [lax.dynamic_slice_in_dim(table, f * width, width, 1), table[:, INNER:]], axis=1
        )
        small.append((gain, cw, hp, gout))

    win = [(near_z0, far_z0, near_x0, far_x0), None]
    expand = (
        jnp.arange(heads)[:, None] == jnp.arange(width)[None, :] // HEAD_DIM
    ).astype(BF16)
    zero_state = jnp.zeros((STATE, width), F32)
    zero_edge = jnp.zeros((8, width + GROUP), F32)

    def project_x(normed, layer):
        return project(ids, normed, win[layer][2], win[layer][3], layer)

    def project_z(normed, layer):
        return project(ids, normed, win[layer][0], win[layer][1], layer)

    def decay_of(px, hp):
        decay = jax.nn.softplus(px[:, width + GROUP :] + hp[0:1]) * hp[1:2]
        return jnp.repeat(jnp.exp(jnp.sum(decay, axis=0)), HEAD_DIM)[None, :]

    def scan(px, layer):
        _, cw, hp, _ = small[layer]
        args = (px, cw, hp)
        if segments == 1:
            return run_forward(*args, zero_state, zero_edge, rows), zero_state
        edge = next_segment(px[-8:, : width + GROUP], 1)
        local = run_forward(*args, zero_state, edge, rows)[2][-1]
        state = relay(decay_of(px, hp), local, False)
        return run_forward(*args, state, edge, rows), state

    def unscan(pz, px, fwd, dn, rc, layer):
        (y, filt, states), state = fwd
        _, cw, hp, gout = small[layer]
        args = (pz, px, y, filt, dn, rc, states, state, cw, hp, expand, gout)
        if segments == 1:
            return run_backward(*args, zero_state, zero_edge, rows, n)[:6]
        local = run_backward(*args, zero_state, zero_edge, rows, n)[6]
        grad = relay(decay_of(px, hp), local, True)
        edge = next_segment(run_backward(*args, grad, zero_edge, rows, n)[7], -1)
        return run_backward(*args, grad, edge, rows, n)[:6]

    def gate(pz, y):
        return y * jax.nn.silu(pz)

    def gated(pz, y, r, layer):
        return (gate(pz, y) * r[:, None] * small[layer][3]).astype(BF16)

    def sum_of_shares(v):
        return jnp.sum(to_all(v), axis=0)

    normed_in0 = normalised(all_h0.astype(F32), small[0][0]).astype(BF16)
    px0 = project_x(normed_in0, 0)
    px0, pieces_x1, pieces_z1, own_ct, wo_mine, own_len = tie(
        (px0, pieces_x, pieces_z, at(cotangent, c)[0], w_out[0], at(lengths, c))
    )
    near_x1, far_x1 = fetch(pieces_x1, 1)
    wo_other = swap_section(wo_mine)
    wo = (pick(wo_mine, wo_other), pick(wo_other, wo_mine))
    slot_pairs = [
        ((j * n + i) * n + k, (j * n + k) * n + i)
        for j in range(segments)
        for i in range(n)
        for k in range(n)
    ]
    length = lax.ppermute(own_len, ("seq", "fsdp"), slot_pairs)
    first_row = (place // n) * n * rows
    all_valid = first_row + jnp.arange(n * rows, dtype=jnp.int32) < length[0]
    all_valid = all_valid.astype(F32)[:, None]
    own_rows = lambda v: lax.dynamic_slice_in_dim(v, f * rows, rows, 0)
    valid = own_rows(all_valid)
    h0 = own_rows(all_h0)
    fwd0 = scan(px0, 0)
    pz0 = project_z(normed_in0, 0)
    g0 = gate(pz0, fwd0[0][0])
    stat0 = sum_of_shares(jnp.sum(g0 * g0, axis=1).reshape(n, rows)).reshape(-1)
    r0 = lax.rsqrt(stat0 / INNER + EPS)
    normed0 = gated(pz0, fwd0[0][0], r0, 0)
    part_ct = in_group(exchange(quarters(own_ct)))
    normed0, wo, near_x1, part_ct = tie((normed0, wo, near_x1, part_ct))
    far_x1 = [lax.ppermute(v, "section", [(1, 0)]) for v in near_x1]
    mixed0 = scatter_sum(jnp.dot(normed0, wo[0], preferred_element_type=F32).astype(BF16))
    out0 = valid * (h0.astype(F32) + mixed0)
    h1 = out0.astype(BF16)

    normed_in1 = gather_rows(normalised(h1.astype(F32), small[1][0]).astype(BF16))
    normed_in1, far_x1, part_ct, pieces_z1 = tie((normed_in1, far_x1, part_ct, pieces_z1))
    near_z1, far_z1 = fetch(pieces_z1, 1)
    win[1] = (near_z1, far_z1, near_x1, far_x1)
    px1 = project_x(normed_in1, 1)
    all_ct = whole_slot(part_ct)
    fwd1 = scan(px1, 1)
    fwd1, all_ct, near_z1 = tie((fwd1, all_ct, near_z1))
    far_z1 = [lax.ppermute(v, "section", [(1, 0)]) for v in near_z1]
    win[1] = (near_z1, far_z1, near_x1, far_x1)
    dout1 = own_rows(all_ct).astype(F32)
    dmixed1 = (all_valid * all_ct.astype(F32)).astype(BF16)
    dn1 = dot_cols(dmixed1, wo[1])
    pz1 = project_z(normed_in1, 1)
    g1 = gate(pz1, fwd1[0][0])
    stat1 = sum_of_shares(
        jnp.stack(
            [
                jnp.sum(g1 * g1, axis=1).reshape(n, rows),
                jnp.sum(g1 * dn1 * small[1][3], axis=1).reshape(n, rows),
            ]
        )
    ).reshape(2, -1)
    r1 = lax.rsqrt(stat1[0] / INNER + EPS)
    normed1 = gated(pz1, fwd1[0][0], r1, 1)

    part_width = width // 4

    def cut_half(v, k):
        size = v.shape[1] // 2
        return lax.dynamic_slice_in_dim(v, k * size, size, 1)

    def half_of(parts, k):
        return jnp.concatenate([cut_half(v, k) for v in parts], axis=1)

    def away_in(normed_in, parts):
        return swap_section(dot_rows(normed_in, half_of(parts, 1 - c)).astype(BF16))

    def own_in_pieces(normed_in, parts, away):
        own = half_of(parts, c)
        result = []
        for cols in (slice(0, part_width), slice(part_width, own.shape[1])):
            total = dot_rows(normed_in, own[:, cols]) + away[:, cols].astype(F32)
            result.append(total.astype(BF16).reshape(n, share, -1))
        return result

    def away_out(normed, dmixed):
        return swap_section(dot_rows(cut_half(normed, 1 - c), dmixed).astype(BF16))

    def own_out_pieces(normed, dmixed, away):
        own = cut_half(normed, c)
        result = []
        for cols in (slice(0, D // 2), slice(D // 2, D)):
            total = dot_rows(own, dmixed[:, cols]) + away[:, cols].astype(F32)
            result.append(total.astype(BF16))
        return result

    def with_group(dxs, dbc):
        total = jnp.sum(exchange(dbc), axis=0).astype(BF16)
        column = jnp.arange(GROUP)[None, :] // group
        own = jnp.where(column == f, jnp.concatenate([total] * n, axis=1), 0)
        full = lax.dynamic_update_slice(dxs, own.astype(BF16), (0, width))
        return full, [dxs[:, :width], total, dxs[:, width + GROUP :]]

    def back_in(dz, full, layer):
        near_z, far_z, near_x, far_x = win[layer]
        return project_back(ids, dz, full, (near_z, near_x), (far_z, far_x), layer)

    def back_norm(dout, dnormed_in, h, gain):
        h = h.astype(F32)
        r = lax.rsqrt(jnp.mean(h * h, axis=-1, keepdims=True) + EPS)
        u = dnormed_in * gain
        mean = jnp.mean(u * h, axis=-1, keepdims=True)
        dgain = jnp.sum(dnormed_in * h * r, axis=0)
        return valid * dout + r * u - h * (r * r * r) * mean, dgain

    def scales(r, coef):
        top = jnp.stack([r.reshape(n, rows), coef.reshape(n, rows)], axis=1)
        return jnp.concatenate([top, jnp.zeros((n, 6, rows), F32)], axis=1)

    def packed(dgin, d, out, mixed):
        dgain, dconv, dhp = d[3][0], d[4][:5], d[5][:3]
        put = lambda v, size, at_lane: lax.dynamic_update_slice(
            jnp.zeros(v.shape[:-1] + (size,), F32), v, (0,) * (v.ndim - 1) + (at_lane,)
        )
        conv = put(dconv[:, :width], CHANNELS, f * width)
        conv = conv.at[:, INNER:].set(dconv[:, width:])
        totals = jnp.stack(
            [jnp.sum(out * out), jnp.sum((valid * mixed) ** 2), jnp.sum(valid)]
        )
        return jnp.concatenate(
            [
                dgin,
                conv.reshape(-1),
                put(dhp, HEADS, f * heads).reshape(-1),
                put(dgain, INNER, f * width),
                totals,
            ]
        )

    def hand_over(v, layer):
        return lax.ppermute(v, "section", [(1 - layer, layer)])

    sums = SeqSums()
    rc1 = scales(r1, (r1 * r1 * r1 / INNER) * stat1[1])
    away = away_out(normed1, dmixed1)
    go1 = sums.add(own_out_pieces(normed1, dmixed1, away))
    rc1, normed1, dn1 = sums.end((rc1, normed1, dn1))

    sums.begin()
    d1 = unscan(pz1, px1, fwd1, dn1, rc1, 1)
    mixed1 = scatter_sum(jnp.dot(normed1, wo[1], preferred_element_type=F32).astype(BF16))
    d1, mixed1 = sums.end((d1, mixed1))

    sums.begin()
    away = away_in(normed_in1, [d1[0]])
    full1, xs1 = with_group(d1[1], d1[2])
    back1 = back_in(d1[0], full1, 1)
    back1, xs1, away, full1 = sums.end((back1, xs1, away, full1))

    sums.begin()
    dnin1 = scatter_sum(back1)
    gz = own_in_pieces(normed_in1, [d1[0]], away)
    away = away_in(normed_in1, xs1)
    dnin1, gz, away = sums.end((dnin1, gz, away))
    gz1 = sums.add(gz)

    sums.begin()
    grad1, dgin1 = back_norm(dout1, dnin1, h1, small[1][0])
    dout0 = grad1.astype(BF16).astype(F32)
    dmixed0_own = (valid * dout0).astype(BF16)
    dmixed0 = gather_rows(dmixed0_own)
    along0 = to_all(jnp.sum(dmixed0_own.astype(F32) * mixed0, axis=-1)).reshape(-1)
    rc0 = scales(r0, (r0 * r0 / INNER) * along0)
    gx = own_in_pieces(normed_in1, xs1, away)
    out1 = valid * (h1.astype(F32) + mixed1)
    grad1, dgin1, dmixed0, rc0, gx, out1 = sums.end((grad1, dgin1, dmixed0, rc0, gx, out1))
    gx1 = sums.add(gx)

    sums.begin()
    dn0 = dot_cols(dmixed0, wo[0])
    d0 = unscan(pz0, px0, fwd0, dn0, rc0, 0)
    d0 = sums.end(d0)

    sums.begin()
    away_z = away_in(normed_in0, [d0[0]])
    away_o = away_out(normed0, dmixed0)
    full0, xs0 = with_group(d0[1], d0[2])
    gz = own_in_pieces(normed_in0, [d0[0]], away_z)
    go = own_out_pieces(normed0, dmixed0, away_o)
    full0, xs0, gz, go = sums.end((full0, xs0, gz, go))
    go0 = sums.add(go)

    sums.begin()
    away = away_in(normed_in0, xs0)
    gz = [exchange(v) for v in gz]
    gx = own_in_pieces(normed_in0, xs0, away)
    gz, gx, full0 = sums.end((gz, gx, full0))
    gz0 = sums.add(gz)

    sums.begin()
    gx = [exchange(v) for v in gx]
    back0 = back_in(d0[0], full0, 0)
    gx, back0 = sums.end((gx, back0))
    gx0 = sums.add(gx)

    sums.begin()
    dnin0 = scatter_sum(back0)
    grad0, dgin0 = back_norm(dout0, dnin0, h0, small[0][0])
    p = jnp.stack([packed(dgin0, d0, out0, mixed0), packed(dgin1, d1, out1, mixed1)])
    p = p + swap_section(p)
    p, grad0, grad1, h1, out1 = sums.end((p, grad0, grad1, h1, out1))

    names = {"own": {}, "away": {}}
    order = [(k, 1, "out") for k in go1] + [(k, 1, "in") for k in gz1 + gx1]
    order += [(k, 0, "out") for k in go0] + [(k, 0, "in") for k in gz0 + gx0]
    back = jnp.concatenate([h1, out1.astype(BF16), grad0.astype(BF16), grad1.astype(BF16)])
    back_steps = [lambda v: exchange(quarters(v)), in_group, lambda v: joined(exchange(v))]
    p_steps = [lambda v, m=m: move_fsdp(v, m) for m in (1 << j for j in range(n.bit_length() - 1))]
    p_steps += [lambda v, m=m: move_seq(v, m) for m in (1 << j for j in range(nz.bit_length() - 1))]
    exchanged = set()
    while order:
        sums.begin()
        moving = [k for k, _ in sums.moving]
        ready = [e for e in order if e[0] not in moving and sums.done([e[0]])]
        turn = [e for e in ready if e[1:] == (1, "in") and e[0] not in exchanged][:2]
        if back_steps:
            back = back_steps.pop(0)(back)
            turn = turn[:1]
        if p_steps:
            p = p + p_steps.pop(0)(p)
        swapped = {e[0]: exchange(sums.values[e[0]]) for e in turn}
        final = [e for e in ready if e[1:] != (1, "in") or e[0] in exchanged][:2]
        fresh = {e[0]: hand_over(sums.values[e[0]], e[1]) for e in final}
        kept = {e[0]: sums.values[e[0]] for e in final}
        swapped, fresh, kept, back, p = sums.end((swapped, fresh, kept, back, p))
        for k, v in swapped.items():
            sums.values[k] = v
            exchanged.add(k)
        for k in fresh:
            names["own"][k], names["away"][k] = kept[k], fresh[k]
        order = [e for e in order if e not in final]
    p = pick(p[0], p[1])

    used = 0

    def part(size):
        nonlocal used
        used += size
        return p[used - size : used]

    mine_of = lambda v, size: lax.dynamic_slice_in_dim(v, f * size, size, v.ndim - 1)
    o_gain_in = mine_of(part(D), share)
    o_conv = mine_of(part(5 * CHANNELS).reshape(5, CHANNELS), CHANNELS // n)
    o_heads = mine_of(part(3 * HEADS).reshape(3, HEADS), heads)
    o_gain_out = mine_of(part(INNER), width)
    totals = part(3)
    act_rms = jnp.sqrt(totals[:2] / (totals[2] * D))[None]

    sides = ("own", "away")
    held = [
        [[names[side][k] for k in ks] for ks in (gz0 + gx0 + go0, gz1 + gx1 + go1)]
        for side in sides
    ]

    def both_halves(a, b):
        return jnp.stack([pick(a, b), pick(b, a)], axis=1)

    narrow = [pick(side[0][3], side[1][3])[:, :, part_width:] for side in held]
    narrow = both_halves(*[v.astype(F32).transpose(0, 2, 1) for v in narrow])
    small_in = jnp.concatenate(
        [
            narrow[:, :, : group // 2].reshape(GROUP, share),
            narrow[:, :, group // 2 :].reshape(HEADS, share),
        ]
    )
    g_w_in = []
    shape_in = (2 * INNER + GROUP + HEADS, share)
    for ks, rows_of_small in (((0, 1), None), ((2, 3), (2 * INNER, GROUP + HEADS))):
        arrays, plan = [], []
        for k in ks:
            for s in range(2):
                arrays += [held[s][0][k], held[s][1][k]]
                base = k // 2 * INNER + k % 2 * part_width
                firsts = tuple(base + q * width for q in range(n))
                plan.append((len(arrays) - 2, len(arrays) - 1, s, firsts))
        g_w_in = [
            place_in(
                ids, arrays, tuple(plan), small_in, rows_of_small, g_w_in, shape_in, part_width
            )
        ]
    halves_out = [
        jnp.concatenate([pick(side[0][k], side[1][k]) for k in (4, 5)], axis=1) for side in held
    ]
    g_w_out = both_halves(*[v[None] for v in halves_out]).reshape(width, D).astype(F32)

    back = back.reshape(2, 2, rows, D)
    kept_back = pick(back[:, 0], back[:, 1])
    other_back = swap_section(pick(back[:, 1], back[:, 0]))
    both_back = jnp.stack(
        [pick(kept_back, other_back), pick(other_back, kept_back)], axis=1
    )
    return (
        both_back[0][None, :, None],
        both_back[1].astype(F32)[None, :, None],
        o_gain_in[None],
        g_w_in[0].T[None],
        o_conv[None, :4],
        o_conv[None, 4],
        o_heads[None, 0],
        o_heads[None, 1],
        o_heads[None, 2],
        o_gain_out[None],
        g_w_out[None],
        act_rms,
    )


def solution(mesh):
    in_specs = (
        P(None, "fsdp", "seq", None),
        P(None, "fsdp", "seq", None),
        P(None, "fsdp"),
        P("section", "fsdp"),
        P("section", "fsdp", None),
        P("section", None, "fsdp"),
        P("section", "fsdp"),
        P("section", "fsdp"),
        P("section", "fsdp"),
        P("section", "fsdp"),
        P("section", "fsdp"),
        P("section", "fsdp", None),
    )
    out_specs = (
        P("section", None, "fsdp", "seq", None),
        P("section", None, "fsdp", "seq", None),
        P("section", "fsdp"),
        P("section", "fsdp", None),
        P("section", None, "fsdp"),
        P("section", "fsdp"),
        P("section", "fsdp"),
        P("section", "fsdp"),
        P("section", "fsdp"),
        P("section", "fsdp"),
        P("section", "fsdp", None),
        P("section", None),
    )
    return jax.shard_map(
        per_device, mesh=mesh, in_specs=in_specs, out_specs=out_specs, check_vma=False
    )
```

```python
import functools

import jax
import jax.numpy as jnp
from jax import lax
from jax.experimental import pallas as pl
from jax.experimental.pallas import tpu as pltpu
from jax.sharding import PartitionSpec as P

D = 2048
INNER = 4096
HEADS = 64
HEAD_DIM = 64
STATE = 128
KERNEL = 4
GROUP = 2 * STATE
CHANNELS = INNER + GROUP
LANES = 128
EPS = 1e-05
F32 = jnp.float32
BF16 = jnp.bfloat16
VMEM_BYTES = 48 * 1024 * 1024


def split(v):
    hi = v.astype(BF16)
    return hi, (v - hi.astype(F32)).astype(BF16)


def dot32(a, b, ca, cb):
    (ah, al), (bh, bl) = (v if isinstance(v, tuple) else split(v) for v in (a, b))
    one = lambda p, q: lax.dot_general(
        p, q, (((ca,), (cb,)), ((), ())), preferred_element_type=F32
    )
    return one(ah, bh) + (one(ah, bl) + one(al, bh))


def step_sizes(raw, hp, rows):
    shifted = raw + hp[0:1, :]
    dt = jnp.maximum(shifted, 0.0) + jnp.log1p(jnp.exp(-jnp.abs(shifted)))
    decay = dt * hp[1:2, :]
    row = lax.broadcasted_iota(jnp.int32, (rows, rows), 0)
    col = lax.broadcasted_iota(jnp.int32, (rows, rows), 1)
    lower = (row >= col).astype(F32)
    cum = dot32(lower, decay, 1, 0)
    cum_t = dot32(decay, lower, 0, 1)
    return shifted, dt, cum, cum_t, row, col, lower


def pair_lanes(v, j, first):
    return jnp.where(first, v[:, 2 * j : 2 * j + 1], v[:, 2 * j + 1 : 2 * j + 2])


def head_sums(v, table):
    hi, low = split(v)
    one = lambda p: lax.dot_general(
        p, table, (((1,), (1,)), ((), ())), preferred_element_type=F32
    )
    return one(hi) + one(low)


def forward_kernel(proj, cw, hp, s0, e0, y_ref, filt_ref, st_ref, state, xp, xw_s, last_s):
    i = pl.program_id(0)
    rows, width = y_ref.shape

    @pl.when(i == 0)
    def _():
        state[...] = s0[...]
        xp[0:8, :] = e0[...]

    xp[8 : 8 + rows, :] = proj[:, : width + GROUP]

    def conv_tile(lo):
        acc = cw[4:5, lo : lo + LANES]
        for k in range(KERNEL):
            acc = acc + cw[k : k + 1, lo : lo + LANES] * xp[5 + k : 5 + k + rows, lo : lo + LANES]
        filt_ref[:, lo : lo + LANES] = acc
        return acc * jax.nn.sigmoid(acc)

    b_c = conv_tile(width)
    c_c = conv_tile(width + STATE)
    _, dt, cum, cum_t, row, col, _ = step_sizes(proj[:, width + GROUP :], hp, rows)
    last = cum[rows - 1 : rows, :]
    ecum = jnp.exp(cum)
    weight = jnp.exp(last - cum) * dt
    elast = jnp.exp(last)
    b_c, c_c = split(b_c), split(c_c)
    carried = dot32(c_c, state[...], 1, 0)
    scores = dot32(c_c, b_c, 1, 1)
    causal = row >= col
    lane = lax.broadcasted_iota(jnp.int32, (rows, LANES), 1)
    first = lane < HEAD_DIM
    for j in range(width // LANES):
        lo = j * LANES
        here = slice(lo, lo + LANES)
        x = conv_tile(lo)
        xd = x * pair_lanes(dt, j, first)
        m = []
        for h in (2 * j, 2 * j + 1):
            gap = cum[:, h : h + 1] - cum_t[h : h + 1, :]
            m.append(jnp.exp(jnp.where(causal, gap, -1e30)) * scores)
        xd2 = jnp.concatenate([jnp.where(first, xd, 0.0), jnp.where(first, 0.0, xd)])
        y = (
            dot32(jnp.concatenate(m, axis=1), xd2, 1, 0)
            + carried[:, here] * pair_lanes(ecum, j, first)
            + pair_lanes(hp[2:3, :], j, first[0:1]) * x
        )
        y_ref[:, here] = y
        xw_s[:, here] = x * pair_lanes(weight, j, first)
        last_s[0:1, here] = pair_lanes(elast, j, first[0:1])
    state[...] = state[...] * last_s[0:1, :] + dot32(b_c, xw_s[...], 0, 0)
    st_ref[0] = state[...]
    xp[0:8, :] = xp[rows : rows + 8, :]


def backward_kernel(
    pz,
    proj,
    y_ref,
    filt,
    dn,
    rc,
    st_before,
    st_out,
    s0,
    cw,
    hp,
    table,
    gain,
    g0,
    e0,
    dz_ref,
    dproj,
    dbc_ref,
    dgain_ref,
    dconv_ref,
    dhp_ref,
    gfin_ref,
    efin_ref,
    grad,
    dfp,
    both,
    xw_s,
    dyc_s,
    rowv,
):
    i = pl.program_id(0)
    rows, width = y_ref.shape
    heads = hp.shape[1]

    @pl.when(i == 0)
    def _():
        grad[...] = g0[...]
        dfp[rows : rows + 8, :] = e0[...]
        dgain_ref[...] = jnp.zeros_like(dgain_ref)
        dconv_ref[...] = jnp.zeros_like(dconv_ref)
        dhp_ref[...] = jnp.zeros_like(dhp_ref)

    def silu_pair(v):
        s = jax.nn.sigmoid(v)
        a = v * s
        return a, s * (1.0 + v - a)

    b_c, b_d = silu_pair(filt[:, width : width + STATE])
    c_c, c_d = silu_pair(filt[:, width + STATE :])
    shifted, dt, cum, cum_t, row, col, lower = step_sizes(proj[:, width + GROUP :], hp, rows)
    last = cum[rows - 1 : rows, :]
    tail = jnp.exp(last - cum)
    ecum = jnp.exp(cum)
    elast = jnp.exp(last)
    b_c, c_c = split(b_c), split(c_c)
    grad_p = split(grad[...])
    k_all = dot32(b_c, grad_p, 1, 0)
    scores_t = dot32(b_c, c_c, 1, 1)
    causal_t = row <= col
    lane = lax.broadcasted_iota(jnp.int32, (rows, LANES), 1)
    first = lane < HEAD_DIM
    dcb_t = jnp.zeros((rows, rows), F32)
    rc_t = dot32((row == col).astype(F32), rc[0], 1, 1)
    r = rc_t[:, 0:1]
    coef = rc_t[:, 1:2]
    rowv[0:1, :] = jnp.sum(grad[...] * st_out[0], axis=0, keepdims=True)
    for j in range(width // LANES):
        lo = j * LANES
        here = slice(lo, lo + LANES)
        z = pz[:, here]
        y = y_ref[:, here]
        sz, dsz = silu_pair(z)
        g = y * sz
        dnt = dn[:, here]
        dg = dnt * gain[0:1, here] * r - g * coef
        dgain_ref[0:1, here] += jnp.sum(dnt * g * r, axis=0, keepdims=True)
        dy = dg * sz
        dz_ref[:, here] = (dg * y * dsz).astype(BF16)
        x, xder = silu_pair(filt[:, here])
        dt_e = pair_lanes(dt, j, first)
        tail_e = pair_lanes(tail, j, first)
        xd = x * dt_e
        dy2 = split(jnp.concatenate([jnp.where(first, dy, 0.0), jnp.where(first, 0.0, dy)]))
        decays = []
        for h in (2 * j, 2 * j + 1):
            gap = cum_t[h : h + 1, :] - cum[:, h : h + 1]
            decays.append(jnp.exp(jnp.where(causal_t, gap, -1e30)))
        m = jnp.concatenate([d * scores_t for d in decays], axis=1)
        dm = dot32(xd, dy2, 1, 1)
        dcb_t = dcb_t + (decays[0] * dm[:, :rows] + decays[1] * dm[:, rows:])
        v = dot32(m, dy2, 1, 0) + k_all[:, here] * tail_e
        skip = pair_lanes(hp[2:3, :], j, first[0:1])
        dx = dt_e * v + skip * dy
        both[0:rows, here] = x * v
        both[rows : 2 * rows, here] = dy * (y - skip * x)
        rowv[1:2, here] = jnp.sum(dy * x, axis=0, keepdims=True)
        rowv[2:3, here] = pair_lanes(elast, j, first[0:1])
        xw_s[:, here] = xd * tail_e
        dyc_s[:, here] = dy * pair_lanes(ecum, j, first)
        dfp[0:rows, here] = dx * xder
    dcb_t = split(dcb_t)
    dyc = split(dyc_s[...])
    st_in = jnp.where(i == pl.num_programs(0) - 1, s0[...], st_before[0])
    dc = dot32(dcb_t, b_c, 0, 0) + dot32(dyc, st_in, 1, 1)
    db = dot32(dcb_t, c_c, 1, 0) + dot32(xw_s[...], grad_p, 1, 1)
    dfp[0:rows, width : width + STATE] = db * b_d
    dfp[0:rows, width + STATE :] = dc * c_d
    grad[...] = grad[...] * rowv[2:3, :] + dot32(c_c, dyc, 0, 0)
    gfin_ref[...] = grad[...]

    sums = head_sums(both[...], table[...])
    rsums = head_sums(rowv[...], table[...])
    ddt_x = sums[0:rows]
    dcum = sums[rows : 2 * rows] - dt * ddt_x
    upto = lax.broadcasted_iota(jnp.int32, (rows, heads), 0)
    dcum = dcum + jnp.where(upto == rows - 1, rsums[0:1, :], 0.0)
    ddecay = dot32(lower, dcum, 0, 0)
    ddt = ddt_x + hp[1:2, :] * ddecay
    draw = ddt * jax.nn.sigmoid(shifted)
    dproj[:, width + GROUP :] = draw.astype(BF16)
    dhp_ref[0:1, :] += jnp.sum(draw, axis=0, keepdims=True)
    dhp_ref[1:2, :] += jnp.sum(ddecay * dt, axis=0, keepdims=True) * hp[1:2, :]
    dhp_ref[2:3, :] += rsums[1:2, :]

    for lo in range(0, width + GROUP, LANES):
        here = slice(lo, lo + LANES)
        src = proj[:, here]
        total = jnp.zeros((rows, LANES), F32)
        for k in range(KERNEL):
            shift = KERNEL - 1 - k
            moved = dfp[shift : shift + rows, here]
            total = total + cw[k : k + 1, here] * moved
            dconv_ref[k : k + 1, here] += jnp.sum(src * moved, axis=0, keepdims=True)
        dconv_ref[4:5, here] += jnp.sum(dfp[0:rows, here], axis=0, keepdims=True)
        if lo < width:
            dproj[:, here] = total.astype(BF16)
        else:
            dproj[:, here] = jnp.zeros((rows, LANES), BF16)
            share = dbc_ref.shape[2]
            for k in range(LANES // share):
                dbc_ref[(lo - width) // share + k] = total[:, k * share : (k + 1) * share]
    dfp[rows : rows + 8, :] = dfp[0:8, :]
    efin_ref[...] = dfp[0:8, :]


def whole(shape):
    return pl.BlockSpec(shape, lambda i: (0,) * len(shape))


def run_forward(proj, cw, hp, s0, e0, rows):
    total, width = proj.shape[0], s0.shape[1]
    count = total // rows
    block = lambda w: pl.BlockSpec((rows, w), lambda i: (i, 0))
    shape = jax.ShapeDtypeStruct
    return pl.pallas_call(
        forward_kernel,
        grid=(count,),
        in_specs=[block(proj.shape[1])] + [whole(v.shape) for v in (cw, hp, s0, e0)],
        out_specs=[
            block(width),
            block(width + GROUP),
            pl.BlockSpec((1, STATE, width), lambda i: (i, 0, 0)),
        ],
        scratch_shapes=[
            pltpu.VMEM((STATE, width), F32),
            pltpu.VMEM((rows + 8, width + GROUP), F32),
            pltpu.VMEM((rows, width), F32),
            pltpu.VMEM((8, width), F32),
        ],
        out_shape=[
            shape((total, width), F32),
            shape((total, width + GROUP), F32),
            shape((count, STATE, width), F32),
        ],
        compiler_params=pltpu.CompilerParams(vmem_limit_bytes=VMEM_BYTES),
        name="scan_forward",
    )(proj, cw, hp, s0, e0)


def run_backward(pz, proj, y, filt, dn, rc, states, s0, cw, hp, table, gain, g0, e0, rows, places):
    total, (heads, width) = proj.shape[0], table.shape
    count = total // rows
    turn = lambda i: count - 1 - i
    block = lambda w: pl.BlockSpec((rows, w), lambda i: (turn(i), 0))
    shape = jax.ShapeDtypeStruct
    share = GROUP // places
    return pl.pallas_call(
        backward_kernel,
        grid=(count,),
        in_specs=[
            block(width),
            block(proj.shape[1]),
            block(width),
            block(width + GROUP),
            block(width),
            pl.BlockSpec((1, 8, rows), lambda i: (turn(i), 0, 0)),
            pl.BlockSpec((1, STATE, width), lambda i: (jnp.maximum(turn(i) - 1, 0), 0, 0)),
            pl.BlockSpec((1, STATE, width), lambda i: (turn(i), 0, 0)),
        ]
        + [whole(v.shape) for v in (s0, cw, hp, table, gain, g0, e0)],
        out_specs=[
            block(width),
            block(proj.shape[1]),
            pl.BlockSpec((places, rows, share), lambda i: (0, turn(i), 0)),
            whole((8, width)),
            whole((8, width + GROUP)),
            whole((8, heads)),
            whole((STATE, width)),
            whole((8, width + GROUP)),
        ],
        scratch_shapes=[
            pltpu.VMEM((STATE, width), F32),
            pltpu.VMEM((rows + 8, width + GROUP), F32),
            pltpu.VMEM((2 * rows, width), F32),
            pltpu.VMEM((rows, width), F32),
            pltpu.VMEM((rows, width), F32),
            pltpu.VMEM((8, width), F32),
        ],
        out_shape=[
            shape((total, width), BF16),
            shape(proj.shape, BF16),
            shape((places, total, share), F32),
            shape((8, width), F32),
            shape((8, width + GROUP), F32),
            shape((8, heads), F32),
            shape((STATE, width), F32),
            shape((8, width + GROUP), F32),
        ],
        compiler_params=pltpu.CompilerParams(vmem_limit_bytes=VMEM_BYTES),
        name="scan_backward",
    )(pz, proj, y, filt, dn, rc, states, states, s0, cw, hp, table, gain, g0, e0)


def bring(step, pieces, buffers, sems, own):
    for near, far, buffer, sem in zip(*pieces, buffers, sems):
        to, done = buffer.at[step % 2], sem.at[step % 2]

        @pl.when(own)
        def _():
            pltpu.make_async_copy(near[step], to, done).start()

        @pl.when(jnp.logical_not(own))
        def _():
            pltpu.make_async_copy(far[step], to, done).start()


def arrived(step, pieces, buffers, sems):
    for near, buffer, sem in zip(pieces[0], buffers, sems):
        pltpu.make_async_copy(near[step], buffer.at[step % 2], sem.at[step % 2]).wait()
    return [buffer.at[step % 2] for buffer in buffers]


def project_kernel(ids, normed, *refs, layer, n):
    near, far = [refs[0:n]], [refs[n : 2 * n]]
    out, buffer, sem = refs[2 * n :]
    pieces = (near, far)
    own = ids[1] == layer
    columns = out.shape[1]
    share = buffer.shape[2]
    bring(0, pieces, [buffer], [sem], own)
    for m in range(n):
        if m + 1 < n:
            bring(m + 1, pieces, [buffer], [sem], own)
        (w,) = arrived(m, pieces, [buffer], [sem])
        from_place = pl.multiple_of(jnp.bitwise_xor(ids[0], m) * share, share)
        a = normed[:, pl.ds(from_place, share)]
        for lo in range(0, columns, 256):
            here = slice(lo, min(lo + 256, columns))
            v = lax.dot_general(
                a, w[here, :], (((1,), (1,)), ((), ())), preferred_element_type=F32
            )
            out[:, here] = v if m == 0 else out[:, here] + v


def project(ids, normed, near, far, layer):
    n = len(near)
    columns, share = near[0].shape
    rows = normed.shape[0]
    vmem = pl.BlockSpec(memory_space=pltpu.VMEM)
    return pl.pallas_call(
        functools.partial(project_kernel, layer=layer, n=n),
        in_specs=[pl.BlockSpec(memory_space=pltpu.SMEM), vmem]
        + [pl.BlockSpec(memory_space=pl.ANY)] * (2 * n),
        out_specs=vmem,
        scratch_shapes=[
            pltpu.VMEM((2, columns, share), BF16),
            pltpu.SemaphoreType.DMA((2,)),
        ],
        out_shape=jax.ShapeDtypeStruct((rows, columns), F32),
        compiler_params=pltpu.CompilerParams(vmem_limit_bytes=VMEM_BYTES),
        cost_estimate=pl.CostEstimate(
            flops=2 * rows * columns * share * n,
            bytes_accessed=columns * share * n * 2 + rows * columns * 4,
            transcendentals=0,
        ),
        name="project",
    )(ids, normed, *near, *far)


def back_kernel(ids, dz, dx, *refs, layer, n):
    near = (refs[0:n], refs[n : 2 * n])
    far = (refs[2 * n : 3 * n], refs[3 * n : 4 * n])
    out, zbuf, xbuf, zsem, xsem = refs[4 * n :]
    pieces = (near, far)
    own = ids[1] == layer
    share = zbuf.shape[2]
    args = ([zbuf, xbuf], [zsem, xsem])
    bring(0, pieces, *args, own)
    for m in range(n):
        if m + 1 < n:
            bring(m + 1, pieces, *args, own)
        wz, wx = arrived(m, pieces, *args)
        for lo in range(0, share, 256):
            here = slice(lo, lo + 256)
            v = jnp.dot(dz[...], wz[:, here], preferred_element_type=F32) + jnp.dot(
                dx[...], wx[:, here], preferred_element_type=F32
            )
            at_lane = pl.multiple_of(jnp.bitwise_xor(ids[0], m) * share + lo, 256)
            out[:, pl.ds(at_lane, 256)] = v.astype(BF16)


def project_back(ids, dz, dx, near, far, layer):
    n = len(near[0])
    share = near[0][0].shape[1]
    rows = dz.shape[0]
    columns = dz.shape[1] + dx.shape[1]
    vmem = pl.BlockSpec(memory_space=pltpu.VMEM)
    return pl.pallas_call(
        functools.partial(back_kernel, layer=layer, n=n),
        in_specs=[pl.BlockSpec(memory_space=pltpu.SMEM), vmem, vmem]
        + [pl.BlockSpec(memory_space=pl.ANY)] * (4 * n),
        out_specs=vmem,
        scratch_shapes=[
            pltpu.VMEM((2, dz.shape[1], share), BF16),
            pltpu.VMEM((2, dx.shape[1], share), BF16),
            pltpu.SemaphoreType.DMA((2,)),
            pltpu.SemaphoreType.DMA((2,)),
        ],
        out_shape=jax.ShapeDtypeStruct((rows, n * share), BF16),
        compiler_params=pltpu.CompilerParams(vmem_limit_bytes=VMEM_BYTES),
        cost_estimate=pl.CostEstimate(
            flops=2 * rows * columns * share * n,
            bytes_accessed=columns * share * n * 2 + rows * n * share * 2,
            transcendentals=0,
        ),
        name="project_back",
    )(ids, dz, dx, *near[0], *near[1], *far[0], *far[1])


def place_kernel(ids, *refs, plan, count, rows_of_small):
    small = refs[count]
    out, eye, pieces, blocks, in_sem, out_sem = refs[-6:]
    core = ids[1]
    size, share = blocks.shape[1:]

    def fetch(k):
        for layer in range(2):

            @pl.when(core == layer)
            def _():
                src = refs[plan[k][layer]]
                pltpu.make_async_copy(
                    src.at[:, pl.ds(0, share)], pieces.at[k % 2], in_sem.at[k % 2]
                ).start()

    def send(step, first, count):
        return pltpu.make_async_copy(
            blocks.at[step % 2, pl.ds(0, count)],
            out.at[pl.ds(first, count)],
            out_sem.at[step % 2],
        )

    eye[...] = (
        lax.broadcasted_iota(jnp.int32, eye.shape, 0)
        == lax.broadcasted_iota(jnp.int32, eye.shape, 1)
    ).astype(BF16)
    fetch(0)
    sent = []
    for k, (_, _, side, firsts) in enumerate(plan):
        if k + 1 < len(plan):
            fetch(k + 1)
        pltpu.make_async_copy(pieces.at[k % 2], pieces.at[k % 2], in_sem.at[k % 2]).wait()
        shift = jnp.where(side == 0, core, 1 - core) * (2 * size)
        for p, first in enumerate(firsts):
            step = len(sent)
            if step >= 2:
                sent[step - 2].wait()
            blocks[step % 2] = lax.dot_general(
                pieces[k % 2, p],
                eye[...],
                (((0,), (0,)), ((), ())),
                preferred_element_type=F32,
            )
            sent.append(send(step, pl.multiple_of(first + shift, 8), size))
            sent[-1].start()
    if rows_of_small:
        step = len(sent)
        sent[step - 2].wait()
        first, count = rows_of_small
        sent.append(
            pltpu.make_async_copy(small, out.at[pl.ds(first, count)], out_sem.at[step % 2])
        )
        sent[-1].start()
    sent[-2].wait()
    sent[-1].wait()


def place_in(ids, arrays, plan, small, rows_of_small, before, shape, size):
    places, share = arrays[0].shape[0], shape[1]
    any_space = pl.BlockSpec(memory_space=pl.ANY)
    return pl.pallas_call(
        functools.partial(
            place_kernel, plan=plan, count=len(arrays), rows_of_small=rows_of_small
        ),
        in_specs=[pl.BlockSpec(memory_space=pltpu.SMEM)]
        + [any_space] * len(arrays)
        + [pl.BlockSpec(memory_space=pltpu.VMEM)]
        + [any_space] * len(before),
        out_specs=any_space,
        scratch_shapes=[
            pltpu.VMEM((share, share), BF16),
            pltpu.VMEM((2, places, share, size), BF16),
            pltpu.VMEM((2, size, share), F32),
            pltpu.SemaphoreType.DMA((2,)),
            pltpu.SemaphoreType.DMA((2,)),
        ],
        out_shape=jax.ShapeDtypeStruct(shape, F32),
        input_output_aliases={len(arrays) + 2: 0} if before else {},
        compiler_params=pltpu.CompilerParams(vmem_limit_bytes=VMEM_BYTES),
        name="place_in",
    )(ids, *arrays, small, *before)


def swap_section(v):
    return lax.ppermute(v, "section", [(0, 1), (1, 0)])


def at(v, k):
    return lax.dynamic_index_in_dim(v, k, 0, False)


def exchange(v):
    return lax.all_to_all(v, "fsdp", 0, 0, tiled=True)


def to_all(v):
    n = lax.axis_size("fsdp")
    return exchange(jnp.broadcast_to(v[None], (n,) + v.shape))


def gather_rows(v):
    return to_all(v).reshape(-1, v.shape[-1])


def scatter_sum(partial):
    n = lax.axis_size("fsdp")
    got = exchange(partial.reshape(n, -1, partial.shape[-1]))
    return jnp.sum(got.astype(F32), axis=0)


def in_group(v):
    n, s = lax.axis_size("fsdp"), lax.axis_size("seq")
    groups = [[j * n + i for i in range(n)] for j in range(s // n)]
    return lax.all_to_all(v, "seq", 0, 0, axis_index_groups=groups, tiled=True)


def quarters(v):
    n = lax.axis_size("fsdp")
    return v.reshape(v.shape[0], n, -1).transpose(1, 0, 2)


def joined(v):
    return v.transpose(1, 0, 2).reshape(v.shape[1], -1)


def move_fsdp(v, m):
    n = lax.axis_size("fsdp")
    return lax.ppermute(v, "fsdp", [(k, k ^ m) for k in range(n)])


def move_seq(v, m):
    s = lax.axis_size("seq")
    return lax.ppermute(v, "seq", [(k, k ^ m) for k in range(s)])


class SeqSums:
    def __init__(self):
        s = lax.axis_size("seq")
        half = s // 2
        self.pairs = [[(j, j + 1), (s - 1 - j, s - 2 - j)] for j in range(half - 1)]
        self.pairs.append([(half - 1, half), (half, half - 1)])
        self.inward = half
        self.pairs += [[(j + 1, j), (s - 2 - j, s - 1 - j)] for j in reversed(range(half - 1))]
        self.values, self.phase = [], []
        self.came, self.moving, self.fresh = [], [], []

    def add(self, values):
        first = len(self.values)
        self.values += values
        self.phase += [0] * len(values)
        return list(range(first, len(self.values)))

    def begin(self):
        place = lax.axis_index("seq")
        for k, got in self.came:
            step, v = self.phase[k] - 1, self.values[k]
            if step < self.inward:
                v = (v.astype(F32) + got.astype(F32)).astype(BF16)
            else:
                here = functools.reduce(
                    jnp.logical_or, [place == to for _, to in self.pairs[step]]
                )
                v = jnp.where(here, got, v)
            self.fresh.append((k, v))
        taken = set()
        waiting = [k for k, _ in self.came]
        for k, step in enumerate(self.phase):
            if step == len(self.pairs) or step in taken or k in waiting:
                continue
            taken.add(step)
            self.moving.append((k, lax.ppermute(self.values[k], "seq", self.pairs[step])))
            self.phase[k] = step + 1

    def end(self, work):
        still = [k for k, p in enumerate(self.phase) if p == 0]
        work, fresh, came, rest = lax.optimization_barrier(
            (
                work,
                [v for _, v in self.fresh],
                [v for _, v in self.moving],
                [self.values[k] for k in still],
            )
        )
        for (k, _), v in zip(self.fresh, fresh):
            self.values[k] = v
        for k, v in zip(still, rest):
            self.values[k] = v
        self.came = [(k, v) for (k, _), v in zip(self.moving, came)]
        self.moving, self.fresh = [], []
        return work

    def done(self, k):
        busy = [j for j, _ in self.came + self.moving + self.fresh]
        return self.phase[k] == len(self.pairs) and k not in busy


def relay(total, local, reverse):
    n, s = lax.axis_size("fsdp"), lax.axis_size("seq")
    segments = s // n
    place = lax.axis_index("seq") // n
    own = lax.axis_index("seq") % n
    totals = lax.all_gather(total, "seq")
    locals_ = lax.all_gather(local, "seq")
    state = jnp.zeros_like(local)
    order = range(segments - 1, -1, -1) if reverse else range(segments)
    for j in order:
        use = (j > place) if reverse else (j < place)
        t = lax.dynamic_index_in_dim(totals, j * n + own, 0, False)
        v = lax.dynamic_index_in_dim(locals_, j * n + own, 0, False)
        state = jnp.where(use, t * state + v, state)
    return state


def next_segment(v, step):
    n, s = lax.axis_size("fsdp"), lax.axis_size("seq")
    pairs = [(k, k + step * n) for k in range(s) if 0 <= k + step * n < s]
    return lax.ppermute(v, "seq", pairs)


def dot_rows(a, b):
    return lax.dot_general(a, b, (((0,), (0,)), ((), ())), preferred_element_type=F32)


def dot_cols(a, b):
    return lax.dot_general(a, b, (((1,), (1,)), ((), ())), preferred_element_type=F32)


def normalised(h, gain):
    return h * lax.rsqrt(jnp.mean(h * h, axis=-1, keepdims=True) + EPS) * gain


def per_device(
    inputs,
    cotangent,
    lengths,
    gain_in,
    w_in,
    conv_w,
    conv_b,
    dt_bias,
    a_log,
    d_skip,
    gain_out,
    w_out,
):
    n = lax.axis_size("fsdp")
    nz = lax.axis_size("seq")
    segments = nz // n
    c = lax.axis_index("section")
    f = lax.axis_index("fsdp")
    place = lax.axis_index("seq")
    upper = c == 0
    rows = inputs.shape[2]
    width = INNER // n
    heads = HEADS // n
    share = D // n
    half = share // 2
    group = GROUP // n
    ids = jnp.stack([f, c]).astype(jnp.int32)
    tie = lax.optimization_barrier

    def pick(a, b):
        return jnp.where(upper, a, b)

    w = w_in[0].T

    def cut(first, size):
        return lax.dynamic_slice_in_dim(w, first, size, 0)

    def piece_z(m):
        return cut((f ^ m) * width, width)

    def piece_x(m):
        return jnp.concatenate(
            [
                cut(INNER + (f ^ m) * width, width),
                w[2 * INNER : 2 * INNER + GROUP],
                cut(2 * INNER + GROUP + (f ^ m) * heads, heads),
            ]
        )

    def fetch(pieces, layer):
        pairs = lambda m: [(layer * n + i, layer * n + (i ^ m)) for i in range(n)]
        near = [
            v if m == 0 else lax.ppermute(v, ("section", "fsdp"), pairs(m))
            for m, v in enumerate(pieces)
        ]
        return near, [lax.ppermute(v, "section", [(layer, 1 - layer)]) for v in near]

    def whole_slot(v):
        return joined(to_all(v.reshape(n * rows, share)))

    pack = jnp.concatenate(
        [
            gain_in[0],
            dt_bias[0],
            a_log[0],
            d_skip[0],
            gain_out[0],
            conv_w[0].reshape(-1),
            conv_b[0],
        ]
    )
    mine, part_h0, pieces_x = tie(
        (to_all(pack), exchange(quarters(at(inputs, c)[0])), [piece_x(m) for m in range(n)])
    )
    near_x0, far_x0 = fetch(pieces_x, 0)
    part_h0 = in_group(part_h0)
    near_x0, part_h0 = tie((near_x0, part_h0))
    far_x0 = [lax.ppermute(v, "section", [(0, 1)]) for v in near_x0]
    all_h0 = whole_slot(part_h0)
    pieces_z, all_h0 = tie(([piece_z(m) for m in range(n)], all_h0))
    near_z0, far_z0 = fetch(pieces_z, 0)

    theirs = swap_section(mine)
    small = []
    for full in (pick(mine, theirs), pick(theirs, mine)):
        full = full.astype(F32)
        used = 0

        def take(size):
            nonlocal used
            used += size
            return full[:, used - size : used]

        gain = take(share).reshape(1, D)
        hp = [at(take(heads), f)[None] for _ in range(3)]
        hp = jnp.concatenate([hp[0], -jnp.exp(hp[1]), hp[2], jnp.zeros((5, heads), F32)])
        gout = at(take(width), f)[None]
        per = CHANNELS // n
        taps = take(KERNEL * per).reshape(n, KERNEL, per).transpose(1, 0, 2)
        bias = take(per).reshape(1, CHANNELS)
        table = jnp.concatenate(
            [taps.reshape(KERNEL, CHANNELS), bias, jnp.zeros((3, CHANNELS), F32)]
        )
        cw = jnp.concatenate(
            [lax.dynamic_slice_in_dim(table, f * width, width, 1), table[:, INNER:]], axis=1
        )
        small.append((gain, cw, hp, gout))

    win = [(near_z0, far_z0, near_x0, far_x0), None]
    expand = (
        jnp.arange(heads)[:, None] == jnp.arange(width)[None, :] // HEAD_DIM
    ).astype(BF16)
    zero_state = jnp.zeros((STATE, width), F32)
    zero_edge = jnp.zeros((8, width + GROUP), F32)

    def project_x(normed, layer):
        return project(ids, normed, win[layer][2], win[layer][3], layer)

    def project_z(normed, layer):
        return project(ids, normed, win[layer][0], win[layer][1], layer)

    def decay_of(px, hp):
        decay = jax.nn.softplus(px[:, width + GROUP :] + hp[0:1]) * hp[1:2]
        return jnp.repeat(jnp.exp(jnp.sum(decay, axis=0)), HEAD_DIM)[None, :]

    def scan(px, layer):
        _, cw, hp, _ = small[layer]
        args = (px, cw, hp)
        if segments == 1:
            return run_forward(*args, zero_state, zero_edge, rows), zero_state
        edge = next_segment(px[-8:, : width + GROUP], 1)
        local = run_forward(*args, zero_state, edge, rows)[2][-1]
        state = relay(decay_of(px, hp), local, False)
        return run_forward(*args, state, edge, rows), state

    def unscan(pz, px, fwd, dn, rc, layer):
        (y, filt, states), state = fwd
        _, cw, hp, gout = small[layer]
        args = (pz, px, y, filt, dn, rc, states, state, cw, hp, expand, gout)
        if segments == 1:
            return run_backward(*args, zero_state, zero_edge, rows, n)[:6]
        local = run_backward(*args, zero_state, zero_edge, rows, n)[6]
        grad = relay(decay_of(px, hp), local, True)
        edge = next_segment(run_backward(*args, grad, zero_edge, rows, n)[7], -1)
        return run_backward(*args, grad, edge, rows, n)[:6]

    def gate(pz, y):
        return y * jax.nn.silu(pz)

    def gated(pz, y, r, layer):
        return (gate(pz, y) * r[:, None] * small[layer][3]).astype(BF16)

    def sum_of_shares(v):
        return jnp.sum(to_all(v), axis=0)

    normed_in0 = normalised(all_h0.astype(F32), small[0][0]).astype(BF16)
    px0 = project_x(normed_in0, 0)
    px0, near_z0, pieces_x1, pieces_z1, own_ct, wo_mine, own_len = tie(
        (px0, near_z0, pieces_x, pieces_z, at(cotangent, c)[0], w_out[0], at(lengths, c))
    )
    far_z0 = [lax.ppermute(v, "section", [(0, 1)]) for v in near_z0]
    win[0] = (near_z0, far_z0, near_x0, far_x0)
    near_x1, far_x1 = fetch(pieces_x1, 1)
    wo_other = swap_section(wo_mine)
    wo = (pick(wo_mine, wo_other), pick(wo_other, wo_mine))
    slot_pairs = [
        ((j * n + i) * n + k, (j * n + k) * n + i)
        for j in range(segments)
        for i in range(n)
        for k in range(n)
    ]
    length = lax.ppermute(own_len, ("seq", "fsdp"), slot_pairs)
    first_row = (place // n) * n * rows
    all_valid = first_row + jnp.arange(n * rows, dtype=jnp.int32) < length[0]
    all_valid = all_valid.astype(F32)[:, None]
    own_rows = lambda v: lax.dynamic_slice_in_dim(v, f * rows, rows, 0)
    valid = own_rows(all_valid)
    h0 = own_rows(all_h0)
    fwd0 = scan(px0, 0)
    pz0 = project_z(normed_in0, 0)
    g0 = gate(pz0, fwd0[0][0])
    stat0, near_x1, pieces_z1 = tie((jnp.sum(g0 * g0, axis=1), near_x1, pieces_z1))
    near_z1, far_z1 = fetch(pieces_z1, 1)
    stat0 = sum_of_shares(stat0.reshape(n, rows)).reshape(-1)
    r0 = lax.rsqrt(stat0 / INNER + EPS)
    normed0 = gated(pz0, fwd0[0][0], r0, 0)
    part_ct = in_group(exchange(quarters(own_ct)))
    normed0, wo, part_ct = tie((normed0, wo, part_ct))
    far_x1 = [lax.ppermute(v, "section", [(1, 0)]) for v in near_x1]
    mixed0 = scatter_sum(jnp.dot(normed0, wo[0], preferred_element_type=F32).astype(BF16))
    out0 = valid * (h0.astype(F32) + mixed0)
    h1 = out0.astype(BF16)

    h1, near_z1 = tie((h1, near_z1))
    far_z1 = [lax.ppermute(v, "section", [(1, 0)]) for v in near_z1]
    win[1] = (near_z1, far_z1, near_x1, far_x1)
    normed_in1 = gather_rows(normalised(h1.astype(F32), small[1][0]).astype(BF16))
    normed_in1, far_x1, part_ct = tie((normed_in1, far_x1, part_ct))
    px1 = project_x(normed_in1, 1)
    all_ct = whole_slot(part_ct)
    fwd1 = scan(px1, 1)
    fwd1, all_ct = tie((fwd1, all_ct))
    dout1 = own_rows(all_ct).astype(F32)
    dmixed1 = (all_valid * all_ct.astype(F32)).astype(BF16)
    dn1 = dot_cols(dmixed1, wo[1])
    pz1 = project_z(normed_in1, 1)
    g1 = gate(pz1, fwd1[0][0])
    stat1 = sum_of_shares(
        jnp.stack(
            [
                jnp.sum(g1 * g1, axis=1).reshape(n, rows),
                jnp.sum(g1 * dn1 * small[1][3], axis=1).reshape(n, rows),
            ]
        )
    ).reshape(2, -1)
    r1 = lax.rsqrt(stat1[0] / INNER + EPS)
    normed1 = gated(pz1, fwd1[0][0], r1, 1)

    part_width = width // 4

    def cut_half(v, k):
        size = v.shape[1] // 2
        return lax.dynamic_slice_in_dim(v, k * size, size, 1)

    def narrow_of(parts, k):
        return jnp.concatenate([cut_half(v, k) for v in parts], axis=1)

    def away_in(normed_in, part, narrow=()):
        away = [dot_rows(normed_in, cut_half(part, 1 - c)).astype(BF16)]
        if narrow:
            away.append(dot_rows(narrow_of(narrow, 1 - c), normed_in).astype(BF16))
        return [swap_section(v) for v in away]

    def own_in_pieces(normed_in, part, away, narrow=()):
        own = cut_half(part, c)
        result = []
        for cols in (slice(0, part_width), slice(part_width, 2 * part_width)):
            total = dot_rows(normed_in, own[:, cols]) + away[0][:, cols].astype(F32)
            result.append(total.astype(BF16).reshape(n, share, -1))
        if narrow:
            total = dot_rows(narrow_of(narrow, c), normed_in) + away[1].astype(F32)
            rest = total.astype(BF16).reshape(-1, n, share).transpose(1, 0, 2)
            rest = rest.reshape(n, -1, part_width)
            result[1] = jnp.concatenate([result[1], rest], axis=1)
        return result

    def away_out(normed, dmixed):
        return swap_section(dot_rows(cut_half(normed, 1 - c), dmixed).astype(BF16))

    def own_out_pieces(normed, dmixed, away):
        own = cut_half(normed, c)
        result = []
        for cols in (slice(0, D // 2), slice(D // 2, D)):
            total = dot_rows(own, dmixed[:, cols]) + away[:, cols].astype(F32)
            result.append(total.astype(BF16))
        return result

    def with_group(dxs, dbc):
        total = jnp.sum(exchange(dbc), axis=0).astype(BF16)
        column = jnp.arange(GROUP)[None, :] // group
        own = jnp.where(column == f, jnp.concatenate([total] * n, axis=1), 0)
        full = lax.dynamic_update_slice(dxs, own.astype(BF16), (0, width))
        return full, (dxs[:, :width], [total, dxs[:, width + GROUP :]])

    def back_in(dz, full, layer):
        near_z, far_z, near_x, far_x = win[layer]
        return project_back(ids, dz, full, (near_z, near_x), (far_z, far_x), layer)

    def back_norm(dout, dnormed_in, h, gain):
        h = h.astype(F32)
        r = lax.rsqrt(jnp.mean(h * h, axis=-1, keepdims=True) + EPS)
        u = dnormed_in * gain
        mean = jnp.mean(u * h, axis=-1, keepdims=True)
        dgain = jnp.sum(dnormed_in * h * r, axis=0)
        return valid * dout + r * u - h * (r * r * r) * mean, dgain

    def scales(r, coef):
        top = jnp.stack([r.reshape(n, rows), coef.reshape(n, rows)], axis=1)
        return jnp.concatenate([top, jnp.zeros((n, 6, rows), F32)], axis=1)

    def packed(dgin, d, out, mixed):
        dgain, dconv, dhp = d[3][0], d[4][:5], d[5][:3]
        put = lambda v, size, at_lane: lax.dynamic_update_slice(
            jnp.zeros(v.shape[:-1] + (size,), F32), v, (0,) * (v.ndim - 1) + (at_lane,)
        )
        conv = put(dconv[:, :width], CHANNELS, f * width)
        conv = conv.at[:, INNER:].set(dconv[:, width:])
        totals = jnp.stack(
            [jnp.sum(out * out), jnp.sum((valid * mixed) ** 2), jnp.sum(valid)]
        )
        return jnp.concatenate(
            [
                dgin,
                conv.reshape(-1),
                put(dhp, HEADS, f * heads).reshape(-1),
                put(dgain, INNER, f * width),
                totals,
            ]
        )

    def hand_over(v, layer):
        return lax.ppermute(v, "section", [(1 - layer, layer)])

    sums = SeqSums()
    rc1 = scales(r1, (r1 * r1 * r1 / INNER) * stat1[1])
    away = away_out(normed1, dmixed1)
    go1 = sums.add(own_out_pieces(normed1, dmixed1, away))
    rc1, normed1, dn1 = sums.end((rc1, normed1, dn1))

    sums.begin()
    d1 = unscan(pz1, px1, fwd1, dn1, rc1, 1)
    mixed1 = scatter_sum(jnp.dot(normed1, wo[1], preferred_element_type=F32).astype(BF16))
    d1, mixed1 = sums.end((d1, mixed1))

    sums.begin()
    away = away_in(normed_in1, d1[0])
    full1, xs1 = with_group(d1[1], d1[2])
    back1 = back_in(d1[0], full1, 1)
    back1, xs1, away, full1 = sums.end((back1, xs1, away, full1))

    sums.begin()
    dnin1 = scatter_sum(back1)
    gz = own_in_pieces(normed_in1, d1[0], away)
    away = away_in(normed_in1, *xs1)
    dnin1, gz, away = sums.end((dnin1, gz, away))
    gz1 = sums.add(gz)

    sums.begin()
    grad1, dgin1 = back_norm(dout1, dnin1, h1, small[1][0])
    dout0 = grad1.astype(BF16).astype(F32)
    dmixed0_own = (valid * dout0).astype(BF16)
    dmixed0 = gather_rows(dmixed0_own)
    along0 = to_all(jnp.sum(dmixed0_own.astype(F32) * mixed0, axis=-1)).reshape(-1)
    rc0 = scales(r0, (r0 * r0 / INNER) * along0)
    gx = own_in_pieces(normed_in1, xs1[0], away, xs1[1])
    out1 = valid * (h1.astype(F32) + mixed1)
    grad1, dgin1, dmixed0, rc0, gx, out1 = sums.end((grad1, dgin1, dmixed0, rc0, gx, out1))
    gx1 = sums.add(gx)

    sums.begin()
    dn0 = dot_cols(dmixed0, wo[0])
    d0 = unscan(pz0, px0, fwd0, dn0, rc0, 0)
    d0 = sums.end(d0)

    sums.begin()
    away_z = away_in(normed_in0, d0[0])
    away_o = away_out(normed0, dmixed0)
    full0, xs0 = with_group(d0[1], d0[2])
    gz = own_in_pieces(normed_in0, d0[0], away_z)
    go = own_out_pieces(normed0, dmixed0, away_o)
    full0, xs0, gz, go = sums.end((full0, xs0, gz, go))
    go0 = sums.add(go)

    sums.begin()
    away = away_in(normed_in0, *xs0)
    gz = [exchange(v) for v in gz]
    gx = own_in_pieces(normed_in0, xs0[0], away, xs0[1])
    gz, gx, full0 = sums.end((gz, gx, full0))
    gz0 = sums.add(gz)

    sums.begin()
    gx = [exchange(v) for v in gx]
    back0 = back_in(d0[0], full0, 0)
    gx, back0 = sums.end((gx, back0))
    gx0 = sums.add(gx)

    sums.begin()
    dnin0 = scatter_sum(back0)
    grad0, dgin0 = back_norm(dout0, dnin0, h0, small[0][0])
    p = jnp.stack([packed(dgin0, d0, out0, mixed0), packed(dgin1, d1, out1, mixed1)])
    p = p + swap_section(p)
    p, grad0, grad1, h1, out1 = sums.end((p, grad0, grad1, h1, out1))

    names = {"own": {}, "away": {}}
    order = [(k, 1, "out") for k in go1] + [(k, 1, "in") for k in gz1 + gx1]
    order += [(k, 0, "out") for k in go0] + [(k, 0, "in") for k in gz0 + gx0]
    back = jnp.concatenate([h1, out1.astype(BF16), grad0.astype(BF16), grad1.astype(BF16)])
    back_steps = [lambda v: exchange(quarters(v)), in_group, lambda v: joined(exchange(v))]
    p_steps = [lambda v, m=m: move_fsdp(v, m) for m in (1 << j for j in range(n.bit_length() - 1))]
    p_steps += [lambda v, m=m: move_seq(v, m) for m in (1 << j for j in range(nz.bit_length() - 1))]
    exchanged = set()
    while order:
        sums.begin()
        ready = [e for e in order if sums.done(e[0])]
        turn = [e for e in ready if e[1:] == (1, "in") and e[0] not in exchanged][:2]
        if back_steps:
            back = back_steps.pop(0)(back)
            turn = turn[:1]
        if p_steps:
            p = p + p_steps.pop(0)(p)
        swapped = {e[0]: exchange(sums.values[e[0]]) for e in turn}
        final = [e for e in ready if e[1:] != (1, "in") or e[0] in exchanged][:2]
        fresh = {e[0]: hand_over(sums.values[e[0]], e[1]) for e in final}
        kept = {e[0]: sums.values[e[0]] for e in final}
        swapped, fresh, kept, back, p = sums.end((swapped, fresh, kept, back, p))
        for k, v in swapped.items():
            sums.values[k] = v
            exchanged.add(k)
        for k in fresh:
            names["own"][k], names["away"][k] = kept[k], fresh[k]
        order = [e for e in order if e not in final]
    p = pick(p[0], p[1])

    used = 0

    def part(size):
        nonlocal used
        used += size
        return p[used - size : used]

    mine_of = lambda v, size: lax.dynamic_slice_in_dim(v, f * size, size, v.ndim - 1)
    o_gain_in = mine_of(part(D), share)
    o_conv = mine_of(part(5 * CHANNELS).reshape(5, CHANNELS), CHANNELS // n)
    o_heads = mine_of(part(3 * HEADS).reshape(3, HEADS), heads)
    o_gain_out = mine_of(part(INNER), width)
    totals = part(3)
    act_rms = jnp.sqrt(totals[:2] / (totals[2] * D))[None]

    sides = ("own", "away")
    held = [
        [[names[side][k] for k in ks] for ks in (gz0 + gx0 + go0, gz1 + gx1 + go1)]
        for side in sides
    ]

    def both_halves(a, b):
        return jnp.stack([pick(a, b), pick(b, a)], axis=1)

    narrow = [pick(side[0][3], side[1][3])[:, share:] for side in held]
    narrow = both_halves(*[v.astype(F32).reshape(n, -1, share) for v in narrow])
    small_in = jnp.concatenate(
        [
            narrow[:, :, : group // 2].reshape(GROUP, share),
            narrow[:, :, group // 2 :].reshape(HEADS, share),
        ]
    )
    g_w_in = []
    shape_in = (2 * INNER + GROUP + HEADS, share)
    for ks, rows_of_small in (((0, 1), None), ((2, 3), (2 * INNER, GROUP + HEADS))):
        arrays, plan = [], []
        for k in ks:
            for s in range(2):
                arrays += [held[s][0][k], held[s][1][k]]
                base = k // 2 * INNER + k % 2 * part_width
                firsts = tuple(base + q * width for q in range(n))
                plan.append((len(arrays) - 2, len(arrays) - 1, s, firsts))
        g_w_in = [
            place_in(
                ids, arrays, tuple(plan), small_in, rows_of_small, g_w_in, shape_in, part_width
            )
        ]
    halves_out = [
        jnp.concatenate([pick(side[0][k], side[1][k]) for k in (4, 5)], axis=1) for side in held
    ]
    g_w_out = both_halves(*[v[None] for v in halves_out]).reshape(width, D).astype(F32)

    back = back.reshape(2, 2, rows, D)
    kept_back = pick(back[:, 0], back[:, 1])
    other_back = swap_section(pick(back[:, 1], back[:, 0]))
    both_back = jnp.stack(
        [pick(kept_back, other_back), pick(other_back, kept_back)], axis=1
    )
    return (
        both_back[0][None, :, None],
        both_back[1].astype(F32)[None, :, None],
        o_gain_in[None],
        g_w_in[0].T[None],
        o_conv[None, :4],
        o_conv[None, 4],
        o_heads[None, 0],
        o_heads[None, 1],
        o_heads[None, 2],
        o_gain_out[None],
        g_w_out[None],
        act_rms,
    )


def solution(mesh):
    in_specs = (
        P(None, "fsdp", "seq", None),
        P(None, "fsdp", "seq", None),
        P(None, "fsdp"),
        P("section", "fsdp"),
        P("section", "fsdp", None),
        P("section", None, "fsdp"),
        P("section", "fsdp"),
        P("section", "fsdp"),
        P("section", "fsdp"),
        P("section", "fsdp"),
        P("section", "fsdp"),
        P("section", "fsdp", None),
    )
    out_specs = (
        P("section", None, "fsdp", "seq", None),
        P("section", None, "fsdp", "seq", None),
        P("section", "fsdp"),
        P("section", "fsdp", None),
        P("section", None, "fsdp"),
        P("section", "fsdp"),
        P("section", "fsdp"),
        P("section", "fsdp"),
        P("section", "fsdp"),
        P("section", "fsdp"),
        P("section", "fsdp", None),
        P("section", None),
    )
    return jax.shard_map(
        per_device, mesh=mesh, in_specs=in_specs, out_specs=out_specs, check_vma=False
    )
```

```python
import functools

import jax
import jax.numpy as jnp
from jax import lax
from jax.experimental import pallas as pl
from jax.experimental.pallas import tpu as pltpu
from jax.sharding import PartitionSpec as P

D = 2048
INNER = 4096
HEADS = 64
HEAD_DIM = 64
STATE = 128
KERNEL = 4
GROUP = 2 * STATE
CHANNELS = INNER + GROUP
LANES = 128
EPS = 1e-05
F32 = jnp.float32
BF16 = jnp.bfloat16
VMEM_BYTES = 48 * 1024 * 1024


def split(v):
    hi = v.astype(BF16)
    return hi, (v - hi.astype(F32)).astype(BF16)


def dot32(a, b, ca, cb):
    (ah, al), (bh, bl) = (v if isinstance(v, tuple) else split(v) for v in (a, b))
    one = lambda p, q: lax.dot_general(
        p, q, (((ca,), (cb,)), ((), ())), preferred_element_type=F32
    )
    return one(ah, bh) + (one(ah, bl) + one(al, bh))


def step_sizes(raw, hp, rows):
    shifted = raw + hp[0:1, :]
    dt = jnp.maximum(shifted, 0.0) + jnp.log1p(jnp.exp(-jnp.abs(shifted)))
    decay = dt * hp[1:2, :]
    row = lax.broadcasted_iota(jnp.int32, (rows, rows), 0)
    col = lax.broadcasted_iota(jnp.int32, (rows, rows), 1)
    lower = (row >= col).astype(F32)
    cum = dot32(lower, decay, 1, 0)
    cum_t = dot32(decay, lower, 0, 1)
    return shifted, dt, cum, cum_t, row, col, lower


def pair_lanes(v, j, first):
    return jnp.where(first, v[:, 2 * j : 2 * j + 1], v[:, 2 * j + 1 : 2 * j + 2])


def head_sums(v, table):
    hi, low = split(v)
    one = lambda p: lax.dot_general(
        p, table, (((1,), (1,)), ((), ())), preferred_element_type=F32
    )
    return one(hi) + one(low)


def forward_kernel(proj, cw, hp, s0, e0, y_ref, filt_ref, st_ref, state, xp, xw_s, last_s):
    i = pl.program_id(0)
    rows, width = y_ref.shape

    @pl.when(i == 0)
    def _():
        state[...] = s0[...]
        xp[0:8, :] = e0[...]

    xp[8 : 8 + rows, :] = proj[:, : width + GROUP]

    def conv_tile(lo):
        acc = cw[4:5, lo : lo + LANES]
        for k in range(KERNEL):
            acc = acc + cw[k : k + 1, lo : lo + LANES] * xp[5 + k : 5 + k + rows, lo : lo + LANES]
        filt_ref[:, lo : lo + LANES] = acc
        return acc * jax.nn.sigmoid(acc)

    b_c = conv_tile(width)
    c_c = conv_tile(width + STATE)
    _, dt, cum, cum_t, row, col, _ = step_sizes(proj[:, width + GROUP :], hp, rows)
    last = cum[rows - 1 : rows, :]
    ecum = jnp.exp(cum)
    weight = jnp.exp(last - cum) * dt
    elast = jnp.exp(last)
    b_c, c_c = split(b_c), split(c_c)
    carried = dot32(c_c, state[...], 1, 0)
    scores = dot32(c_c, b_c, 1, 1)
    causal = row >= col
    lane = lax.broadcasted_iota(jnp.int32, (rows, LANES), 1)
    first = lane < HEAD_DIM
    for j in range(width // LANES):
        lo = j * LANES
        here = slice(lo, lo + LANES)
        x = conv_tile(lo)
        xd = x * pair_lanes(dt, j, first)
        m = []
        for h in (2 * j, 2 * j + 1):
            gap = cum[:, h : h + 1] - cum_t[h : h + 1, :]
            m.append(jnp.exp(jnp.where(causal, gap, -1e30)) * scores)
        xd2 = jnp.concatenate([jnp.where(first, xd, 0.0), jnp.where(first, 0.0, xd)])
        y = (
            dot32(jnp.concatenate(m, axis=1), xd2, 1, 0)
            + carried[:, here] * pair_lanes(ecum, j, first)
            + pair_lanes(hp[2:3, :], j, first[0:1]) * x
        )
        y_ref[:, here] = y
        xw_s[:, here] = x * pair_lanes(weight, j, first)
        last_s[0:1, here] = pair_lanes(elast, j, first[0:1])
    state[...] = state[...] * last_s[0:1, :] + dot32(b_c, xw_s[...], 0, 0)
    st_ref[0] = state[...]
    xp[0:8, :] = xp[rows : rows + 8, :]


def backward_kernel(
    pz,
    proj,
    y_ref,
    filt,
    dn,
    rc,
    st_before,
    st_out,
    s0,
    cw,
    hp,
    table,
    gain,
    g0,
    e0,
    dz_ref,
    dproj,
    dbc_ref,
    dgain_ref,
    dconv_ref,
    dhp_ref,
    gfin_ref,
    efin_ref,
    grad,
    dfp,
    both,
    xw_s,
    dyc_s,
    rowv,
):
    i = pl.program_id(0)
    rows, width = y_ref.shape
    heads = hp.shape[1]

    @pl.when(i == 0)
    def _():
        grad[...] = g0[...]
        dfp[rows : rows + 8, :] = e0[...]
        dgain_ref[...] = jnp.zeros_like(dgain_ref)
        dconv_ref[...] = jnp.zeros_like(dconv_ref)
        dhp_ref[...] = jnp.zeros_like(dhp_ref)

    def silu_pair(v):
        s = jax.nn.sigmoid(v)
        a = v * s
        return a, s * (1.0 + v - a)

    b_c, b_d = silu_pair(filt[:, width : width + STATE])
    c_c, c_d = silu_pair(filt[:, width + STATE :])
    shifted, dt, cum, cum_t, row, col, lower = step_sizes(proj[:, width + GROUP :], hp, rows)
    last = cum[rows - 1 : rows, :]
    tail = jnp.exp(last - cum)
    ecum = jnp.exp(cum)
    elast = jnp.exp(last)
    b_c, c_c = split(b_c), split(c_c)
    grad_p = split(grad[...])
    k_all = dot32(b_c, grad_p, 1, 0)
    scores_t = dot32(b_c, c_c, 1, 1)
    causal_t = row <= col
    lane = lax.broadcasted_iota(jnp.int32, (rows, LANES), 1)
    first = lane < HEAD_DIM
    dcb_t = jnp.zeros((rows, rows), F32)
    rc_t = dot32((row == col).astype(F32), rc[0], 1, 1)
    r = rc_t[:, 0:1]
    coef = rc_t[:, 1:2]
    rowv[0:1, :] = jnp.sum(grad[...] * st_out[0], axis=0, keepdims=True)
    for j in range(width // LANES):
        lo = j * LANES
        here = slice(lo, lo + LANES)
        z = pz[:, here]
        y = y_ref[:, here]
        sz, dsz = silu_pair(z)
        g = y * sz
        dnt = dn[:, here]
        dg = dnt * gain[0:1, here] * r - g * coef
        dgain_ref[0:1, here] += jnp.sum(dnt * g * r, axis=0, keepdims=True)
        dy = dg * sz
        dz_ref[:, here] = (dg * y * dsz).astype(BF16)
        x, xder = silu_pair(filt[:, here])
        dt_e = pair_lanes(dt, j, first)
        tail_e = pair_lanes(tail, j, first)
        xd = x * dt_e
        dy2 = split(jnp.concatenate([jnp.where(first, dy, 0.0), jnp.where(first, 0.0, dy)]))
        decays = []
        for h in (2 * j, 2 * j + 1):
            gap = cum_t[h : h + 1, :] - cum[:, h : h + 1]
            decays.append(jnp.exp(jnp.where(causal_t, gap, -1e30)))
        m = jnp.concatenate([d * scores_t for d in decays], axis=1)
        dm = dot32(xd, dy2, 1, 1)
        dcb_t = dcb_t + (decays[0] * dm[:, :rows] + decays[1] * dm[:, rows:])
        v = dot32(m, dy2, 1, 0) + k_all[:, here] * tail_e
        skip = pair_lanes(hp[2:3, :], j, first[0:1])
        dx = dt_e * v + skip * dy
        both[0:rows, here] = x * v
        both[rows : 2 * rows, here] = dy * (y - skip * x)
        rowv[1:2, here] = jnp.sum(dy * x, axis=0, keepdims=True)
        rowv[2:3, here] = pair_lanes(elast, j, first[0:1])
        xw_s[:, here] = xd * tail_e
        dyc_s[:, here] = dy * pair_lanes(ecum, j, first)
        dfp[0:rows, here] = dx * xder
    dcb_t = split(dcb_t)
    dyc = split(dyc_s[...])
    st_in = jnp.where(i == pl.num_programs(0) - 1, s0[...], st_before[0])
    dc = dot32(dcb_t, b_c, 0, 0) + dot32(dyc, st_in, 1, 1)
    db = dot32(dcb_t, c_c, 1, 0) + dot32(xw_s[...], grad_p, 1, 1)
    dfp[0:rows, width : width + STATE] = db * b_d
    dfp[0:rows, width + STATE :] = dc * c_d
    grad[...] = grad[...] * rowv[2:3, :] + dot32(c_c, dyc, 0, 0)
    gfin_ref[...] = grad[...]

    sums = head_sums(both[...], table[...])
    rsums = head_sums(rowv[...], table[...])
    ddt_x = sums[0:rows]
    dcum = sums[rows : 2 * rows] - dt * ddt_x
    upto = lax.broadcasted_iota(jnp.int32, (rows, heads), 0)
    dcum = dcum + jnp.where(upto == rows - 1, rsums[0:1, :], 0.0)
    ddecay = dot32(lower, dcum, 0, 0)
    ddt = ddt_x + hp[1:2, :] * ddecay
    draw = ddt * jax.nn.sigmoid(shifted)
    dproj[:, width + GROUP :] = draw.astype(BF16)
    dhp_ref[0:1, :] += jnp.sum(draw, axis=0, keepdims=True)
    dhp_ref[1:2, :] += jnp.sum(ddecay * dt, axis=0, keepdims=True) * hp[1:2, :]
    dhp_ref[2:3, :] += rsums[1:2, :]

    for lo in range(0, width + GROUP, LANES):
        here = slice(lo, lo + LANES)
        src = proj[:, here]
        total = jnp.zeros((rows, LANES), F32)
        for k in range(KERNEL):
            shift = KERNEL - 1 - k
            moved = dfp[shift : shift + rows, here]
            total = total + cw[k : k + 1, here] * moved
            dconv_ref[k : k + 1, here] += jnp.sum(src * moved, axis=0, keepdims=True)
        dconv_ref[4:5, here] += jnp.sum(dfp[0:rows, here], axis=0, keepdims=True)
        if lo < width:
            dproj[:, here] = total.astype(BF16)
        else:
            dproj[:, here] = jnp.zeros((rows, LANES), BF16)
            share = dbc_ref.shape[2]
            for k in range(LANES // share):
                dbc_ref[(lo - width) // share + k] = total[:, k * share : (k + 1) * share]
    dfp[rows : rows + 8, :] = dfp[0:8, :]
    efin_ref[...] = dfp[0:8, :]


def whole(shape):
    return pl.BlockSpec(shape, lambda i: (0,) * len(shape))


def run_forward(proj, cw, hp, s0, e0, rows):
    total, width = proj.shape[0], s0.shape[1]
    count = total // rows
    block = lambda w: pl.BlockSpec((rows, w), lambda i: (i, 0))
    shape = jax.ShapeDtypeStruct
    return pl.pallas_call(
        forward_kernel,
        grid=(count,),
        in_specs=[block(proj.shape[1])] + [whole(v.shape) for v in (cw, hp, s0, e0)],
        out_specs=[
            block(width),
            block(width + GROUP),
            pl.BlockSpec((1, STATE, width), lambda i: (i, 0, 0)),
        ],
        scratch_shapes=[
            pltpu.VMEM((STATE, width), F32),
            pltpu.VMEM((rows + 8, width + GROUP), F32),
            pltpu.VMEM((rows, width), F32),
            pltpu.VMEM((8, width), F32),
        ],
        out_shape=[
            shape((total, width), F32),
            shape((total, width + GROUP), F32),
            shape((count, STATE, width), F32),
        ],
        compiler_params=pltpu.CompilerParams(vmem_limit_bytes=VMEM_BYTES),
        name="scan_forward",
    )(proj, cw, hp, s0, e0)


def run_backward(pz, proj, y, filt, dn, rc, states, s0, cw, hp, table, gain, g0, e0, rows, places):
    total, (heads, width) = proj.shape[0], table.shape
    count = total // rows
    turn = lambda i: count - 1 - i
    block = lambda w: pl.BlockSpec((rows, w), lambda i: (turn(i), 0))
    shape = jax.ShapeDtypeStruct
    share = GROUP // places
    return pl.pallas_call(
        backward_kernel,
        grid=(count,),
        in_specs=[
            block(width),
            block(proj.shape[1]),
            block(width),
            block(width + GROUP),
            block(width),
            pl.BlockSpec((1, 8, rows), lambda i: (turn(i), 0, 0)),
            pl.BlockSpec((1, STATE, width), lambda i: (jnp.maximum(turn(i) - 1, 0), 0, 0)),
            pl.BlockSpec((1, STATE, width), lambda i: (turn(i), 0, 0)),
        ]
        + [whole(v.shape) for v in (s0, cw, hp, table, gain, g0, e0)],
        out_specs=[
            block(width),
            block(proj.shape[1]),
            pl.BlockSpec((places, rows, share), lambda i: (0, turn(i), 0)),
            whole((8, width)),
            whole((8, width + GROUP)),
            whole((8, heads)),
            whole((STATE, width)),
            whole((8, width + GROUP)),
        ],
        scratch_shapes=[
            pltpu.VMEM((STATE, width), F32),
            pltpu.VMEM((rows + 8, width + GROUP), F32),
            pltpu.VMEM((2 * rows, width), F32),
            pltpu.VMEM((rows, width), F32),
            pltpu.VMEM((rows, width), F32),
            pltpu.VMEM((8, width), F32),
        ],
        out_shape=[
            shape((total, width), BF16),
            shape(proj.shape, BF16),
            shape((places, total, share), F32),
            shape((8, width), F32),
            shape((8, width + GROUP), F32),
            shape((8, heads), F32),
            shape((STATE, width), F32),
            shape((8, width + GROUP), F32),
        ],
        compiler_params=pltpu.CompilerParams(vmem_limit_bytes=VMEM_BYTES),
        name="scan_backward",
    )(pz, proj, y, filt, dn, rc, states, states, s0, cw, hp, table, gain, g0, e0)


def bring(step, pieces, buffers, sems, own):
    for near, far, buffer, sem in zip(*pieces, buffers, sems):
        to, done = buffer.at[step % 2], sem.at[step % 2]

        @pl.when(own)
        def _():
            pltpu.make_async_copy(near[step], to, done).start()

        @pl.when(jnp.logical_not(own))
        def _():
            pltpu.make_async_copy(far[step], to, done).start()


def arrived(step, pieces, buffers, sems):
    for near, buffer, sem in zip(pieces[0], buffers, sems):
        pltpu.make_async_copy(near[step], buffer.at[step % 2], sem.at[step % 2]).wait()
    return [buffer.at[step % 2] for buffer in buffers]


def project_kernel(ids, normed, *refs, layer, n):
    near, far = [refs[0:n]], [refs[n : 2 * n]]
    out, buffer, sem = refs[2 * n :]
    pieces = (near, far)
    own = ids[1] == layer
    columns = out.shape[1]
    share = buffer.shape[2]
    bring(0, pieces, [buffer], [sem], own)
    for m in range(n):
        if m + 1 < n:
            bring(m + 1, pieces, [buffer], [sem], own)
        (w,) = arrived(m, pieces, [buffer], [sem])
        from_place = pl.multiple_of(jnp.bitwise_xor(ids[0], m) * share, share)
        a = normed[:, pl.ds(from_place, share)]
        for lo in range(0, columns, 256):
            here = slice(lo, min(lo + 256, columns))
            v = lax.dot_general(
                a, w[here, :], (((1,), (1,)), ((), ())), preferred_element_type=F32
            )
            out[:, here] = v if m == 0 else out[:, here] + v


def project(ids, normed, near, far, layer):
    n = len(near)
    columns, share = near[0].shape
    rows = normed.shape[0]
    vmem = pl.BlockSpec(memory_space=pltpu.VMEM)
    return pl.pallas_call(
        functools.partial(project_kernel, layer=layer, n=n),
        in_specs=[pl.BlockSpec(memory_space=pltpu.SMEM), vmem]
        + [pl.BlockSpec(memory_space=pl.ANY)] * (2 * n),
        out_specs=vmem,
        scratch_shapes=[
            pltpu.VMEM((2, columns, share), BF16),
            pltpu.SemaphoreType.DMA((2,)),
        ],
        out_shape=jax.ShapeDtypeStruct((rows, columns), F32),
        compiler_params=pltpu.CompilerParams(vmem_limit_bytes=VMEM_BYTES),
        cost_estimate=pl.CostEstimate(
            flops=2 * rows * columns * share * n,
            bytes_accessed=columns * share * n * 2 + rows * columns * 4,
            transcendentals=0,
        ),
        name="project",
    )(ids, normed, *near, *far)


def back_kernel(ids, dz, dx, *refs, layer, n):
    near = (refs[0:n], refs[n : 2 * n])
    far = (refs[2 * n : 3 * n], refs[3 * n : 4 * n])
    out, zbuf, xbuf, zsem, xsem = refs[4 * n :]
    pieces = (near, far)
    own = ids[1] == layer
    share = zbuf.shape[2]
    args = ([zbuf, xbuf], [zsem, xsem])
    bring(0, pieces, *args, own)
    for m in range(n):
        if m + 1 < n:
            bring(m + 1, pieces, *args, own)
        wz, wx = arrived(m, pieces, *args)
        for lo in range(0, share, 256):
            here = slice(lo, lo + 256)
            v = jnp.dot(dz[...], wz[:, here], preferred_element_type=F32) + jnp.dot(
                dx[...], wx[:, here], preferred_element_type=F32
            )
            at_lane = pl.multiple_of(jnp.bitwise_xor(ids[0], m) * share + lo, 256)
            out[:, pl.ds(at_lane, 256)] = v.astype(out.dtype)


def project_back(ids, dz, dx, near, far, layer, kind):
    n = len(near[0])
    share = near[0][0].shape[1]
    rows = dz.shape[0]
    columns = dz.shape[1] + dx.shape[1]
    vmem = pl.BlockSpec(memory_space=pltpu.VMEM)
    return pl.pallas_call(
        functools.partial(back_kernel, layer=layer, n=n),
        in_specs=[pl.BlockSpec(memory_space=pltpu.SMEM), vmem, vmem]
        + [pl.BlockSpec(memory_space=pl.ANY)] * (4 * n),
        out_specs=vmem,
        scratch_shapes=[
            pltpu.VMEM((2, dz.shape[1], share), BF16),
            pltpu.VMEM((2, dx.shape[1], share), BF16),
            pltpu.SemaphoreType.DMA((2,)),
            pltpu.SemaphoreType.DMA((2,)),
        ],
        out_shape=jax.ShapeDtypeStruct((rows, n * share), kind),
        compiler_params=pltpu.CompilerParams(vmem_limit_bytes=VMEM_BYTES),
        cost_estimate=pl.CostEstimate(
            flops=2 * rows * columns * share * n,
            bytes_accessed=columns * share * n * 2 + rows * n * share * 2,
            transcendentals=0,
        ),
        name="project_back",
    )(ids, dz, dx, *near[0], *near[1], *far[0], *far[1])


def place_kernel(ids, *refs, plan, count, rows_of_small):
    small = refs[count]
    out, eye, pieces, blocks, in_sem, out_sem = refs[-6:]
    core = ids[1]
    size, share = blocks.shape[1:]

    def fetch(k):
        for layer in range(2):

            @pl.when(core == layer)
            def _():
                src = refs[plan[k][layer]]
                pltpu.make_async_copy(
                    src.at[:, pl.ds(0, share)], pieces.at[k % 2], in_sem.at[k % 2]
                ).start()

    def send(step, first, count):
        return pltpu.make_async_copy(
            blocks.at[step % 2, pl.ds(0, count)],
            out.at[pl.ds(first, count)],
            out_sem.at[step % 2],
        )

    eye[...] = (
        lax.broadcasted_iota(jnp.int32, eye.shape, 0)
        == lax.broadcasted_iota(jnp.int32, eye.shape, 1)
    ).astype(BF16)
    fetch(0)
    sent = []
    for k, (_, _, side, firsts) in enumerate(plan):
        if k + 1 < len(plan):
            fetch(k + 1)
        pltpu.make_async_copy(pieces.at[k % 2], pieces.at[k % 2], in_sem.at[k % 2]).wait()
        shift = jnp.where(side == 0, core, 1 - core) * size
        for p, first in enumerate(firsts):
            step = len(sent)
            if step >= 2:
                sent[step - 2].wait()
            blocks[step % 2] = lax.dot_general(
                pieces[k % 2, p],
                eye[...],
                (((0,), (0,)), ((), ())),
                preferred_element_type=F32,
            )
            sent.append(send(step, pl.multiple_of(first + shift, 8), size))
            sent[-1].start()
    if rows_of_small:
        step = len(sent)
        sent[step - 2].wait()
        first, count = rows_of_small
        sent.append(
            pltpu.make_async_copy(small, out.at[pl.ds(first, count)], out_sem.at[step % 2])
        )
        sent[-1].start()
    sent[-2].wait()
    sent[-1].wait()


def place_in(ids, arrays, plan, small, rows_of_small, before, shape, size):
    places, share = arrays[0].shape[0], shape[1]
    any_space = pl.BlockSpec(memory_space=pl.ANY)
    return pl.pallas_call(
        functools.partial(
            place_kernel, plan=plan, count=len(arrays), rows_of_small=rows_of_small
        ),
        in_specs=[pl.BlockSpec(memory_space=pltpu.SMEM)]
        + [any_space] * len(arrays)
        + [pl.BlockSpec(memory_space=pltpu.VMEM)]
        + [any_space] * len(before),
        out_specs=any_space,
        scratch_shapes=[
            pltpu.VMEM((share, share), BF16),
            pltpu.VMEM((2, places, share, size), BF16),
            pltpu.VMEM((2, size, share), F32),
            pltpu.SemaphoreType.DMA((2,)),
            pltpu.SemaphoreType.DMA((2,)),
        ],
        out_shape=jax.ShapeDtypeStruct(shape, F32),
        input_output_aliases={len(arrays) + 2: 0} if before else {},
        compiler_params=pltpu.CompilerParams(vmem_limit_bytes=VMEM_BYTES),
        name="place_in",
    )(ids, *arrays, small, *before)


def combine_kernel(flags, *refs, adds):
    count = len(adds)
    for k, add in enumerate(adds):
        v, got, out = refs[2 * k], refs[2 * k + 1], refs[2 * count + k]
        if add:
            out[...] = (v[...].astype(F32) + got[...].astype(F32)).astype(BF16)
        else:
            out[...] = jnp.where(flags[k] == 1, got[...], v[...])


def combine(items, flags):
    steps = 8
    shapes = [v.shape for v, _, _ in items]
    flat = [(v.reshape(-1, v.shape[-1]), g.reshape(-1, g.shape[-1])) for v, g, _ in items]
    spec = lambda v: pl.BlockSpec((v.shape[0] // steps, v.shape[1]), lambda i: (i, 0))
    out = pl.pallas_call(
        functools.partial(combine_kernel, adds=tuple(add for _, _, add in items)),
        grid=(steps,),
        in_specs=[pl.BlockSpec(memory_space=pltpu.SMEM)] + [spec(v) for p in flat for v in p],
        out_specs=[spec(v) for v, _ in flat],
        out_shape=[jax.ShapeDtypeStruct(v.shape, BF16) for v, _ in flat],
        compiler_params=pltpu.CompilerParams(vmem_limit_bytes=VMEM_BYTES),
        name="combine",
    )(flags, *[v for p in flat for v in p])
    return [v.reshape(shape) for v, shape in zip(out, shapes)]


def swap_section(v):
    return lax.ppermute(v, "section", [(0, 1), (1, 0)])


def at(v, k):
    return lax.dynamic_index_in_dim(v, k, 0, False)


def exchange(v):
    return lax.all_to_all(v, "fsdp", 0, 0, tiled=True)


def to_all(v):
    n = lax.axis_size("fsdp")
    return exchange(jnp.broadcast_to(v[None], (n,) + v.shape))


def gather_rows(v):
    return to_all(v).reshape(-1, v.shape[-1])


def scatter_sum(partial):
    n = lax.axis_size("fsdp")
    got = exchange(partial.reshape(n, -1, partial.shape[-1]))
    return jnp.sum(got.astype(F32), axis=0)


def in_group(v):
    n, s = lax.axis_size("fsdp"), lax.axis_size("seq")
    groups = [[j * n + i for i in range(n)] for j in range(s // n)]
    return lax.all_to_all(v, "seq", 0, 0, axis_index_groups=groups, tiled=True)


def quarters(v):
    n = lax.axis_size("fsdp")
    return v.reshape(v.shape[0], n, -1).transpose(1, 0, 2)


def joined(v):
    return v.transpose(1, 0, 2).reshape(v.shape[1], -1)


def move_fsdp(v, m):
    n = lax.axis_size("fsdp")
    return lax.ppermute(v, "fsdp", [(k, k ^ m) for k in range(n)])


def move_seq(v, m):
    s = lax.axis_size("seq")
    return lax.ppermute(v, "seq", [(k, k ^ m) for k in range(s)])


class SeqSums:
    def __init__(self):
        s = lax.axis_size("seq")
        half = s // 2
        self.pairs = [[(j, j + 1), (s - 1 - j, s - 2 - j)] for j in range(half - 1)]
        self.pairs.append([(half - 1, half), (half, half - 1)])
        self.inward = half
        self.pairs += [[(j + 1, j), (s - 2 - j, s - 1 - j)] for j in reversed(range(half - 1))]
        self.values, self.phase, self.moving = [], [], []

    def add(self, value):
        self.values.append(value)
        self.phase.append(0)
        return len(self.values) - 1

    def begin(self):
        taken = set()
        for k, step in enumerate(self.phase):
            if step == len(self.pairs) or step in taken:
                continue
            taken.add(step)
            self.moving.append((k, lax.ppermute(self.values[k], "seq", self.pairs[step])))

    def end(self, work):
        place = lax.axis_index("seq")
        items, flags = [], []
        for k, got in self.moving:
            step = self.phase[k]
            items.append((self.values[k], got, step < self.inward))
            here = [place == to for _, to in self.pairs[step]]
            flags.append(functools.reduce(jnp.logical_or, here))
            self.phase[k] = step + 1
        moved = combine(items, jnp.stack(flags).astype(jnp.int32)) if items else []
        still = [k for k, p in enumerate(self.phase) if p == 0]
        work, moved, rest = lax.optimization_barrier(
            (work, moved, [self.values[k] for k in still])
        )
        for (k, _), v in zip(self.moving, moved):
            self.values[k] = v
        for k, v in zip(still, rest):
            self.values[k] = v
        self.moving = []
        return work

    def finish(self, chunks):
        while any(self.phase[k] < len(self.pairs) for k in chunks):
            self.begin()
            self.end(())


def relay(total, local, reverse):
    n, s = lax.axis_size("fsdp"), lax.axis_size("seq")
    segments = s // n
    place = lax.axis_index("seq") // n
    own = lax.axis_index("seq") % n
    totals = lax.all_gather(total, "seq")
    locals_ = lax.all_gather(local, "seq")
    state = jnp.zeros_like(local)
    order = range(segments - 1, -1, -1) if reverse else range(segments)
    for j in order:
        use = (j > place) if reverse else (j < place)
        t = lax.dynamic_index_in_dim(totals, j * n + own, 0, False)
        v = lax.dynamic_index_in_dim(locals_, j * n + own, 0, False)
        state = jnp.where(use, t * state + v, state)
    return state


def next_segment(v, step):
    n, s = lax.axis_size("fsdp"), lax.axis_size("seq")
    pairs = [(k, k + step * n) for k in range(s) if 0 <= k + step * n < s]
    return lax.ppermute(v, "seq", pairs)


def dot_rows(a, b):
    return lax.dot_general(a, b, (((0,), (0,)), ((), ())), preferred_element_type=F32)


def dot_cols(a, b):
    return lax.dot_general(a, b, (((1,), (1,)), ((), ())), preferred_element_type=F32)


def normalised(h, gain):
    return h * lax.rsqrt(jnp.mean(h * h, axis=-1, keepdims=True) + EPS) * gain


def per_device(
    inputs,
    cotangent,
    lengths,
    gain_in,
    w_in,
    conv_w,
    conv_b,
    dt_bias,
    a_log,
    d_skip,
    gain_out,
    w_out,
):
    n = lax.axis_size("fsdp")
    nz = lax.axis_size("seq")
    segments = nz // n
    c = lax.axis_index("section")
    f = lax.axis_index("fsdp")
    place = lax.axis_index("seq")
    upper = c == 0
    rows = inputs.shape[2]
    width = INNER // n
    heads = HEADS // n
    share = D // n
    half = share // 2
    group = GROUP // n
    ids = jnp.stack([f, c]).astype(jnp.int32)
    tie = lax.optimization_barrier

    def pick(a, b):
        return jnp.where(upper, a, b)

    w = w_in[0].T

    def cut(first, size):
        return lax.dynamic_slice_in_dim(w, first, size, 0)

    def piece_z(m):
        return cut((f ^ m) * width, width)

    def piece_x(m):
        return jnp.concatenate(
            [
                cut(INNER + (f ^ m) * width, width),
                w[2 * INNER : 2 * INNER + GROUP],
                cut(2 * INNER + GROUP + (f ^ m) * heads, heads),
            ]
        )

    def fetch(pieces, layer):
        pairs = lambda m: [(layer * n + i, layer * n + (i ^ m)) for i in range(n)]
        near = [
            v if m == 0 else lax.ppermute(v, ("section", "fsdp"), pairs(m))
            for m, v in enumerate(pieces)
        ]
        return near, [lax.ppermute(v, "section", [(layer, 1 - layer)]) for v in near]

    def whole_slot(v):
        return joined(to_all(v.reshape(n * rows, share)))

    pack = jnp.concatenate(
        [
            gain_in[0],
            dt_bias[0],
            a_log[0],
            d_skip[0],
            gain_out[0],
            conv_w[0].reshape(-1),
            conv_b[0],
        ]
    )
    mine, part_h0, pieces_x = tie(
        (to_all(pack), exchange(quarters(at(inputs, c)[0])), [piece_x(m) for m in range(n)])
    )
    near_x0, far_x0 = fetch(pieces_x, 0)
    part_h0 = in_group(part_h0)
    near_x0, part_h0 = tie((near_x0, part_h0))
    far_x0 = [lax.ppermute(v, "section", [(0, 1)]) for v in near_x0]
    pieces_z, part_h0 = tie(([piece_z(m) for m in range(n)], part_h0))
    all_h0 = whole_slot(part_h0)
    near_z0, far_z0 = fetch(pieces_z, 0)

    theirs = swap_section(mine)
    small = []
    for full in (pick(mine, theirs), pick(theirs, mine)):
        full = full.astype(F32)
        used = 0

        def take(size):
            nonlocal used
            used += size
            return full[:, used - size : used]

        gain = take(share).reshape(1, D)
        hp = [at(take(heads), f)[None] for _ in range(3)]
        hp = jnp.concatenate([hp[0], -jnp.exp(hp[1]), hp[2], jnp.zeros((5, heads), F32)])
        gout = at(take(width), f)[None]
        per = CHANNELS // n
        taps = take(KERNEL * per).reshape(n, KERNEL, per).transpose(1, 0, 2)
        bias = take(per).reshape(1, CHANNELS)
        table = jnp.concatenate(
            [taps.reshape(KERNEL, CHANNELS), bias, jnp.zeros((3, CHANNELS), F32)]
        )
        cw = jnp.concatenate(
            [lax.dynamic_slice_in_dim(table, f * width, width, 1), table[:, INNER:]], axis=1
        )
        small.append((gain, cw, hp, gout))

    win = [(near_z0, far_z0, near_x0, far_x0), None]
    expand = (
        jnp.arange(heads)[:, None] == jnp.arange(width)[None, :] // HEAD_DIM
    ).astype(BF16)
    zero_state = jnp.zeros((STATE, width), F32)
    zero_edge = jnp.zeros((8, width + GROUP), F32)

    def project_x(normed, layer):
        return project(ids, normed, win[layer][2], win[layer][3], layer)

    def project_z(normed, layer):
        return project(ids, normed, win[layer][0], win[layer][1], layer)

    def decay_of(px, hp):
        decay = jax.nn.softplus(px[:, width + GROUP :] + hp[0:1]) * hp[1:2]
        return jnp.repeat(jnp.exp(jnp.sum(decay, axis=0)), HEAD_DIM)[None, :]

    def scan(px, layer):
        _, cw, hp, _ = small[layer]
        args = (px, cw, hp)
        if segments == 1:
            return run_forward(*args, zero_state, zero_edge, rows), zero_state
        edge = next_segment(px[-8:, : width + GROUP], 1)
        local = run_forward(*args, zero_state, edge, rows)[2][-1]
        state = relay(decay_of(px, hp), local, False)
        return run_forward(*args, state, edge, rows), state

    def unscan(pz, px, fwd, dn, rc, layer):
        (y, filt, states), state = fwd
        _, cw, hp, gout = small[layer]
        args = (pz, px, y, filt, dn, rc, states, state, cw, hp, expand, gout)
        if segments == 1:
            return run_backward(*args, zero_state, zero_edge, rows, n)[:6]
        local = run_backward(*args, zero_state, zero_edge, rows, n)[6]
        grad = relay(decay_of(px, hp), local, True)
        edge = next_segment(run_backward(*args, grad, zero_edge, rows, n)[7], -1)
        return run_backward(*args, grad, edge, rows, n)[:6]

    def gate(pz, y):
        return y * jax.nn.silu(pz)

    def gated(pz, y, r, layer):
        return (gate(pz, y) * r[:, None] * small[layer][3]).astype(BF16)

    def sum_of_shares(v):
        return jnp.sum(to_all(v), axis=0)

    normed_in0 = normalised(all_h0.astype(F32), small[0][0]).astype(BF16)
    px0 = project_x(normed_in0, 0)
    px0, pieces_x1, pieces_z1, own_ct, wo_mine, own_len = tie(
        (px0, pieces_x, pieces_z, at(cotangent, c)[0], w_out[0], at(lengths, c))
    )
    near_x1, far_x1 = fetch(pieces_x1, 1)
    wo_other = swap_section(wo_mine)
    wo = (pick(wo_mine, wo_other), pick(wo_other, wo_mine))
    slot_pairs = [
        ((j * n + i) * n + k, (j * n + k) * n + i)
        for j in range(segments)
        for i in range(n)
        for k in range(n)
    ]
    length = lax.ppermute(own_len, ("seq", "fsdp"), slot_pairs)
    first_row = (place // n) * n * rows
    all_valid = first_row + jnp.arange(n * rows, dtype=jnp.int32) < length[0]
    all_valid = all_valid.astype(F32)[:, None]
    own_rows = lambda v: lax.dynamic_slice_in_dim(v, f * rows, rows, 0)
    valid = own_rows(all_valid)
    h0 = own_rows(all_h0)
    fwd0, near_z0 = tie((scan(px0, 0), near_z0))
    far_z0 = [lax.ppermute(v, "section", [(0, 1)]) for v in near_z0]
    win[0] = (near_z0, far_z0, near_x0, far_x0)
    pz0 = project_z(normed_in0, 0)
    g0 = gate(pz0, fwd0[0][0])
    stat0, near_x1, pieces_z1 = tie((jnp.sum(g0 * g0, axis=1), near_x1, pieces_z1))
    near_z1, far_z1 = fetch(pieces_z1, 1)
    stat0 = sum_of_shares(stat0.reshape(n, rows)).reshape(-1)
    r0 = lax.rsqrt(stat0 / INNER + EPS)
    normed0 = gated(pz0, fwd0[0][0], r0, 0)
    part_ct = in_group(exchange(quarters(own_ct)))
    normed0, wo, part_ct = tie((normed0, wo, part_ct))
    far_x1 = [lax.ppermute(v, "section", [(1, 0)]) for v in near_x1]
    mixed0 = scatter_sum(jnp.dot(normed0, wo[0], preferred_element_type=F32))
    out0 = valid * (h0.astype(F32) + mixed0)
    h1 = out0.astype(BF16)

    normed_in1 = gather_rows(normalised(h1.astype(F32), small[1][0]).astype(BF16))
    normed_in1, far_x1, part_ct, near_z1 = tie((normed_in1, far_x1, part_ct, near_z1))
    far_z1 = [lax.ppermute(v, "section", [(1, 0)]) for v in near_z1]
    win[1] = (near_z1, far_z1, near_x1, far_x1)
    px1 = project_x(normed_in1, 1)
    all_ct = whole_slot(part_ct)
    fwd1 = scan(px1, 1)
    fwd1, all_ct = tie((fwd1, all_ct))
    dout1 = own_rows(all_ct).astype(F32)
    dmixed1 = (all_valid * all_ct.astype(F32)).astype(BF16)
    dn1 = dot_cols(dmixed1, wo[1])
    pz1 = project_z(normed_in1, 1)
    g1 = gate(pz1, fwd1[0][0])
    stat1 = sum_of_shares(
        jnp.stack(
            [
                jnp.sum(g1 * g1, axis=1).reshape(n, rows),
                jnp.sum(g1 * dn1 * small[1][3], axis=1).reshape(n, rows),
            ]
        )
    ).reshape(2, -1)
    r1 = lax.rsqrt(stat1[0] / INNER + EPS)
    normed1 = gated(pz1, fwd1[0][0], r1, 1)

    part_width = width // 2

    def cut_half(v, k):
        size = v.shape[1] // 2
        return lax.dynamic_slice_in_dim(v, k * size, size, 1)

    def narrow_of(parts, k):
        return jnp.concatenate([cut_half(v, k) for v in parts], axis=1)

    def away_in(normed_in, part, narrow=()):
        away = [dot_rows(normed_in, cut_half(part, 1 - c)).astype(BF16)]
        if narrow:
            away.append(dot_rows(narrow_of(narrow, 1 - c), normed_in).astype(BF16))
        return [swap_section(v) for v in away]

    def own_in_piece(normed_in, part, away, narrow=()):
        total = dot_rows(normed_in, cut_half(part, c)) + away[0].astype(F32)
        result = total.astype(BF16).reshape(n, share, -1)
        if narrow:
            total = (dot_rows(narrow_of(narrow, c), normed_in) + away[1].astype(F32)).astype(BF16)
            fill = jnp.zeros((-total.shape[0] % 64, D), BF16)
            rest = jnp.concatenate([total, fill]).reshape(-1, n, share).transpose(1, 0, 2)
            result = jnp.concatenate([result, rest], axis=1)
        return result

    def away_out(normed, dmixed):
        return swap_section(dot_rows(cut_half(normed, 1 - c), dmixed).astype(BF16))

    def own_out_piece(normed, dmixed, away):
        return (dot_rows(cut_half(normed, c), dmixed) + away.astype(F32)).astype(BF16)

    def with_group(dxs, dbc):
        total = jnp.sum(exchange(dbc), axis=0).astype(BF16)
        column = jnp.arange(GROUP)[None, :] // group
        own = jnp.where(column == f, jnp.concatenate([total] * n, axis=1), 0)
        full = lax.dynamic_update_slice(dxs, own.astype(BF16), (0, width))
        return full, (dxs[:, :width], [total, dxs[:, width + GROUP :]])

    def back_in(dz, full, layer, kind):
        near_z, far_z, near_x, far_x = win[layer]
        return project_back(ids, dz, full, (near_z, near_x), (far_z, far_x), layer, kind)

    def back_norm(dout, dnormed_in, h, gain):
        h = h.astype(F32)
        r = lax.rsqrt(jnp.mean(h * h, axis=-1, keepdims=True) + EPS)
        u = dnormed_in * gain
        mean = jnp.mean(u * h, axis=-1, keepdims=True)
        dgain = jnp.sum(dnormed_in * h * r, axis=0)
        return valid * dout + r * u - h * (r * r * r) * mean, dgain

    def scales(r, coef):
        top = jnp.stack([r.reshape(n, rows), coef.reshape(n, rows)], axis=1)
        return jnp.concatenate([top, jnp.zeros((n, 6, rows), F32)], axis=1)

    def packed(dgin, d, out, mixed):
        dgain, dconv, dhp = d[3][0], d[4][:5], d[5][:3]
        put = lambda v, size, at_lane: lax.dynamic_update_slice(
            jnp.zeros(v.shape[:-1] + (size,), F32), v, (0,) * (v.ndim - 1) + (at_lane,)
        )
        conv = put(dconv[:, :width], CHANNELS, f * width)
        conv = conv.at[:, INNER:].set(dconv[:, width:])
        totals = jnp.stack(
            [jnp.sum(out * out), jnp.sum((valid * mixed) ** 2), jnp.sum(valid)]
        )
        return jnp.concatenate(
            [
                dgin,
                conv.reshape(-1),
                put(dhp, HEADS, f * heads).reshape(-1),
                put(dgain, INNER, f * width),
                totals,
            ]
        )

    def hand_over(v, layer):
        return lax.ppermute(v, "section", [(1 - layer, layer)])

    sums = SeqSums()
    rc1 = scales(r1, (r1 * r1 * r1 / INNER) * stat1[1])
    away = away_out(normed1, dmixed1)
    o1 = sums.add(own_out_piece(normed1, dmixed1, away))
    rc1, normed1, dn1 = sums.end((rc1, normed1, dn1))

    sums.begin()
    d1 = unscan(pz1, px1, fwd1, dn1, rc1, 1)
    mixed1 = scatter_sum(jnp.dot(normed1, wo[1], preferred_element_type=F32).astype(BF16))
    d1, mixed1 = sums.end((d1, mixed1))

    sums.begin()
    away = away_in(normed_in1, d1[0])
    full1, xs1 = with_group(d1[1], d1[2])
    back1 = back_in(d1[0], full1, 1, F32)
    gz = own_in_piece(normed_in1, d1[0], away)
    back1, xs1, full1, gz = sums.end((back1, xs1, full1, gz))
    z1 = sums.add(gz)

    sums.begin()
    dnin1 = scatter_sum(back1)
    away = away_in(normed_in1, *xs1)
    gx = own_in_piece(normed_in1, xs1[0], away, xs1[1])
    dnin1, gx = sums.end((dnin1, gx))
    x1 = sums.add(gx)

    sums.begin()
    grad1, dgin1 = back_norm(dout1, dnin1, h1, small[1][0])
    dout0 = grad1.astype(BF16).astype(F32)
    dmixed0_own = (valid * dout0).astype(BF16)
    dmixed0 = gather_rows(dmixed0_own)
    along0 = to_all(jnp.sum(dmixed0_own.astype(F32) * mixed0, axis=-1)).reshape(-1)
    rc0 = scales(r0, (r0 * r0 / INNER) * along0)
    out1 = valid * (h1.astype(F32) + mixed1)
    grad1, dgin1, dmixed0, rc0, out1 = sums.end((grad1, dgin1, dmixed0, rc0, out1))

    sums.begin()
    back_h = exchange(quarters(jnp.concatenate([h1, out1.astype(BF16)])))
    dn0 = dot_cols(dmixed0, wo[0])
    d0 = unscan(pz0, px0, fwd0, dn0, rc0, 0)
    go = own_out_piece(normed0, dmixed0, away_out(normed0, dmixed0))
    d0, go, back_h = sums.end((d0, go, back_h))
    o0 = sums.add(go)

    sums.begin()
    back_h = in_group(back_h)
    away = away_in(normed_in0, d0[0])
    full0, xs0 = with_group(d0[1], d0[2])
    gz = own_in_piece(normed_in0, d0[0], away)
    away = away_in(normed_in0, *xs0)
    gx = own_in_piece(normed_in0, xs0[0], away, xs0[1])
    full0, gz, gx, back_h = sums.end((full0, gz, gx, back_h))
    z0 = sums.add(gz)

    sums.begin()
    gx = exchange(gx)
    back0 = back_in(d0[0], full0, 0, BF16)
    back_h = joined(exchange(back_h))
    gx, back0, back_h = sums.end((gx, back0, back_h))
    x0 = sums.add(gx)

    def hand_over(v, layer):
        return lax.ppermute(v, "section", [(1 - layer, layer)])

    sums.finish([o1, z1])
    sums.begin()
    dnin0 = scatter_sum(back0)
    own_z1 = exchange(sums.values[z1])
    own_o1 = sums.values[o1]
    away_o1 = hand_over(own_o1, 1)
    dnin0, own_z1, own_o1, away_o1 = sums.end((dnin0, own_z1, own_o1, away_o1))

    sums.finish([x1, o0])
    sums.begin()
    own_x1 = exchange(sums.values[x1])
    away_z1 = hand_over(own_z1, 1)
    own_o0 = sums.values[o0]
    away_o0 = hand_over(own_o0, 0)
    grad0, dgin0 = back_norm(dout0, dnin0, h0, small[0][0])
    back_g = exchange(quarters(jnp.concatenate([grad0.astype(BF16), grad1.astype(BF16)])))
    p = jnp.stack([packed(dgin0, d0, out0, mixed0), packed(dgin1, d1, out1, mixed1)])
    p = p + swap_section(p)
    p, back_g, own_x1, own_z1, away_z1, own_o0, away_o0 = sums.end(
        (p, back_g, own_x1, own_z1, away_z1, own_o0, away_o0)
    )

    sums.finish([z0])
    sums.begin()
    back_g = in_group(back_g)
    own_z0 = exchange(sums.values[z0])
    away_x1 = hand_over(own_x1, 1)
    m = 1
    while m < n:
        p = p + move_fsdp(p, m)
        m *= 2
    p, back_g, own_z0, own_x1, away_x1 = sums.end((p, back_g, own_z0, own_x1, away_x1))
    sums.finish([x0])
    away_z0 = hand_over(own_z0, 0)
    own_x0 = sums.values[x0]
    away_x0 = hand_over(own_x0, 0)
    back_g = joined(exchange(back_g))
    m = 1
    while m < nz:
        p = p + move_seq(p, m)
        m *= 2
    p = pick(p[0], p[1])
    back = jnp.concatenate([back_h, back_g])

    used = 0

    def part(size):
        nonlocal used
        used += size
        return p[used - size : used]

    mine_of = lambda v, size: lax.dynamic_slice_in_dim(v, f * size, size, v.ndim - 1)
    o_gain_in = mine_of(part(D), share)
    o_conv = mine_of(part(5 * CHANNELS).reshape(5, CHANNELS), CHANNELS // n)
    o_heads = mine_of(part(3 * HEADS).reshape(3, HEADS), heads)
    o_gain_out = mine_of(part(INNER), width)
    totals = part(3)
    act_rms = jnp.sqrt(totals[:2] / (totals[2] * D))[None]

    held = [
        [(own_z0, own_x0, own_o0), (own_z1, own_x1, own_o1)],
        [(away_z0, away_x0, away_o0), (away_z1, away_x1, away_o1)],
    ]

    def both_halves(a, b):
        return jnp.stack([pick(a, b), pick(b, a)], axis=1)

    rows_of = GROUP // n // 2, HEADS // n // 2
    narrow = [pick(side[0][1], side[1][1])[:, share : share + sum(rows_of)] for side in held]
    narrow = both_halves(*[v.astype(F32) for v in narrow])
    small_in = jnp.concatenate(
        [
            narrow[:, :, : rows_of[0]].reshape(GROUP, share),
            narrow[:, :, rows_of[0] :].reshape(HEADS, share),
        ]
    )
    g_w_in = []
    shape_in = (2 * INNER + GROUP + HEADS, share)
    for k, rows_of_small in ((0, None), (1, (2 * INNER, GROUP + HEADS))):
        arrays, plan = [], []
        for s in range(2):
            arrays += [held[s][0][k], held[s][1][k]]
            firsts = tuple(k * INNER + q * width for q in range(n))
            plan.append((len(arrays) - 2, len(arrays) - 1, s, firsts))
        g_w_in = [
            place_in(
                ids, arrays, tuple(plan), small_in, rows_of_small, g_w_in, shape_in, part_width
            )
        ]
    halves_out = [pick(side[0][2], side[1][2]) for side in held]
    g_w_out = jnp.concatenate([pick(*halves_out), pick(*halves_out[::-1])]).astype(F32)

    back = back.reshape(2, 2, rows, D)
    kept_back = pick(back[:, 0], back[:, 1])
    other_back = swap_section(pick(back[:, 1], back[:, 0]))
    both_back = jnp.stack(
        [pick(kept_back, other_back), pick(other_back, kept_back)], axis=1
    )
    return (
        both_back[0][None, :, None],
        both_back[1].astype(F32)[None, :, None],
        o_gain_in[None],
        g_w_in[0].T[None],
        o_conv[None, :4],
        o_conv[None, 4],
        o_heads[None, 0],
        o_heads[None, 1],
        o_heads[None, 2],
        o_gain_out[None],
        g_w_out[None],
        act_rms,
    )


def solution(mesh):
    in_specs = (
        P(None, "fsdp", "seq", None),
        P(None, "fsdp", "seq", None),
        P(None, "fsdp"),
        P("section", "fsdp"),
        P("section", "fsdp", None),
        P("section", None, "fsdp"),
        P("section", "fsdp"),
        P("section", "fsdp"),
        P("section", "fsdp"),
        P("section", "fsdp"),
        P("section", "fsdp"),
        P("section", "fsdp", None),
    )
    out_specs = (
        P("section", None, "fsdp", "seq", None),
        P("section", None, "fsdp", "seq", None),
        P("section", "fsdp"),
        P("section", "fsdp", None),
        P("section", None, "fsdp"),
        P("section", "fsdp"),
        P("section", "fsdp"),
        P("section", "fsdp"),
        P("section", "fsdp"),
        P("section", "fsdp"),
        P("section", "fsdp", None),
        P("section", None),
    )
    return jax.shard_map(
        per_device, mesh=mesh, in_specs=in_specs, out_specs=out_specs, check_vma=False
    )
```

```python
import functools

import jax
import jax.numpy as jnp
from jax import lax
from jax.experimental import pallas as pl
from jax.experimental.pallas import tpu as pltpu
from jax.sharding import PartitionSpec as P

D = 2048
INNER = 4096
HEADS = 64
HEAD_DIM = 64
STATE = 128
KERNEL = 4
GROUP = 2 * STATE
CHANNELS = INNER + GROUP
LANES = 128
EPS = 1e-05
F32 = jnp.float32
BF16 = jnp.bfloat16
VMEM_BYTES = 48 * 1024 * 1024


def split(v):
    hi = v.astype(BF16)
    return hi, (v - hi.astype(F32)).astype(BF16)


def dot32(a, b, ca, cb):
    (ah, al), (bh, bl) = (v if isinstance(v, tuple) else split(v) for v in (a, b))
    one = lambda p, q: lax.dot_general(
        p, q, (((ca,), (cb,)), ((), ())), preferred_element_type=F32
    )
    return one(ah, bh) + (one(ah, bl) + one(al, bh))


def step_sizes(raw, hp, rows):
    shifted = raw + hp[0:1, :]
    dt = jnp.maximum(shifted, 0.0) + jnp.log1p(jnp.exp(-jnp.abs(shifted)))
    decay = dt * hp[1:2, :]
    row = lax.broadcasted_iota(jnp.int32, (rows, rows), 0)
    col = lax.broadcasted_iota(jnp.int32, (rows, rows), 1)
    lower = (row >= col).astype(F32)
    cum = dot32(lower, decay, 1, 0)
    cum_t = dot32(decay, lower, 0, 1)
    return shifted, dt, cum, cum_t, row, col, lower


def pair_lanes(v, j, first):
    return jnp.where(first, v[:, 2 * j : 2 * j + 1], v[:, 2 * j + 1 : 2 * j + 2])


def head_sums(v, table):
    hi, low = split(v)
    one = lambda p: lax.dot_general(
        p, table, (((1,), (1,)), ((), ())), preferred_element_type=F32
    )
    return one(hi) + one(low)


def forward_kernel(proj, cw, hp, s0, e0, y_ref, filt_ref, st_ref, state, xp, xw_s, last_s):
    i = pl.program_id(0)
    rows, width = y_ref.shape

    @pl.when(i == 0)
    def _():
        state[...] = s0[...]
        xp[0:8, :] = e0[...]

    xp[8 : 8 + rows, :] = proj[:, : width + GROUP]

    def conv_tile(lo):
        acc = cw[4:5, lo : lo + LANES]
        for k in range(KERNEL):
            acc = acc + cw[k : k + 1, lo : lo + LANES] * xp[5 + k : 5 + k + rows, lo : lo + LANES]
        filt_ref[:, lo : lo + LANES] = acc
        return acc * jax.nn.sigmoid(acc)

    b_c = conv_tile(width)
    c_c = conv_tile(width + STATE)
    _, dt, cum, cum_t, row, col, _ = step_sizes(proj[:, width + GROUP :], hp, rows)
    last = cum[rows - 1 : rows, :]
    ecum = jnp.exp(cum)
    weight = jnp.exp(last - cum) * dt
    elast = jnp.exp(last)
    b_c, c_c = split(b_c), split(c_c)
    carried = dot32(c_c, state[...], 1, 0)
    scores = dot32(c_c, b_c, 1, 1)
    causal = row >= col
    lane = lax.broadcasted_iota(jnp.int32, (rows, LANES), 1)
    first = lane < HEAD_DIM
    for j in range(width // LANES):
        lo = j * LANES
        here = slice(lo, lo + LANES)
        x = conv_tile(lo)
        xd = x * pair_lanes(dt, j, first)
        m = []
        for h in (2 * j, 2 * j + 1):
            gap = cum[:, h : h + 1] - cum_t[h : h + 1, :]
            m.append(jnp.exp(jnp.where(causal, gap, -1e30)) * scores)
        xd2 = jnp.concatenate([jnp.where(first, xd, 0.0), jnp.where(first, 0.0, xd)])
        y = (
            dot32(jnp.concatenate(m, axis=1), xd2, 1, 0)
            + carried[:, here] * pair_lanes(ecum, j, first)
            + pair_lanes(hp[2:3, :], j, first[0:1]) * x
        )
        y_ref[:, here] = y
        xw_s[:, here] = x * pair_lanes(weight, j, first)
        last_s[0:1, here] = pair_lanes(elast, j, first[0:1])
    state[...] = state[...] * last_s[0:1, :] + dot32(b_c, xw_s[...], 0, 0)
    st_ref[0] = state[...]
    xp[0:8, :] = xp[rows : rows + 8, :]


def backward_kernel(
    pz,
    proj,
    y_ref,
    filt,
    dn,
    rc,
    st_before,
    st_out,
    s0,
    cw,
    hp,
    table,
    gain,
    g0,
    e0,
    dz_ref,
    dproj,
    dbc_ref,
    dgain_ref,
    dconv_ref,
    dhp_ref,
    gfin_ref,
    efin_ref,
    grad,
    dfp,
    both,
    xw_s,
    dyc_s,
    rowv,
):
    i = pl.program_id(0)
    rows, width = y_ref.shape
    heads = hp.shape[1]

    @pl.when(i == 0)
    def _():
        grad[...] = g0[...]
        dfp[rows : rows + 8, :] = e0[...]
        dgain_ref[...] = jnp.zeros_like(dgain_ref)
        dconv_ref[...] = jnp.zeros_like(dconv_ref)
        dhp_ref[...] = jnp.zeros_like(dhp_ref)

    def silu_pair(v):
        s = jax.nn.sigmoid(v)
        a = v * s
        return a, s * (1.0 + v - a)

    b_c, b_d = silu_pair(filt[:, width : width + STATE])
    c_c, c_d = silu_pair(filt[:, width + STATE :])
    shifted, dt, cum, cum_t, row, col, lower = step_sizes(proj[:, width + GROUP :], hp, rows)
    last = cum[rows - 1 : rows, :]
    tail = jnp.exp(last - cum)
    ecum = jnp.exp(cum)
    elast = jnp.exp(last)
    b_c, c_c = split(b_c), split(c_c)
    grad_p = split(grad[...])
    k_all = dot32(b_c, grad_p, 1, 0)
    scores_t = dot32(b_c, c_c, 1, 1)
    causal_t = row <= col
    lane = lax.broadcasted_iota(jnp.int32, (rows, LANES), 1)
    first = lane < HEAD_DIM
    dcb_t = jnp.zeros((rows, rows), F32)
    rc_t = dot32((row == col).astype(F32), rc[0], 1, 1)
    r = rc_t[:, 0:1]
    coef = rc_t[:, 1:2]
    rowv[0:1, :] = jnp.sum(grad[...] * st_out[0], axis=0, keepdims=True)
    for j in range(width // LANES):
        lo = j * LANES
        here = slice(lo, lo + LANES)
        z = pz[:, here]
        y = y_ref[:, here]
        sz, dsz = silu_pair(z)
        g = y * sz
        dnt = dn[:, here]
        dg = dnt * gain[0:1, here] * r - g * coef
        dgain_ref[0:1, here] += jnp.sum(dnt * g * r, axis=0, keepdims=True)
        dy = dg * sz
        dz_ref[:, here] = (dg * y * dsz).astype(BF16)
        x, xder = silu_pair(filt[:, here])
        dt_e = pair_lanes(dt, j, first)
        tail_e = pair_lanes(tail, j, first)
        xd = x * dt_e
        dy2 = split(jnp.concatenate([jnp.where(first, dy, 0.0), jnp.where(first, 0.0, dy)]))
        decays = []
        for h in (2 * j, 2 * j + 1):
            gap = cum_t[h : h + 1, :] - cum[:, h : h + 1]
            decays.append(jnp.exp(jnp.where(causal_t, gap, -1e30)))
        m = jnp.concatenate([d * scores_t for d in decays], axis=1)
        dm = dot32(xd, dy2, 1, 1)
        dcb_t = dcb_t + (decays[0] * dm[:, :rows] + decays[1] * dm[:, rows:])
        v = dot32(m, dy2, 1, 0) + k_all[:, here] * tail_e
        skip = pair_lanes(hp[2:3, :], j, first[0:1])
        dx = dt_e * v + skip * dy
        both[0:rows, here] = x * v
        both[rows : 2 * rows, here] = dy * (y - skip * x)
        rowv[1:2, here] = jnp.sum(dy * x, axis=0, keepdims=True)
        rowv[2:3, here] = pair_lanes(elast, j, first[0:1])
        xw_s[:, here] = xd * tail_e
        dyc_s[:, here] = dy * pair_lanes(ecum, j, first)
        dfp[0:rows, here] = dx * xder
    dcb_t = split(dcb_t)
    dyc = split(dyc_s[...])
    st_in = jnp.where(i == pl.num_programs(0) - 1, s0[...], st_before[0])
    dc = dot32(dcb_t, b_c, 0, 0) + dot32(dyc, st_in, 1, 1)
    db = dot32(dcb_t, c_c, 1, 0) + dot32(xw_s[...], grad_p, 1, 1)
    dfp[0:rows, width : width + STATE] = db * b_d
    dfp[0:rows, width + STATE :] = dc * c_d
    grad[...] = grad[...] * rowv[2:3, :] + dot32(c_c, dyc, 0, 0)
    gfin_ref[...] = grad[...]

    sums = head_sums(both[...], table[...])
    rsums = head_sums(rowv[...], table[...])
    ddt_x = sums[0:rows]
    dcum = sums[rows : 2 * rows] - dt * ddt_x
    upto = lax.broadcasted_iota(jnp.int32, (rows, heads), 0)
    dcum = dcum + jnp.where(upto == rows - 1, rsums[0:1, :], 0.0)
    ddecay = dot32(lower, dcum, 0, 0)
    ddt = ddt_x + hp[1:2, :] * ddecay
    draw = ddt * jax.nn.sigmoid(shifted)
    dproj[:, width + GROUP :] = draw.astype(BF16)
    dhp_ref[0:1, :] += jnp.sum(draw, axis=0, keepdims=True)
    dhp_ref[1:2, :] += jnp.sum(ddecay * dt, axis=0, keepdims=True) * hp[1:2, :]
    dhp_ref[2:3, :] += rsums[1:2, :]

    for lo in range(0, width + GROUP, LANES):
        here = slice(lo, lo + LANES)
        src = proj[:, here]
        total = jnp.zeros((rows, LANES), F32)
        for k in range(KERNEL):
            shift = KERNEL - 1 - k
            moved = dfp[shift : shift + rows, here]
            total = total + cw[k : k + 1, here] * moved
            dconv_ref[k : k + 1, here] += jnp.sum(src * moved, axis=0, keepdims=True)
        dconv_ref[4:5, here] += jnp.sum(dfp[0:rows, here], axis=0, keepdims=True)
        if lo < width:
            dproj[:, here] = total.astype(BF16)
        else:
            dproj[:, here] = jnp.zeros((rows, LANES), BF16)
            share = dbc_ref.shape[2]
            for k in range(LANES // share):
                dbc_ref[(lo - width) // share + k] = total[:, k * share : (k + 1) * share]
    dfp[rows : rows + 8, :] = dfp[0:8, :]
    efin_ref[...] = dfp[0:8, :]


def whole(shape):
    return pl.BlockSpec(shape, lambda i: (0,) * len(shape))


def run_forward(proj, cw, hp, s0, e0, rows):
    total, width = proj.shape[0], s0.shape[1]
    count = total // rows
    block = lambda w: pl.BlockSpec((rows, w), lambda i: (i, 0))
    shape = jax.ShapeDtypeStruct
    return pl.pallas_call(
        forward_kernel,
        grid=(count,),
        in_specs=[block(proj.shape[1])] + [whole(v.shape) for v in (cw, hp, s0, e0)],
        out_specs=[
            block(width),
            block(width + GROUP),
            pl.BlockSpec((1, STATE, width), lambda i: (i, 0, 0)),
        ],
        scratch_shapes=[
            pltpu.VMEM((STATE, width), F32),
            pltpu.VMEM((rows + 8, width + GROUP), F32),
            pltpu.VMEM((rows, width), F32),
            pltpu.VMEM((8, width), F32),
        ],
        out_shape=[
            shape((total, width), F32),
            shape((total, width + GROUP), F32),
            shape((count, STATE, width), F32),
        ],
        compiler_params=pltpu.CompilerParams(vmem_limit_bytes=VMEM_BYTES),
        name="scan_forward",
    )(proj, cw, hp, s0, e0)


def run_backward(pz, proj, y, filt, dn, rc, states, s0, cw, hp, table, gain, g0, e0, rows, places):
    total, (heads, width) = proj.shape[0], table.shape
    count = total // rows
    turn = lambda i: count - 1 - i
    block = lambda w: pl.BlockSpec((rows, w), lambda i: (turn(i), 0))
    shape = jax.ShapeDtypeStruct
    share = GROUP // places
    return pl.pallas_call(
        backward_kernel,
        grid=(count,),
        in_specs=[
            block(width),
            block(proj.shape[1]),
            block(width),
            block(width + GROUP),
            block(width),
            pl.BlockSpec((1, 8, rows), lambda i: (turn(i), 0, 0)),
            pl.BlockSpec((1, STATE, width), lambda i: (jnp.maximum(turn(i) - 1, 0), 0, 0)),
            pl.BlockSpec((1, STATE, width), lambda i: (turn(i), 0, 0)),
        ]
        + [whole(v.shape) for v in (s0, cw, hp, table, gain, g0, e0)],
        out_specs=[
            block(width),
            block(proj.shape[1]),
            pl.BlockSpec((places, rows, share), lambda i: (0, turn(i), 0)),
            whole((8, width)),
            whole((8, width + GROUP)),
            whole((8, heads)),
            whole((STATE, width)),
            whole((8, width + GROUP)),
        ],
        scratch_shapes=[
            pltpu.VMEM((STATE, width), F32),
            pltpu.VMEM((rows + 8, width + GROUP), F32),
            pltpu.VMEM((2 * rows, width), F32),
            pltpu.VMEM((rows, width), F32),
            pltpu.VMEM((rows, width), F32),
            pltpu.VMEM((8, width), F32),
        ],
        out_shape=[
            shape((total, width), BF16),
            shape(proj.shape, BF16),
            shape((places, total, share), F32),
            shape((8, width), F32),
            shape((8, width + GROUP), F32),
            shape((8, heads), F32),
            shape((STATE, width), F32),
            shape((8, width + GROUP), F32),
        ],
        compiler_params=pltpu.CompilerParams(vmem_limit_bytes=VMEM_BYTES),
        name="scan_backward",
    )(pz, proj, y, filt, dn, rc, states, states, s0, cw, hp, table, gain, g0, e0)


def bring(step, pieces, buffers, sems, own):
    for near, far, buffer, sem in zip(*pieces, buffers, sems):
        to, done = buffer.at[step % 2], sem.at[step % 2]

        @pl.when(own)
        def _():
            pltpu.make_async_copy(near[step], to, done).start()

        @pl.when(jnp.logical_not(own))
        def _():
            pltpu.make_async_copy(far[step], to, done).start()


def arrived(step, pieces, buffers, sems):
    for near, buffer, sem in zip(pieces[0], buffers, sems):
        pltpu.make_async_copy(near[step], buffer.at[step % 2], sem.at[step % 2]).wait()
    return [buffer.at[step % 2] for buffer in buffers]


def project_kernel(ids, normed, *refs, layer, n):
    near, far = [refs[0:n]], [refs[n : 2 * n]]
    out, buffer, sem = refs[2 * n :]
    pieces = (near, far)
    own = ids[1] == layer
    columns = out.shape[1]
    share = buffer.shape[2]
    bring(0, pieces, [buffer], [sem], own)
    for m in range(n):
        if m + 1 < n:
            bring(m + 1, pieces, [buffer], [sem], own)
        (w,) = arrived(m, pieces, [buffer], [sem])
        from_place = pl.multiple_of(jnp.bitwise_xor(ids[0], m) * share, share)
        a = normed[:, pl.ds(from_place, share)]
        for lo in range(0, columns, 256):
            here = slice(lo, min(lo + 256, columns))
            v = lax.dot_general(
                a, w[here, :], (((1,), (1,)), ((), ())), preferred_element_type=F32
            )
            out[:, here] = v if m == 0 else out[:, here] + v


def project(ids, normed, near, far, layer):
    n = len(near)
    columns, share = near[0].shape
    rows = normed.shape[0]
    vmem = pl.BlockSpec(memory_space=pltpu.VMEM)
    return pl.pallas_call(
        functools.partial(project_kernel, layer=layer, n=n),
        in_specs=[pl.BlockSpec(memory_space=pltpu.SMEM), vmem]
        + [pl.BlockSpec(memory_space=pl.ANY)] * (2 * n),
        out_specs=vmem,
        scratch_shapes=[
            pltpu.VMEM((2, columns, share), BF16),
            pltpu.SemaphoreType.DMA((2,)),
        ],
        out_shape=jax.ShapeDtypeStruct((rows, columns), F32),
        compiler_params=pltpu.CompilerParams(vmem_limit_bytes=VMEM_BYTES),
        cost_estimate=pl.CostEstimate(
            flops=2 * rows * columns * share * n,
            bytes_accessed=columns * share * n * 2 + rows * columns * 4,
            transcendentals=0,
        ),
        name="project",
    )(ids, normed, *near, *far)


def back_kernel(ids, dz, dx, *refs, layer, n):
    near = (refs[0:n], refs[n : 2 * n])
    far = (refs[2 * n : 3 * n], refs[3 * n : 4 * n])
    out, zbuf, xbuf, zsem, xsem = refs[4 * n :]
    pieces = (near, far)
    own = ids[1] == layer
    share = zbuf.shape[2]
    args = ([zbuf, xbuf], [zsem, xsem])
    bring(0, pieces, *args, own)
    for m in range(n):
        if m + 1 < n:
            bring(m + 1, pieces, *args, own)
        wz, wx = arrived(m, pieces, *args)
        for lo in range(0, share, 256):
            here = slice(lo, lo + 256)
            v = jnp.dot(dz[...], wz[:, here], preferred_element_type=F32) + jnp.dot(
                dx[...], wx[:, here], preferred_element_type=F32
            )
            at_lane = pl.multiple_of(jnp.bitwise_xor(ids[0], m) * share + lo, 256)
            out[:, pl.ds(at_lane, 256)] = v.astype(out.dtype)


def project_back(ids, dz, dx, near, far, layer, kind):
    n = len(near[0])
    share = near[0][0].shape[1]
    rows = dz.shape[0]
    columns = dz.shape[1] + dx.shape[1]
    vmem = pl.BlockSpec(memory_space=pltpu.VMEM)
    return pl.pallas_call(
        functools.partial(back_kernel, layer=layer, n=n),
        in_specs=[pl.BlockSpec(memory_space=pltpu.SMEM), vmem, vmem]
        + [pl.BlockSpec(memory_space=pl.ANY)] * (4 * n),
        out_specs=vmem,
        scratch_shapes=[
            pltpu.VMEM((2, dz.shape[1], share), BF16),
            pltpu.VMEM((2, dx.shape[1], share), BF16),
            pltpu.SemaphoreType.DMA((2,)),
            pltpu.SemaphoreType.DMA((2,)),
        ],
        out_shape=jax.ShapeDtypeStruct((rows, n * share), kind),
        compiler_params=pltpu.CompilerParams(vmem_limit_bytes=VMEM_BYTES),
        cost_estimate=pl.CostEstimate(
            flops=2 * rows * columns * share * n,
            bytes_accessed=columns * share * n * 2 + rows * n * share * 2,
            transcendentals=0,
        ),
        name="project_back",
    )(ids, dz, dx, *near[0], *near[1], *far[0], *far[1])


def place_kernel(ids, *refs, plan, count, rows_of_small):
    small = refs[count]
    out, eye, pieces, blocks, in_sem, out_sem = refs[-6:]
    core = ids[1]
    size, share = blocks.shape[1:]

    def fetch(k):
        for layer in range(2):

            @pl.when(core == layer)
            def _():
                src = refs[plan[k][layer]]
                pltpu.make_async_copy(
                    src.at[:, pl.ds(0, share)], pieces.at[k % 2], in_sem.at[k % 2]
                ).start()

    def send(step, first, count):
        return pltpu.make_async_copy(
            blocks.at[step % 2, pl.ds(0, count)],
            out.at[pl.ds(first, count)],
            out_sem.at[step % 2],
        )

    eye[...] = (
        lax.broadcasted_iota(jnp.int32, eye.shape, 0)
        == lax.broadcasted_iota(jnp.int32, eye.shape, 1)
    ).astype(BF16)
    fetch(0)
    sent = []
    for k, (_, _, side, firsts) in enumerate(plan):
        if k + 1 < len(plan):
            fetch(k + 1)
        pltpu.make_async_copy(pieces.at[k % 2], pieces.at[k % 2], in_sem.at[k % 2]).wait()
        shift = jnp.where(side == 0, core, 1 - core) * size
        for p, first in enumerate(firsts):
            step = len(sent)
            if step >= 2:
                sent[step - 2].wait()
            blocks[step % 2] = lax.dot_general(
                pieces[k % 2, p],
                eye[...],
                (((0,), (0,)), ((), ())),
                preferred_element_type=F32,
            )
            sent.append(send(step, pl.multiple_of(first + shift, 8), size))
            sent[-1].start()
    if rows_of_small:
        step = len(sent)
        sent[step - 2].wait()
        first, count = rows_of_small
        sent.append(
            pltpu.make_async_copy(small, out.at[pl.ds(first, count)], out_sem.at[step % 2])
        )
        sent[-1].start()
    sent[-2].wait()
    sent[-1].wait()


def place_in(ids, arrays, plan, small, rows_of_small, before, shape, size):
    places, share = arrays[0].shape[0], shape[1]
    any_space = pl.BlockSpec(memory_space=pl.ANY)
    return pl.pallas_call(
        functools.partial(
            place_kernel, plan=plan, count=len(arrays), rows_of_small=rows_of_small
        ),
        in_specs=[pl.BlockSpec(memory_space=pltpu.SMEM)]
        + [any_space] * len(arrays)
        + [pl.BlockSpec(memory_space=pltpu.VMEM)]
        + [any_space] * len(before),
        out_specs=any_space,
        scratch_shapes=[
            pltpu.VMEM((share, share), BF16),
            pltpu.VMEM((2, places, share, size), BF16),
            pltpu.VMEM((2, size, share), F32),
            pltpu.SemaphoreType.DMA((2,)),
            pltpu.SemaphoreType.DMA((2,)),
        ],
        out_shape=jax.ShapeDtypeStruct(shape, F32),
        input_output_aliases={len(arrays) + 2: 0} if before else {},
        compiler_params=pltpu.CompilerParams(vmem_limit_bytes=VMEM_BYTES),
        name="place_in",
    )(ids, *arrays, small, *before)


def swap_section(v):
    return lax.ppermute(v, "section", [(0, 1), (1, 0)])


def at(v, k):
    return lax.dynamic_index_in_dim(v, k, 0, False)


def exchange(v):
    return lax.all_to_all(v, "fsdp", 0, 0, tiled=True)


def to_all(v):
    n = lax.axis_size("fsdp")
    return exchange(jnp.broadcast_to(v[None], (n,) + v.shape))


def gather_rows(v):
    return to_all(v).reshape(-1, v.shape[-1])


def scatter_sum(partial):
    n = lax.axis_size("fsdp")
    got = exchange(partial.reshape(n, -1, partial.shape[-1]))
    return jnp.sum(got.astype(F32), axis=0)


def in_group(v):
    n, s = lax.axis_size("fsdp"), lax.axis_size("seq")
    groups = [[j * n + i for i in range(n)] for j in range(s // n)]
    return lax.all_to_all(v, "seq", 0, 0, axis_index_groups=groups, tiled=True)


def quarters(v):
    n = lax.axis_size("fsdp")
    return v.reshape(v.shape[0], n, -1).transpose(1, 0, 2)


def joined(v):
    return v.transpose(1, 0, 2).reshape(v.shape[1], -1)


def move_fsdp(v, m):
    n = lax.axis_size("fsdp")
    return lax.ppermute(v, "fsdp", [(k, k ^ m) for k in range(n)])


def move_seq(v, m):
    s = lax.axis_size("seq")
    return lax.ppermute(v, "seq", [(k, k ^ m) for k in range(s)])


class SeqSums:
    def __init__(self):
        self.last = None

    def add(self, v):
        if self.last is not None:
            v, _ = lax.optimization_barrier((v, self.last))
        self.last = lax.psum(v, "seq")
        return self.last


def relay(total, local, reverse):
    n, s = lax.axis_size("fsdp"), lax.axis_size("seq")
    segments = s // n
    place = lax.axis_index("seq") // n
    own = lax.axis_index("seq") % n
    totals = lax.all_gather(total, "seq")
    locals_ = lax.all_gather(local, "seq")
    state = jnp.zeros_like(local)
    order = range(segments - 1, -1, -1) if reverse else range(segments)
    for j in order:
        use = (j > place) if reverse else (j < place)
        t = lax.dynamic_index_in_dim(totals, j * n + own, 0, False)
        v = lax.dynamic_index_in_dim(locals_, j * n + own, 0, False)
        state = jnp.where(use, t * state + v, state)
    return state


def next_segment(v, step):
    n, s = lax.axis_size("fsdp"), lax.axis_size("seq")
    pairs = [(k, k + step * n) for k in range(s) if 0 <= k + step * n < s]
    return lax.ppermute(v, "seq", pairs)


def dot_rows(a, b):
    return lax.dot_general(a, b, (((0,), (0,)), ((), ())), preferred_element_type=F32)


def dot_cols(a, b):
    return lax.dot_general(a, b, (((1,), (1,)), ((), ())), preferred_element_type=F32)


def normalised(h, gain):
    return h * lax.rsqrt(jnp.mean(h * h, axis=-1, keepdims=True) + EPS) * gain


def per_device(
    inputs,
    cotangent,
    lengths,
    gain_in,
    w_in,
    conv_w,
    conv_b,
    dt_bias,
    a_log,
    d_skip,
    gain_out,
    w_out,
):
    n = lax.axis_size("fsdp")
    nz = lax.axis_size("seq")
    segments = nz // n
    c = lax.axis_index("section")
    f = lax.axis_index("fsdp")
    place = lax.axis_index("seq")
    upper = c == 0
    rows = inputs.shape[2]
    width = INNER // n
    heads = HEADS // n
    share = D // n
    half = share // 2
    group = GROUP // n
    ids = jnp.stack([f, c]).astype(jnp.int32)
    tie = lax.optimization_barrier

    def pick(a, b):
        return jnp.where(upper, a, b)

    w = w_in[0].T

    def cut(first, size):
        return lax.dynamic_slice_in_dim(w, first, size, 0)

    def piece_z(m):
        return cut((f ^ m) * width, width)

    def piece_x(m):
        return jnp.concatenate(
            [
                cut(INNER + (f ^ m) * width, width),
                w[2 * INNER : 2 * INNER + GROUP],
                cut(2 * INNER + GROUP + (f ^ m) * heads, heads),
            ]
        )

    def fetch(pieces, layer):
        pairs = lambda m: [(layer * n + i, layer * n + (i ^ m)) for i in range(n)]
        near = [
            v if m == 0 else lax.ppermute(v, ("section", "fsdp"), pairs(m))
            for m, v in enumerate(pieces)
        ]
        return near, [lax.ppermute(v, "section", [(layer, 1 - layer)]) for v in near]

    def whole_slot(v):
        return joined(to_all(v.reshape(n * rows, share)))

    pack = jnp.concatenate(
        [
            gain_in[0],
            dt_bias[0],
            a_log[0],
            d_skip[0],
            gain_out[0],
            conv_w[0].reshape(-1),
            conv_b[0],
        ]
    )
    mine, part_h0, pieces_x = tie(
        (to_all(pack), exchange(quarters(at(inputs, c)[0])), [piece_x(m) for m in range(n)])
    )
    near_x0, far_x0 = fetch(pieces_x, 0)
    part_h0 = in_group(part_h0)
    near_x0, part_h0 = tie((near_x0, part_h0))
    far_x0 = [lax.ppermute(v, "section", [(0, 1)]) for v in near_x0]
    pieces_z, part_h0 = tie(([piece_z(m) for m in range(n)], part_h0))
    all_h0 = whole_slot(part_h0)
    near_z0, far_z0 = fetch(pieces_z, 0)

    theirs = swap_section(mine)
    small = []
    for full in (pick(mine, theirs), pick(theirs, mine)):
        full = full.astype(F32)
        used = 0

        def take(size):
            nonlocal used
            used += size
            return full[:, used - size : used]

        gain = take(share).reshape(1, D)
        hp = [at(take(heads), f)[None] for _ in range(3)]
        hp = jnp.concatenate([hp[0], -jnp.exp(hp[1]), hp[2], jnp.zeros((5, heads), F32)])
        gout = at(take(width), f)[None]
        per = CHANNELS // n
        taps = take(KERNEL * per).reshape(n, KERNEL, per).transpose(1, 0, 2)
        bias = take(per).reshape(1, CHANNELS)
        table = jnp.concatenate(
            [taps.reshape(KERNEL, CHANNELS), bias, jnp.zeros((3, CHANNELS), F32)]
        )
        cw = jnp.concatenate(
            [lax.dynamic_slice_in_dim(table, f * width, width, 1), table[:, INNER:]], axis=1
        )
        small.append((gain, cw, hp, gout))

    win = [(near_z0, far_z0, near_x0, far_x0), None]
    expand = (
        jnp.arange(heads)[:, None] == jnp.arange(width)[None, :] // HEAD_DIM
    ).astype(BF16)
    zero_state = jnp.zeros((STATE, width), F32)
    zero_edge = jnp.zeros((8, width + GROUP), F32)

    def project_x(normed, layer):
        return project(ids, normed, win[layer][2], win[layer][3], layer)

    def project_z(normed, layer):
        return project(ids, normed, win[layer][0], win[layer][1], layer)

    def decay_of(px, hp):
        decay = jax.nn.softplus(px[:, width + GROUP :] + hp[0:1]) * hp[1:2]
        return jnp.repeat(jnp.exp(jnp.sum(decay, axis=0)), HEAD_DIM)[None, :]

    def scan(px, layer):
        _, cw, hp, _ = small[layer]
        args = (px, cw, hp)
        if segments == 1:
            return run_forward(*args, zero_state, zero_edge, rows), zero_state
        edge = next_segment(px[-8:, : width + GROUP], 1)
        local = run_forward(*args, zero_state, edge, rows)[2][-1]
        state = relay(decay_of(px, hp), local, False)
        return run_forward(*args, state, edge, rows), state

    def unscan(pz, px, fwd, dn, rc, layer):
        (y, filt, states), state = fwd
        _, cw, hp, gout = small[layer]
        args = (pz, px, y, filt, dn, rc, states, state, cw, hp, expand, gout)
        if segments == 1:
            return run_backward(*args, zero_state, zero_edge, rows, n)[:6]
        local = run_backward(*args, zero_state, zero_edge, rows, n)[6]
        grad = relay(decay_of(px, hp), local, True)
        edge = next_segment(run_backward(*args, grad, zero_edge, rows, n)[7], -1)
        return run_backward(*args, grad, edge, rows, n)[:6]

    def gate(pz, y):
        return y * jax.nn.silu(pz)

    def gated(pz, y, r, layer):
        return (gate(pz, y) * r[:, None] * small[layer][3]).astype(BF16)

    def sum_of_shares(v):
        return jnp.sum(to_all(v), axis=0)

    normed_in0 = normalised(all_h0.astype(F32), small[0][0]).astype(BF16)
    px0 = project_x(normed_in0, 0)
    px0, pieces_x1, pieces_z1, own_ct, wo_mine, own_len = tie(
        (px0, pieces_x, pieces_z, at(cotangent, c)[0], w_out[0], at(lengths, c))
    )
    near_x1, far_x1 = fetch(pieces_x1, 1)
    wo_other = swap_section(wo_mine)
    wo = (pick(wo_mine, wo_other), pick(wo_other, wo_mine))
    slot_pairs = [
        ((j * n + i) * n + k, (j * n + k) * n + i)
        for j in range(segments)
        for i in range(n)
        for k in range(n)
    ]
    length = lax.ppermute(own_len, ("seq", "fsdp"), slot_pairs)
    first_row = (place // n) * n * rows
    all_valid = first_row + jnp.arange(n * rows, dtype=jnp.int32) < length[0]
    all_valid = all_valid.astype(F32)[:, None]
    own_rows = lambda v: lax.dynamic_slice_in_dim(v, f * rows, rows, 0)
    valid = own_rows(all_valid)
    h0 = own_rows(all_h0)
    fwd0, near_z0 = tie((scan(px0, 0), near_z0))
    far_z0 = [lax.ppermute(v, "section", [(0, 1)]) for v in near_z0]
    win[0] = (near_z0, far_z0, near_x0, far_x0)
    pz0 = project_z(normed_in0, 0)
    g0 = gate(pz0, fwd0[0][0])
    stat0, near_x1, pieces_z1 = tie((jnp.sum(g0 * g0, axis=1), near_x1, pieces_z1))
    near_z1, far_z1 = fetch(pieces_z1, 1)
    stat0 = sum_of_shares(stat0.reshape(n, rows)).reshape(-1)
    r0 = lax.rsqrt(stat0 / INNER + EPS)
    normed0 = gated(pz0, fwd0[0][0], r0, 0)
    part_ct = in_group(exchange(quarters(own_ct)))
    normed0, wo, part_ct = tie((normed0, wo, part_ct))
    far_x1 = [lax.ppermute(v, "section", [(1, 0)]) for v in near_x1]
    mixed0 = scatter_sum(jnp.dot(normed0, wo[0], preferred_element_type=F32))
    out0 = valid * (h0.astype(F32) + mixed0)
    h1 = out0.astype(BF16)

    normed_in1 = gather_rows(normalised(h1.astype(F32), small[1][0]).astype(BF16))
    normed_in1, far_x1, part_ct, near_z1 = tie((normed_in1, far_x1, part_ct, near_z1))
    far_z1 = [lax.ppermute(v, "section", [(1, 0)]) for v in near_z1]
    win[1] = (near_z1, far_z1, near_x1, far_x1)
    px1 = project_x(normed_in1, 1)
    all_ct = whole_slot(part_ct)
    fwd1 = scan(px1, 1)
    fwd1, all_ct = tie((fwd1, all_ct))
    dout1 = own_rows(all_ct).astype(F32)
    dmixed1 = (all_valid * all_ct.astype(F32)).astype(BF16)
    dn1 = dot_cols(dmixed1, wo[1])
    pz1 = project_z(normed_in1, 1)
    g1 = gate(pz1, fwd1[0][0])
    stat1 = sum_of_shares(
        jnp.stack(
            [
                jnp.sum(g1 * g1, axis=1).reshape(n, rows),
                jnp.sum(g1 * dn1 * small[1][3], axis=1).reshape(n, rows),
            ]
        )
    ).reshape(2, -1)
    r1 = lax.rsqrt(stat1[0] / INNER + EPS)
    normed1 = gated(pz1, fwd1[0][0], r1, 1)

    part_width = width // 2

    def cut_half(v, k):
        size = v.shape[1] // 2
        return lax.dynamic_slice_in_dim(v, k * size, size, 1)

    def narrow_of(parts, k):
        return jnp.concatenate([cut_half(v, k) for v in parts], axis=1)

    def away_in(normed_in, part, narrow=()):
        away = [dot_rows(normed_in, cut_half(part, 1 - c)).astype(BF16)]
        if narrow:
            away.append(dot_rows(narrow_of(narrow, 1 - c), normed_in).astype(BF16))
        return [swap_section(v) for v in away]

    def own_in_piece(normed_in, part, away, narrow=()):
        total = dot_rows(normed_in, cut_half(part, c)) + away[0].astype(F32)
        result = total.astype(BF16).reshape(n, share, -1)
        if narrow:
            total = (dot_rows(narrow_of(narrow, c), normed_in) + away[1].astype(F32)).astype(BF16)
            fill = jnp.zeros((-total.shape[0] % 64, D), BF16)
            rest = jnp.concatenate([total, fill]).reshape(-1, n, share).transpose(1, 0, 2)
            result = jnp.concatenate([result, rest], axis=1)
        return result

    def away_out(normed, dmixed):
        return swap_section(dot_rows(cut_half(normed, 1 - c), dmixed).astype(BF16))

    def own_out_piece(normed, dmixed, away):
        return (dot_rows(cut_half(normed, c), dmixed) + away.astype(F32)).astype(BF16)

    def with_group(dxs, dbc):
        total = jnp.sum(exchange(dbc), axis=0).astype(BF16)
        column = jnp.arange(GROUP)[None, :] // group
        own = jnp.where(column == f, jnp.concatenate([total] * n, axis=1), 0)
        full = lax.dynamic_update_slice(dxs, own.astype(BF16), (0, width))
        return full, (dxs[:, :width], [total, dxs[:, width + GROUP :]])

    def back_in(dz, full, layer, kind):
        near_z, far_z, near_x, far_x = win[layer]
        return project_back(ids, dz, full, (near_z, near_x), (far_z, far_x), layer, kind)

    def back_norm(dout, dnormed_in, h, gain):
        h = h.astype(F32)
        r = lax.rsqrt(jnp.mean(h * h, axis=-1, keepdims=True) + EPS)
        u = dnormed_in * gain
        mean = jnp.mean(u * h, axis=-1, keepdims=True)
        dgain = jnp.sum(dnormed_in * h * r, axis=0)
        return valid * dout + r * u - h * (r * r * r) * mean, dgain

    def scales(r, coef):
        top = jnp.stack([r.reshape(n, rows), coef.reshape(n, rows)], axis=1)
        return jnp.concatenate([top, jnp.zeros((n, 6, rows), F32)], axis=1)

    def packed(dgin, d, out, mixed):
        dgain, dconv, dhp = d[3][0], d[4][:5], d[5][:3]
        put = lambda v, size, at_lane: lax.dynamic_update_slice(
            jnp.zeros(v.shape[:-1] + (size,), F32), v, (0,) * (v.ndim - 1) + (at_lane,)
        )
        conv = put(dconv[:, :width], CHANNELS, f * width)
        conv = conv.at[:, INNER:].set(dconv[:, width:])
        totals = jnp.stack(
            [jnp.sum(out * out), jnp.sum((valid * mixed) ** 2), jnp.sum(valid)]
        )
        return jnp.concatenate(
            [
                dgin,
                conv.reshape(-1),
                put(dhp, HEADS, f * heads).reshape(-1),
                put(dgain, INNER, f * width),
                totals,
            ]
        )

    def hand_over(v, layer):
        return lax.ppermute(v, "section", [(1 - layer, layer)])

    sums = SeqSums()
    rc1 = scales(r1, (r1 * r1 * r1 / INNER) * stat1[1])
    away = away_out(normed1, dmixed1)
    go = own_out_piece(normed1, dmixed1, away)
    rc1, normed1, dn1, go = tie((rc1, normed1, dn1, go))
    o1 = sums.add(go)

    d1 = unscan(pz1, px1, fwd1, dn1, rc1, 1)
    mixed1 = scatter_sum(jnp.dot(normed1, wo[1], preferred_element_type=F32).astype(BF16))
    d1, mixed1 = tie((d1, mixed1))

    away = away_in(normed_in1, d1[0])
    full1, xs1 = with_group(d1[1], d1[2])
    back1 = back_in(d1[0], full1, 1, F32)
    gz = own_in_piece(normed_in1, d1[0], away)
    back1, xs1, gz = tie((back1, xs1, gz))
    z1 = sums.add(gz)

    dnin1 = scatter_sum(back1)
    away = away_in(normed_in1, *xs1)
    gx = own_in_piece(normed_in1, xs1[0], away, xs1[1])
    dnin1, gx, o1 = tie((dnin1, gx, o1))
    x1 = sums.add(gx)

    grad1, dgin1 = back_norm(dout1, dnin1, h1, small[1][0])
    dout0 = grad1.astype(BF16).astype(F32)
    dmixed0_own = (valid * dout0).astype(BF16)
    dmixed0 = gather_rows(dmixed0_own)
    along0 = to_all(jnp.sum(dmixed0_own.astype(F32) * mixed0, axis=-1)).reshape(-1)
    rc0 = scales(r0, (r0 * r0 / INNER) * along0)
    out1 = valid * (h1.astype(F32) + mixed1)
    grad1, dgin1, dmixed0, rc0, out1 = tie((grad1, dgin1, dmixed0, rc0, out1))

    back_h = exchange(quarters(jnp.concatenate([h1, out1.astype(BF16)])))
    dn0 = dot_cols(dmixed0, wo[0])
    d0 = unscan(pz0, px0, fwd0, dn0, rc0, 0)
    go = own_out_piece(normed0, dmixed0, away_out(normed0, dmixed0))
    d0, go, back_h, z1 = tie((d0, go, back_h, z1))
    o0 = sums.add(go)

    away = away_in(normed_in0, d0[0])
    full0, xs0 = with_group(d0[1], d0[2])
    gz = own_in_piece(normed_in0, d0[0], away)
    away = away_in(normed_in0, *xs0)
    gx = own_in_piece(normed_in0, xs0[0], away, xs0[1])
    full0, gz, gx, back_h = tie((full0, gz, gx, back_h))
    z0 = sums.add(gz)
    gx = exchange(gx)
    back0 = back_in(d0[0], full0, 0, BF16)
    gx, back0, x1 = tie((gx, back0, x1))
    x0 = sums.add(gx)

    def hand_over(v, layer):
        return lax.ppermute(v, "section", [(1 - layer, layer)])

    dnin0 = scatter_sum(back0)
    back_h = joined(exchange(in_group(back_h)))
    own_z1 = exchange(z1)
    own_o1 = o1
    away_o1 = hand_over(own_o1, 1)
    grad0, dgin0 = back_norm(dout0, dnin0, h0, small[0][0])
    p = jnp.stack([packed(dgin0, d0, out0, mixed0), packed(dgin1, d1, out1, mixed1)])
    p, grad0, back_h, own_z1, away_o1, o0 = tie((p, grad0, back_h, own_z1, away_o1, o0))

    own_x1 = exchange(x1)
    away_z1 = hand_over(own_z1, 1)
    own_o0 = o0
    away_o0 = hand_over(own_o0, 0)
    back_g = exchange(quarters(jnp.concatenate([grad0.astype(BF16), grad1.astype(BF16)])))
    back_g = joined(exchange(in_group(back_g)))
    away_x1 = hand_over(own_x1, 1)
    p = p + swap_section(p)
    m = 1
    while m < n:
        p = p + move_fsdp(p, m)
        m *= 2
    m = 1
    while m < nz:
        p = p + move_seq(p, m)
        m *= 2
    p = pick(p[0], p[1])
    p, own_x1, away_x1, away_z1, away_o0, back_g, z0 = tie(
        (p, own_x1, away_x1, away_z1, away_o0, back_g, z0)
    )
    own_z0 = exchange(z0)
    away_z0 = hand_over(own_z0, 0)
    own_z0, away_z0, x0 = tie((own_z0, away_z0, x0))
    own_x0 = x0
    away_x0 = hand_over(own_x0, 0)
    back = jnp.concatenate([back_h, back_g])

    used = 0

    def part(size):
        nonlocal used
        used += size
        return p[used - size : used]

    mine_of = lambda v, size: lax.dynamic_slice_in_dim(v, f * size, size, v.ndim - 1)
    o_gain_in = mine_of(part(D), share)
    o_conv = mine_of(part(5 * CHANNELS).reshape(5, CHANNELS), CHANNELS // n)
    o_heads = mine_of(part(3 * HEADS).reshape(3, HEADS), heads)
    o_gain_out = mine_of(part(INNER), width)
    totals = part(3)
    act_rms = jnp.sqrt(totals[:2] / (totals[2] * D))[None]

    held = [
        [(own_z0, own_x0, own_o0), (own_z1, own_x1, own_o1)],
        [(away_z0, away_x0, away_o0), (away_z1, away_x1, away_o1)],
    ]

    def both_halves(a, b):
        return jnp.stack([pick(a, b), pick(b, a)], axis=1)

    rows_of = GROUP // n // 2, HEADS // n // 2
    narrow = [pick(side[0][1], side[1][1])[:, share : share + sum(rows_of)] for side in held]
    narrow = both_halves(*[v.astype(F32) for v in narrow])
    small_in = jnp.concatenate(
        [
            narrow[:, :, : rows_of[0]].reshape(GROUP, share),
            narrow[:, :, rows_of[0] :].reshape(HEADS, share),
        ]
    )
    g_w_in = []
    shape_in = (2 * INNER + GROUP + HEADS, share)
    for k, rows_of_small in ((0, None), (1, (2 * INNER, GROUP + HEADS))):
        arrays, plan = [], []
        for s in range(2):
            arrays += [held[s][0][k], held[s][1][k]]
            firsts = tuple(k * INNER + q * width for q in range(n))
            plan.append((len(arrays) - 2, len(arrays) - 1, s, firsts))
        g_w_in = [
            place_in(
                ids, arrays, tuple(plan), small_in, rows_of_small, g_w_in, shape_in, part_width
            )
        ]
    halves_out = [pick(side[0][2], side[1][2]) for side in held]
    g_w_out = jnp.concatenate([pick(*halves_out), pick(*halves_out[::-1])]).astype(F32)

    back = back.reshape(2, 2, rows, D)
    kept_back = pick(back[:, 0], back[:, 1])
    other_back = swap_section(pick(back[:, 1], back[:, 0]))
    both_back = jnp.stack(
        [pick(kept_back, other_back), pick(other_back, kept_back)], axis=1
    )
    return (
        both_back[0][None, :, None],
        both_back[1].astype(F32)[None, :, None],
        o_gain_in[None],
        g_w_in[0].T[None],
        o_conv[None, :4],
        o_conv[None, 4],
        o_heads[None, 0],
        o_heads[None, 1],
        o_heads[None, 2],
        o_gain_out[None],
        g_w_out[None],
        act_rms,
    )


def solution(mesh):
    in_specs = (
        P(None, "fsdp", "seq", None),
        P(None, "fsdp", "seq", None),
        P(None, "fsdp"),
        P("section", "fsdp"),
        P("section", "fsdp", None),
        P("section", None, "fsdp"),
        P("section", "fsdp"),
        P("section", "fsdp"),
        P("section", "fsdp"),
        P("section", "fsdp"),
        P("section", "fsdp"),
        P("section", "fsdp", None),
    )
    out_specs = (
        P("section", None, "fsdp", "seq", None),
        P("section", None, "fsdp", "seq", None),
        P("section", "fsdp"),
        P("section", "fsdp", None),
        P("section", None, "fsdp"),
        P("section", "fsdp"),
        P("section", "fsdp"),
        P("section", "fsdp"),
        P("section", "fsdp"),
        P("section", "fsdp"),
        P("section", "fsdp", None),
        P("section", None),
    )
    return jax.shard_map(
        per_device, mesh=mesh, in_specs=in_specs, out_specs=out_specs, check_vma=False
    )
```

```python
import functools

import jax
import jax.numpy as jnp
from jax import lax
from jax.experimental import pallas as pl
from jax.experimental.pallas import tpu as pltpu
from jax.sharding import PartitionSpec as P

D = 2048
INNER = 4096
HEADS = 64
HEAD_DIM = 64
STATE = 128
KERNEL = 4
GROUP = 2 * STATE
CHANNELS = INNER + GROUP
LANES = 128
EPS = 1e-05
F32 = jnp.float32
BF16 = jnp.bfloat16
VMEM_BYTES = 48 * 1024 * 1024


def split(v):
    hi = v.astype(BF16)
    return hi, (v - hi.astype(F32)).astype(BF16)


def dot32(a, b, ca, cb):
    (ah, al), (bh, bl) = (v if isinstance(v, tuple) else split(v) for v in (a, b))
    one = lambda p, q: lax.dot_general(
        p, q, (((ca,), (cb,)), ((), ())), preferred_element_type=F32
    )
    return one(ah, bh) + (one(ah, bl) + one(al, bh))


def step_sizes(raw, hp, rows):
    shifted = raw + hp[0:1, :]
    dt = jnp.maximum(shifted, 0.0) + jnp.log1p(jnp.exp(-jnp.abs(shifted)))
    decay = dt * hp[1:2, :]
    row = lax.broadcasted_iota(jnp.int32, (rows, rows), 0)
    col = lax.broadcasted_iota(jnp.int32, (rows, rows), 1)
    lower = (row >= col).astype(F32)
    cum = dot32(lower, decay, 1, 0)
    cum_t = dot32(decay, lower, 0, 1)
    return shifted, dt, cum, cum_t, row, col, lower


def pair_lanes(v, j, first):
    return jnp.where(first, v[:, 2 * j : 2 * j + 1], v[:, 2 * j + 1 : 2 * j + 2])


def head_sums(v, table):
    hi, low = split(v)
    one = lambda p: lax.dot_general(
        p, table, (((1,), (1,)), ((), ())), preferred_element_type=F32
    )
    return one(hi) + one(low)


def forward_kernel(proj, cw, hp, s0, e0, y_ref, filt_ref, st_ref, state, xp, xw_s, last_s):
    i = pl.program_id(0)
    rows, width = y_ref.shape

    @pl.when(i == 0)
    def _():
        state[...] = s0[...]
        xp[0:8, :] = e0[...]

    xp[8 : 8 + rows, :] = proj[:, : width + GROUP]

    def conv_tile(lo):
        acc = cw[4:5, lo : lo + LANES]
        for k in range(KERNEL):
            acc = acc + cw[k : k + 1, lo : lo + LANES] * xp[5 + k : 5 + k + rows, lo : lo + LANES]
        filt_ref[:, lo : lo + LANES] = acc
        return acc * jax.nn.sigmoid(acc)

    b_c = conv_tile(width)
    c_c = conv_tile(width + STATE)
    _, dt, cum, cum_t, row, col, _ = step_sizes(proj[:, width + GROUP :], hp, rows)
    last = cum[rows - 1 : rows, :]
    ecum = jnp.exp(cum)
    weight = jnp.exp(last - cum) * dt
    elast = jnp.exp(last)
    b_c, c_c = split(b_c), split(c_c)
    carried = dot32(c_c, state[...], 1, 0)
    scores = dot32(c_c, b_c, 1, 1)
    causal = row >= col
    lane = lax.broadcasted_iota(jnp.int32, (rows, LANES), 1)
    first = lane < HEAD_DIM
    for j in range(width // LANES):
        lo = j * LANES
        here = slice(lo, lo + LANES)
        x = conv_tile(lo)
        xd = x * pair_lanes(dt, j, first)
        m = []
        for h in (2 * j, 2 * j + 1):
            gap = cum[:, h : h + 1] - cum_t[h : h + 1, :]
            m.append(jnp.exp(jnp.where(causal, gap, -1e30)) * scores)
        xd2 = jnp.concatenate([jnp.where(first, xd, 0.0), jnp.where(first, 0.0, xd)])
        y = (
            dot32(jnp.concatenate(m, axis=1), xd2, 1, 0)
            + carried[:, here] * pair_lanes(ecum, j, first)
            + pair_lanes(hp[2:3, :], j, first[0:1]) * x
        )
        y_ref[:, here] = y
        xw_s[:, here] = x * pair_lanes(weight, j, first)
        last_s[0:1, here] = pair_lanes(elast, j, first[0:1])
    state[...] = state[...] * last_s[0:1, :] + dot32(b_c, xw_s[...], 0, 0)
    st_ref[0] = state[...]
    xp[0:8, :] = xp[rows : rows + 8, :]


def backward_kernel(
    pz,
    proj,
    y_ref,
    filt,
    dn,
    rc,
    st_before,
    st_out,
    s0,
    cw,
    hp,
    table,
    gain,
    g0,
    e0,
    dz_ref,
    dproj,
    dbc_ref,
    dgain_ref,
    dconv_ref,
    dhp_ref,
    gfin_ref,
    efin_ref,
    grad,
    dfp,
    both,
    xw_s,
    dyc_s,
    rowv,
):
    i = pl.program_id(0)
    rows, width = y_ref.shape
    heads = hp.shape[1]

    @pl.when(i == 0)
    def _():
        grad[...] = g0[...]
        dfp[rows : rows + 8, :] = e0[...]
        dgain_ref[...] = jnp.zeros_like(dgain_ref)
        dconv_ref[...] = jnp.zeros_like(dconv_ref)
        dhp_ref[...] = jnp.zeros_like(dhp_ref)

    def silu_pair(v):
        s = jax.nn.sigmoid(v)
        a = v * s
        return a, s * (1.0 + v - a)

    b_c, b_d = silu_pair(filt[:, width : width + STATE])
    c_c, c_d = silu_pair(filt[:, width + STATE :])
    shifted, dt, cum, cum_t, row, col, lower = step_sizes(proj[:, width + GROUP :], hp, rows)
    last = cum[rows - 1 : rows, :]
    tail = jnp.exp(last - cum)
    ecum = jnp.exp(cum)
    elast = jnp.exp(last)
    b_c, c_c = split(b_c), split(c_c)
    grad_p = split(grad[...])
    k_all = dot32(b_c, grad_p, 1, 0)
    scores_t = dot32(b_c, c_c, 1, 1)
    causal_t = row <= col
    lane = lax.broadcasted_iota(jnp.int32, (rows, LANES), 1)
    first = lane < HEAD_DIM
    dcb_t = jnp.zeros((rows, rows), F32)
    rc_t = dot32((row == col).astype(F32), rc[0], 1, 1)
    r = rc_t[:, 0:1]
    coef = rc_t[:, 1:2]
    rowv[0:1, :] = jnp.sum(grad[...] * st_out[0], axis=0, keepdims=True)
    for j in range(width // LANES):
        lo = j * LANES
        here = slice(lo, lo + LANES)
        z = pz[:, here]
        y = y_ref[:, here]
        sz, dsz = silu_pair(z)
        g = y * sz
        dnt = dn[:, here]
        dg = dnt * gain[0:1, here] * r - g * coef
        dgain_ref[0:1, here] += jnp.sum(dnt * g * r, axis=0, keepdims=True)
        dy = dg * sz
        dz_ref[:, here] = (dg * y * dsz).astype(BF16)
        x, xder = silu_pair(filt[:, here])
        dt_e = pair_lanes(dt, j, first)
        tail_e = pair_lanes(tail, j, first)
        xd = x * dt_e
        dy2 = split(jnp.concatenate([jnp.where(first, dy, 0.0), jnp.where(first, 0.0, dy)]))
        decays = []
        for h in (2 * j, 2 * j + 1):
            gap = cum_t[h : h + 1, :] - cum[:, h : h + 1]
            decays.append(jnp.exp(jnp.where(causal_t, gap, -1e30)))
        m = jnp.concatenate([d * scores_t for d in decays], axis=1)
        dm = dot32(xd, dy2, 1, 1)
        dcb_t = dcb_t + (decays[0] * dm[:, :rows] + decays[1] * dm[:, rows:])
        v = dot32(m, dy2, 1, 0) + k_all[:, here] * tail_e
        skip = pair_lanes(hp[2:3, :], j, first[0:1])
        dx = dt_e * v + skip * dy
        both[0:rows, here] = x * v
        both[rows : 2 * rows, here] = dy * (y - skip * x)
        rowv[1:2, here] = jnp.sum(dy * x, axis=0, keepdims=True)
        rowv[2:3, here] = pair_lanes(elast, j, first[0:1])
        xw_s[:, here] = xd * tail_e
        dyc_s[:, here] = dy * pair_lanes(ecum, j, first)
        dfp[0:rows, here] = dx * xder
    dcb_t = split(dcb_t)
    dyc = split(dyc_s[...])
    st_in = jnp.where(i == pl.num_programs(0) - 1, s0[...], st_before[0])
    dc = dot32(dcb_t, b_c, 0, 0) + dot32(dyc, st_in, 1, 1)
    db = dot32(dcb_t, c_c, 1, 0) + dot32(xw_s[...], grad_p, 1, 1)
    dfp[0:rows, width : width + STATE] = db * b_d
    dfp[0:rows, width + STATE :] = dc * c_d
    grad[...] = grad[...] * rowv[2:3, :] + dot32(c_c, dyc, 0, 0)
    gfin_ref[...] = grad[...]

    sums = head_sums(both[...], table[...])
    rsums = head_sums(rowv[...], table[...])
    ddt_x = sums[0:rows]
    dcum = sums[rows : 2 * rows] - dt * ddt_x
    upto = lax.broadcasted_iota(jnp.int32, (rows, heads), 0)
    dcum = dcum + jnp.where(upto == rows - 1, rsums[0:1, :], 0.0)
    ddecay = dot32(lower, dcum, 0, 0)
    ddt = ddt_x + hp[1:2, :] * ddecay
    draw = ddt * jax.nn.sigmoid(shifted)
    dproj[:, width + GROUP :] = draw.astype(BF16)
    dhp_ref[0:1, :] += jnp.sum(draw, axis=0, keepdims=True)
    dhp_ref[1:2, :] += jnp.sum(ddecay * dt, axis=0, keepdims=True) * hp[1:2, :]
    dhp_ref[2:3, :] += rsums[1:2, :]

    for lo in range(0, width + GROUP, LANES):
        here = slice(lo, lo + LANES)
        src = proj[:, here]
        total = jnp.zeros((rows, LANES), F32)
        for k in range(KERNEL):
            shift = KERNEL - 1 - k
            moved = dfp[shift : shift + rows, here]
            total = total + cw[k : k + 1, here] * moved
            dconv_ref[k : k + 1, here] += jnp.sum(src * moved, axis=0, keepdims=True)
        dconv_ref[4:5, here] += jnp.sum(dfp[0:rows, here], axis=0, keepdims=True)
        if lo < width:
            dproj[:, here] = total.astype(BF16)
        else:
            dproj[:, here] = jnp.zeros((rows, LANES), BF16)
            share = dbc_ref.shape[2]
            for k in range(LANES // share):
                dbc_ref[(lo - width) // share + k] = total[:, k * share : (k + 1) * share]
    dfp[rows : rows + 8, :] = dfp[0:8, :]
    efin_ref[...] = dfp[0:8, :]


def whole(shape):
    return pl.BlockSpec(shape, lambda i: (0,) * len(shape))


def run_forward(proj, cw, hp, s0, e0, rows):
    total, width = proj.shape[0], s0.shape[1]
    count = total // rows
    block = lambda w: pl.BlockSpec((rows, w), lambda i: (i, 0))
    shape = jax.ShapeDtypeStruct
    return pl.pallas_call(
        forward_kernel,
        grid=(count,),
        in_specs=[block(proj.shape[1])] + [whole(v.shape) for v in (cw, hp, s0, e0)],
        out_specs=[
            block(width),
            block(width + GROUP),
            pl.BlockSpec((1, STATE, width), lambda i: (i, 0, 0)),
        ],
        scratch_shapes=[
            pltpu.VMEM((STATE, width), F32),
            pltpu.VMEM((rows + 8, width + GROUP), F32),
            pltpu.VMEM((rows, width), F32),
            pltpu.VMEM((8, width), F32),
        ],
        out_shape=[
            shape((total, width), F32),
            shape((total, width + GROUP), F32),
            shape((count, STATE, width), F32),
        ],
        compiler_params=pltpu.CompilerParams(vmem_limit_bytes=VMEM_BYTES),
        name="scan_forward",
    )(proj, cw, hp, s0, e0)


def run_backward(pz, proj, y, filt, dn, rc, states, s0, cw, hp, table, gain, g0, e0, rows, places):
    total, (heads, width) = proj.shape[0], table.shape
    count = total // rows
    turn = lambda i: count - 1 - i
    block = lambda w: pl.BlockSpec((rows, w), lambda i: (turn(i), 0))
    shape = jax.ShapeDtypeStruct
    share = GROUP // places
    return pl.pallas_call(
        backward_kernel,
        grid=(count,),
        in_specs=[
            block(width),
            block(proj.shape[1]),
            block(width),
            block(width + GROUP),
            block(width),
            pl.BlockSpec((1, 8, rows), lambda i: (turn(i), 0, 0)),
            pl.BlockSpec((1, STATE, width), lambda i: (jnp.maximum(turn(i) - 1, 0), 0, 0)),
            pl.BlockSpec((1, STATE, width), lambda i: (turn(i), 0, 0)),
        ]
        + [whole(v.shape) for v in (s0, cw, hp, table, gain, g0, e0)],
        out_specs=[
            block(width),
            block(proj.shape[1]),
            pl.BlockSpec((places, rows, share), lambda i: (0, turn(i), 0)),
            whole((8, width)),
            whole((8, width + GROUP)),
            whole((8, heads)),
            whole((STATE, width)),
            whole((8, width + GROUP)),
        ],
        scratch_shapes=[
            pltpu.VMEM((STATE, width), F32),
            pltpu.VMEM((rows + 8, width + GROUP), F32),
            pltpu.VMEM((2 * rows, width), F32),
            pltpu.VMEM((rows, width), F32),
            pltpu.VMEM((rows, width), F32),
            pltpu.VMEM((8, width), F32),
        ],
        out_shape=[
            shape((total, width), BF16),
            shape(proj.shape, BF16),
            shape((places, total, share), F32),
            shape((8, width), F32),
            shape((8, width + GROUP), F32),
            shape((8, heads), F32),
            shape((STATE, width), F32),
            shape((8, width + GROUP), F32),
        ],
        compiler_params=pltpu.CompilerParams(vmem_limit_bytes=VMEM_BYTES),
        name="scan_backward",
    )(pz, proj, y, filt, dn, rc, states, states, s0, cw, hp, table, gain, g0, e0)


def bring(step, pieces, buffers, sems, own):
    for near, far, buffer, sem in zip(*pieces, buffers, sems):
        to, done = buffer.at[step % 2], sem.at[step % 2]

        @pl.when(own)
        def _():
            pltpu.make_async_copy(near[step], to, done).start()

        @pl.when(jnp.logical_not(own))
        def _():
            pltpu.make_async_copy(far[step], to, done).start()


def arrived(step, pieces, buffers, sems):
    for near, buffer, sem in zip(pieces[0], buffers, sems):
        pltpu.make_async_copy(near[step], buffer.at[step % 2], sem.at[step % 2]).wait()
    return [buffer.at[step % 2] for buffer in buffers]


def project_kernel(ids, normed, *refs, layer, n):
    near, far = [refs[0:n]], [refs[n : 2 * n]]
    out, buffer, sem = refs[2 * n :]
    pieces = (near, far)
    own = ids[1] == layer
    columns = out.shape[1]
    share = buffer.shape[2]
    bring(0, pieces, [buffer], [sem], own)
    for m in range(n):
        if m + 1 < n:
            bring(m + 1, pieces, [buffer], [sem], own)
        (w,) = arrived(m, pieces, [buffer], [sem])
        from_place = pl.multiple_of(jnp.bitwise_xor(ids[0], m) * share, share)
        a = normed[:, pl.ds(from_place, share)]
        for lo in range(0, columns, 256):
            here = slice(lo, min(lo + 256, columns))
            v = lax.dot_general(
                a, w[here, :], (((1,), (1,)), ((), ())), preferred_element_type=F32
            )
            out[:, here] = v if m == 0 else out[:, here] + v


def project(ids, normed, near, far, layer):
    n = len(near)
    columns, share = near[0].shape
    rows = normed.shape[0]
    vmem = pl.BlockSpec(memory_space=pltpu.VMEM)
    return pl.pallas_call(
        functools.partial(project_kernel, layer=layer, n=n),
        in_specs=[pl.BlockSpec(memory_space=pltpu.SMEM), vmem]
        + [pl.BlockSpec(memory_space=pl.ANY)] * (2 * n),
        out_specs=vmem,
        scratch_shapes=[
            pltpu.VMEM((2, columns, share), BF16),
            pltpu.SemaphoreType.DMA((2,)),
        ],
        out_shape=jax.ShapeDtypeStruct((rows, columns), F32),
        compiler_params=pltpu.CompilerParams(vmem_limit_bytes=VMEM_BYTES),
        cost_estimate=pl.CostEstimate(
            flops=2 * rows * columns * share * n,
            bytes_accessed=columns * share * n * 2 + rows * columns * 4,
            transcendentals=0,
        ),
        name="project",
    )(ids, normed, *near, *far)


def back_kernel(ids, dz, dx, *refs, layer, n):
    near = (refs[0:n], refs[n : 2 * n])
    far = (refs[2 * n : 3 * n], refs[3 * n : 4 * n])
    out, zbuf, xbuf, zsem, xsem = refs[4 * n :]
    pieces = (near, far)
    own = ids[1] == layer
    share = zbuf.shape[2]
    args = ([zbuf, xbuf], [zsem, xsem])
    bring(0, pieces, *args, own)
    for m in range(n):
        if m + 1 < n:
            bring(m + 1, pieces, *args, own)
        wz, wx = arrived(m, pieces, *args)
        for lo in range(0, share, 256):
            here = slice(lo, lo + 256)
            v = jnp.dot(dz[...], wz[:, here], preferred_element_type=F32) + jnp.dot(
                dx[...], wx[:, here], preferred_element_type=F32
            )
            at_lane = pl.multiple_of(jnp.bitwise_xor(ids[0], m) * share + lo, 256)
            out[:, pl.ds(at_lane, 256)] = v.astype(out.dtype)


def project_back(ids, dz, dx, near, far, layer, kind):
    n = len(near[0])
    share = near[0][0].shape[1]
    rows = dz.shape[0]
    columns = dz.shape[1] + dx.shape[1]
    vmem = pl.BlockSpec(memory_space=pltpu.VMEM)
    return pl.pallas_call(
        functools.partial(back_kernel, layer=layer, n=n),
        in_specs=[pl.BlockSpec(memory_space=pltpu.SMEM), vmem, vmem]
        + [pl.BlockSpec(memory_space=pl.ANY)] * (4 * n),
        out_specs=vmem,
        scratch_shapes=[
            pltpu.VMEM((2, dz.shape[1], share), BF16),
            pltpu.VMEM((2, dx.shape[1], share), BF16),
            pltpu.SemaphoreType.DMA((2,)),
            pltpu.SemaphoreType.DMA((2,)),
        ],
        out_shape=jax.ShapeDtypeStruct((rows, n * share), kind),
        compiler_params=pltpu.CompilerParams(vmem_limit_bytes=VMEM_BYTES),
        cost_estimate=pl.CostEstimate(
            flops=2 * rows * columns * share * n,
            bytes_accessed=columns * share * n * 2 + rows * n * share * 2,
            transcendentals=0,
        ),
        name="project_back",
    )(ids, dz, dx, *near[0], *near[1], *far[0], *far[1])


def place_kernel(ids, *refs, plan, count, rows_of_small):
    small = refs[count]
    out, eye, pieces, blocks, in_sem, out_sem = refs[-6:]
    core = ids[1]
    size, share = blocks.shape[1:]

    def fetch(k):
        for layer in range(2):

            @pl.when(core == layer)
            def _():
                src = refs[plan[k][layer]]
                pltpu.make_async_copy(
                    src.at[:, pl.ds(0, share)], pieces.at[k % 2], in_sem.at[k % 2]
                ).start()

    def send(step, first, count):
        return pltpu.make_async_copy(
            blocks.at[step % 2, pl.ds(0, count)],
            out.at[pl.ds(first, count)],
            out_sem.at[step % 2],
        )

    eye[...] = (
        lax.broadcasted_iota(jnp.int32, eye.shape, 0)
        == lax.broadcasted_iota(jnp.int32, eye.shape, 1)
    ).astype(BF16)
    fetch(0)
    sent = []
    for k, (_, _, side, firsts) in enumerate(plan):
        if k + 1 < len(plan):
            fetch(k + 1)
        pltpu.make_async_copy(pieces.at[k % 2], pieces.at[k % 2], in_sem.at[k % 2]).wait()
        shift = jnp.where(side == 0, core, 1 - core) * size
        for p, first in enumerate(firsts):
            step = len(sent)
            if step >= 2:
                sent[step - 2].wait()
            blocks[step % 2] = lax.dot_general(
                pieces[k % 2, p],
                eye[...],
                (((0,), (0,)), ((), ())),
                preferred_element_type=F32,
            )
            sent.append(send(step, pl.multiple_of(first + shift, 8), size))
            sent[-1].start()
    if rows_of_small:
        step = len(sent)
        sent[step - 2].wait()
        first, count = rows_of_small
        sent.append(
            pltpu.make_async_copy(small, out.at[pl.ds(first, count)], out_sem.at[step % 2])
        )
        sent[-1].start()
    sent[-2].wait()
    sent[-1].wait()


def place_in(ids, arrays, plan, small, rows_of_small, before, shape, size):
    places, share = arrays[0].shape[0], shape[1]
    any_space = pl.BlockSpec(memory_space=pl.ANY)
    return pl.pallas_call(
        functools.partial(
            place_kernel, plan=plan, count=len(arrays), rows_of_small=rows_of_small
        ),
        in_specs=[pl.BlockSpec(memory_space=pltpu.SMEM)]
        + [any_space] * len(arrays)
        + [pl.BlockSpec(memory_space=pltpu.VMEM)]
        + [any_space] * len(before),
        out_specs=any_space,
        scratch_shapes=[
            pltpu.VMEM((share, share), BF16),
            pltpu.VMEM((2, places, share, size), BF16),
            pltpu.VMEM((2, size, share), F32),
            pltpu.SemaphoreType.DMA((2,)),
            pltpu.SemaphoreType.DMA((2,)),
        ],
        out_shape=jax.ShapeDtypeStruct(shape, F32),
        input_output_aliases={len(arrays) + 2: 0} if before else {},
        compiler_params=pltpu.CompilerParams(vmem_limit_bytes=VMEM_BYTES),
        name="place_in",
    )(ids, *arrays, small, *before)


def combine_kernel(flags, *refs, adds):
    count = len(adds)
    for k, add in enumerate(adds):
        v, got, out = refs[2 * k], refs[2 * k + 1], refs[2 * count + k]
        if add:
            out[...] = (v[...].astype(F32) + got[...].astype(F32)).astype(BF16)
        else:
            out[...] = jnp.where(flags[k] == 1, got[...], v[...])


def combine(items, flags):
    steps = 8
    shapes = [v.shape for v, _, _ in items]
    flat = [(v.reshape(-1, v.shape[-1]), g.reshape(-1, g.shape[-1])) for v, g, _ in items]
    spec = lambda v: pl.BlockSpec((v.shape[0] // steps, v.shape[1]), lambda i: (i, 0))
    out = pl.pallas_call(
        functools.partial(combine_kernel, adds=tuple(add for _, _, add in items)),
        grid=(steps,),
        in_specs=[pl.BlockSpec(memory_space=pltpu.SMEM)] + [spec(v) for p in flat for v in p],
        out_specs=[spec(v) for v, _ in flat],
        out_shape=[jax.ShapeDtypeStruct(v.shape, BF16) for v, _ in flat],
        compiler_params=pltpu.CompilerParams(vmem_limit_bytes=VMEM_BYTES),
        name="combine",
    )(flags, *[v for p in flat for v in p])
    return [v.reshape(shape) for v, shape in zip(out, shapes)]


def swap_section(v):
    return lax.ppermute(v, "section", [(0, 1), (1, 0)])


def at(v, k):
    return lax.dynamic_index_in_dim(v, k, 0, False)


def exchange(v):
    return lax.all_to_all(v, "fsdp", 0, 0, tiled=True)


def to_all(v):
    n = lax.axis_size("fsdp")
    return exchange(jnp.broadcast_to(v[None], (n,) + v.shape))


def gather_rows(v):
    return to_all(v).reshape(-1, v.shape[-1])


def scatter_sum(partial):
    n = lax.axis_size("fsdp")
    got = exchange(partial.reshape(n, -1, partial.shape[-1]))
    return jnp.sum(got.astype(F32), axis=0)


def in_group(v):
    n, s = lax.axis_size("fsdp"), lax.axis_size("seq")
    groups = [[j * n + i for i in range(n)] for j in range(s // n)]
    return lax.all_to_all(v, "seq", 0, 0, axis_index_groups=groups, tiled=True)


def quarters(v):
    n = lax.axis_size("fsdp")
    return v.reshape(v.shape[0], n, -1).transpose(1, 0, 2)


def joined(v):
    return v.transpose(1, 0, 2).reshape(v.shape[1], -1)


def move_fsdp(v, m):
    n = lax.axis_size("fsdp")
    return lax.ppermute(v, "fsdp", [(k, k ^ m) for k in range(n)])


def move_seq(v, m):
    s = lax.axis_size("seq")
    return lax.ppermute(v, "seq", [(k, k ^ m) for k in range(s)])


class SeqSums:
    def __init__(self):
        s = lax.axis_size("seq")
        half = s // 2
        self.pairs = [[(j, j + 1), (s - 1 - j, s - 2 - j)] for j in range(half - 1)]
        self.pairs.append([(half - 1, half), (half, half - 1)])
        self.inward = half
        self.pairs += [[(j + 1, j), (s - 2 - j, s - 1 - j)] for j in reversed(range(half - 1))]
        self.values, self.phase, self.moving = [], [], []

    def add(self, value):
        self.values.append(value)
        self.phase.append(0)
        return len(self.values) - 1

    def begin(self):
        taken = set()
        for k, step in enumerate(self.phase):
            if step == len(self.pairs) or step in taken:
                continue
            taken.add(step)
            self.moving.append((k, lax.ppermute(self.values[k], "seq", self.pairs[step])))

    def end(self, work):
        place = lax.axis_index("seq")
        items, flags = [], []
        for k, got in self.moving:
            step = self.phase[k]
            items.append((self.values[k], got, step < self.inward))
            here = [place == to for _, to in self.pairs[step]]
            flags.append(functools.reduce(jnp.logical_or, here))
            self.phase[k] = step + 1
        moved = combine(items, jnp.stack(flags).astype(jnp.int32)) if items else []
        still = [k for k, p in enumerate(self.phase) if p == 0]
        work, moved, rest = lax.optimization_barrier(
            (work, moved, [self.values[k] for k in still])
        )
        for (k, _), v in zip(self.moving, moved):
            self.values[k] = v
        for k, v in zip(still, rest):
            self.values[k] = v
        self.moving = []
        return work

    def finish(self, chunks):
        while any(self.phase[k] < len(self.pairs) for k in chunks):
            self.begin()
            self.end(())


def relay(total, local, reverse):
    n, s = lax.axis_size("fsdp"), lax.axis_size("seq")
    segments = s // n
    place = lax.axis_index("seq") // n
    own = lax.axis_index("seq") % n
    totals = lax.all_gather(total, "seq")
    locals_ = lax.all_gather(local, "seq")
    state = jnp.zeros_like(local)
    order = range(segments - 1, -1, -1) if reverse else range(segments)
    for j in order:
        use = (j > place) if reverse else (j < place)
        t = lax.dynamic_index_in_dim(totals, j * n + own, 0, False)
        v = lax.dynamic_index_in_dim(locals_, j * n + own, 0, False)
        state = jnp.where(use, t * state + v, state)
    return state


def next_segment(v, step):
    n, s = lax.axis_size("fsdp"), lax.axis_size("seq")
    pairs = [(k, k + step * n) for k in range(s) if 0 <= k + step * n < s]
    return lax.ppermute(v, "seq", pairs)


def dot_rows(a, b):
    return lax.dot_general(a, b, (((0,), (0,)), ((), ())), preferred_element_type=F32)


def dot_cols(a, b):
    return lax.dot_general(a, b, (((1,), (1,)), ((), ())), preferred_element_type=F32)


def normalised(h, gain):
    return h * lax.rsqrt(jnp.mean(h * h, axis=-1, keepdims=True) + EPS) * gain


def per_device(
    inputs,
    cotangent,
    lengths,
    gain_in,
    w_in,
    conv_w,
    conv_b,
    dt_bias,
    a_log,
    d_skip,
    gain_out,
    w_out,
):
    n = lax.axis_size("fsdp")
    nz = lax.axis_size("seq")
    segments = nz // n
    c = lax.axis_index("section")
    f = lax.axis_index("fsdp")
    place = lax.axis_index("seq")
    upper = c == 0
    rows = inputs.shape[2]
    width = INNER // n
    heads = HEADS // n
    share = D // n
    half = share // 2
    group = GROUP // n
    ids = jnp.stack([f, c]).astype(jnp.int32)
    tie = lax.optimization_barrier

    def pick(a, b):
        return jnp.where(upper, a, b)

    w = w_in[0].T

    def cut(first, size):
        return lax.dynamic_slice_in_dim(w, first, size, 0)

    def piece_z(m):
        return cut((f ^ m) * width, width)

    def piece_x(m):
        return jnp.concatenate(
            [
                cut(INNER + (f ^ m) * width, width),
                w[2 * INNER : 2 * INNER + GROUP],
                cut(2 * INNER + GROUP + (f ^ m) * heads, heads),
            ]
        )

    def fetch(pieces, layer):
        pairs = lambda m: [(layer * n + i, layer * n + (i ^ m)) for i in range(n)]
        near = [
            v if m == 0 else lax.ppermute(v, ("section", "fsdp"), pairs(m))
            for m, v in enumerate(pieces)
        ]
        return near, [lax.ppermute(v, "section", [(layer, 1 - layer)]) for v in near]

    def whole_slot(v):
        return joined(to_all(v.reshape(n * rows, share)))

    pack = jnp.concatenate(
        [
            gain_in[0],
            dt_bias[0],
            a_log[0],
            d_skip[0],
            gain_out[0],
            conv_w[0].reshape(-1),
            conv_b[0],
        ]
    )
    more = -(-pack.shape[0] // (16 * share)) * 16
    filled = jnp.concatenate([pack, jnp.zeros((more * share - pack.shape[0],), BF16)])
    filled = jnp.broadcast_to(filled.reshape(1, more, share), (n, more, share))
    first = exchange(jnp.concatenate([quarters(at(inputs, c)[0]), filled], axis=1))
    first, pieces_x = tie((first, [piece_x(m) for m in range(n)]))
    part_h0 = first[:, :rows]
    mine = first[:, rows:].reshape(n, -1)[:, : pack.shape[0]]
    near_x0, far_x0 = fetch(pieces_x, 0)
    part_h0 = in_group(part_h0)
    near_x0, part_h0 = tie((near_x0, part_h0))
    far_x0 = [lax.ppermute(v, "section", [(0, 1)]) for v in near_x0]
    pieces_z, part_h0 = tie(([piece_z(m) for m in range(n)], part_h0))
    all_h0 = whole_slot(part_h0)
    near_z0, far_z0 = fetch(pieces_z, 0)

    theirs = swap_section(mine)
    small = []
    for full in (pick(mine, theirs), pick(theirs, mine)):
        full = full.astype(F32)
        used = 0

        def take(size):
            nonlocal used
            used += size
            return full[:, used - size : used]

        gain = take(share).reshape(1, D)
        hp = [at(take(heads), f)[None] for _ in range(3)]
        hp = jnp.concatenate([hp[0], -jnp.exp(hp[1]), hp[2], jnp.zeros((5, heads), F32)])
        gout = at(take(width), f)[None]
        per = CHANNELS // n
        taps = take(KERNEL * per).reshape(n, KERNEL, per).transpose(1, 0, 2)
        bias = take(per).reshape(1, CHANNELS)
        table = jnp.concatenate(
            [taps.reshape(KERNEL, CHANNELS), bias, jnp.zeros((3, CHANNELS), F32)]
        )
        cw = jnp.concatenate(
            [lax.dynamic_slice_in_dim(table, f * width, width, 1), table[:, INNER:]], axis=1
        )
        small.append((gain, cw, hp, gout))

    win = [(near_z0, far_z0, near_x0, far_x0), None]
    expand = (
        jnp.arange(heads)[:, None] == jnp.arange(width)[None, :] // HEAD_DIM
    ).astype(BF16)
    zero_state = jnp.zeros((STATE, width), F32)
    zero_edge = jnp.zeros((8, width + GROUP), F32)

    def project_x(normed, layer):
        return project(ids, normed, win[layer][2], win[layer][3], layer)

    def project_z(normed, layer):
        return project(ids, normed, win[layer][0], win[layer][1], layer)

    def decay_of(px, hp):
        decay = jax.nn.softplus(px[:, width + GROUP :] + hp[0:1]) * hp[1:2]
        return jnp.repeat(jnp.exp(jnp.sum(decay, axis=0)), HEAD_DIM)[None, :]

    def scan(px, layer):
        _, cw, hp, _ = small[layer]
        args = (px, cw, hp)
        if segments == 1:
            return run_forward(*args, zero_state, zero_edge, rows), zero_state
        edge = next_segment(px[-8:, : width + GROUP], 1)
        local = run_forward(*args, zero_state, edge, rows)[2][-1]
        state = relay(decay_of(px, hp), local, False)
        return run_forward(*args, state, edge, rows), state

    def unscan(pz, px, fwd, dn, rc, layer):
        (y, filt, states), state = fwd
        _, cw, hp, gout = small[layer]
        args = (pz, px, y, filt, dn, rc, states, state, cw, hp, expand, gout)
        if segments == 1:
            return run_backward(*args, zero_state, zero_edge, rows, n)[:6]
        local = run_backward(*args, zero_state, zero_edge, rows, n)[6]
        grad = relay(decay_of(px, hp), local, True)
        edge = next_segment(run_backward(*args, grad, zero_edge, rows, n)[7], -1)
        return run_backward(*args, grad, edge, rows, n)[:6]

    def gate(pz, y):
        return y * jax.nn.silu(pz)

    def gated(pz, y, r, layer):
        return (gate(pz, y) * r[:, None] * small[layer][3]).astype(BF16)

    def sum_of_shares(v):
        return jnp.sum(to_all(v), axis=0)

    normed_in0 = normalised(all_h0.astype(F32), small[0][0]).astype(BF16)
    px0 = project_x(normed_in0, 0)
    px0, pieces_x1, pieces_z1, own_ct, wo_mine, own_len = tie(
        (px0, pieces_x, pieces_z, at(cotangent, c)[0], w_out[0], at(lengths, c))
    )
    near_x1, far_x1 = fetch(pieces_x1, 1)
    wo_other = swap_section(wo_mine)
    wo = (pick(wo_mine, wo_other), pick(wo_other, wo_mine))
    slot_pairs = [
        ((j * n + i) * n + k, (j * n + k) * n + i)
        for j in range(segments)
        for i in range(n)
        for k in range(n)
    ]
    length = lax.ppermute(own_len, ("seq", "fsdp"), slot_pairs)
    first_row = (place // n) * n * rows
    all_valid = first_row + jnp.arange(n * rows, dtype=jnp.int32) < length[0]
    all_valid = all_valid.astype(F32)[:, None]
    own_rows = lambda v: lax.dynamic_slice_in_dim(v, f * rows, rows, 0)
    valid = own_rows(all_valid)
    h0 = own_rows(all_h0)
    fwd0, near_z0, wo = tie((scan(px0, 0), near_z0, wo))
    far_z0 = [lax.ppermute(v, "section", [(0, 1)]) for v in near_z0]
    win[0] = (near_z0, far_z0, near_x0, far_x0)
    pz0 = project_z(normed_in0, 0)
    g0 = gate(pz0, fwd0[0][0])
    stat0 = jnp.sum(g0 * g0, axis=1)
    stat0 = sum_of_shares(stat0.reshape(n, rows)).reshape(-1)
    r0 = lax.rsqrt(stat0 / INNER + EPS)
    normed0 = gated(pz0, fwd0[0][0], r0, 0)
    normed0, near_x1, own_ct = tie((normed0, near_x1, own_ct))
    part_ct = in_group(exchange(quarters(own_ct)))
    far_x1 = [lax.ppermute(v, "section", [(1, 0)]) for v in near_x1]
    mixed0 = scatter_sum(jnp.dot(normed0, wo[0], preferred_element_type=F32))
    mixed0, part_ct, pieces_z1 = tie((mixed0, part_ct, pieces_z1))
    near_z1, far_z1 = fetch(pieces_z1, 1)
    out0 = valid * (h0.astype(F32) + mixed0)
    h1 = out0.astype(BF16)

    normed_in1 = gather_rows(normalised(h1.astype(F32), small[1][0]).astype(BF16))
    normed_in1, far_x1 = tie((normed_in1, far_x1))
    win[1] = (near_z1, far_z1, near_x1, far_x1)
    px1 = project_x(normed_in1, 1)
    px1, near_z1, part_ct = tie((px1, near_z1, part_ct))
    far_z1 = [lax.ppermute(v, "section", [(1, 0)]) for v in near_z1]
    win[1] = (near_z1, far_z1, near_x1, far_x1)
    all_ct = whole_slot(part_ct)
    fwd1 = scan(px1, 1)
    fwd1, all_ct = tie((fwd1, all_ct))
    dout1 = own_rows(all_ct).astype(F32)
    dmixed1 = (all_valid * all_ct.astype(F32)).astype(BF16)
    dn1 = dot_cols(dmixed1, wo[1])
    pz1 = project_z(normed_in1, 1)
    g1 = gate(pz1, fwd1[0][0])
    stat1 = sum_of_shares(
        jnp.stack(
            [
                jnp.sum(g1 * g1, axis=1).reshape(n, rows),
                jnp.sum(g1 * dn1 * small[1][3], axis=1).reshape(n, rows),
            ]
        )
    ).reshape(2, -1)
    r1 = lax.rsqrt(stat1[0] / INNER + EPS)
    normed1 = gated(pz1, fwd1[0][0], r1, 1)

    part_width = width // 2

    def cut_half(v, k):
        size = v.shape[1] // 2
        return lax.dynamic_slice_in_dim(v, k * size, size, 1)

    def narrow_of(parts, k):
        return jnp.concatenate([cut_half(v, k) for v in parts], axis=1)

    def away_in(normed_in, part, narrow=()):
        away = [dot_rows(normed_in, cut_half(part, 1 - c)).astype(BF16)]
        if narrow:
            away.append(dot_rows(narrow_of(narrow, 1 - c), normed_in).astype(BF16))
        return [swap_section(v) for v in away]

    def own_in_piece(normed_in, part, away, narrow=()):
        total = dot_rows(normed_in, cut_half(part, c)) + away[0].astype(F32)
        result = total.astype(BF16).reshape(n, share, -1)
        if narrow:
            total = (dot_rows(narrow_of(narrow, c), normed_in) + away[1].astype(F32)).astype(BF16)
            fill = jnp.zeros((-total.shape[0] % 64, D), BF16)
            rest = jnp.concatenate([total, fill]).reshape(-1, n, share).transpose(1, 0, 2)
            result = jnp.concatenate([result, rest], axis=1)
        return result

    def away_out(normed, dmixed):
        return swap_section(dot_rows(cut_half(normed, 1 - c), dmixed).astype(BF16))

    def own_out_piece(normed, dmixed, away):
        return (dot_rows(cut_half(normed, c), dmixed) + away.astype(F32)).astype(BF16)

    def with_group(dxs, dbc):
        total = jnp.sum(exchange(dbc), axis=0).astype(BF16)
        column = jnp.arange(GROUP)[None, :] // group
        own = jnp.where(column == f, jnp.concatenate([total] * n, axis=1), 0)
        full = lax.dynamic_update_slice(dxs, own.astype(BF16), (0, width))
        return full, (dxs[:, :width], [total, dxs[:, width + GROUP :]])

    def back_in(dz, full, layer, kind):
        near_z, far_z, near_x, far_x = win[layer]
        return project_back(ids, dz, full, (near_z, near_x), (far_z, far_x), layer, kind)

    def back_norm(dout, dnormed_in, h, gain):
        h = h.astype(F32)
        r = lax.rsqrt(jnp.mean(h * h, axis=-1, keepdims=True) + EPS)
        u = dnormed_in * gain
        mean = jnp.mean(u * h, axis=-1, keepdims=True)
        dgain = jnp.sum(dnormed_in * h * r, axis=0)
        return valid * dout + r * u - h * (r * r * r) * mean, dgain

    def scales(r, coef):
        top = jnp.stack([r.reshape(n, rows), coef.reshape(n, rows)], axis=1)
        return jnp.concatenate([top, jnp.zeros((n, 6, rows), F32)], axis=1)

    def packed(dgin, d, out, mixed):
        dgain, dconv, dhp = d[3][0], d[4][:5], d[5][:3]
        put = lambda v, size, at_lane: lax.dynamic_update_slice(
            jnp.zeros(v.shape[:-1] + (size,), F32), v, (0,) * (v.ndim - 1) + (at_lane,)
        )
        conv = put(dconv[:, :width], CHANNELS, f * width)
        conv = conv.at[:, INNER:].set(dconv[:, width:])
        totals = jnp.stack(
            [jnp.sum(out * out), jnp.sum((valid * mixed) ** 2), jnp.sum(valid)]
        )
        return jnp.concatenate(
            [
                dgin,
                conv.reshape(-1),
                put(dhp, HEADS, f * heads).reshape(-1),
                put(dgain, INNER, f * width),
                totals,
            ]
        )

    def hand_over(v, layer):
        return lax.ppermute(v, "section", [(1 - layer, layer)])

    sums = SeqSums()
    rc1 = scales(r1, (r1 * r1 * r1 / INNER) * stat1[1])
    away = away_out(normed1, dmixed1)
    o1 = sums.add(own_out_piece(normed1, dmixed1, away))
    rc1, normed1, dn1 = sums.end((rc1, normed1, dn1))

    sums.begin()
    d1 = unscan(pz1, px1, fwd1, dn1, rc1, 1)
    mixed1 = scatter_sum(jnp.dot(normed1, wo[1], preferred_element_type=F32).astype(BF16))
    d1, mixed1 = sums.end((d1, mixed1))

    sums.begin()
    away = away_in(normed_in1, d1[0])
    full1, xs1 = with_group(d1[1], d1[2])
    back1 = back_in(d1[0], full1, 1, F32)
    gz = own_in_piece(normed_in1, d1[0], away)
    out1 = valid * (h1.astype(F32) + mixed1)
    back_h = exchange(quarters(jnp.concatenate([h1, out1.astype(BF16)])))
    back1, xs1, full1, gz, out1, back_h = sums.end((back1, xs1, full1, gz, out1, back_h))
    z1 = sums.add(gz)

    sums.begin()
    dnin1 = scatter_sum(back1)
    away = away_in(normed_in1, *xs1)
    gx = own_in_piece(normed_in1, xs1[0], away, xs1[1])
    back_h = in_group(back_h)
    dnin1, gx, back_h = sums.end((dnin1, gx, back_h))
    x1 = sums.add(gx)

    sums.begin()
    grad1, dgin1 = back_norm(dout1, dnin1, h1, small[1][0])
    dout0 = grad1.astype(BF16).astype(F32)
    dmixed0_own = (valid * dout0).astype(BF16)
    dmixed0 = gather_rows(dmixed0_own)
    along0 = to_all(jnp.sum(dmixed0_own.astype(F32) * mixed0, axis=-1)).reshape(-1)
    rc0 = scales(r0, (r0 * r0 / INNER) * along0)
    back_h = joined(exchange(back_h))
    grad1, dgin1, dmixed0, rc0, back_h = sums.end((grad1, dgin1, dmixed0, rc0, back_h))

    sums.begin()
    dn0 = dot_cols(dmixed0, wo[0])
    d0 = unscan(pz0, px0, fwd0, dn0, rc0, 0)
    go = own_out_piece(normed0, dmixed0, away_out(normed0, dmixed0))
    d0, go = sums.end((d0, go))
    o0 = sums.add(go)

    sums.begin()
    away = away_in(normed_in0, d0[0])
    full0, xs0 = with_group(d0[1], d0[2])
    gz = own_in_piece(normed_in0, d0[0], away)
    away = away_in(normed_in0, *xs0)
    gx = own_in_piece(normed_in0, xs0[0], away, xs0[1])
    full0, gz, gx = sums.end((full0, gz, gx))
    z0 = sums.add(gz)

    sums.begin()
    gx = exchange(gx)
    back0 = back_in(d0[0], full0, 0, BF16)
    gx, back0 = sums.end((gx, back0))
    x0 = sums.add(gx)

    def hand_over(v, layer):
        return lax.ppermute(v, "section", [(1 - layer, layer)])

    sums.finish([o1, z1])
    sums.begin()
    dnin0 = scatter_sum(back0)
    own_z1 = exchange(sums.values[z1])
    own_o1 = sums.values[o1]
    away_o1 = hand_over(own_o1, 1)
    dnin0, own_z1, own_o1, away_o1 = sums.end((dnin0, own_z1, own_o1, away_o1))

    sums.finish([x1, o0])
    sums.begin()
    own_x1 = exchange(sums.values[x1])
    away_z1 = hand_over(own_z1, 1)
    own_o0 = sums.values[o0]
    away_o0 = hand_over(own_o0, 0)
    grad0, dgin0 = back_norm(dout0, dnin0, h0, small[0][0])
    back_g = exchange(quarters(jnp.concatenate([grad0.astype(BF16), grad1.astype(BF16)])))
    p = jnp.stack([packed(dgin0, d0, out0, mixed0), packed(dgin1, d1, out1, mixed1)])
    p = p + swap_section(p)
    p, back_g, own_x1, own_z1, away_z1, own_o0, away_o0 = sums.end(
        (p, back_g, own_x1, own_z1, away_z1, own_o0, away_o0)
    )

    sums.finish([z0])
    sums.begin()
    back_g = in_group(back_g)
    own_z0 = exchange(sums.values[z0])
    away_x1 = hand_over(own_x1, 1)
    m = 1
    while m < n:
        p = p + move_fsdp(p, m)
        m *= 2
    m = 1
    while m < nz:
        p = p + move_seq(p, m)
        m *= 2
    p, back_g, own_z0, own_x1, away_x1 = sums.end((p, back_g, own_z0, own_x1, away_x1))
    sums.finish([x0])
    away_z0 = hand_over(own_z0, 0)
    own_x0 = sums.values[x0]
    away_x0 = hand_over(own_x0, 0)
    back_g = joined(exchange(back_g))
    p = pick(p[0], p[1])
    back = jnp.concatenate([back_h, back_g])

    used = 0

    def part(size):
        nonlocal used
        used += size
        return p[used - size : used]

    mine_of = lambda v, size: lax.dynamic_slice_in_dim(v, f * size, size, v.ndim - 1)
    o_gain_in = mine_of(part(D), share)
    o_conv = mine_of(part(5 * CHANNELS).reshape(5, CHANNELS), CHANNELS // n)
    o_heads = mine_of(part(3 * HEADS).reshape(3, HEADS), heads)
    o_gain_out = mine_of(part(INNER), width)
    totals = part(3)
    act_rms = jnp.sqrt(totals[:2] / (totals[2] * D))[None]

    held = [
        [(own_z0, own_x0, own_o0), (own_z1, own_x1, own_o1)],
        [(away_z0, away_x0, away_o0), (away_z1, away_x1, away_o1)],
    ]

    def both_halves(a, b):
        return jnp.stack([pick(a, b), pick(b, a)], axis=1)

    rows_of = GROUP // n // 2, HEADS // n // 2
    narrow = [pick(side[0][1], side[1][1])[:, share : share + sum(rows_of)] for side in held]
    narrow = both_halves(*[v.astype(F32) for v in narrow])
    small_in = jnp.concatenate(
        [
            narrow[:, :, : rows_of[0]].reshape(GROUP, share),
            narrow[:, :, rows_of[0] :].reshape(HEADS, share),
        ]
    )
    g_w_in = []
    shape_in = (2 * INNER + GROUP + HEADS, share)
    for k, rows_of_small in ((0, None), (1, (2 * INNER, GROUP + HEADS))):
        arrays, plan = [], []
        for s in range(2):
            arrays += [held[s][0][k], held[s][1][k]]
            firsts = tuple(k * INNER + q * width for q in range(n))
            plan.append((len(arrays) - 2, len(arrays) - 1, s, firsts))
        g_w_in = [
            place_in(
                ids, arrays, tuple(plan), small_in, rows_of_small, g_w_in, shape_in, part_width
            )
        ]
    halves_out = [pick(side[0][2], side[1][2]) for side in held]
    g_w_out = jnp.concatenate([pick(*halves_out), pick(*halves_out[::-1])]).astype(F32)

    back = back.reshape(2, 2, rows, D)
    kept_back = pick(back[:, 0], back[:, 1])
    other_back = swap_section(pick(back[:, 1], back[:, 0]))
    both_back = jnp.stack(
        [pick(kept_back, other_back), pick(other_back, kept_back)], axis=1
    )
    return (
        both_back[0][None, :, None],
        both_back[1].astype(F32)[None, :, None],
        o_gain_in[None],
        g_w_in[0].T[None],
        o_conv[None, :4],
        o_conv[None, 4],
        o_heads[None, 0],
        o_heads[None, 1],
        o_heads[None, 2],
        o_gain_out[None],
        g_w_out[None],
        act_rms,
    )


def solution(mesh):
    in_specs = (
        P(None, "fsdp", "seq", None),
        P(None, "fsdp", "seq", None),
        P(None, "fsdp"),
        P("section", "fsdp"),
        P("section", "fsdp", None),
        P("section", None, "fsdp"),
        P("section", "fsdp"),
        P("section", "fsdp"),
        P("section", "fsdp"),
        P("section", "fsdp"),
        P("section", "fsdp"),
        P("section", "fsdp", None),
    )
    out_specs = (
        P("section", None, "fsdp", "seq", None),
        P("section", None, "fsdp", "seq", None),
        P("section", "fsdp"),
        P("section", "fsdp", None),
        P("section", None, "fsdp"),
        P("section", "fsdp"),
        P("section", "fsdp"),
        P("section", "fsdp"),
        P("section", "fsdp"),
        P("section", "fsdp"),
        P("section", "fsdp", None),
        P("section", None),
    )
    return jax.shard_map(
        per_device, mesh=mesh, in_specs=in_specs, out_specs=out_specs, check_vma=False
    )
```

```python
import functools

import jax
import jax.numpy as jnp
from jax import lax
from jax.experimental import pallas as pl
from jax.experimental.pallas import tpu as pltpu
from jax.sharding import PartitionSpec as P

D = 2048
INNER = 4096
HEADS = 64
HEAD_DIM = 64
STATE = 128
KERNEL = 4
GROUP = 2 * STATE
CHANNELS = INNER + GROUP
LANES = 128
EPS = 1e-05
F32 = jnp.float32
BF16 = jnp.bfloat16
VMEM_BYTES = 48 * 1024 * 1024


def split(v):
    hi = v.astype(BF16)
    return hi, (v - hi.astype(F32)).astype(BF16)


def dot32(a, b, ca, cb):
    (ah, al), (bh, bl) = (v if isinstance(v, tuple) else split(v) for v in (a, b))
    one = lambda p, q: lax.dot_general(
        p, q, (((ca,), (cb,)), ((), ())), preferred_element_type=F32
    )
    return one(ah, bh) + (one(ah, bl) + one(al, bh))


def step_sizes(raw, hp, rows):
    shifted = raw + hp[0:1, :]
    dt = jnp.maximum(shifted, 0.0) + jnp.log1p(jnp.exp(-jnp.abs(shifted)))
    decay = dt * hp[1:2, :]
    row = lax.broadcasted_iota(jnp.int32, (rows, rows), 0)
    col = lax.broadcasted_iota(jnp.int32, (rows, rows), 1)
    lower = (row >= col).astype(F32)
    cum = dot32(lower, decay, 1, 0)
    cum_t = dot32(decay, lower, 0, 1)
    return shifted, dt, cum, cum_t, row, col, lower


def pair_lanes(v, j, first):
    return jnp.where(first, v[:, 2 * j : 2 * j + 1], v[:, 2 * j + 1 : 2 * j + 2])


def head_sums(v, table):
    hi, low = split(v)
    one = lambda p: lax.dot_general(
        p, table, (((1,), (1,)), ((), ())), preferred_element_type=F32
    )
    return one(hi) + one(low)


def forward_kernel(proj, cw, hp, s0, e0, y_ref, filt_ref, st_ref, state, xp, xw_s, last_s):
    i = pl.program_id(0)
    rows, width = y_ref.shape

    @pl.when(i == 0)
    def _():
        state[...] = s0[...]
        xp[0:8, :] = e0[...]

    xp[8 : 8 + rows, :] = proj[:, : width + GROUP]

    def conv_tile(lo):
        acc = cw[4:5, lo : lo + LANES]
        for k in range(KERNEL):
            acc = acc + cw[k : k + 1, lo : lo + LANES] * xp[5 + k : 5 + k + rows, lo : lo + LANES]
        filt_ref[:, lo : lo + LANES] = acc
        return acc * jax.nn.sigmoid(acc)

    b_c = conv_tile(width)
    c_c = conv_tile(width + STATE)
    _, dt, cum, cum_t, row, col, _ = step_sizes(proj[:, width + GROUP :], hp, rows)
    last = cum[rows - 1 : rows, :]
    ecum = jnp.exp(cum)
    weight = jnp.exp(last - cum) * dt
    elast = jnp.exp(last)
    b_c, c_c = split(b_c), split(c_c)
    carried = dot32(c_c, state[...], 1, 0)
    scores = dot32(c_c, b_c, 1, 1)
    causal = row >= col
    lane = lax.broadcasted_iota(jnp.int32, (rows, LANES), 1)
    first = lane < HEAD_DIM
    for j in range(width // LANES):
        lo = j * LANES
        here = slice(lo, lo + LANES)
        x = conv_tile(lo)
        xd = x * pair_lanes(dt, j, first)
        m = []
        for h in (2 * j, 2 * j + 1):
            gap = cum[:, h : h + 1] - cum_t[h : h + 1, :]
            m.append(jnp.exp(jnp.where(causal, gap, -1e30)) * scores)
        xd2 = jnp.concatenate([jnp.where(first, xd, 0.0), jnp.where(first, 0.0, xd)])
        y = (
            dot32(jnp.concatenate(m, axis=1), xd2, 1, 0)
            + carried[:, here] * pair_lanes(ecum, j, first)
            + pair_lanes(hp[2:3, :], j, first[0:1]) * x
        )
        y_ref[:, here] = y
        xw_s[:, here] = x * pair_lanes(weight, j, first)
        last_s[0:1, here] = pair_lanes(elast, j, first[0:1])
    state[...] = state[...] * last_s[0:1, :] + dot32(b_c, xw_s[...], 0, 0)
    st_ref[0] = state[...]
    xp[0:8, :] = xp[rows : rows + 8, :]


def backward_kernel(
    pz,
    proj,
    y_ref,
    filt,
    dn,
    rc,
    st_before,
    st_out,
    s0,
    cw,
    hp,
    table,
    gain,
    g0,
    e0,
    dz_ref,
    dproj,
    dbc_ref,
    dgain_ref,
    dconv_ref,
    dhp_ref,
    gfin_ref,
    efin_ref,
    grad,
    dfp,
    both,
    xw_s,
    dyc_s,
    rowv,
):
    i = pl.program_id(0)
    rows, width = y_ref.shape
    heads = hp.shape[1]

    @pl.when(i == 0)
    def _():
        grad[...] = g0[...]
        dfp[rows : rows + 8, :] = e0[...]
        dgain_ref[...] = jnp.zeros_like(dgain_ref)
        dconv_ref[...] = jnp.zeros_like(dconv_ref)
        dhp_ref[...] = jnp.zeros_like(dhp_ref)

    def silu_pair(v):
        s = jax.nn.sigmoid(v)
        a = v * s
        return a, s * (1.0 + v - a)

    b_c, b_d = silu_pair(filt[:, width : width + STATE])
    c_c, c_d = silu_pair(filt[:, width + STATE :])
    shifted, dt, cum, cum_t, row, col, lower = step_sizes(proj[:, width + GROUP :], hp, rows)
    last = cum[rows - 1 : rows, :]
    tail = jnp.exp(last - cum)
    ecum = jnp.exp(cum)
    elast = jnp.exp(last)
    b_c, c_c = split(b_c), split(c_c)
    grad_p = split(grad[...])
    k_all = dot32(b_c, grad_p, 1, 0)
    scores_t = dot32(b_c, c_c, 1, 1)
    causal_t = row <= col
    lane = lax.broadcasted_iota(jnp.int32, (rows, LANES), 1)
    first = lane < HEAD_DIM
    dcb_t = jnp.zeros((rows, rows), F32)
    rc_t = dot32((row == col).astype(F32), rc[0], 1, 1)
    r = rc_t[:, 0:1]
    coef = rc_t[:, 1:2]
    rowv[0:1, :] = jnp.sum(grad[...] * st_out[0], axis=0, keepdims=True)
    for j in range(width // LANES):
        lo = j * LANES
        here = slice(lo, lo + LANES)
        z = pz[:, here]
        y = y_ref[:, here]
        sz, dsz = silu_pair(z)
        g = y * sz
        dnt = dn[:, here]
        dg = dnt * gain[0:1, here] * r - g * coef
        dgain_ref[0:1, here] += jnp.sum(dnt * g * r, axis=0, keepdims=True)
        dy = dg * sz
        dz_ref[:, here] = (dg * y * dsz).astype(BF16)
        x, xder = silu_pair(filt[:, here])
        dt_e = pair_lanes(dt, j, first)
        tail_e = pair_lanes(tail, j, first)
        xd = x * dt_e
        dy2 = split(jnp.concatenate([jnp.where(first, dy, 0.0), jnp.where(first, 0.0, dy)]))
        decays = []
        for h in (2 * j, 2 * j + 1):
            gap = cum_t[h : h + 1, :] - cum[:, h : h + 1]
            decays.append(jnp.exp(jnp.where(causal_t, gap, -1e30)))
        m = jnp.concatenate([d * scores_t for d in decays], axis=1)
        dm = dot32(xd, dy2, 1, 1)
        dcb_t = dcb_t + (decays[0] * dm[:, :rows] + decays[1] * dm[:, rows:])
        v = dot32(m, dy2, 1, 0) + k_all[:, here] * tail_e
        skip = pair_lanes(hp[2:3, :], j, first[0:1])
        dx = dt_e * v + skip * dy
        both[0:rows, here] = x * v
        both[rows : 2 * rows, here] = dy * (y - skip * x)
        rowv[1:2, here] = jnp.sum(dy * x, axis=0, keepdims=True)
        rowv[2:3, here] = pair_lanes(elast, j, first[0:1])
        xw_s[:, here] = xd * tail_e
        dyc_s[:, here] = dy * pair_lanes(ecum, j, first)
        dfp[0:rows, here] = dx * xder
    dcb_t = split(dcb_t)
    dyc = split(dyc_s[...])
    st_in = jnp.where(i == pl.num_programs(0) - 1, s0[...], st_before[0])
    dc = dot32(dcb_t, b_c, 0, 0) + dot32(dyc, st_in, 1, 1)
    db = dot32(dcb_t, c_c, 1, 0) + dot32(xw_s[...], grad_p, 1, 1)
    dfp[0:rows, width : width + STATE] = db * b_d
    dfp[0:rows, width + STATE :] = dc * c_d
    grad[...] = grad[...] * rowv[2:3, :] + dot32(c_c, dyc, 0, 0)
    gfin_ref[...] = grad[...]

    sums = head_sums(both[...], table[...])
    rsums = head_sums(rowv[...], table[...])
    ddt_x = sums[0:rows]
    dcum = sums[rows : 2 * rows] - dt * ddt_x
    upto = lax.broadcasted_iota(jnp.int32, (rows, heads), 0)
    dcum = dcum + jnp.where(upto == rows - 1, rsums[0:1, :], 0.0)
    ddecay = dot32(lower, dcum, 0, 0)
    ddt = ddt_x + hp[1:2, :] * ddecay
    draw = ddt * jax.nn.sigmoid(shifted)
    dproj[:, width + GROUP :] = draw.astype(BF16)
    dhp_ref[0:1, :] += jnp.sum(draw, axis=0, keepdims=True)
    dhp_ref[1:2, :] += jnp.sum(ddecay * dt, axis=0, keepdims=True) * hp[1:2, :]
    dhp_ref[2:3, :] += rsums[1:2, :]

    for lo in range(0, width + GROUP, LANES):
        here = slice(lo, lo + LANES)
        src = proj[:, here]
        total = jnp.zeros((rows, LANES), F32)
        for k in range(KERNEL):
            shift = KERNEL - 1 - k
            moved = dfp[shift : shift + rows, here]
            total = total + cw[k : k + 1, here] * moved
            dconv_ref[k : k + 1, here] += jnp.sum(src * moved, axis=0, keepdims=True)
        dconv_ref[4:5, here] += jnp.sum(dfp[0:rows, here], axis=0, keepdims=True)
        if lo < width:
            dproj[:, here] = total.astype(BF16)
        else:
            dproj[:, here] = jnp.zeros((rows, LANES), BF16)
            share = dbc_ref.shape[2]
            for k in range(LANES // share):
                dbc_ref[(lo - width) // share + k] = total[:, k * share : (k + 1) * share]
    dfp[rows : rows + 8, :] = dfp[0:8, :]
    efin_ref[...] = dfp[0:8, :]


def whole(shape):
    return pl.BlockSpec(shape, lambda i: (0,) * len(shape))


def run_forward(proj, cw, hp, s0, e0, rows):
    total, width = proj.shape[0], s0.shape[1]
    count = total // rows
    block = lambda w: pl.BlockSpec((rows, w), lambda i: (i, 0))
    shape = jax.ShapeDtypeStruct
    return pl.pallas_call(
        forward_kernel,
        grid=(count,),
        in_specs=[block(proj.shape[1])] + [whole(v.shape) for v in (cw, hp, s0, e0)],
        out_specs=[
            block(width),
            block(width + GROUP),
            pl.BlockSpec((1, STATE, width), lambda i: (i, 0, 0)),
        ],
        scratch_shapes=[
            pltpu.VMEM((STATE, width), F32),
            pltpu.VMEM((rows + 8, width + GROUP), F32),
            pltpu.VMEM((rows, width), F32),
            pltpu.VMEM((8, width), F32),
        ],
        out_shape=[
            shape((total, width), F32),
            shape((total, width + GROUP), F32),
            shape((count, STATE, width), F32),
        ],
        compiler_params=pltpu.CompilerParams(vmem_limit_bytes=VMEM_BYTES),
        name="scan_forward",
    )(proj, cw, hp, s0, e0)


def run_backward(pz, proj, y, filt, dn, rc, states, s0, cw, hp, table, gain, g0, e0, rows, places):
    total, (heads, width) = proj.shape[0], table.shape
    count = total // rows
    turn = lambda i: count - 1 - i
    block = lambda w: pl.BlockSpec((rows, w), lambda i: (turn(i), 0))
    shape = jax.ShapeDtypeStruct
    share = GROUP // places
    return pl.pallas_call(
        backward_kernel,
        grid=(count,),
        in_specs=[
            block(width),
            block(proj.shape[1]),
            block(width),
            block(width + GROUP),
            block(width),
            pl.BlockSpec((1, 8, rows), lambda i: (turn(i), 0, 0)),
            pl.BlockSpec((1, STATE, width), lambda i: (jnp.maximum(turn(i) - 1, 0), 0, 0)),
            pl.BlockSpec((1, STATE, width), lambda i: (turn(i), 0, 0)),
        ]
        + [whole(v.shape) for v in (s0, cw, hp, table, gain, g0, e0)],
        out_specs=[
            block(width),
            block(proj.shape[1]),
            pl.BlockSpec((places, rows, share), lambda i: (0, turn(i), 0)),
            whole((8, width)),
            whole((8, width + GROUP)),
            whole((8, heads)),
            whole((STATE, width)),
            whole((8, width + GROUP)),
        ],
        scratch_shapes=[
            pltpu.VMEM((STATE, width), F32),
            pltpu.VMEM((rows + 8, width + GROUP), F32),
            pltpu.VMEM((2 * rows, width), F32),
            pltpu.VMEM((rows, width), F32),
            pltpu.VMEM((rows, width), F32),
            pltpu.VMEM((8, width), F32),
        ],
        out_shape=[
            shape((total, width), BF16),
            shape(proj.shape, BF16),
            shape((places, total, share), F32),
            shape((8, width), F32),
            shape((8, width + GROUP), F32),
            shape((8, heads), F32),
            shape((STATE, width), F32),
            shape((8, width + GROUP), F32),
        ],
        compiler_params=pltpu.CompilerParams(vmem_limit_bytes=VMEM_BYTES),
        name="scan_backward",
    )(pz, proj, y, filt, dn, rc, states, states, s0, cw, hp, table, gain, g0, e0)


def bring(step, pieces, buffers, sems, own):
    for near, far, buffer, sem in zip(*pieces, buffers, sems):
        to, done = buffer.at[step % 2], sem.at[step % 2]

        @pl.when(own)
        def _():
            pltpu.make_async_copy(near[step], to, done).start()

        @pl.when(jnp.logical_not(own))
        def _():
            pltpu.make_async_copy(far[step], to, done).start()


def arrived(step, pieces, buffers, sems):
    for near, buffer, sem in zip(pieces[0], buffers, sems):
        pltpu.make_async_copy(near[step], buffer.at[step % 2], sem.at[step % 2]).wait()
    return [buffer.at[step % 2] for buffer in buffers]


def project_kernel(ids, normed, *refs, layer, n):
    near, far = [refs[0:n]], [refs[n : 2 * n]]
    out, buffer, sem = refs[2 * n :]
    pieces = (near, far)
    own = ids[1] == layer
    columns = out.shape[1]
    share = buffer.shape[2]
    bring(0, pieces, [buffer], [sem], own)
    for m in range(n):
        if m + 1 < n:
            bring(m + 1, pieces, [buffer], [sem], own)
        (w,) = arrived(m, pieces, [buffer], [sem])
        from_place = pl.multiple_of(jnp.bitwise_xor(ids[0], m) * share, share)
        a = normed[:, pl.ds(from_place, share)]
        for lo in range(0, columns, 256):
            here = slice(lo, min(lo + 256, columns))
            v = lax.dot_general(
                a, w[here, :], (((1,), (1,)), ((), ())), preferred_element_type=F32
            )
            out[:, here] = v if m == 0 else out[:, here] + v


def project(ids, normed, near, far, layer):
    n = len(near)
    columns, share = near[0].shape
    rows = normed.shape[0]
    vmem = pl.BlockSpec(memory_space=pltpu.VMEM)
    return pl.pallas_call(
        functools.partial(project_kernel, layer=layer, n=n),
        in_specs=[pl.BlockSpec(memory_space=pltpu.SMEM), vmem]
        + [pl.BlockSpec(memory_space=pl.ANY)] * (2 * n),
        out_specs=vmem,
        scratch_shapes=[
            pltpu.VMEM((2, columns, share), BF16),
            pltpu.SemaphoreType.DMA((2,)),
        ],
        out_shape=jax.ShapeDtypeStruct((rows, columns), F32),
        compiler_params=pltpu.CompilerParams(vmem_limit_bytes=VMEM_BYTES),
        cost_estimate=pl.CostEstimate(
            flops=2 * rows * columns * share * n,
            bytes_accessed=columns * share * n * 2 + rows * columns * 4,
            transcendentals=0,
        ),
        name="project",
    )(ids, normed, *near, *far)


def back_kernel(ids, dz, dx, *refs, layer, n):
    near = (refs[0:n], refs[n : 2 * n])
    far = (refs[2 * n : 3 * n], refs[3 * n : 4 * n])
    out, zbuf, xbuf, zsem, xsem = refs[4 * n :]
    pieces = (near, far)
    own = ids[1] == layer
    share = zbuf.shape[2]
    args = ([zbuf, xbuf], [zsem, xsem])
    bring(0, pieces, *args, own)
    for m in range(n):
        if m + 1 < n:
            bring(m + 1, pieces, *args, own)
        wz, wx = arrived(m, pieces, *args)
        for lo in range(0, share, 256):
            here = slice(lo, lo + 256)
            v = jnp.dot(dz[...], wz[:, here], preferred_element_type=F32) + jnp.dot(
                dx[...], wx[:, here], preferred_element_type=F32
            )
            at_lane = pl.multiple_of(jnp.bitwise_xor(ids[0], m) * share + lo, 256)
            out[:, pl.ds(at_lane, 256)] = v.astype(out.dtype)


def project_back(ids, dz, dx, near, far, layer, kind):
    n = len(near[0])
    share = near[0][0].shape[1]
    rows = dz.shape[0]
    columns = dz.shape[1] + dx.shape[1]
    vmem = pl.BlockSpec(memory_space=pltpu.VMEM)
    return pl.pallas_call(
        functools.partial(back_kernel, layer=layer, n=n),
        in_specs=[pl.BlockSpec(memory_space=pltpu.SMEM), vmem, vmem]
        + [pl.BlockSpec(memory_space=pl.ANY)] * (4 * n),
        out_specs=vmem,
        scratch_shapes=[
            pltpu.VMEM((2, dz.shape[1], share), BF16),
            pltpu.VMEM((2, dx.shape[1], share), BF16),
            pltpu.SemaphoreType.DMA((2,)),
            pltpu.SemaphoreType.DMA((2,)),
        ],
        out_shape=jax.ShapeDtypeStruct((rows, n * share), kind),
        compiler_params=pltpu.CompilerParams(vmem_limit_bytes=VMEM_BYTES),
        cost_estimate=pl.CostEstimate(
            flops=2 * rows * columns * share * n,
            bytes_accessed=columns * share * n * 2 + rows * n * share * 2,
            transcendentals=0,
        ),
        name="project_back",
    )(ids, dz, dx, *near[0], *near[1], *far[0], *far[1])


def place_kernel(ids, *refs, plan, count, rows_of_small):
    small = refs[count]
    out, eye, pieces, blocks, in_sem, out_sem = refs[-6:]
    core = ids[1]
    size, share = blocks.shape[1:]

    def fetch(k):
        for layer in range(2):

            @pl.when(core == layer)
            def _():
                src = refs[plan[k][layer]]
                pltpu.make_async_copy(
                    src.at[:, pl.ds(0, share)], pieces.at[k % 2], in_sem.at[k % 2]
                ).start()

    def send(step, first, count):
        return pltpu.make_async_copy(
            blocks.at[step % 2, pl.ds(0, count)],
            out.at[pl.ds(first, count)],
            out_sem.at[step % 2],
        )

    eye[...] = (
        lax.broadcasted_iota(jnp.int32, eye.shape, 0)
        == lax.broadcasted_iota(jnp.int32, eye.shape, 1)
    ).astype(BF16)
    fetch(0)
    sent = []
    for k, (_, _, side, firsts) in enumerate(plan):
        if k + 1 < len(plan):
            fetch(k + 1)
        pltpu.make_async_copy(pieces.at[k % 2], pieces.at[k % 2], in_sem.at[k % 2]).wait()
        shift = jnp.where(side == 0, core, 1 - core) * size
        for p, first in enumerate(firsts):
            step = len(sent)
            if step >= 2:
                sent[step - 2].wait()
            blocks[step % 2] = lax.dot_general(
                pieces[k % 2, p],
                eye[...],
                (((0,), (0,)), ((), ())),
                preferred_element_type=F32,
            )
            sent.append(send(step, pl.multiple_of(first + shift, 8), size))
            sent[-1].start()
    if rows_of_small:
        step = len(sent)
        sent[step - 2].wait()
        first, count = rows_of_small
        sent.append(
            pltpu.make_async_copy(small, out.at[pl.ds(first, count)], out_sem.at[step % 2])
        )
        sent[-1].start()
    sent[-2].wait()
    sent[-1].wait()


def place_in(ids, arrays, plan, small, rows_of_small, before, shape, size):
    places, share = arrays[0].shape[0], shape[1]
    any_space = pl.BlockSpec(memory_space=pl.ANY)
    return pl.pallas_call(
        functools.partial(
            place_kernel, plan=plan, count=len(arrays), rows_of_small=rows_of_small
        ),
        in_specs=[pl.BlockSpec(memory_space=pltpu.SMEM)]
        + [any_space] * len(arrays)
        + [pl.BlockSpec(memory_space=pltpu.VMEM)]
        + [any_space] * len(before),
        out_specs=any_space,
        scratch_shapes=[
            pltpu.VMEM((share, share), BF16),
            pltpu.VMEM((2, places, share, size), BF16),
            pltpu.VMEM((2, size, share), F32),
            pltpu.SemaphoreType.DMA((2,)),
            pltpu.SemaphoreType.DMA((2,)),
        ],
        out_shape=jax.ShapeDtypeStruct(shape, F32),
        input_output_aliases={len(arrays) + 2: 0} if before else {},
        compiler_params=pltpu.CompilerParams(vmem_limit_bytes=VMEM_BYTES),
        name="place_in",
    )(ids, *arrays, small, *before)


def combine_kernel(flags, *refs, adds):
    count = len(adds)
    for k, add in enumerate(adds):
        v, got, out = refs[2 * k], refs[2 * k + 1], refs[2 * count + k]
        if add:
            out[...] = (v[...].astype(F32) + got[...].astype(F32)).astype(BF16)
        else:
            out[...] = jnp.where(flags[k] == 1, got[...], v[...])


def combine(items, flags):
    steps = 8
    shapes = [v.shape for v, _, _ in items]
    flat = [(v.reshape(-1, v.shape[-1]), g.reshape(-1, g.shape[-1])) for v, g, _ in items]
    spec = lambda v: pl.BlockSpec((v.shape[0] // steps, v.shape[1]), lambda i: (i, 0))
    out = pl.pallas_call(
        functools.partial(combine_kernel, adds=tuple(add for _, _, add in items)),
        grid=(steps,),
        in_specs=[pl.BlockSpec(memory_space=pltpu.SMEM)] + [spec(v) for p in flat for v in p],
        out_specs=[spec(v) for v, _ in flat],
        out_shape=[jax.ShapeDtypeStruct(v.shape, BF16) for v, _ in flat],
        compiler_params=pltpu.CompilerParams(vmem_limit_bytes=VMEM_BYTES),
        name="combine",
    )(flags, *[v for p in flat for v in p])
    return [v.reshape(shape) for v, shape in zip(out, shapes)]


def swap_section(v):
    return lax.ppermute(v, "section", [(0, 1), (1, 0)])


def at(v, k):
    return lax.dynamic_index_in_dim(v, k, 0, False)


def exchange(v):
    return lax.all_to_all(v, "fsdp", 0, 0, tiled=True)


def to_all(v):
    n = lax.axis_size("fsdp")
    return exchange(jnp.broadcast_to(v[None], (n,) + v.shape))


def gather_rows(v):
    return to_all(v).reshape(-1, v.shape[-1])


def scatter_sum(partial):
    n = lax.axis_size("fsdp")
    got = exchange(partial.reshape(n, -1, partial.shape[-1]))
    return jnp.sum(got.astype(F32), axis=0)


def in_group(v):
    n, s = lax.axis_size("fsdp"), lax.axis_size("seq")
    groups = [[j * n + i for i in range(n)] for j in range(s // n)]
    return lax.all_to_all(v, "seq", 0, 0, axis_index_groups=groups, tiled=True)


def quarters(v):
    n = lax.axis_size("fsdp")
    return v.reshape(v.shape[0], n, -1).transpose(1, 0, 2)


def joined(v):
    return v.transpose(1, 0, 2).reshape(v.shape[1], -1)


def move_fsdp(v, m):
    n = lax.axis_size("fsdp")
    return lax.ppermute(v, "fsdp", [(k, k ^ m) for k in range(n)])


def move_seq(v, m):
    s = lax.axis_size("seq")
    return lax.ppermute(v, "seq", [(k, k ^ m) for k in range(s)])


class SeqSums:
    def __init__(self):
        s = lax.axis_size("seq")
        half = s // 2
        self.pairs = [[(j, j + 1), (s - 1 - j, s - 2 - j)] for j in range(half - 1)]
        self.pairs.append([(half - 1, half), (half, half - 1)])
        self.inward = half
        self.pairs += [[(j + 1, j), (s - 2 - j, s - 1 - j)] for j in reversed(range(half - 1))]
        self.values, self.phase, self.moving = [], [], []

    def add(self, value):
        self.values.append(value)
        self.phase.append(0)
        return len(self.values) - 1

    def begin(self):
        taken = set()
        for k, step in enumerate(self.phase):
            if step == len(self.pairs) or step in taken:
                continue
            taken.add(step)
            self.moving.append((k, lax.ppermute(self.values[k], "seq", self.pairs[step])))

    def end(self, work):
        place = lax.axis_index("seq")
        items, flags = [], []
        for k, got in self.moving:
            step = self.phase[k]
            items.append((self.values[k], got, step < self.inward))
            here = [place == to for _, to in self.pairs[step]]
            flags.append(functools.reduce(jnp.logical_or, here))
            self.phase[k] = step + 1
        moved = combine(items, jnp.stack(flags).astype(jnp.int32)) if items else []
        still = [k for k, p in enumerate(self.phase) if p == 0]
        work, moved, rest = lax.optimization_barrier(
            (work, moved, [self.values[k] for k in still])
        )
        for (k, _), v in zip(self.moving, moved):
            self.values[k] = v
        for k, v in zip(still, rest):
            self.values[k] = v
        self.moving = []
        return work

    def finish(self, chunks):
        while any(self.phase[k] < len(self.pairs) for k in chunks):
            self.begin()
            self.end(())


def relay(total, local, reverse):
    n, s = lax.axis_size("fsdp"), lax.axis_size("seq")
    segments = s // n
    place = lax.axis_index("seq") // n
    own = lax.axis_index("seq") % n
    totals = lax.all_gather(total, "seq")
    locals_ = lax.all_gather(local, "seq")
    state = jnp.zeros_like(local)
    order = range(segments - 1, -1, -1) if reverse else range(segments)
    for j in order:
        use = (j > place) if reverse else (j < place)
        t = lax.dynamic_index_in_dim(totals, j * n + own, 0, False)
        v = lax.dynamic_index_in_dim(locals_, j * n + own, 0, False)
        state = jnp.where(use, t * state + v, state)
    return state


def next_segment(v, step):
    n, s = lax.axis_size("fsdp"), lax.axis_size("seq")
    pairs = [(k, k + step * n) for k in range(s) if 0 <= k + step * n < s]
    return lax.ppermute(v, "seq", pairs)


def dot_rows(a, b):
    return lax.dot_general(a, b, (((0,), (0,)), ((), ())), preferred_element_type=F32)


def dot_cols(a, b):
    return lax.dot_general(a, b, (((1,), (1,)), ((), ())), preferred_element_type=F32)


def normalised(h, gain):
    return h * lax.rsqrt(jnp.mean(h * h, axis=-1, keepdims=True) + EPS) * gain


def per_device(
    inputs,
    cotangent,
    lengths,
    gain_in,
    w_in,
    conv_w,
    conv_b,
    dt_bias,
    a_log,
    d_skip,
    gain_out,
    w_out,
):
    n = lax.axis_size("fsdp")
    nz = lax.axis_size("seq")
    segments = nz // n
    c = lax.axis_index("section")
    f = lax.axis_index("fsdp")
    place = lax.axis_index("seq")
    upper = c == 0
    rows = inputs.shape[2]
    width = INNER // n
    heads = HEADS // n
    share = D // n
    half = share // 2
    group = GROUP // n
    ids = jnp.stack([f, c]).astype(jnp.int32)
    tie = lax.optimization_barrier

    def pick(a, b):
        return jnp.where(upper, a, b)

    w = w_in[0].T

    def cut(first, size):
        return lax.dynamic_slice_in_dim(w, first, size, 0)

    def piece_z(m):
        return cut((f ^ m) * width, width)

    def piece_x(m):
        return jnp.concatenate(
            [
                cut(INNER + (f ^ m) * width, width),
                w[2 * INNER : 2 * INNER + GROUP],
                cut(2 * INNER + GROUP + (f ^ m) * heads, heads),
            ]
        )

    def fetch(pieces, layer):
        pairs = lambda m: [(layer * n + i, layer * n + (i ^ m)) for i in range(n)]
        near = [
            v if m == 0 else lax.ppermute(v, ("section", "fsdp"), pairs(m))
            for m, v in enumerate(pieces)
        ]
        return near, [lax.ppermute(v, "section", [(layer, 1 - layer)]) for v in near]

    def whole_slot(v):
        return joined(to_all(v.reshape(n * rows, share)))

    pack = jnp.concatenate(
        [
            gain_in[0],
            dt_bias[0],
            a_log[0],
            d_skip[0],
            gain_out[0],
            conv_w[0].reshape(-1),
            conv_b[0],
        ]
    )
    more = -(-pack.shape[0] // (16 * share)) * 16
    filled = jnp.concatenate([pack, jnp.zeros((more * share - pack.shape[0],), BF16)])
    filled = jnp.broadcast_to(filled.reshape(1, more, share), (n, more, share))
    first = exchange(jnp.concatenate([quarters(at(inputs, c)[0]), filled], axis=1))
    first, pieces_x = tie((first, [piece_x(m) for m in range(n)]))
    part_h0 = first[:, :rows]
    mine = first[:, rows:].reshape(n, -1)[:, : pack.shape[0]]
    near_x0, far_x0 = fetch(pieces_x, 0)
    part_h0 = in_group(part_h0)
    near_x0, part_h0 = tie((near_x0, part_h0))
    far_x0 = [lax.ppermute(v, "section", [(0, 1)]) for v in near_x0]
    pieces_z, part_h0 = tie(([piece_z(m) for m in range(n)], part_h0))
    all_h0 = whole_slot(part_h0)
    near_z0, far_z0 = fetch(pieces_z, 0)

    theirs = swap_section(mine)
    small = []
    for full in (pick(mine, theirs), pick(theirs, mine)):
        full = full.astype(F32)
        used = 0

        def take(size):
            nonlocal used
            used += size
            return full[:, used - size : used]

        gain = take(share).reshape(1, D)
        hp = [at(take(heads), f)[None] for _ in range(3)]
        hp = jnp.concatenate([hp[0], -jnp.exp(hp[1]), hp[2], jnp.zeros((5, heads), F32)])
        gout = at(take(width), f)[None]
        per = CHANNELS // n
        taps = take(KERNEL * per).reshape(n, KERNEL, per).transpose(1, 0, 2)
        bias = take(per).reshape(1, CHANNELS)
        table = jnp.concatenate(
            [taps.reshape(KERNEL, CHANNELS), bias, jnp.zeros((3, CHANNELS), F32)]
        )
        cw = jnp.concatenate(
            [lax.dynamic_slice_in_dim(table, f * width, width, 1), table[:, INNER:]], axis=1
        )
        small.append((gain, cw, hp, gout))

    win = [(near_z0, far_z0, near_x0, far_x0), None]
    expand = (
        jnp.arange(heads)[:, None] == jnp.arange(width)[None, :] // HEAD_DIM
    ).astype(BF16)
    zero_state = jnp.zeros((STATE, width), F32)
    zero_edge = jnp.zeros((8, width + GROUP), F32)

    def project_x(normed, layer):
        return project(ids, normed, win[layer][2], win[layer][3], layer)

    def project_z(normed, layer):
        return project(ids, normed, win[layer][0], win[layer][1], layer)

    def decay_of(px, hp):
        decay = jax.nn.softplus(px[:, width + GROUP :] + hp[0:1]) * hp[1:2]
        return jnp.repeat(jnp.exp(jnp.sum(decay, axis=0)), HEAD_DIM)[None, :]

    def scan(px, layer):
        _, cw, hp, _ = small[layer]
        args = (px, cw, hp)
        if segments == 1:
            return run_forward(*args, zero_state, zero_edge, rows), zero_state
        edge = next_segment(px[-8:, : width + GROUP], 1)
        local = run_forward(*args, zero_state, edge, rows)[2][-1]
        state = relay(decay_of(px, hp), local, False)
        return run_forward(*args, state, edge, rows), state

    def unscan(pz, px, fwd, dn, rc, layer):
        (y, filt, states), state = fwd
        _, cw, hp, gout = small[layer]
        args = (pz, px, y, filt, dn, rc, states, state, cw, hp, expand, gout)
        if segments == 1:
            return run_backward(*args, zero_state, zero_edge, rows, n)[:6]
        local = run_backward(*args, zero_state, zero_edge, rows, n)[6]
        grad = relay(decay_of(px, hp), local, True)
        edge = next_segment(run_backward(*args, grad, zero_edge, rows, n)[7], -1)
        return run_backward(*args, grad, edge, rows, n)[:6]

    def gate(pz, y):
        return y * jax.nn.silu(pz)

    def gated(pz, y, r, layer):
        return (gate(pz, y) * r[:, None] * small[layer][3]).astype(BF16)

    def sum_of_shares(v):
        return jnp.sum(to_all(v), axis=0)

    normed_in0 = normalised(all_h0.astype(F32), small[0][0]).astype(BF16)
    px0 = project_x(normed_in0, 0)
    px0, pieces_x1, pieces_z1, own_ct, wo_mine, own_len = tie(
        (px0, pieces_x, pieces_z, at(cotangent, c)[0], w_out[0], at(lengths, c))
    )
    near_x1, far_x1 = fetch(pieces_x1, 1)
    wo_other = swap_section(wo_mine)
    wo = (pick(wo_mine, wo_other), pick(wo_other, wo_mine))
    slot_pairs = [
        ((j * n + i) * n + k, (j * n + k) * n + i)
        for j in range(segments)
        for i in range(n)
        for k in range(n)
    ]
    length = lax.ppermute(own_len, ("seq", "fsdp"), slot_pairs)
    first_row = (place // n) * n * rows
    all_valid = first_row + jnp.arange(n * rows, dtype=jnp.int32) < length[0]
    all_valid = all_valid.astype(F32)[:, None]
    own_rows = lambda v: lax.dynamic_slice_in_dim(v, f * rows, rows, 0)
    valid = own_rows(all_valid)
    h0 = own_rows(all_h0)
    fwd0, near_z0, wo = tie((scan(px0, 0), near_z0, wo))
    far_z0 = [lax.ppermute(v, "section", [(0, 1)]) for v in near_z0]
    win[0] = (near_z0, far_z0, near_x0, far_x0)
    pz0 = project_z(normed_in0, 0)
    g0 = gate(pz0, fwd0[0][0])
    stat0 = jnp.sum(g0 * g0, axis=1)
    stat0 = sum_of_shares(stat0.reshape(n, rows)).reshape(-1)
    r0 = lax.rsqrt(stat0 / INNER + EPS)
    normed0 = gated(pz0, fwd0[0][0], r0, 0)
    normed0, near_x1, own_ct = tie((normed0, near_x1, own_ct))
    part_ct = in_group(exchange(quarters(own_ct)))
    far_x1 = [lax.ppermute(v, "section", [(1, 0)]) for v in near_x1]
    mixed0 = scatter_sum(jnp.dot(normed0, wo[0], preferred_element_type=F32))
    mixed0, part_ct, pieces_z1 = tie((mixed0, part_ct, pieces_z1))
    near_z1, far_z1 = fetch(pieces_z1, 1)
    out0 = valid * (h0.astype(F32) + mixed0)
    h1 = out0.astype(BF16)

    normed_in1 = gather_rows(normalised(h1.astype(F32), small[1][0]).astype(BF16))
    normed_in1, far_x1 = tie((normed_in1, far_x1))
    win[1] = (near_z1, far_z1, near_x1, far_x1)
    px1 = project_x(normed_in1, 1)
    px1, near_z1, part_ct = tie((px1, near_z1, part_ct))
    far_z1 = [lax.ppermute(v, "section", [(1, 0)]) for v in near_z1]
    win[1] = (near_z1, far_z1, near_x1, far_x1)
    all_ct = whole_slot(part_ct)
    fwd1 = scan(px1, 1)
    fwd1, all_ct = tie((fwd1, all_ct))
    dout1 = own_rows(all_ct).astype(F32)
    dmixed1 = (all_valid * all_ct.astype(F32)).astype(BF16)
    dn1 = dot_cols(dmixed1, wo[1])
    pz1 = project_z(normed_in1, 1)
    g1 = gate(pz1, fwd1[0][0])
    stat1 = sum_of_shares(
        jnp.stack(
            [
                jnp.sum(g1 * g1, axis=1).reshape(n, rows),
                jnp.sum(g1 * dn1 * small[1][3], axis=1).reshape(n, rows),
            ]
        )
    ).reshape(2, -1)
    r1 = lax.rsqrt(stat1[0] / INNER + EPS)
    normed1 = gated(pz1, fwd1[0][0], r1, 1)

    part_width = width // 2

    def cut_half(v, k):
        size = v.shape[1] // 2
        return lax.dynamic_slice_in_dim(v, k * size, size, 1)

    def narrow_of(parts, k):
        return jnp.concatenate([cut_half(v, k) for v in parts], axis=1)

    def away_in(normed_in, part, narrow=()):
        away = [dot_rows(normed_in, cut_half(part, 1 - c)).astype(BF16)]
        if narrow:
            away.append(dot_rows(narrow_of(narrow, 1 - c), normed_in).astype(BF16))
        return [swap_section(v) for v in away]

    def own_in_piece(normed_in, part, away, narrow=()):
        total = dot_rows(normed_in, cut_half(part, c)) + away[0].astype(F32)
        result = total.astype(BF16).reshape(n, share, -1)
        if narrow:
            total = (dot_rows(narrow_of(narrow, c), normed_in) + away[1].astype(F32)).astype(BF16)
            fill = jnp.zeros((-total.shape[0] % 64, D), BF16)
            rest = jnp.concatenate([total, fill]).reshape(-1, n, share).transpose(1, 0, 2)
            result = jnp.concatenate([result, rest], axis=1)
        return result

    def away_out(normed, dmixed):
        return swap_section(dot_rows(cut_half(normed, 1 - c), dmixed).astype(BF16))

    def own_out_piece(normed, dmixed, away):
        return (dot_rows(cut_half(normed, c), dmixed) + away.astype(F32)).astype(BF16)

    def with_group(dxs, dbc):
        total = jnp.sum(exchange(dbc), axis=0).astype(BF16)
        column = jnp.arange(GROUP)[None, :] // group
        own = jnp.where(column == f, jnp.concatenate([total] * n, axis=1), 0)
        full = lax.dynamic_update_slice(dxs, own.astype(BF16), (0, width))
        return full, (dxs[:, :width], [total, dxs[:, width + GROUP :]])

    def back_in(dz, full, layer, kind):
        near_z, far_z, near_x, far_x = win[layer]
        return project_back(ids, dz, full, (near_z, near_x), (far_z, far_x), layer, kind)

    def back_norm(dout, dnormed_in, h, gain):
        h = h.astype(F32)
        r = lax.rsqrt(jnp.mean(h * h, axis=-1, keepdims=True) + EPS)
        u = dnormed_in * gain
        mean = jnp.mean(u * h, axis=-1, keepdims=True)
        dgain = jnp.sum(dnormed_in * h * r, axis=0)
        return valid * dout + r * u - h * (r * r * r) * mean, dgain

    def scales(r, coef):
        top = jnp.stack([r.reshape(n, rows), coef.reshape(n, rows)], axis=1)
        return jnp.concatenate([top, jnp.zeros((n, 6, rows), F32)], axis=1)

    def packed(dgin, d, out, mixed):
        dgain, dconv, dhp = d[3][0], d[4][:5], d[5][:3]
        put = lambda v, size, at_lane: lax.dynamic_update_slice(
            jnp.zeros(v.shape[:-1] + (size,), F32), v, (0,) * (v.ndim - 1) + (at_lane,)
        )
        conv = put(dconv[:, :width], CHANNELS, f * width)
        conv = conv.at[:, INNER:].set(dconv[:, width:])
        totals = jnp.stack(
            [jnp.sum(out * out), jnp.sum((valid * mixed) ** 2), jnp.sum(valid)]
        )
        return jnp.concatenate(
            [
                dgin,
                conv.reshape(-1),
                put(dhp, HEADS, f * heads).reshape(-1),
                put(dgain, INNER, f * width),
                totals,
            ]
        )

    def hand_over(v, layer):
        return lax.ppermute(v, "section", [(1 - layer, layer)])

    sums = SeqSums()
    rc1 = scales(r1, (r1 * r1 * r1 / INNER) * stat1[1])
    away = away_out(normed1, dmixed1)
    o1 = sums.add(own_out_piece(normed1, dmixed1, away))
    rc1, normed1, dn1 = sums.end((rc1, normed1, dn1))

    sums.begin()
    d1 = unscan(pz1, px1, fwd1, dn1, rc1, 1)
    mixed1 = scatter_sum(jnp.dot(normed1, wo[1], preferred_element_type=F32).astype(BF16))
    d1, mixed1 = sums.end((d1, mixed1))

    sums.begin()
    away = away_in(normed_in1, d1[0])
    full1, xs1 = with_group(d1[1], d1[2])
    back1 = back_in(d1[0], full1, 1, F32)
    gz = own_in_piece(normed_in1, d1[0], away)
    out1 = valid * (h1.astype(F32) + mixed1)
    back_h = exchange(quarters(jnp.concatenate([h1, out1.astype(BF16)])))
    back1, xs1, full1, gz, out1, back_h = sums.end((back1, xs1, full1, gz, out1, back_h))
    z1 = sums.add(gz)

    sums.begin()
    dnin1 = scatter_sum(back1)
    away = away_in(normed_in1, *xs1)
    gx = own_in_piece(normed_in1, xs1[0], away, xs1[1])
    back_h = in_group(back_h)
    dnin1, gx, back_h = sums.end((dnin1, gx, back_h))
    x1 = sums.add(gx)

    sums.begin()
    grad1, dgin1 = back_norm(dout1, dnin1, h1, small[1][0])
    dout0 = grad1.astype(BF16).astype(F32)
    dmixed0_own = (valid * dout0).astype(BF16)
    dmixed0 = gather_rows(dmixed0_own)
    along0 = to_all(jnp.sum(dmixed0_own.astype(F32) * mixed0, axis=-1)).reshape(-1)
    rc0 = scales(r0, (r0 * r0 / INNER) * along0)
    back_h = joined(exchange(back_h))
    grad1, dgin1, dmixed0, rc0, back_h = sums.end((grad1, dgin1, dmixed0, rc0, back_h))

    sums.begin()
    dn0 = dot_cols(dmixed0, wo[0])
    d0 = unscan(pz0, px0, fwd0, dn0, rc0, 0)
    go = own_out_piece(normed0, dmixed0, away_out(normed0, dmixed0))
    p1 = packed(dgin1, d1, out1, mixed1)
    d0, go, p1 = sums.end((d0, go, p1))
    o0 = sums.add(go)

    sums.finish([o1, z1])
    sums.begin()
    away = away_in(normed_in0, d0[0])
    full0, xs0 = with_group(d0[1], d0[2])
    gz = own_in_piece(normed_in0, d0[0], away)
    away = away_in(normed_in0, *xs0)
    gx = own_in_piece(normed_in0, xs0[0], away, xs0[1])
    own_z1 = exchange(sums.values[z1])
    full0, gz, gx, own_z1 = sums.end((full0, gz, gx, own_z1))
    z0 = sums.add(gz)

    sums.begin()
    gx = exchange(gx)
    back0 = back_in(d0[0], full0, 0, BF16)
    gx, back0 = sums.end((gx, back0))
    x0 = sums.add(gx)

    def hand_over(v, layer):
        return lax.ppermute(v, "section", [(1 - layer, layer)])

    sums.begin()
    dnin0 = scatter_sum(back0)
    own_o1 = sums.values[o1]
    away_o1 = hand_over(own_o1, 1)
    away_z1 = hand_over(own_z1, 1)
    dnin0, own_z1, away_z1, own_o1, away_o1 = sums.end(
        (dnin0, own_z1, away_z1, own_o1, away_o1)
    )

    sums.finish([x1, o0])
    sums.begin()
    own_x1 = exchange(sums.values[x1])
    own_o0 = sums.values[o0]
    away_o0 = hand_over(own_o0, 0)
    grad0, dgin0 = back_norm(dout0, dnin0, h0, small[0][0])
    back_g = exchange(quarters(jnp.concatenate([grad0.astype(BF16), grad1.astype(BF16)])))
    p = jnp.stack([packed(dgin0, d0, out0, mixed0), p1])
    p = p + swap_section(p)
    p, back_g, own_x1, own_o0, away_o0 = sums.end((p, back_g, own_x1, own_o0, away_o0))

    sums.finish([z0])
    sums.begin()
    own_z0 = exchange(sums.values[z0])
    away_x1 = hand_over(own_x1, 1)
    m = 1
    while m < n:
        p = p + move_fsdp(p, m)
        m *= 2
    m = 1
    while m < nz:
        p = p + move_seq(p, m)
        m *= 2
    away_z0 = hand_over(own_z0, 0)
    p, back_g, own_z0, away_z0, own_x1, away_x1 = sums.end(
        (p, back_g, own_z0, away_z0, own_x1, away_x1)
    )
    sums.finish([x0])
    own_x0 = sums.values[x0]
    away_x0 = hand_over(own_x0, 0)
    back_g = joined(exchange(in_group(back_g)))
    p = pick(p[0], p[1])
    back = jnp.concatenate([back_h, back_g])

    used = 0

    def part(size):
        nonlocal used
        used += size
        return p[used - size : used]

    mine_of = lambda v, size: lax.dynamic_slice_in_dim(v, f * size, size, v.ndim - 1)
    o_gain_in = mine_of(part(D), share)
    o_conv = mine_of(part(5 * CHANNELS).reshape(5, CHANNELS), CHANNELS // n)
    o_heads = mine_of(part(3 * HEADS).reshape(3, HEADS), heads)
    o_gain_out = mine_of(part(INNER), width)
    totals = part(3)
    act_rms = jnp.sqrt(totals[:2] / (totals[2] * D))[None]

    held = [
        [(own_z0, own_x0, own_o0), (own_z1, own_x1, own_o1)],
        [(away_z0, away_x0, away_o0), (away_z1, away_x1, away_o1)],
    ]

    def both_halves(a, b):
        return jnp.stack([pick(a, b), pick(b, a)], axis=1)

    rows_of = GROUP // n // 2, HEADS // n // 2
    narrow = [pick(side[0][1], side[1][1])[:, share : share + sum(rows_of)] for side in held]
    narrow = both_halves(*[v.astype(F32) for v in narrow])
    small_in = jnp.concatenate(
        [
            narrow[:, :, : rows_of[0]].reshape(GROUP, share),
            narrow[:, :, rows_of[0] :].reshape(HEADS, share),
        ]
    )
    g_w_in = []
    shape_in = (2 * INNER + GROUP + HEADS, share)
    for k, rows_of_small in ((0, None), (1, (2 * INNER, GROUP + HEADS))):
        arrays, plan = [], []
        for s in range(2):
            arrays += [held[s][0][k], held[s][1][k]]
            firsts = tuple(k * INNER + q * width for q in range(n))
            plan.append((len(arrays) - 2, len(arrays) - 1, s, firsts))
        g_w_in = [
            place_in(
                ids, arrays, tuple(plan), small_in, rows_of_small, g_w_in, shape_in, part_width
            )
        ]
    halves_out = [pick(side[0][2], side[1][2]) for side in held]
    g_w_out = jnp.concatenate([pick(*halves_out), pick(*halves_out[::-1])]).astype(F32)

    back = back.reshape(2, 2, rows, D)
    kept_back = pick(back[:, 0], back[:, 1])
    other_back = swap_section(pick(back[:, 1], back[:, 0]))
    both_back = jnp.stack(
        [pick(kept_back, other_back), pick(other_back, kept_back)], axis=1
    )
    return (
        both_back[0][None, :, None],
        both_back[1].astype(F32)[None, :, None],
        o_gain_in[None],
        g_w_in[0].T[None],
        o_conv[None, :4],
        o_conv[None, 4],
        o_heads[None, 0],
        o_heads[None, 1],
        o_heads[None, 2],
        o_gain_out[None],
        g_w_out[None],
        act_rms,
    )


def solution(mesh):
    in_specs = (
        P(None, "fsdp", "seq", None),
        P(None, "fsdp", "seq", None),
        P(None, "fsdp"),
        P("section", "fsdp"),
        P("section", "fsdp", None),
        P("section", None, "fsdp"),
        P("section", "fsdp"),
        P("section", "fsdp"),
        P("section", "fsdp"),
        P("section", "fsdp"),
        P("section", "fsdp"),
        P("section", "fsdp", None),
    )
    out_specs = (
        P("section", None, "fsdp", "seq", None),
        P("section", None, "fsdp", "seq", None),
        P("section", "fsdp"),
        P("section", "fsdp", None),
        P("section", None, "fsdp"),
        P("section", "fsdp"),
        P("section", "fsdp"),
        P("section", "fsdp"),
        P("section", "fsdp"),
        P("section", "fsdp"),
        P("section", "fsdp", None),
        P("section", None),
    )
    return jax.shard_map(
        per_device, mesh=mesh, in_specs=in_specs, out_specs=out_specs, check_vma=False
    )
```

```python
import functools

import jax
import jax.numpy as jnp
from jax import lax
from jax.experimental import pallas as pl
from jax.experimental.pallas import tpu as pltpu
from jax.sharding import PartitionSpec as P

D = 2048
INNER = 4096
HEADS = 64
HEAD_DIM = 64
STATE = 128
KERNEL = 4
GROUP = 2 * STATE
CHANNELS = INNER + GROUP
LANES = 128
EPS = 1e-05
F32 = jnp.float32
BF16 = jnp.bfloat16
VMEM_BYTES = 48 * 1024 * 1024


def split(v):
    hi = v.astype(BF16)
    return hi, (v - hi.astype(F32)).astype(BF16)


def dot32(a, b, ca, cb):
    (ah, al), (bh, bl) = (v if isinstance(v, tuple) else split(v) for v in (a, b))
    one = lambda p, q: lax.dot_general(
        p, q, (((ca,), (cb,)), ((), ())), preferred_element_type=F32
    )
    return one(ah, bh) + (one(ah, bl) + one(al, bh))


def step_sizes(raw, hp, rows):
    shifted = raw + hp[0:1, :]
    dt = jnp.maximum(shifted, 0.0) + jnp.log1p(jnp.exp(-jnp.abs(shifted)))
    decay = dt * hp[1:2, :]
    row = lax.broadcasted_iota(jnp.int32, (rows, rows), 0)
    col = lax.broadcasted_iota(jnp.int32, (rows, rows), 1)
    lower = (row >= col).astype(F32)
    cum = dot32(lower, decay, 1, 0)
    cum_t = dot32(decay, lower, 0, 1)
    return shifted, dt, cum, cum_t, row, col, lower


def pair_lanes(v, j, first):
    return jnp.where(first, v[:, 2 * j : 2 * j + 1], v[:, 2 * j + 1 : 2 * j + 2])


def head_sums(v, table):
    hi, low = split(v)
    one = lambda p: lax.dot_general(
        p, table, (((1,), (1,)), ((), ())), preferred_element_type=F32
    )
    return one(hi) + one(low)


def forward_kernel(proj, cw, hp, s0, e0, y_ref, filt_ref, st_ref, state, xp, xw_s, last_s):
    i = pl.program_id(0)
    rows, width = y_ref.shape

    @pl.when(i == 0)
    def _():
        state[...] = s0[...]
        xp[0:8, :] = e0[...]

    xp[8 : 8 + rows, :] = proj[:, : width + GROUP]

    def conv_tile(lo):
        acc = cw[4:5, lo : lo + LANES]
        for k in range(KERNEL):
            acc = acc + cw[k : k + 1, lo : lo + LANES] * xp[5 + k : 5 + k + rows, lo : lo + LANES]
        filt_ref[:, lo : lo + LANES] = acc
        return acc * jax.nn.sigmoid(acc)

    b_c = conv_tile(width)
    c_c = conv_tile(width + STATE)
    _, dt, cum, cum_t, row, col, _ = step_sizes(proj[:, width + GROUP :], hp, rows)
    last = cum[rows - 1 : rows, :]
    ecum = jnp.exp(cum)
    weight = jnp.exp(last - cum) * dt
    elast = jnp.exp(last)
    b_c, c_c = split(b_c), split(c_c)
    carried = dot32(c_c, state[...], 1, 0)
    scores = dot32(c_c, b_c, 1, 1)
    causal = row >= col
    lane = lax.broadcasted_iota(jnp.int32, (rows, LANES), 1)
    first = lane < HEAD_DIM
    for j in range(width // LANES):
        lo = j * LANES
        here = slice(lo, lo + LANES)
        x = conv_tile(lo)
        xd = x * pair_lanes(dt, j, first)
        m = []
        for h in (2 * j, 2 * j + 1):
            gap = cum[:, h : h + 1] - cum_t[h : h + 1, :]
            m.append(jnp.exp(jnp.where(causal, gap, -1e30)) * scores)
        xd2 = jnp.concatenate([jnp.where(first, xd, 0.0), jnp.where(first, 0.0, xd)])
        y = (
            dot32(jnp.concatenate(m, axis=1), xd2, 1, 0)
            + carried[:, here] * pair_lanes(ecum, j, first)
            + pair_lanes(hp[2:3, :], j, first[0:1]) * x
        )
        y_ref[:, here] = y
        xw_s[:, here] = x * pair_lanes(weight, j, first)
        last_s[0:1, here] = pair_lanes(elast, j, first[0:1])
    state[...] = state[...] * last_s[0:1, :] + dot32(b_c, xw_s[...], 0, 0)
    st_ref[0] = state[...]
    xp[0:8, :] = xp[rows : rows + 8, :]


def backward_kernel(
    pz,
    proj,
    y_ref,
    filt,
    dn,
    rc,
    st_before,
    st_out,
    s0,
    cw,
    hp,
    table,
    gain,
    g0,
    e0,
    dz_ref,
    dproj,
    dbc_ref,
    dgain_ref,
    dconv_ref,
    dhp_ref,
    gfin_ref,
    efin_ref,
    grad,
    dfp,
    both,
    xw_s,
    dyc_s,
    rowv,
):
    i = pl.program_id(0)
    rows, width = y_ref.shape
    heads = hp.shape[1]

    @pl.when(i == 0)
    def _():
        grad[...] = g0[...]
        dfp[rows : rows + 8, :] = e0[...]
        dgain_ref[...] = jnp.zeros_like(dgain_ref)
        dconv_ref[...] = jnp.zeros_like(dconv_ref)
        dhp_ref[...] = jnp.zeros_like(dhp_ref)

    def silu_pair(v):
        s = jax.nn.sigmoid(v)
        a = v * s
        return a, s * (1.0 + v - a)

    b_c, b_d = silu_pair(filt[:, width : width + STATE])
    c_c, c_d = silu_pair(filt[:, width + STATE :])
    shifted, dt, cum, cum_t, row, col, lower = step_sizes(proj[:, width + GROUP :], hp, rows)
    last = cum[rows - 1 : rows, :]
    tail = jnp.exp(last - cum)
    ecum = jnp.exp(cum)
    elast = jnp.exp(last)
    b_c, c_c = split(b_c), split(c_c)
    grad_p = split(grad[...])
    k_all = dot32(b_c, grad_p, 1, 0)
    scores_t = dot32(b_c, c_c, 1, 1)
    causal_t = row <= col
    lane = lax.broadcasted_iota(jnp.int32, (rows, LANES), 1)
    first = lane < HEAD_DIM
    dcb_t = jnp.zeros((rows, rows), F32)
    rc_t = dot32((row == col).astype(F32), rc[0], 1, 1)
    r = rc_t[:, 0:1]
    coef = rc_t[:, 1:2]
    rowv[0:1, :] = jnp.sum(grad[...] * st_out[0], axis=0, keepdims=True)
    for j in range(width // LANES):
        lo = j * LANES
        here = slice(lo, lo + LANES)
        z = pz[:, here]
        y = y_ref[:, here]
        sz, dsz = silu_pair(z)
        g = y * sz
        dnt = dn[:, here]
        dg = dnt * gain[0:1, here] * r - g * coef
        dgain_ref[0:1, here] += jnp.sum(dnt * g * r, axis=0, keepdims=True)
        dy = dg * sz
        dz_ref[:, here] = (dg * y * dsz).astype(BF16)
        x, xder = silu_pair(filt[:, here])
        dt_e = pair_lanes(dt, j, first)
        tail_e = pair_lanes(tail, j, first)
        xd = x * dt_e
        dy2 = split(jnp.concatenate([jnp.where(first, dy, 0.0), jnp.where(first, 0.0, dy)]))
        decays = []
        for h in (2 * j, 2 * j + 1):
            gap = cum_t[h : h + 1, :] - cum[:, h : h + 1]
            decays.append(jnp.exp(jnp.where(causal_t, gap, -1e30)))
        m = jnp.concatenate([d * scores_t for d in decays], axis=1)
        dm = dot32(xd, dy2, 1, 1)
        dcb_t = dcb_t + (decays[0] * dm[:, :rows] + decays[1] * dm[:, rows:])
        v = dot32(m, dy2, 1, 0) + k_all[:, here] * tail_e
        skip = pair_lanes(hp[2:3, :], j, first[0:1])
        dx = dt_e * v + skip * dy
        both[0:rows, here] = x * v
        both[rows : 2 * rows, here] = dy * (y - skip * x)
        rowv[1:2, here] = jnp.sum(dy * x, axis=0, keepdims=True)
        rowv[2:3, here] = pair_lanes(elast, j, first[0:1])
        xw_s[:, here] = xd * tail_e
        dyc_s[:, here] = dy * pair_lanes(ecum, j, first)
        dfp[0:rows, here] = dx * xder
    dcb_t = split(dcb_t)
    dyc = split(dyc_s[...])
    st_in = jnp.where(i == pl.num_programs(0) - 1, s0[...], st_before[0])
    dc = dot32(dcb_t, b_c, 0, 0) + dot32(dyc, st_in, 1, 1)
    db = dot32(dcb_t, c_c, 1, 0) + dot32(xw_s[...], grad_p, 1, 1)
    dfp[0:rows, width : width + STATE] = db * b_d
    dfp[0:rows, width + STATE :] = dc * c_d
    grad[...] = grad[...] * rowv[2:3, :] + dot32(c_c, dyc, 0, 0)
    gfin_ref[...] = grad[...]

    sums = head_sums(both[...], table[...])
    rsums = head_sums(rowv[...], table[...])
    ddt_x = sums[0:rows]
    dcum = sums[rows : 2 * rows] - dt * ddt_x
    upto = lax.broadcasted_iota(jnp.int32, (rows, heads), 0)
    dcum = dcum + jnp.where(upto == rows - 1, rsums[0:1, :], 0.0)
    ddecay = dot32(lower, dcum, 0, 0)
    ddt = ddt_x + hp[1:2, :] * ddecay
    draw = ddt * jax.nn.sigmoid(shifted)
    dproj[:, width + GROUP :] = draw.astype(BF16)
    dhp_ref[0:1, :] += jnp.sum(draw, axis=0, keepdims=True)
    dhp_ref[1:2, :] += jnp.sum(ddecay * dt, axis=0, keepdims=True) * hp[1:2, :]
    dhp_ref[2:3, :] += rsums[1:2, :]

    for lo in range(0, width + GROUP, LANES):
        here = slice(lo, lo + LANES)
        src = proj[:, here]
        total = jnp.zeros((rows, LANES), F32)
        for k in range(KERNEL):
            shift = KERNEL - 1 - k
            moved = dfp[shift : shift + rows, here]
            total = total + cw[k : k + 1, here] * moved
            dconv_ref[k : k + 1, here] += jnp.sum(src * moved, axis=0, keepdims=True)
        dconv_ref[4:5, here] += jnp.sum(dfp[0:rows, here], axis=0, keepdims=True)
        if lo < width:
            dproj[:, here] = total.astype(BF16)
        else:
            dproj[:, here] = jnp.zeros((rows, LANES), BF16)
            share = dbc_ref.shape[2]
            for k in range(LANES // share):
                dbc_ref[(lo - width) // share + k] = total[:, k * share : (k + 1) * share]
    dfp[rows : rows + 8, :] = dfp[0:8, :]
    efin_ref[...] = dfp[0:8, :]


def whole(shape):
    return pl.BlockSpec(shape, lambda i: (0,) * len(shape))


def run_forward(proj, cw, hp, s0, e0, rows):
    total, width = proj.shape[0], s0.shape[1]
    count = total // rows
    block = lambda w: pl.BlockSpec((rows, w), lambda i: (i, 0))
    shape = jax.ShapeDtypeStruct
    return pl.pallas_call(
        forward_kernel,
        grid=(count,),
        in_specs=[block(proj.shape[1])] + [whole(v.shape) for v in (cw, hp, s0, e0)],
        out_specs=[
            block(width),
            block(width + GROUP),
            pl.BlockSpec((1, STATE, width), lambda i: (i, 0, 0)),
        ],
        scratch_shapes=[
            pltpu.VMEM((STATE, width), F32),
            pltpu.VMEM((rows + 8, width + GROUP), F32),
            pltpu.VMEM((rows, width), F32),
            pltpu.VMEM((8, width), F32),
        ],
        out_shape=[
            shape((total, width), F32),
            shape((total, width + GROUP), F32),
            shape((count, STATE, width), F32),
        ],
        compiler_params=pltpu.CompilerParams(vmem_limit_bytes=VMEM_BYTES),
        name="scan_forward",
    )(proj, cw, hp, s0, e0)


def run_backward(pz, proj, y, filt, dn, rc, states, s0, cw, hp, table, gain, g0, e0, rows, places):
    total, (heads, width) = proj.shape[0], table.shape
    count = total // rows
    turn = lambda i: count - 1 - i
    block = lambda w: pl.BlockSpec((rows, w), lambda i: (turn(i), 0))
    shape = jax.ShapeDtypeStruct
    share = GROUP // places
    return pl.pallas_call(
        backward_kernel,
        grid=(count,),
        in_specs=[
            block(width),
            block(proj.shape[1]),
            block(width),
            block(width + GROUP),
            block(width),
            pl.BlockSpec((1, 8, rows), lambda i: (turn(i), 0, 0)),
            pl.BlockSpec((1, STATE, width), lambda i: (jnp.maximum(turn(i) - 1, 0), 0, 0)),
            pl.BlockSpec((1, STATE, width), lambda i: (turn(i), 0, 0)),
        ]
        + [whole(v.shape) for v in (s0, cw, hp, table, gain, g0, e0)],
        out_specs=[
            block(width),
            block(proj.shape[1]),
            pl.BlockSpec((places, rows, share), lambda i: (0, turn(i), 0)),
            whole((8, width)),
            whole((8, width + GROUP)),
            whole((8, heads)),
            whole((STATE, width)),
            whole((8, width + GROUP)),
        ],
        scratch_shapes=[
            pltpu.VMEM((STATE, width), F32),
            pltpu.VMEM((rows + 8, width + GROUP), F32),
            pltpu.VMEM((2 * rows, width), F32),
            pltpu.VMEM((rows, width), F32),
            pltpu.VMEM((rows, width), F32),
            pltpu.VMEM((8, width), F32),
        ],
        out_shape=[
            shape((total, width), BF16),
            shape(proj.shape, BF16),
            shape((places, total, share), F32),
            shape((8, width), F32),
            shape((8, width + GROUP), F32),
            shape((8, heads), F32),
            shape((STATE, width), F32),
            shape((8, width + GROUP), F32),
        ],
        compiler_params=pltpu.CompilerParams(vmem_limit_bytes=VMEM_BYTES),
        name="scan_backward",
    )(pz, proj, y, filt, dn, rc, states, states, s0, cw, hp, table, gain, g0, e0)


def bring(step, pieces, buffers, sems, own):
    for near, far, buffer, sem in zip(*pieces, buffers, sems):
        to, done = buffer.at[step % 2], sem.at[step % 2]

        @pl.when(own)
        def _():
            pltpu.make_async_copy(near[step], to, done).start()

        @pl.when(jnp.logical_not(own))
        def _():
            pltpu.make_async_copy(far[step], to, done).start()


def arrived(step, pieces, buffers, sems):
    for near, buffer, sem in zip(pieces[0], buffers, sems):
        pltpu.make_async_copy(near[step], buffer.at[step % 2], sem.at[step % 2]).wait()
    return [buffer.at[step % 2] for buffer in buffers]


def project_kernel(ids, normed, *refs, layer, n):
    near, far = [refs[0:n]], [refs[n : 2 * n]]
    out, buffer, sem = refs[2 * n :]
    pieces = (near, far)
    own = ids[1] == layer
    columns = out.shape[1]
    share = buffer.shape[2]
    bring(0, pieces, [buffer], [sem], own)
    for m in range(n):
        if m + 1 < n:
            bring(m + 1, pieces, [buffer], [sem], own)
        (w,) = arrived(m, pieces, [buffer], [sem])
        from_place = pl.multiple_of(jnp.bitwise_xor(ids[0], m) * share, share)
        a = normed[:, pl.ds(from_place, share)]
        for lo in range(0, columns, 256):
            here = slice(lo, min(lo + 256, columns))
            v = lax.dot_general(
                a, w[here, :], (((1,), (1,)), ((), ())), preferred_element_type=F32
            )
            out[:, here] = v if m == 0 else out[:, here] + v


def project(ids, normed, near, far, layer):
    n = len(near)
    columns, share = near[0].shape
    rows = normed.shape[0]
    vmem = pl.BlockSpec(memory_space=pltpu.VMEM)
    return pl.pallas_call(
        functools.partial(project_kernel, layer=layer, n=n),
        in_specs=[pl.BlockSpec(memory_space=pltpu.SMEM), vmem]
        + [pl.BlockSpec(memory_space=pl.ANY)] * (2 * n),
        out_specs=vmem,
        scratch_shapes=[
            pltpu.VMEM((2, columns, share), BF16),
            pltpu.SemaphoreType.DMA((2,)),
        ],
        out_shape=jax.ShapeDtypeStruct((rows, columns), F32),
        compiler_params=pltpu.CompilerParams(vmem_limit_bytes=VMEM_BYTES),
        cost_estimate=pl.CostEstimate(
            flops=2 * rows * columns * share * n,
            bytes_accessed=columns * share * n * 2 + rows * columns * 4,
            transcendentals=0,
        ),
        name="project",
    )(ids, normed, *near, *far)


def back_kernel(ids, dz, dx, *refs, layer, n):
    near = (refs[0:n], refs[n : 2 * n])
    far = (refs[2 * n : 3 * n], refs[3 * n : 4 * n])
    out, zbuf, xbuf, zsem, xsem = refs[4 * n :]
    pieces = (near, far)
    own = ids[1] == layer
    share = zbuf.shape[2]
    args = ([zbuf, xbuf], [zsem, xsem])
    bring(0, pieces, *args, own)
    for m in range(n):
        if m + 1 < n:
            bring(m + 1, pieces, *args, own)
        wz, wx = arrived(m, pieces, *args)
        for lo in range(0, share, 256):
            here = slice(lo, lo + 256)
            v = jnp.dot(dz[...], wz[:, here], preferred_element_type=F32) + jnp.dot(
                dx[...], wx[:, here], preferred_element_type=F32
            )
            at_lane = pl.multiple_of(jnp.bitwise_xor(ids[0], m) * share + lo, 256)
            out[:, pl.ds(at_lane, 256)] = v.astype(out.dtype)


def project_back(ids, dz, dx, near, far, layer, kind):
    n = len(near[0])
    share = near[0][0].shape[1]
    rows = dz.shape[0]
    columns = dz.shape[1] + dx.shape[1]
    vmem = pl.BlockSpec(memory_space=pltpu.VMEM)
    return pl.pallas_call(
        functools.partial(back_kernel, layer=layer, n=n),
        in_specs=[pl.BlockSpec(memory_space=pltpu.SMEM), vmem, vmem]
        + [pl.BlockSpec(memory_space=pl.ANY)] * (4 * n),
        out_specs=vmem,
        scratch_shapes=[
            pltpu.VMEM((2, dz.shape[1], share), BF16),
            pltpu.VMEM((2, dx.shape[1], share), BF16),
            pltpu.SemaphoreType.DMA((2,)),
            pltpu.SemaphoreType.DMA((2,)),
        ],
        out_shape=jax.ShapeDtypeStruct((rows, n * share), kind),
        compiler_params=pltpu.CompilerParams(vmem_limit_bytes=VMEM_BYTES),
        cost_estimate=pl.CostEstimate(
            flops=2 * rows * columns * share * n,
            bytes_accessed=columns * share * n * 2 + rows * n * share * 2,
            transcendentals=0,
        ),
        name="project_back",
    )(ids, dz, dx, *near[0], *near[1], *far[0], *far[1])


def place_kernel(ids, *refs, plan, count, rows_of_small):
    small = refs[count]
    out, eye, pieces, blocks, in_sem, out_sem = refs[-6:]
    core = ids[1]
    size, share = blocks.shape[1:]

    def fetch(k):
        for layer in range(2):

            @pl.when(core == layer)
            def _():
                src = refs[plan[k][layer]]
                pltpu.make_async_copy(
                    src.at[:, pl.ds(0, share)], pieces.at[k % 2], in_sem.at[k % 2]
                ).start()

    def send(step, first, count):
        return pltpu.make_async_copy(
            blocks.at[step % 2, pl.ds(0, count)],
            out.at[pl.ds(first, count)],
            out_sem.at[step % 2],
        )

    eye[...] = (
        lax.broadcasted_iota(jnp.int32, eye.shape, 0)
        == lax.broadcasted_iota(jnp.int32, eye.shape, 1)
    ).astype(BF16)
    fetch(0)
    sent = []
    for k, (_, _, side, firsts) in enumerate(plan):
        if k + 1 < len(plan):
            fetch(k + 1)
        pltpu.make_async_copy(pieces.at[k % 2], pieces.at[k % 2], in_sem.at[k % 2]).wait()
        shift = jnp.where(side == 0, core, 1 - core) * size
        for p, first in enumerate(firsts):
            step = len(sent)
            if step >= 2:
                sent[step - 2].wait()
            blocks[step % 2] = lax.dot_general(
                pieces[k % 2, p],
                eye[...],
                (((0,), (0,)), ((), ())),
                preferred_element_type=F32,
            )
            sent.append(send(step, pl.multiple_of(first + shift, 8), size))
            sent[-1].start()
    if rows_of_small:
        step = len(sent)
        sent[step - 2].wait()
        first, count = rows_of_small
        sent.append(
            pltpu.make_async_copy(small, out.at[pl.ds(first, count)], out_sem.at[step % 2])
        )
        sent[-1].start()
    sent[-2].wait()
    sent[-1].wait()


def place_in(ids, arrays, plan, small, rows_of_small, before, shape, size):
    places, share = arrays[0].shape[0], shape[1]
    any_space = pl.BlockSpec(memory_space=pl.ANY)
    return pl.pallas_call(
        functools.partial(
            place_kernel, plan=plan, count=len(arrays), rows_of_small=rows_of_small
        ),
        in_specs=[pl.BlockSpec(memory_space=pltpu.SMEM)]
        + [any_space] * len(arrays)
        + [pl.BlockSpec(memory_space=pltpu.VMEM)]
        + [any_space] * len(before),
        out_specs=any_space,
        scratch_shapes=[
            pltpu.VMEM((share, share), BF16),
            pltpu.VMEM((2, places, share, size), BF16),
            pltpu.VMEM((2, size, share), F32),
            pltpu.SemaphoreType.DMA((2,)),
            pltpu.SemaphoreType.DMA((2,)),
        ],
        out_shape=jax.ShapeDtypeStruct(shape, F32),
        input_output_aliases={len(arrays) + 2: 0} if before else {},
        compiler_params=pltpu.CompilerParams(vmem_limit_bytes=VMEM_BYTES),
        name="place_in",
    )(ids, *arrays, small, *before)


def combine_kernel(flags, *refs, adds):
    count = len(adds)
    for k, add in enumerate(adds):
        v, got, out = refs[2 * k], refs[2 * k + 1], refs[2 * count + k]
        if add:
            out[...] = (v[...].astype(F32) + got[...].astype(F32)).astype(BF16)
        else:
            out[...] = jnp.where(flags[k] == 1, got[...], v[...])


def combine(items, flags):
    steps = 8
    shapes = [v.shape for v, _, _ in items]
    flat = [(v.reshape(-1, v.shape[-1]), g.reshape(-1, g.shape[-1])) for v, g, _ in items]
    spec = lambda v: pl.BlockSpec((v.shape[0] // steps, v.shape[1]), lambda i: (i, 0))
    out = pl.pallas_call(
        functools.partial(combine_kernel, adds=tuple(add for _, _, add in items)),
        grid=(steps,),
        in_specs=[pl.BlockSpec(memory_space=pltpu.SMEM)] + [spec(v) for p in flat for v in p],
        out_specs=[spec(v) for v, _ in flat],
        out_shape=[jax.ShapeDtypeStruct(v.shape, BF16) for v, _ in flat],
        compiler_params=pltpu.CompilerParams(vmem_limit_bytes=VMEM_BYTES),
        name="combine",
    )(flags, *[v for p in flat for v in p])
    return [v.reshape(shape) for v, shape in zip(out, shapes)]


def swap_section(v):
    return lax.ppermute(v, "section", [(0, 1), (1, 0)])


def at(v, k):
    return lax.dynamic_index_in_dim(v, k, 0, False)


def exchange(v):
    return lax.all_to_all(v, "fsdp", 0, 0, tiled=True)


def to_all(v):
    n = lax.axis_size("fsdp")
    return exchange(jnp.broadcast_to(v[None], (n,) + v.shape))


def gather_rows(v):
    return to_all(v).reshape(-1, v.shape[-1])


def scatter_sum(partial):
    n = lax.axis_size("fsdp")
    got = exchange(partial.reshape(n, -1, partial.shape[-1]))
    return jnp.sum(got.astype(F32), axis=0)


def in_group(v):
    n, s = lax.axis_size("fsdp"), lax.axis_size("seq")
    groups = [[j * n + i for i in range(n)] for j in range(s // n)]
    return lax.all_to_all(v, "seq", 0, 0, axis_index_groups=groups, tiled=True)


def quarters(v):
    n = lax.axis_size("fsdp")
    return v.reshape(v.shape[0], n, -1).transpose(1, 0, 2)


def joined(v):
    return v.transpose(1, 0, 2).reshape(v.shape[1], -1)


def move_fsdp(v, m):
    n = lax.axis_size("fsdp")
    return lax.ppermute(v, "fsdp", [(k, k ^ m) for k in range(n)])


def move_seq(v, m):
    s = lax.axis_size("seq")
    return lax.ppermute(v, "seq", [(k, k ^ m) for k in range(s)])


class SeqSums:
    def __init__(self):
        s = lax.axis_size("seq")
        half = s // 2
        self.pairs = [[(j, j + 1), (s - 1 - j, s - 2 - j)] for j in range(half - 1)]
        self.pairs.append([(half - 1, half), (half, half - 1)])
        self.inward = half
        self.pairs += [[(j + 1, j), (s - 2 - j, s - 1 - j)] for j in reversed(range(half - 1))]
        self.values, self.phase, self.moving = [], [], []

    def add(self, value):
        self.values.append(value)
        self.phase.append(0)
        return len(self.values) - 1

    def begin(self):
        taken = set()
        for k, step in enumerate(self.phase):
            if step == len(self.pairs) or step in taken:
                continue
            taken.add(step)
            self.moving.append((k, lax.ppermute(self.values[k], "seq", self.pairs[step])))

    def end(self, work):
        place = lax.axis_index("seq")
        items, flags = [], []
        for k, got in self.moving:
            step = self.phase[k]
            items.append((self.values[k], got, step < self.inward))
            here = [place == to for _, to in self.pairs[step]]
            flags.append(functools.reduce(jnp.logical_or, here))
            self.phase[k] = step + 1
        moved = combine(items, jnp.stack(flags).astype(jnp.int32)) if items else []
        still = [k for k, p in enumerate(self.phase) if p == 0]
        work, moved, rest = lax.optimization_barrier(
            (work, moved, [self.values[k] for k in still])
        )
        for (k, _), v in zip(self.moving, moved):
            self.values[k] = v
        for k, v in zip(still, rest):
            self.values[k] = v
        self.moving = []
        return work

    def finish(self, chunks):
        while any(self.phase[k] < len(self.pairs) for k in chunks):
            self.begin()
            self.end(())


def relay(total, local, reverse):
    n, s = lax.axis_size("fsdp"), lax.axis_size("seq")
    segments = s // n
    place = lax.axis_index("seq") // n
    own = lax.axis_index("seq") % n
    totals = lax.all_gather(total, "seq")
    locals_ = lax.all_gather(local, "seq")
    state = jnp.zeros_like(local)
    order = range(segments - 1, -1, -1) if reverse else range(segments)
    for j in order:
        use = (j > place) if reverse else (j < place)
        t = lax.dynamic_index_in_dim(totals, j * n + own, 0, False)
        v = lax.dynamic_index_in_dim(locals_, j * n + own, 0, False)
        state = jnp.where(use, t * state + v, state)
    return state


def next_segment(v, step):
    n, s = lax.axis_size("fsdp"), lax.axis_size("seq")
    pairs = [(k, k + step * n) for k in range(s) if 0 <= k + step * n < s]
    return lax.ppermute(v, "seq", pairs)


def dot_rows(a, b):
    return lax.dot_general(a, b, (((0,), (0,)), ((), ())), preferred_element_type=F32)


def dot_cols(a, b):
    return lax.dot_general(a, b, (((1,), (1,)), ((), ())), preferred_element_type=F32)


def normalised(h, gain):
    return h * lax.rsqrt(jnp.mean(h * h, axis=-1, keepdims=True) + EPS) * gain


def per_device(
    inputs,
    cotangent,
    lengths,
    gain_in,
    w_in,
    conv_w,
    conv_b,
    dt_bias,
    a_log,
    d_skip,
    gain_out,
    w_out,
):
    n = lax.axis_size("fsdp")
    nz = lax.axis_size("seq")
    segments = nz // n
    c = lax.axis_index("section")
    f = lax.axis_index("fsdp")
    place = lax.axis_index("seq")
    upper = c == 0
    rows = inputs.shape[2]
    width = INNER // n
    heads = HEADS // n
    share = D // n
    half = share // 2
    group = GROUP // n
    ids = jnp.stack([f, c]).astype(jnp.int32)
    tie = lax.optimization_barrier

    def pick(a, b):
        return jnp.where(upper, a, b)

    w = w_in[0].T

    def cut(first, size):
        return lax.dynamic_slice_in_dim(w, first, size, 0)

    def piece_z(m):
        return cut((f ^ m) * width, width)

    def piece_x(m):
        return jnp.concatenate(
            [
                cut(INNER + (f ^ m) * width, width),
                w[2 * INNER : 2 * INNER + GROUP],
                cut(2 * INNER + GROUP + (f ^ m) * heads, heads),
            ]
        )

    def fetch(pieces, layer):
        pairs = lambda m: [(layer * n + i, layer * n + (i ^ m)) for i in range(n)]
        near = [
            v if m == 0 else lax.ppermute(v, ("section", "fsdp"), pairs(m))
            for m, v in enumerate(pieces)
        ]
        return near, [lax.ppermute(v, "section", [(layer, 1 - layer)]) for v in near]

    def whole_slot(v):
        return joined(to_all(v.reshape(n * rows, share)))

    pack = jnp.concatenate(
        [
            gain_in[0],
            dt_bias[0],
            a_log[0],
            d_skip[0],
            gain_out[0],
            conv_w[0].reshape(-1),
            conv_b[0],
        ]
    )
    more = -(-pack.shape[0] // (16 * share)) * 16
    filled = jnp.concatenate([pack, jnp.zeros((more * share - pack.shape[0],), BF16)])
    filled = jnp.broadcast_to(filled.reshape(1, more, share), (n, more, share))
    first = exchange(jnp.concatenate([quarters(at(inputs, c)[0]), filled], axis=1))
    first, pieces_x = tie((first, [piece_x(m) for m in range(n)]))
    part_h0 = first[:, :rows]
    mine = first[:, rows:].reshape(n, -1)[:, : pack.shape[0]]
    near_x0, far_x0 = fetch(pieces_x, 0)
    part_h0 = in_group(part_h0)
    near_x0, part_h0 = tie((near_x0, part_h0))
    far_x0 = [lax.ppermute(v, "section", [(0, 1)]) for v in near_x0]
    pieces_z, part_h0 = tie(([piece_z(m) for m in range(n)], part_h0))
    all_h0 = whole_slot(part_h0)
    near_z0, far_z0 = fetch(pieces_z, 0)

    theirs = swap_section(mine)
    small = []
    for full in (pick(mine, theirs), pick(theirs, mine)):
        full = full.astype(F32)
        used = 0

        def take(size):
            nonlocal used
            used += size
            return full[:, used - size : used]

        gain = take(share).reshape(1, D)
        hp = [at(take(heads), f)[None] for _ in range(3)]
        hp = jnp.concatenate([hp[0], -jnp.exp(hp[1]), hp[2], jnp.zeros((5, heads), F32)])
        gout = at(take(width), f)[None]
        per = CHANNELS // n
        taps = take(KERNEL * per).reshape(n, KERNEL, per).transpose(1, 0, 2)
        bias = take(per).reshape(1, CHANNELS)
        table = jnp.concatenate(
            [taps.reshape(KERNEL, CHANNELS), bias, jnp.zeros((3, CHANNELS), F32)]
        )
        cw = jnp.concatenate(
            [lax.dynamic_slice_in_dim(table, f * width, width, 1), table[:, INNER:]], axis=1
        )
        small.append((gain, cw, hp, gout))

    win = [(near_z0, far_z0, near_x0, far_x0), None]
    expand = (
        jnp.arange(heads)[:, None] == jnp.arange(width)[None, :] // HEAD_DIM
    ).astype(BF16)
    zero_state = jnp.zeros((STATE, width), F32)
    zero_edge = jnp.zeros((8, width + GROUP), F32)

    def project_x(normed, layer):
        return project(ids, normed, win[layer][2], win[layer][3], layer)

    def project_z(normed, layer):
        return project(ids, normed, win[layer][0], win[layer][1], layer)

    def decay_of(px, hp):
        decay = jax.nn.softplus(px[:, width + GROUP :] + hp[0:1]) * hp[1:2]
        return jnp.repeat(jnp.exp(jnp.sum(decay, axis=0)), HEAD_DIM)[None, :]

    def scan(px, layer):
        _, cw, hp, _ = small[layer]
        args = (px, cw, hp)
        if segments == 1:
            return run_forward(*args, zero_state, zero_edge, rows), zero_state
        edge = next_segment(px[-8:, : width + GROUP], 1)
        local = run_forward(*args, zero_state, edge, rows)[2][-1]
        state = relay(decay_of(px, hp), local, False)
        return run_forward(*args, state, edge, rows), state

    def unscan(pz, px, fwd, dn, rc, layer):
        (y, filt, states), state = fwd
        _, cw, hp, gout = small[layer]
        args = (pz, px, y, filt, dn, rc, states, state, cw, hp, expand, gout)
        if segments == 1:
            return run_backward(*args, zero_state, zero_edge, rows, n)[:6]
        local = run_backward(*args, zero_state, zero_edge, rows, n)[6]
        grad = relay(decay_of(px, hp), local, True)
        edge = next_segment(run_backward(*args, grad, zero_edge, rows, n)[7], -1)
        return run_backward(*args, grad, edge, rows, n)[:6]

    def gate(pz, y):
        return y * jax.nn.silu(pz)

    def gated(pz, y, r, layer):
        return (gate(pz, y) * r[:, None] * small[layer][3]).astype(BF16)

    def sum_of_shares(v):
        return jnp.sum(to_all(v), axis=0)

    normed_in0 = normalised(all_h0.astype(F32), small[0][0]).astype(BF16)
    px0 = project_x(normed_in0, 0)
    px0, pieces_x1, pieces_z1, own_ct, wo_mine, own_len = tie(
        (px0, pieces_x, pieces_z, at(cotangent, c)[0], w_out[0], at(lengths, c))
    )
    near_x1, far_x1 = fetch(pieces_x1, 1)
    wo_other = swap_section(wo_mine)
    wo = (pick(wo_mine, wo_other), pick(wo_other, wo_mine))
    slot_pairs = [
        ((j * n + i) * n + k, (j * n + k) * n + i)
        for j in range(segments)
        for i in range(n)
        for k in range(n)
    ]
    length = lax.ppermute(own_len, ("seq", "fsdp"), slot_pairs)
    first_row = (place // n) * n * rows
    all_valid = first_row + jnp.arange(n * rows, dtype=jnp.int32) < length[0]
    all_valid = all_valid.astype(F32)[:, None]
    own_rows = lambda v: lax.dynamic_slice_in_dim(v, f * rows, rows, 0)
    valid = own_rows(all_valid)
    h0 = own_rows(all_h0)
    fwd0, near_z0, wo = tie((scan(px0, 0), near_z0, wo))
    far_z0 = [lax.ppermute(v, "section", [(0, 1)]) for v in near_z0]
    win[0] = (near_z0, far_z0, near_x0, far_x0)
    pz0 = project_z(normed_in0, 0)
    g0 = gate(pz0, fwd0[0][0])
    stat0 = jnp.sum(g0 * g0, axis=1)
    stat0 = sum_of_shares(stat0.reshape(n, rows)).reshape(-1)
    r0 = lax.rsqrt(stat0 / INNER + EPS)
    normed0 = gated(pz0, fwd0[0][0], r0, 0)
    normed0, near_x1, own_ct = tie((normed0, near_x1, own_ct))
    part_ct = in_group(exchange(quarters(own_ct)))
    far_x1 = [lax.ppermute(v, "section", [(1, 0)]) for v in near_x1]
    mixed0 = scatter_sum(jnp.dot(normed0, wo[0], preferred_element_type=F32))
    mixed0, part_ct, pieces_z1 = tie((mixed0, part_ct, pieces_z1))
    near_z1, far_z1 = fetch(pieces_z1, 1)
    out0 = valid * (h0.astype(F32) + mixed0)
    h1 = out0.astype(BF16)

    normed_in1 = gather_rows(normalised(h1.astype(F32), small[1][0]).astype(BF16))
    normed_in1, far_x1 = tie((normed_in1, far_x1))
    win[1] = (near_z1, far_z1, near_x1, far_x1)
    px1 = project_x(normed_in1, 1)
    px1, near_z1, part_ct = tie((px1, near_z1, part_ct))
    far_z1 = [lax.ppermute(v, "section", [(1, 0)]) for v in near_z1]
    win[1] = (near_z1, far_z1, near_x1, far_x1)
    all_ct = whole_slot(part_ct)
    fwd1 = scan(px1, 1)
    fwd1, all_ct = tie((fwd1, all_ct))
    dout1 = own_rows(all_ct).astype(F32)
    dmixed1 = (all_valid * all_ct.astype(F32)).astype(BF16)
    dn1 = dot_cols(dmixed1, wo[1])
    pz1 = project_z(normed_in1, 1)
    g1 = gate(pz1, fwd1[0][0])
    stat1 = sum_of_shares(
        jnp.stack(
            [
                jnp.sum(g1 * g1, axis=1).reshape(n, rows),
                jnp.sum(g1 * dn1 * small[1][3], axis=1).reshape(n, rows),
            ]
        )
    ).reshape(2, -1)
    r1 = lax.rsqrt(stat1[0] / INNER + EPS)
    normed1 = gated(pz1, fwd1[0][0], r1, 1)

    part_width = width // 2

    def cut_half(v, k):
        size = v.shape[1] // 2
        return lax.dynamic_slice_in_dim(v, k * size, size, 1)

    def narrow_of(parts, k):
        return jnp.concatenate([cut_half(v, k) for v in parts], axis=1)

    def away_in(normed_in, part, narrow=()):
        away = [dot_rows(normed_in, cut_half(part, 1 - c)).astype(BF16)]
        if narrow:
            away.append(dot_rows(narrow_of(narrow, 1 - c), normed_in).astype(BF16))
        return [swap_section(v) for v in away]

    def own_in_piece(normed_in, part, away, narrow=()):
        total = dot_rows(normed_in, cut_half(part, c)) + away[0].astype(F32)
        result = total.astype(BF16).reshape(n, share, -1)
        if narrow:
            total = (dot_rows(narrow_of(narrow, c), normed_in) + away[1].astype(F32)).astype(BF16)
            fill = jnp.zeros((-total.shape[0] % 64, D), BF16)
            rest = jnp.concatenate([total, fill]).reshape(-1, n, share).transpose(1, 0, 2)
            result = jnp.concatenate([result, rest], axis=1)
        return result

    def away_out(normed, dmixed):
        return swap_section(dot_rows(cut_half(normed, 1 - c), dmixed).astype(BF16))

    def own_out_piece(normed, dmixed, away):
        return (dot_rows(cut_half(normed, c), dmixed) + away.astype(F32)).astype(BF16)

    def with_group(dxs, dbc):
        total = jnp.sum(exchange(dbc), axis=0).astype(BF16)
        column = jnp.arange(GROUP)[None, :] // group
        own = jnp.where(column == f, jnp.concatenate([total] * n, axis=1), 0)
        full = lax.dynamic_update_slice(dxs, own.astype(BF16), (0, width))
        return full, (dxs[:, :width], [total, dxs[:, width + GROUP :]])

    def back_in(dz, full, layer, kind):
        near_z, far_z, near_x, far_x = win[layer]
        return project_back(ids, dz, full, (near_z, near_x), (far_z, far_x), layer, kind)

    def back_norm(dout, dnormed_in, h, gain):
        h = h.astype(F32)
        r = lax.rsqrt(jnp.mean(h * h, axis=-1, keepdims=True) + EPS)
        u = dnormed_in * gain
        mean = jnp.mean(u * h, axis=-1, keepdims=True)
        dgain = jnp.sum(dnormed_in * h * r, axis=0)
        return valid * dout + r * u - h * (r * r * r) * mean, dgain

    def scales(r, coef):
        top = jnp.stack([r.reshape(n, rows), coef.reshape(n, rows)], axis=1)
        return jnp.concatenate([top, jnp.zeros((n, 6, rows), F32)], axis=1)

    def packed(dgin, d, out, mixed):
        dgain, dconv, dhp = d[3][0], d[4][:5], d[5][:3]
        put = lambda v, size, at_lane: lax.dynamic_update_slice(
            jnp.zeros(v.shape[:-1] + (size,), F32), v, (0,) * (v.ndim - 1) + (at_lane,)
        )
        conv = put(dconv[:, :width], CHANNELS, f * width)
        conv = conv.at[:, INNER:].set(dconv[:, width:])
        totals = jnp.stack(
            [jnp.sum(out * out), jnp.sum((valid * mixed) ** 2), jnp.sum(valid)]
        )
        return jnp.concatenate(
            [
                dgin,
                conv.reshape(-1),
                put(dhp, HEADS, f * heads).reshape(-1),
                put(dgain, INNER, f * width),
                totals,
            ]
        )

    def hand_over(v, layer):
        return lax.ppermute(v, "section", [(1 - layer, layer)])

    sums = SeqSums()
    rc1 = scales(r1, (r1 * r1 * r1 / INNER) * stat1[1])
    away = away_out(normed1, dmixed1)
    o1 = sums.add(own_out_piece(normed1, dmixed1, away))
    rc1, normed1, dn1 = sums.end((rc1, normed1, dn1))

    sums.begin()
    d1 = unscan(pz1, px1, fwd1, dn1, rc1, 1)
    mixed1 = scatter_sum(jnp.dot(normed1, wo[1], preferred_element_type=F32).astype(BF16))
    d1, mixed1 = sums.end((d1, mixed1))

    sums.begin()
    away = away_in(normed_in1, d1[0])
    full1, xs1 = with_group(d1[1], d1[2])
    back1 = back_in(d1[0], full1, 1, F32)
    gz = own_in_piece(normed_in1, d1[0], away)
    out1 = valid * (h1.astype(F32) + mixed1)
    back_h = exchange(quarters(jnp.concatenate([h1, out1.astype(BF16)])))
    back1, xs1, full1, gz, out1, back_h = sums.end((back1, xs1, full1, gz, out1, back_h))
    z1 = sums.add(gz)

    sums.begin()
    dnin1 = scatter_sum(back1)
    away = away_in(normed_in1, *xs1)
    gx = own_in_piece(normed_in1, xs1[0], away, xs1[1])
    back_h = in_group(back_h)
    grad1, dgin1 = back_norm(dout1, dnin1, h1, small[1][0])
    dout0 = grad1.astype(BF16).astype(F32)
    dmixed0_own = (valid * dout0).astype(BF16)
    along0 = jnp.sum(dmixed0_own.astype(F32) * mixed0, axis=-1)
    grad1, dgin1, dout0, dmixed0_own, along0, gx, back_h = sums.end(
        (grad1, dgin1, dout0, dmixed0_own, along0, gx, back_h)
    )
    x1 = sums.add(gx)

    sums.begin()
    dmixed0 = gather_rows(dmixed0_own)
    along0 = to_all(along0).reshape(-1)
    rc0 = scales(r0, (r0 * r0 / INNER) * along0)
    back_h = joined(exchange(back_h))
    dmixed0, rc0, back_h = sums.end((dmixed0, rc0, back_h))

    sums.begin()
    dn0 = dot_cols(dmixed0, wo[0])
    d0 = unscan(pz0, px0, fwd0, dn0, rc0, 0)
    go = own_out_piece(normed0, dmixed0, away_out(normed0, dmixed0))
    p1 = packed(dgin1, d1, out1, mixed1)
    d0, go, p1 = sums.end((d0, go, p1))
    o0 = sums.add(go)

    sums.finish([o1, z1])
    sums.begin()
    away = away_in(normed_in0, d0[0])
    full0, xs0 = with_group(d0[1], d0[2])
    gz = own_in_piece(normed_in0, d0[0], away)
    away = away_in(normed_in0, *xs0)
    gx = own_in_piece(normed_in0, xs0[0], away, xs0[1])
    own_z1 = exchange(sums.values[z1])
    full0, gz, gx, own_z1 = sums.end((full0, gz, gx, own_z1))
    z0 = sums.add(gz)

    sums.begin()
    gx = exchange(gx)
    back0 = back_in(d0[0], full0, 0, BF16)
    gx, back0 = sums.end((gx, back0))
    x0 = sums.add(gx)

    def hand_over(v, layer):
        return lax.ppermute(v, "section", [(1 - layer, layer)])

    sums.begin()
    dnin0 = scatter_sum(back0)
    own_o1 = sums.values[o1]
    away_o1 = hand_over(own_o1, 1)
    away_z1 = hand_over(own_z1, 1)
    grad0, dgin0 = back_norm(dout0, dnin0, h0, small[0][0])
    grad0, dgin0, own_z1, away_z1, own_o1, away_o1 = sums.end(
        (grad0, dgin0, own_z1, away_z1, own_o1, away_o1)
    )

    sums.finish([x1, o0])
    sums.begin()
    own_x1 = exchange(sums.values[x1])
    own_o0 = sums.values[o0]
    away_o0 = hand_over(own_o0, 0)
    back_g = exchange(quarters(jnp.concatenate([grad0.astype(BF16), grad1.astype(BF16)])))
    p = jnp.stack([packed(dgin0, d0, out0, mixed0), p1])
    p = p + swap_section(p)
    p, back_g, own_x1, own_o0, away_o0 = sums.end((p, back_g, own_x1, own_o0, away_o0))

    sums.finish([z0])
    sums.begin()
    own_z0 = exchange(sums.values[z0])
    away_x1 = hand_over(own_x1, 1)
    m = 1
    while m < n:
        p = p + move_fsdp(p, m)
        m *= 2
    away_z0 = hand_over(own_z0, 0)
    p, back_g, own_z0, away_z0, own_x1, away_x1 = sums.end(
        (p, back_g, own_z0, away_z0, own_x1, away_x1)
    )
    sums.finish([x0])
    own_x0 = sums.values[x0]
    away_x0 = hand_over(own_x0, 0)
    back_g = in_group(back_g)
    m = 1
    while m < nz:
        p = p + move_seq(p, m)
        m *= 2
    p = pick(p[0], p[1])

    used = 0

    def part(size):
        nonlocal used
        used += size
        return p[used - size : used]

    mine_of = lambda v, size: lax.dynamic_slice_in_dim(v, f * size, size, v.ndim - 1)
    o_gain_in = mine_of(part(D), share)
    o_conv = mine_of(part(5 * CHANNELS).reshape(5, CHANNELS), CHANNELS // n)
    o_heads = mine_of(part(3 * HEADS).reshape(3, HEADS), heads)
    o_gain_out = mine_of(part(INNER), width)
    totals = part(3)
    act_rms = jnp.sqrt(totals[:2] / (totals[2] * D))[None]

    held = [
        [(own_z0, own_x0, own_o0), (own_z1, own_x1, own_o1)],
        [(away_z0, away_x0, away_o0), (away_z1, away_x1, away_o1)],
    ]

    def both_halves(a, b):
        return jnp.stack([pick(a, b), pick(b, a)], axis=1)

    rows_of = GROUP // n // 2, HEADS // n // 2
    narrow = [pick(side[0][1], side[1][1])[:, share : share + sum(rows_of)] for side in held]
    narrow = both_halves(*[v.astype(F32) for v in narrow])
    small_in = jnp.concatenate(
        [
            narrow[:, :, : rows_of[0]].reshape(GROUP, share),
            narrow[:, :, rows_of[0] :].reshape(HEADS, share),
        ]
    )
    g_w_in = []
    shape_in = (2 * INNER + GROUP + HEADS, share)
    for k, rows_of_small in ((0, None), (1, (2 * INNER, GROUP + HEADS))):
        if g_w_in:
            back_g, g_w_in = tie((back_g, g_w_in))
            back_g = exchange(back_g)
        arrays, plan = [], []
        for s in range(2):
            arrays += [held[s][0][k], held[s][1][k]]
            firsts = tuple(k * INNER + q * width for q in range(n))
            plan.append((len(arrays) - 2, len(arrays) - 1, s, firsts))
        g_w_in = [
            place_in(
                ids, arrays, tuple(plan), small_in, rows_of_small, g_w_in, shape_in, part_width
            )
        ]
    g_w_in, back_g = tie((g_w_in, back_g))
    back = jnp.concatenate([back_h, joined(back_g)])
    halves_out = [pick(side[0][2], side[1][2]) for side in held]
    g_w_out = jnp.concatenate([pick(*halves_out), pick(*halves_out[::-1])]).astype(F32)

    back = back.reshape(2, 2, rows, D)
    kept_back = pick(back[:, 0], back[:, 1])
    other_back = swap_section(pick(back[:, 1], back[:, 0]))
    both_back = jnp.stack(
        [pick(kept_back, other_back), pick(other_back, kept_back)], axis=1
    )
    return (
        both_back[0][None, :, None],
        both_back[1].astype(F32)[None, :, None],
        o_gain_in[None],
        g_w_in[0].T[None],
        o_conv[None, :4],
        o_conv[None, 4],
        o_heads[None, 0],
        o_heads[None, 1],
        o_heads[None, 2],
        o_gain_out[None],
        g_w_out[None],
        act_rms,
    )


def solution(mesh):
    in_specs = (
        P(None, "fsdp", "seq", None),
        P(None, "fsdp", "seq", None),
        P(None, "fsdp"),
        P("section", "fsdp"),
        P("section", "fsdp", None),
        P("section", None, "fsdp"),
        P("section", "fsdp"),
        P("section", "fsdp"),
        P("section", "fsdp"),
        P("section", "fsdp"),
        P("section", "fsdp"),
        P("section", "fsdp", None),
    )
    out_specs = (
        P("section", None, "fsdp", "seq", None),
        P("section", None, "fsdp", "seq", None),
        P("section", "fsdp"),
        P("section", "fsdp", None),
        P("section", None, "fsdp"),
        P("section", "fsdp"),
        P("section", "fsdp"),
        P("section", "fsdp"),
        P("section", "fsdp"),
        P("section", "fsdp"),
        P("section", "fsdp", None),
        P("section", None),
    )
    return jax.shard_map(
        per_device, mesh=mesh, in_specs=in_specs, out_specs=out_specs, check_vma=False
    )
```

```python
import functools

import jax
import jax.numpy as jnp
from jax import lax
from jax.experimental import pallas as pl
from jax.experimental.pallas import tpu as pltpu
from jax.sharding import PartitionSpec as P

D = 2048
INNER = 4096
HEADS = 64
HEAD_DIM = 64
STATE = 128
KERNEL = 4
GROUP = 2 * STATE
CHANNELS = INNER + GROUP
LANES = 128
EPS = 1e-05
F32 = jnp.float32
BF16 = jnp.bfloat16
VMEM_BYTES = 48 * 1024 * 1024


def split(v):
    hi = v.astype(BF16)
    return hi, (v - hi.astype(F32)).astype(BF16)


def dot32(a, b, ca, cb):
    (ah, al), (bh, bl) = (v if isinstance(v, tuple) else split(v) for v in (a, b))
    one = lambda p, q: lax.dot_general(
        p, q, (((ca,), (cb,)), ((), ())), preferred_element_type=F32
    )
    return one(ah, bh) + (one(ah, bl) + one(al, bh))


def step_sizes(raw, hp, rows):
    shifted = raw + hp[0:1, :]
    dt = jnp.maximum(shifted, 0.0) + jnp.log1p(jnp.exp(-jnp.abs(shifted)))
    decay = dt * hp[1:2, :]
    row = lax.broadcasted_iota(jnp.int32, (rows, rows), 0)
    col = lax.broadcasted_iota(jnp.int32, (rows, rows), 1)
    lower = (row >= col).astype(F32)
    cum = dot32(lower, decay, 1, 0)
    cum_t = dot32(decay, lower, 0, 1)
    return shifted, dt, cum, cum_t, row, col, lower


def pair_lanes(v, j, first):
    return jnp.where(first, v[:, 2 * j : 2 * j + 1], v[:, 2 * j + 1 : 2 * j + 2])


def head_sums(v, table):
    hi, low = split(v)
    one = lambda p: lax.dot_general(
        p, table, (((1,), (1,)), ((), ())), preferred_element_type=F32
    )
    return one(hi) + one(low)


def forward_kernel(proj, cw, hp, s0, e0, y_ref, filt_ref, st_ref, state, xp, xw_s, last_s):
    i = pl.program_id(0)
    rows, width = y_ref.shape

    @pl.when(i == 0)
    def _():
        state[...] = s0[...]
        xp[0:8, :] = e0[...]

    xp[8 : 8 + rows, :] = proj[:, : width + GROUP]

    def conv_tile(lo):
        acc = cw[4:5, lo : lo + LANES]
        for k in range(KERNEL):
            acc = acc + cw[k : k + 1, lo : lo + LANES] * xp[5 + k : 5 + k + rows, lo : lo + LANES]
        filt_ref[:, lo : lo + LANES] = acc
        return acc * jax.nn.sigmoid(acc)

    b_c = conv_tile(width)
    c_c = conv_tile(width + STATE)
    _, dt, cum, cum_t, row, col, _ = step_sizes(proj[:, width + GROUP :], hp, rows)
    last = cum[rows - 1 : rows, :]
    ecum = jnp.exp(cum)
    weight = jnp.exp(last - cum) * dt
    elast = jnp.exp(last)
    b_c, c_c = split(b_c), split(c_c)
    carried = dot32(c_c, state[...], 1, 0)
    scores = dot32(c_c, b_c, 1, 1)
    causal = row >= col
    lane = lax.broadcasted_iota(jnp.int32, (rows, LANES), 1)
    first = lane < HEAD_DIM
    for j in range(width // LANES):
        lo = j * LANES
        here = slice(lo, lo + LANES)
        x = conv_tile(lo)
        xd = x * pair_lanes(dt, j, first)
        m = []
        for h in (2 * j, 2 * j + 1):
            gap = cum[:, h : h + 1] - cum_t[h : h + 1, :]
            m.append(jnp.exp(jnp.where(causal, gap, -1e30)) * scores)
        xd2 = jnp.concatenate([jnp.where(first, xd, 0.0), jnp.where(first, 0.0, xd)])
        y = (
            dot32(jnp.concatenate(m, axis=1), xd2, 1, 0)
            + carried[:, here] * pair_lanes(ecum, j, first)
            + pair_lanes(hp[2:3, :], j, first[0:1]) * x
        )
        y_ref[:, here] = y
        xw_s[:, here] = x * pair_lanes(weight, j, first)
        last_s[0:1, here] = pair_lanes(elast, j, first[0:1])
    state[...] = state[...] * last_s[0:1, :] + dot32(b_c, xw_s[...], 0, 0)
    st_ref[0] = state[...]
    xp[0:8, :] = xp[rows : rows + 8, :]


def backward_kernel(
    pz,
    proj,
    y_ref,
    filt,
    dn,
    rc,
    st_before,
    st_out,
    s0,
    cw,
    hp,
    table,
    gain,
    g0,
    e0,
    dz_ref,
    dproj,
    dbc_ref,
    dgain_ref,
    dconv_ref,
    dhp_ref,
    gfin_ref,
    efin_ref,
    grad,
    dfp,
    both,
    xw_s,
    dyc_s,
    rowv,
):
    i = pl.program_id(0)
    rows, width = y_ref.shape
    heads = hp.shape[1]

    @pl.when(i == 0)
    def _():
        grad[...] = g0[...]
        dfp[rows : rows + 8, :] = e0[...]
        dgain_ref[...] = jnp.zeros_like(dgain_ref)
        dconv_ref[...] = jnp.zeros_like(dconv_ref)
        dhp_ref[...] = jnp.zeros_like(dhp_ref)

    def silu_pair(v):
        s = jax.nn.sigmoid(v)
        a = v * s
        return a, s * (1.0 + v - a)

    b_c, b_d = silu_pair(filt[:, width : width + STATE])
    c_c, c_d = silu_pair(filt[:, width + STATE :])
    shifted, dt, cum, cum_t, row, col, lower = step_sizes(proj[:, width + GROUP :], hp, rows)
    last = cum[rows - 1 : rows, :]
    tail = jnp.exp(last - cum)
    ecum = jnp.exp(cum)
    elast = jnp.exp(last)
    b_c, c_c = split(b_c), split(c_c)
    grad_p = split(grad[...])
    k_all = dot32(b_c, grad_p, 1, 0)
    scores_t = dot32(b_c, c_c, 1, 1)
    causal_t = row <= col
    lane = lax.broadcasted_iota(jnp.int32, (rows, LANES), 1)
    first = lane < HEAD_DIM
    dcb_t = jnp.zeros((rows, rows), F32)
    rc_t = dot32((row == col).astype(F32), rc[0], 1, 1)
    r = rc_t[:, 0:1]
    coef = rc_t[:, 1:2]
    rowv[0:1, :] = jnp.sum(grad[...] * st_out[0], axis=0, keepdims=True)
    for j in range(width // LANES):
        lo = j * LANES
        here = slice(lo, lo + LANES)
        z = pz[:, here]
        y = y_ref[:, here]
        sz, dsz = silu_pair(z)
        g = y * sz
        dnt = dn[:, here]
        dg = dnt * gain[0:1, here] * r - g * coef
        dgain_ref[0:1, here] += jnp.sum(dnt * g * r, axis=0, keepdims=True)
        dy = dg * sz
        dz_ref[:, here] = (dg * y * dsz).astype(BF16)
        x, xder = silu_pair(filt[:, here])
        dt_e = pair_lanes(dt, j, first)
        tail_e = pair_lanes(tail, j, first)
        xd = x * dt_e
        dy2 = split(jnp.concatenate([jnp.where(first, dy, 0.0), jnp.where(first, 0.0, dy)]))
        decays = []
        for h in (2 * j, 2 * j + 1):
            gap = cum_t[h : h + 1, :] - cum[:, h : h + 1]
            decays.append(jnp.exp(jnp.where(causal_t, gap, -1e30)))
        m = jnp.concatenate([d * scores_t for d in decays], axis=1)
        dm = dot32(xd, dy2, 1, 1)
        dcb_t = dcb_t + (decays[0] * dm[:, :rows] + decays[1] * dm[:, rows:])
        v = dot32(m, dy2, 1, 0) + k_all[:, here] * tail_e
        skip = pair_lanes(hp[2:3, :], j, first[0:1])
        dx = dt_e * v + skip * dy
        both[0:rows, here] = x * v
        both[rows : 2 * rows, here] = dy * (y - skip * x)
        rowv[1:2, here] = jnp.sum(dy * x, axis=0, keepdims=True)
        rowv[2:3, here] = pair_lanes(elast, j, first[0:1])
        xw_s[:, here] = xd * tail_e
        dyc_s[:, here] = dy * pair_lanes(ecum, j, first)
        dfp[0:rows, here] = dx * xder
    dcb_t = split(dcb_t)
    dyc = split(dyc_s[...])
    st_in = jnp.where(i == pl.num_programs(0) - 1, s0[...], st_before[0])
    dc = dot32(dcb_t, b_c, 0, 0) + dot32(dyc, st_in, 1, 1)
    db = dot32(dcb_t, c_c, 1, 0) + dot32(xw_s[...], grad_p, 1, 1)
    dfp[0:rows, width : width + STATE] = db * b_d
    dfp[0:rows, width + STATE :] = dc * c_d
    grad[...] = grad[...] * rowv[2:3, :] + dot32(c_c, dyc, 0, 0)
    gfin_ref[...] = grad[...]

    sums = head_sums(both[...], table[...])
    rsums = head_sums(rowv[...], table[...])
    ddt_x = sums[0:rows]
    dcum = sums[rows : 2 * rows] - dt * ddt_x
    upto = lax.broadcasted_iota(jnp.int32, (rows, heads), 0)
    dcum = dcum + jnp.where(upto == rows - 1, rsums[0:1, :], 0.0)
    ddecay = dot32(lower, dcum, 0, 0)
    ddt = ddt_x + hp[1:2, :] * ddecay
    draw = ddt * jax.nn.sigmoid(shifted)
    dproj[:, width + GROUP :] = draw.astype(BF16)
    dhp_ref[0:1, :] += jnp.sum(draw, axis=0, keepdims=True)
    dhp_ref[1:2, :] += jnp.sum(ddecay * dt, axis=0, keepdims=True) * hp[1:2, :]
    dhp_ref[2:3, :] += rsums[1:2, :]

    for lo in range(0, width + GROUP, LANES):
        here = slice(lo, lo + LANES)
        src = proj[:, here]
        total = jnp.zeros((rows, LANES), F32)
        for k in range(KERNEL):
            shift = KERNEL - 1 - k
            moved = dfp[shift : shift + rows, here]
            total = total + cw[k : k + 1, here] * moved
            dconv_ref[k : k + 1, here] += jnp.sum(src * moved, axis=0, keepdims=True)
        dconv_ref[4:5, here] += jnp.sum(dfp[0:rows, here], axis=0, keepdims=True)
        if lo < width:
            dproj[:, here] = total.astype(BF16)
        else:
            dproj[:, here] = jnp.zeros((rows, LANES), BF16)
            share = dbc_ref.shape[2]
            for k in range(LANES // share):
                dbc_ref[(lo - width) // share + k] = total[:, k * share : (k + 1) * share]
    dfp[rows : rows + 8, :] = dfp[0:8, :]
    efin_ref[...] = dfp[0:8, :]


def whole(shape):
    return pl.BlockSpec(shape, lambda i: (0,) * len(shape))


def run_forward(proj, cw, hp, s0, e0, rows):
    total, width = proj.shape[0], s0.shape[1]
    count = total // rows
    block = lambda w: pl.BlockSpec((rows, w), lambda i: (i, 0))
    shape = jax.ShapeDtypeStruct
    return pl.pallas_call(
        forward_kernel,
        grid=(count,),
        in_specs=[block(proj.shape[1])] + [whole(v.shape) for v in (cw, hp, s0, e0)],
        out_specs=[
            block(width),
            block(width + GROUP),
            pl.BlockSpec((1, STATE, width), lambda i: (i, 0, 0)),
        ],
        scratch_shapes=[
            pltpu.VMEM((STATE, width), F32),
            pltpu.VMEM((rows + 8, width + GROUP), F32),
            pltpu.VMEM((rows, width), F32),
            pltpu.VMEM((8, width), F32),
        ],
        out_shape=[
            shape((total, width), F32),
            shape((total, width + GROUP), F32),
            shape((count, STATE, width), F32),
        ],
        compiler_params=pltpu.CompilerParams(vmem_limit_bytes=VMEM_BYTES),
        name="scan_forward",
    )(proj, cw, hp, s0, e0)


def run_backward(pz, proj, y, filt, dn, rc, states, s0, cw, hp, table, gain, g0, e0, rows, places):
    total, (heads, width) = proj.shape[0], table.shape
    count = total // rows
    turn = lambda i: count - 1 - i
    block = lambda w: pl.BlockSpec((rows, w), lambda i: (turn(i), 0))
    shape = jax.ShapeDtypeStruct
    share = GROUP // places
    return pl.pallas_call(
        backward_kernel,
        grid=(count,),
        in_specs=[
            block(width),
            block(proj.shape[1]),
            block(width),
            block(width + GROUP),
            block(width),
            pl.BlockSpec((1, 8, rows), lambda i: (turn(i), 0, 0)),
            pl.BlockSpec((1, STATE, width), lambda i: (jnp.maximum(turn(i) - 1, 0), 0, 0)),
            pl.BlockSpec((1, STATE, width), lambda i: (turn(i), 0, 0)),
        ]
        + [whole(v.shape) for v in (s0, cw, hp, table, gain, g0, e0)],
        out_specs=[
            block(width),
            block(proj.shape[1]),
            pl.BlockSpec((places, rows, share), lambda i: (0, turn(i), 0)),
            whole((8, width)),
            whole((8, width + GROUP)),
            whole((8, heads)),
            whole((STATE, width)),
            whole((8, width + GROUP)),
        ],
        scratch_shapes=[
            pltpu.VMEM((STATE, width), F32),
            pltpu.VMEM((rows + 8, width + GROUP), F32),
            pltpu.VMEM((2 * rows, width), F32),
            pltpu.VMEM((rows, width), F32),
            pltpu.VMEM((rows, width), F32),
            pltpu.VMEM((8, width), F32),
        ],
        out_shape=[
            shape((total, width), BF16),
            shape(proj.shape, BF16),
            shape((places, total, share), F32),
            shape((8, width), F32),
            shape((8, width + GROUP), F32),
            shape((8, heads), F32),
            shape((STATE, width), F32),
            shape((8, width + GROUP), F32),
        ],
        compiler_params=pltpu.CompilerParams(vmem_limit_bytes=VMEM_BYTES),
        name="scan_backward",
    )(pz, proj, y, filt, dn, rc, states, states, s0, cw, hp, table, gain, g0, e0)


def bring(step, pieces, buffers, sems, own):
    for near, far, buffer, sem in zip(*pieces, buffers, sems):
        to, done = buffer.at[step % 2], sem.at[step % 2]

        @pl.when(own)
        def _():
            pltpu.make_async_copy(near[step], to, done).start()

        @pl.when(jnp.logical_not(own))
        def _():
            pltpu.make_async_copy(far[step], to, done).start()


def arrived(step, pieces, buffers, sems):
    for near, buffer, sem in zip(pieces[0], buffers, sems):
        pltpu.make_async_copy(near[step], buffer.at[step % 2], sem.at[step % 2]).wait()
    return [buffer.at[step % 2] for buffer in buffers]


def project_kernel(ids, normed, *refs, layer, n):
    near, far = [refs[0:n]], [refs[n : 2 * n]]
    out, buffer, sem = refs[2 * n :]
    pieces = (near, far)
    own = ids[1] == layer
    columns = out.shape[1]
    share = buffer.shape[2]
    bring(0, pieces, [buffer], [sem], own)
    for m in range(n):
        if m + 1 < n:
            bring(m + 1, pieces, [buffer], [sem], own)
        (w,) = arrived(m, pieces, [buffer], [sem])
        from_place = pl.multiple_of(jnp.bitwise_xor(ids[0], m) * share, share)
        a = normed[:, pl.ds(from_place, share)]
        for lo in range(0, columns, 256):
            here = slice(lo, min(lo + 256, columns))
            v = lax.dot_general(
                a, w[here, :], (((1,), (1,)), ((), ())), preferred_element_type=F32
            )
            out[:, here] = v if m == 0 else out[:, here] + v


def project(ids, normed, near, far, layer):
    n = len(near)
    columns, share = near[0].shape
    rows = normed.shape[0]
    vmem = pl.BlockSpec(memory_space=pltpu.VMEM)
    return pl.pallas_call(
        functools.partial(project_kernel, layer=layer, n=n),
        in_specs=[pl.BlockSpec(memory_space=pltpu.SMEM), vmem]
        + [pl.BlockSpec(memory_space=pl.ANY)] * (2 * n),
        out_specs=vmem,
        scratch_shapes=[
            pltpu.VMEM((2, columns, share), BF16),
            pltpu.SemaphoreType.DMA((2,)),
        ],
        out_shape=jax.ShapeDtypeStruct((rows, columns), F32),
        compiler_params=pltpu.CompilerParams(vmem_limit_bytes=VMEM_BYTES),
        cost_estimate=pl.CostEstimate(
            flops=2 * rows * columns * share * n,
            bytes_accessed=columns * share * n * 2 + rows * columns * 4,
            transcendentals=0,
        ),
        name="project",
    )(ids, normed, *near, *far)


def back_kernel(ids, dz, dx, *refs, layer, n):
    near = (refs[0:n], refs[n : 2 * n])
    far = (refs[2 * n : 3 * n], refs[3 * n : 4 * n])
    out, zbuf, xbuf, zsem, xsem = refs[4 * n :]
    pieces = (near, far)
    own = ids[1] == layer
    share = zbuf.shape[2]
    args = ([zbuf, xbuf], [zsem, xsem])
    bring(0, pieces, *args, own)
    for m in range(n):
        if m + 1 < n:
            bring(m + 1, pieces, *args, own)
        wz, wx = arrived(m, pieces, *args)
        for lo in range(0, share, 256):
            here = slice(lo, lo + 256)
            v = jnp.dot(dz[...], wz[:, here], preferred_element_type=F32) + jnp.dot(
                dx[...], wx[:, here], preferred_element_type=F32
            )
            at_lane = pl.multiple_of(jnp.bitwise_xor(ids[0], m) * share + lo, 256)
            out[:, pl.ds(at_lane, 256)] = v.astype(out.dtype)


def project_back(ids, dz, dx, near, far, layer, kind):
    n = len(near[0])
    share = near[0][0].shape[1]
    rows = dz.shape[0]
    columns = dz.shape[1] + dx.shape[1]
    vmem = pl.BlockSpec(memory_space=pltpu.VMEM)
    return pl.pallas_call(
        functools.partial(back_kernel, layer=layer, n=n),
        in_specs=[pl.BlockSpec(memory_space=pltpu.SMEM), vmem, vmem]
        + [pl.BlockSpec(memory_space=pl.ANY)] * (4 * n),
        out_specs=vmem,
        scratch_shapes=[
            pltpu.VMEM((2, dz.shape[1], share), BF16),
            pltpu.VMEM((2, dx.shape[1], share), BF16),
            pltpu.SemaphoreType.DMA((2,)),
            pltpu.SemaphoreType.DMA((2,)),
        ],
        out_shape=jax.ShapeDtypeStruct((rows, n * share), kind),
        compiler_params=pltpu.CompilerParams(vmem_limit_bytes=VMEM_BYTES),
        cost_estimate=pl.CostEstimate(
            flops=2 * rows * columns * share * n,
            bytes_accessed=columns * share * n * 2 + rows * n * share * 2,
            transcendentals=0,
        ),
        name="project_back",
    )(ids, dz, dx, *near[0], *near[1], *far[0], *far[1])


def place_kernel(ids, *refs, plan, count, rows_of_small):
    small = refs[count]
    out, eye, pieces, blocks, in_sem, out_sem = refs[-6:]
    core = ids[1]
    size, share = blocks.shape[1:]

    def fetch(k):
        for layer in range(2):

            @pl.when(core == layer)
            def _():
                src = refs[plan[k][layer]]
                pltpu.make_async_copy(
                    src.at[:, pl.ds(0, share)], pieces.at[k % 2], in_sem.at[k % 2]
                ).start()

    def send(step, first, count):
        return pltpu.make_async_copy(
            blocks.at[step % 2, pl.ds(0, count)],
            out.at[pl.ds(first, count)],
            out_sem.at[step % 2],
        )

    eye[...] = (
        lax.broadcasted_iota(jnp.int32, eye.shape, 0)
        == lax.broadcasted_iota(jnp.int32, eye.shape, 1)
    ).astype(BF16)
    fetch(0)
    sent = []
    for k, (_, _, side, firsts) in enumerate(plan):
        if k + 1 < len(plan):
            fetch(k + 1)
        pltpu.make_async_copy(pieces.at[k % 2], pieces.at[k % 2], in_sem.at[k % 2]).wait()
        shift = jnp.where(side == 0, core, 1 - core) * size
        for p, first in enumerate(firsts):
            step = len(sent)
            if step >= 2:
                sent[step - 2].wait()
            blocks[step % 2] = lax.dot_general(
                pieces[k % 2, p],
                eye[...],
                (((0,), (0,)), ((), ())),
                preferred_element_type=F32,
            )
            sent.append(send(step, pl.multiple_of(first + shift, 8), size))
            sent[-1].start()
    if rows_of_small:
        step = len(sent)
        sent[step - 2].wait()
        first, count = rows_of_small
        sent.append(
            pltpu.make_async_copy(small, out.at[pl.ds(first, count)], out_sem.at[step % 2])
        )
        sent[-1].start()
    sent[-2].wait()
    sent[-1].wait()


def place_in(ids, arrays, plan, small, rows_of_small, before, shape, size):
    places, share = arrays[0].shape[0], shape[1]
    any_space = pl.BlockSpec(memory_space=pl.ANY)
    return pl.pallas_call(
        functools.partial(
            place_kernel, plan=plan, count=len(arrays), rows_of_small=rows_of_small
        ),
        in_specs=[pl.BlockSpec(memory_space=pltpu.SMEM)]
        + [any_space] * len(arrays)
        + [pl.BlockSpec(memory_space=pltpu.VMEM)]
        + [any_space] * len(before),
        out_specs=any_space,
        scratch_shapes=[
            pltpu.VMEM((share, share), BF16),
            pltpu.VMEM((2, places, share, size), BF16),
            pltpu.VMEM((2, size, share), F32),
            pltpu.SemaphoreType.DMA((2,)),
            pltpu.SemaphoreType.DMA((2,)),
        ],
        out_shape=jax.ShapeDtypeStruct(shape, F32),
        input_output_aliases={len(arrays) + 2: 0} if before else {},
        compiler_params=pltpu.CompilerParams(vmem_limit_bytes=VMEM_BYTES),
        name="place_in",
    )(ids, *arrays, small, *before)


def combine_kernel(flags, *refs, adds):
    count = len(adds)
    for k, add in enumerate(adds):
        v, got, out = refs[2 * k], refs[2 * k + 1], refs[2 * count + k]
        if add:
            out[...] = (v[...].astype(F32) + got[...].astype(F32)).astype(BF16)
        else:
            out[...] = jnp.where(flags[k] == 1, got[...], v[...])


def combine(items, flags):
    steps = 8
    shapes = [v.shape for v, _, _ in items]
    flat = [(v.reshape(-1, v.shape[-1]), g.reshape(-1, g.shape[-1])) for v, g, _ in items]
    spec = lambda v: pl.BlockSpec((v.shape[0] // steps, v.shape[1]), lambda i: (i, 0))
    out = pl.pallas_call(
        functools.partial(combine_kernel, adds=tuple(add for _, _, add in items)),
        grid=(steps,),
        in_specs=[pl.BlockSpec(memory_space=pltpu.SMEM)] + [spec(v) for p in flat for v in p],
        out_specs=[spec(v) for v, _ in flat],
        out_shape=[jax.ShapeDtypeStruct(v.shape, BF16) for v, _ in flat],
        compiler_params=pltpu.CompilerParams(vmem_limit_bytes=VMEM_BYTES),
        name="combine",
    )(flags, *[v for p in flat for v in p])
    return [v.reshape(shape) for v, shape in zip(out, shapes)]


def swap_section(v):
    return lax.ppermute(v, "section", [(0, 1), (1, 0)])


def at(v, k):
    return lax.dynamic_index_in_dim(v, k, 0, False)


def exchange(v):
    return lax.all_to_all(v, "fsdp", 0, 0, tiled=True)


def to_all(v):
    n = lax.axis_size("fsdp")
    return exchange(jnp.broadcast_to(v[None], (n,) + v.shape))


def gather_rows(v):
    return to_all(v).reshape(-1, v.shape[-1])


def scatter_sum(partial):
    n = lax.axis_size("fsdp")
    got = exchange(partial.reshape(n, -1, partial.shape[-1]))
    return jnp.sum(got.astype(F32), axis=0)


def in_group(v):
    n, s = lax.axis_size("fsdp"), lax.axis_size("seq")
    groups = [[j * n + i for i in range(n)] for j in range(s // n)]
    return lax.all_to_all(v, "seq", 0, 0, axis_index_groups=groups, tiled=True)


def quarters(v):
    n = lax.axis_size("fsdp")
    return v.reshape(v.shape[0], n, -1).transpose(1, 0, 2)


def joined(v):
    return v.transpose(1, 0, 2).reshape(v.shape[1], -1)


def move_fsdp(v, m):
    n = lax.axis_size("fsdp")
    return lax.ppermute(v, "fsdp", [(k, k ^ m) for k in range(n)])


def move_seq(v, m):
    s = lax.axis_size("seq")
    return lax.ppermute(v, "seq", [(k, k ^ m) for k in range(s)])


class SeqSums:
    def __init__(self):
        s = lax.axis_size("seq")
        half = s // 2
        self.pairs = [[(j, j + 1), (s - 1 - j, s - 2 - j)] for j in range(half - 1)]
        self.pairs.append([(half - 1, half), (half, half - 1)])
        self.inward = half
        self.pairs += [[(j + 1, j), (s - 2 - j, s - 1 - j)] for j in reversed(range(half - 1))]
        self.values, self.phase, self.moving = [], [], []

    def add(self, value):
        self.values.append(value)
        self.phase.append(0)
        return len(self.values) - 1

    def begin(self):
        taken = set()
        for k, step in enumerate(self.phase):
            if step == len(self.pairs) or step in taken:
                continue
            taken.add(step)
            self.moving.append((k, lax.ppermute(self.values[k], "seq", self.pairs[step])))

    def end(self, work):
        place = lax.axis_index("seq")
        items, flags = [], []
        for k, got in self.moving:
            step = self.phase[k]
            items.append((self.values[k], got, step < self.inward))
            here = [place == to for _, to in self.pairs[step]]
            flags.append(functools.reduce(jnp.logical_or, here))
            self.phase[k] = step + 1
        moved = combine(items, jnp.stack(flags).astype(jnp.int32)) if items else []
        still = [k for k, p in enumerate(self.phase) if p == 0]
        work, moved, rest = lax.optimization_barrier(
            (work, moved, [self.values[k] for k in still])
        )
        for (k, _), v in zip(self.moving, moved):
            self.values[k] = v
        for k, v in zip(still, rest):
            self.values[k] = v
        self.moving = []
        return work

    def finish(self, chunks):
        while any(self.phase[k] < len(self.pairs) for k in chunks):
            self.begin()
            self.end(())


def relay(total, local, reverse):
    n, s = lax.axis_size("fsdp"), lax.axis_size("seq")
    segments = s // n
    place = lax.axis_index("seq") // n
    own = lax.axis_index("seq") % n
    totals = lax.all_gather(total, "seq")
    locals_ = lax.all_gather(local, "seq")
    state = jnp.zeros_like(local)
    order = range(segments - 1, -1, -1) if reverse else range(segments)
    for j in order:
        use = (j > place) if reverse else (j < place)
        t = lax.dynamic_index_in_dim(totals, j * n + own, 0, False)
        v = lax.dynamic_index_in_dim(locals_, j * n + own, 0, False)
        state = jnp.where(use, t * state + v, state)
    return state


def next_segment(v, step):
    n, s = lax.axis_size("fsdp"), lax.axis_size("seq")
    pairs = [(k, k + step * n) for k in range(s) if 0 <= k + step * n < s]
    return lax.ppermute(v, "seq", pairs)


def dot_rows(a, b):
    return lax.dot_general(a, b, (((0,), (0,)), ((), ())), preferred_element_type=F32)


def dot_cols(a, b):
    return lax.dot_general(a, b, (((1,), (1,)), ((), ())), preferred_element_type=F32)


def normalised(h, gain):
    return h * lax.rsqrt(jnp.mean(h * h, axis=-1, keepdims=True) + EPS) * gain


def per_device(
    inputs,
    cotangent,
    lengths,
    gain_in,
    w_in,
    conv_w,
    conv_b,
    dt_bias,
    a_log,
    d_skip,
    gain_out,
    w_out,
):
    n = lax.axis_size("fsdp")
    nz = lax.axis_size("seq")
    segments = nz // n
    c = lax.axis_index("section")
    f = lax.axis_index("fsdp")
    place = lax.axis_index("seq")
    upper = c == 0
    rows = inputs.shape[2]
    width = INNER // n
    heads = HEADS // n
    share = D // n
    half = share // 2
    group = GROUP // n
    ids = jnp.stack([f, c]).astype(jnp.int32)
    tie = lax.optimization_barrier

    def pick(a, b):
        return jnp.where(upper, a, b)

    w = w_in[0].T

    def cut(first, size):
        return lax.dynamic_slice_in_dim(w, first, size, 0)

    def piece_z(m):
        return cut((f ^ m) * width, width)

    def piece_x(m):
        return jnp.concatenate(
            [
                cut(INNER + (f ^ m) * width, width),
                w[2 * INNER : 2 * INNER + GROUP],
                cut(2 * INNER + GROUP + (f ^ m) * heads, heads),
            ]
        )

    def fetch(pieces, layer):
        pairs = lambda m: [(layer * n + i, layer * n + (i ^ m)) for i in range(n)]
        near = [
            v if m == 0 else lax.ppermute(v, ("section", "fsdp"), pairs(m))
            for m, v in enumerate(pieces)
        ]
        return near, [lax.ppermute(v, "section", [(layer, 1 - layer)]) for v in near]

    def whole_slot(v):
        return joined(to_all(v.reshape(n * rows, share)))

    pack = jnp.concatenate(
        [
            gain_in[0],
            dt_bias[0],
            a_log[0],
            d_skip[0],
            gain_out[0],
            conv_w[0].reshape(-1),
            conv_b[0],
        ]
    )
    more = -(-pack.shape[0] // (16 * share)) * 16
    filled = jnp.concatenate([pack, jnp.zeros((more * share - pack.shape[0],), BF16)])
    filled = jnp.broadcast_to(filled.reshape(1, more, share), (n, more, share))
    first = exchange(jnp.concatenate([quarters(at(inputs, c)[0]), filled], axis=1))
    first, pieces_x = tie((first, [piece_x(m) for m in range(n)]))
    part_h0 = first[:, :rows]
    mine = first[:, rows:].reshape(n, -1)[:, : pack.shape[0]]
    near_x0, far_x0 = fetch(pieces_x, 0)
    part_h0 = in_group(part_h0)
    near_x0, part_h0 = tie((near_x0, part_h0))
    far_x0 = [lax.ppermute(v, "section", [(0, 1)]) for v in near_x0]
    pieces_z, part_h0 = tie(([piece_z(m) for m in range(n)], part_h0))
    all_h0 = whole_slot(part_h0)
    near_z0, far_z0 = fetch(pieces_z, 0)

    theirs = swap_section(mine)
    small = []
    for full in (pick(mine, theirs), pick(theirs, mine)):
        full = full.astype(F32)
        used = 0

        def take(size):
            nonlocal used
            used += size
            return full[:, used - size : used]

        gain = take(share).reshape(1, D)
        hp = [at(take(heads), f)[None] for _ in range(3)]
        hp = jnp.concatenate([hp[0], -jnp.exp(hp[1]), hp[2], jnp.zeros((5, heads), F32)])
        gout = at(take(width), f)[None]
        per = CHANNELS // n
        taps = take(KERNEL * per).reshape(n, KERNEL, per).transpose(1, 0, 2)
        bias = take(per).reshape(1, CHANNELS)
        table = jnp.concatenate(
            [taps.reshape(KERNEL, CHANNELS), bias, jnp.zeros((3, CHANNELS), F32)]
        )
        cw = jnp.concatenate(
            [lax.dynamic_slice_in_dim(table, f * width, width, 1), table[:, INNER:]], axis=1
        )
        small.append((gain, cw, hp, gout))

    win = [(near_z0, far_z0, near_x0, far_x0), None]
    expand = (
        jnp.arange(heads)[:, None] == jnp.arange(width)[None, :] // HEAD_DIM
    ).astype(BF16)
    zero_state = jnp.zeros((STATE, width), F32)
    zero_edge = jnp.zeros((8, width + GROUP), F32)

    def project_x(normed, layer):
        return project(ids, normed, win[layer][2], win[layer][3], layer)

    def project_z(normed, layer):
        return project(ids, normed, win[layer][0], win[layer][1], layer)

    def decay_of(px, hp):
        decay = jax.nn.softplus(px[:, width + GROUP :] + hp[0:1]) * hp[1:2]
        return jnp.repeat(jnp.exp(jnp.sum(decay, axis=0)), HEAD_DIM)[None, :]

    def scan(px, layer):
        _, cw, hp, _ = small[layer]
        args = (px, cw, hp)
        if segments == 1:
            return run_forward(*args, zero_state, zero_edge, rows), zero_state
        edge = next_segment(px[-8:, : width + GROUP], 1)
        local = run_forward(*args, zero_state, edge, rows)[2][-1]
        state = relay(decay_of(px, hp), local, False)
        return run_forward(*args, state, edge, rows), state

    def unscan(pz, px, fwd, dn, rc, layer):
        (y, filt, states), state = fwd
        _, cw, hp, gout = small[layer]
        args = (pz, px, y, filt, dn, rc, states, state, cw, hp, expand, gout)
        if segments == 1:
            return run_backward(*args, zero_state, zero_edge, rows, n)[:6]
        local = run_backward(*args, zero_state, zero_edge, rows, n)[6]
        grad = relay(decay_of(px, hp), local, True)
        edge = next_segment(run_backward(*args, grad, zero_edge, rows, n)[7], -1)
        return run_backward(*args, grad, edge, rows, n)[:6]

    def gate(pz, y):
        return y * jax.nn.silu(pz)

    def gated(pz, y, r, layer):
        return (gate(pz, y) * r[:, None] * small[layer][3]).astype(BF16)

    def sum_of_shares(v):
        return jnp.sum(to_all(v), axis=0)

    normed_in0 = normalised(all_h0.astype(F32), small[0][0]).astype(BF16)
    px0 = project_x(normed_in0, 0)
    px0, pieces_x1, pieces_z1, own_ct, wo_mine, own_len = tie(
        (px0, pieces_x, pieces_z, at(cotangent, c)[0], w_out[0], at(lengths, c))
    )
    near_x1, far_x1 = fetch(pieces_x1, 1)
    wo_other = swap_section(wo_mine)
    wo = (pick(wo_mine, wo_other), pick(wo_other, wo_mine))
    slot_pairs = [
        ((j * n + i) * n + k, (j * n + k) * n + i)
        for j in range(segments)
        for i in range(n)
        for k in range(n)
    ]
    length = lax.ppermute(own_len, ("seq", "fsdp"), slot_pairs)
    first_row = (place // n) * n * rows
    all_valid = first_row + jnp.arange(n * rows, dtype=jnp.int32) < length[0]
    all_valid = all_valid.astype(F32)[:, None]
    own_rows = lambda v: lax.dynamic_slice_in_dim(v, f * rows, rows, 0)
    valid = own_rows(all_valid)
    h0 = own_rows(all_h0)
    fwd0, near_z0, wo = tie((scan(px0, 0), near_z0, wo))
    far_z0 = [lax.ppermute(v, "section", [(0, 1)]) for v in near_z0]
    win[0] = (near_z0, far_z0, near_x0, far_x0)
    pz0 = project_z(normed_in0, 0)
    g0 = gate(pz0, fwd0[0][0])
    stat0 = jnp.sum(g0 * g0, axis=1)
    stat0 = sum_of_shares(stat0.reshape(n, rows)).reshape(-1)
    r0 = lax.rsqrt(stat0 / INNER + EPS)
    normed0 = gated(pz0, fwd0[0][0], r0, 0)
    normed0, near_x1, own_ct = tie((normed0, near_x1, own_ct))
    part_ct = in_group(exchange(quarters(own_ct)))
    far_x1 = [lax.ppermute(v, "section", [(1, 0)]) for v in near_x1]
    mixed0 = scatter_sum(jnp.dot(normed0, wo[0], preferred_element_type=F32))
    mixed0, part_ct, pieces_z1 = tie((mixed0, part_ct, pieces_z1))
    near_z1, far_z1 = fetch(pieces_z1, 1)
    out0 = valid * (h0.astype(F32) + mixed0)
    h1 = out0.astype(BF16)

    normed_in1 = gather_rows(normalised(h1.astype(F32), small[1][0]).astype(BF16))
    normed_in1, far_x1 = tie((normed_in1, far_x1))
    win[1] = (near_z1, far_z1, near_x1, far_x1)
    px1 = project_x(normed_in1, 1)
    px1, near_z1, part_ct = tie((px1, near_z1, part_ct))
    far_z1 = [lax.ppermute(v, "section", [(1, 0)]) for v in near_z1]
    win[1] = (near_z1, far_z1, near_x1, far_x1)
    all_ct = whole_slot(part_ct)
    fwd1 = scan(px1, 1)
    fwd1, all_ct = tie((fwd1, all_ct))
    dout1 = own_rows(all_ct).astype(F32)
    dmixed1 = (all_valid * all_ct.astype(F32)).astype(BF16)
    dn1 = dot_cols(dmixed1, wo[1])
    pz1 = project_z(normed_in1, 1)
    g1 = gate(pz1, fwd1[0][0])
    stat1 = sum_of_shares(
        jnp.stack(
            [
                jnp.sum(g1 * g1, axis=1).reshape(n, rows),
                jnp.sum(g1 * dn1 * small[1][3], axis=1).reshape(n, rows),
            ]
        )
    ).reshape(2, -1)
    r1 = lax.rsqrt(stat1[0] / INNER + EPS)
    normed1 = gated(pz1, fwd1[0][0], r1, 1)

    part_width = width // 2

    def cut_half(v, k):
        size = v.shape[1] // 2
        return lax.dynamic_slice_in_dim(v, k * size, size, 1)

    def narrow_of(parts, k):
        return jnp.concatenate([cut_half(v, k) for v in parts], axis=1)

    def away_in(normed_in, part, narrow=()):
        away = [dot_rows(normed_in, cut_half(part, 1 - c)).astype(BF16)]
        if narrow:
            away.append(dot_rows(narrow_of(narrow, 1 - c), normed_in).astype(BF16))
        return [swap_section(v) for v in away]

    def own_in_piece(normed_in, part, away, narrow=()):
        total = dot_rows(normed_in, cut_half(part, c)) + away[0].astype(F32)
        result = total.astype(BF16).reshape(n, share, -1)
        if narrow:
            total = (dot_rows(narrow_of(narrow, c), normed_in) + away[1].astype(F32)).astype(BF16)
            fill = jnp.zeros((-total.shape[0] % 64, D), BF16)
            rest = jnp.concatenate([total, fill]).reshape(-1, n, share).transpose(1, 0, 2)
            result = jnp.concatenate([result, rest], axis=1)
        return result

    def away_out(normed, dmixed):
        return swap_section(dot_rows(cut_half(normed, 1 - c), dmixed).astype(BF16))

    def own_out_piece(normed, dmixed, away):
        return (dot_rows(cut_half(normed, c), dmixed) + away.astype(F32)).astype(BF16)

    def with_group(dxs, dbc):
        total = jnp.sum(exchange(dbc), axis=0).astype(BF16)
        column = jnp.arange(GROUP)[None, :] // group
        own = jnp.where(column == f, jnp.concatenate([total] * n, axis=1), 0)
        full = lax.dynamic_update_slice(dxs, own.astype(BF16), (0, width))
        return full, (dxs[:, :width], [total, dxs[:, width + GROUP :]])

    def back_in(dz, full, layer, kind):
        near_z, far_z, near_x, far_x = win[layer]
        return project_back(ids, dz, full, (near_z, near_x), (far_z, far_x), layer, kind)

    def back_norm(dout, dnormed_in, h, gain):
        h = h.astype(F32)
        r = lax.rsqrt(jnp.mean(h * h, axis=-1, keepdims=True) + EPS)
        u = dnormed_in * gain
        mean = jnp.mean(u * h, axis=-1, keepdims=True)
        dgain = jnp.sum(dnormed_in * h * r, axis=0)
        return valid * dout + r * u - h * (r * r * r) * mean, dgain

    def scales(r, coef):
        top = jnp.stack([r.reshape(n, rows), coef.reshape(n, rows)], axis=1)
        return jnp.concatenate([top, jnp.zeros((n, 6, rows), F32)], axis=1)

    def packed(dgin, d, out, mixed):
        dgain, dconv, dhp = d[3][0], d[4][:5], d[5][:3]
        put = lambda v, size, at_lane: lax.dynamic_update_slice(
            jnp.zeros(v.shape[:-1] + (size,), F32), v, (0,) * (v.ndim - 1) + (at_lane,)
        )
        conv = put(dconv[:, :width], CHANNELS, f * width)
        conv = conv.at[:, INNER:].set(dconv[:, width:])
        totals = jnp.stack(
            [jnp.sum(out * out), jnp.sum((valid * mixed) ** 2), jnp.sum(valid)]
        )
        return jnp.concatenate(
            [
                dgin,
                conv.reshape(-1),
                put(dhp, HEADS, f * heads).reshape(-1),
                put(dgain, INNER, f * width),
                totals,
            ]
        )

    def hand_over(v, layer):
        return lax.ppermute(v, "section", [(1 - layer, layer)])

    sums = SeqSums()
    rc1 = scales(r1, (r1 * r1 * r1 / INNER) * stat1[1])
    away = away_out(normed1, dmixed1)
    o1 = sums.add(own_out_piece(normed1, dmixed1, away))
    rc1, normed1, dn1 = sums.end((rc1, normed1, dn1))

    sums.begin()
    d1 = unscan(pz1, px1, fwd1, dn1, rc1, 1)
    mixed1 = scatter_sum(jnp.dot(normed1, wo[1], preferred_element_type=F32).astype(BF16))
    d1, mixed1 = sums.end((d1, mixed1))

    sums.begin()
    away = away_in(normed_in1, d1[0])
    full1, xs1 = with_group(d1[1], d1[2])
    back1 = back_in(d1[0], full1, 1, F32)
    gz = own_in_piece(normed_in1, d1[0], away)
    out1 = valid * (h1.astype(F32) + mixed1)
    back_h = exchange(quarters(jnp.concatenate([h1, out1.astype(BF16)])))
    back1, xs1, full1, gz, out1, back_h = sums.end((back1, xs1, full1, gz, out1, back_h))
    z1 = sums.add(gz)

    sums.begin()
    dnin1 = scatter_sum(back1)
    away = away_in(normed_in1, *xs1)
    gx = own_in_piece(normed_in1, xs1[0], away, xs1[1])
    back_h = in_group(back_h)
    grad1, dgin1 = back_norm(dout1, dnin1, h1, small[1][0])
    dout0 = grad1.astype(BF16).astype(F32)
    dmixed0_own = (valid * dout0).astype(BF16)
    along0 = jnp.sum(dmixed0_own.astype(F32) * mixed0, axis=-1)
    grad1, dgin1, dout0, dmixed0_own, along0, gx, back_h = sums.end(
        (grad1, dgin1, dout0, dmixed0_own, along0, gx, back_h)
    )
    x1 = sums.add(gx)

    sums.begin()
    dmixed0 = gather_rows(dmixed0_own)
    along0 = to_all(along0).reshape(-1)
    rc0 = scales(r0, (r0 * r0 / INNER) * along0)
    back_h = joined(exchange(back_h))
    dmixed0, rc0, back_h = sums.end((dmixed0, rc0, back_h))

    sums.begin()
    dn0 = dot_cols(dmixed0, wo[0])
    d0 = unscan(pz0, px0, fwd0, dn0, rc0, 0)
    go = own_out_piece(normed0, dmixed0, away_out(normed0, dmixed0))
    p1 = packed(dgin1, d1, out1, mixed1)
    d0, go, p1 = sums.end((d0, go, p1))
    o0 = sums.add(go)

    sums.finish([o1, z1])
    sums.begin()
    away = away_in(normed_in0, d0[0])
    full0, xs0 = with_group(d0[1], d0[2])
    gz = own_in_piece(normed_in0, d0[0], away)
    away = away_in(normed_in0, *xs0)
    gx = own_in_piece(normed_in0, xs0[0], away, xs0[1])
    own_z1 = exchange(sums.values[z1])
    full0, gz, gx, own_z1 = sums.end((full0, gz, gx, own_z1))
    z0 = sums.add(gz)

    sums.begin()
    gx = exchange(gx)
    back0 = back_in(d0[0], full0, 0, BF16)
    gx, back0 = sums.end((gx, back0))
    x0 = sums.add(gx)

    def hand_over(v, layer):
        return lax.ppermute(v, "section", [(1 - layer, layer)])

    sums.begin()
    dnin0 = scatter_sum(back0)
    own_o1 = sums.values[o1]
    away_o1 = hand_over(own_o1, 1)
    away_z1 = hand_over(own_z1, 1)
    grad0, dgin0 = back_norm(dout0, dnin0, h0, small[0][0])
    grad0, dgin0, own_z1, away_z1, own_o1, away_o1 = sums.end(
        (grad0, dgin0, own_z1, away_z1, own_o1, away_o1)
    )

    sums.finish([x1, o0])
    sums.begin()
    own_x1 = exchange(sums.values[x1])
    own_o0 = sums.values[o0]
    away_o0 = hand_over(own_o0, 0)
    back_g = exchange(quarters(jnp.concatenate([grad0.astype(BF16), grad1.astype(BF16)])))
    p = jnp.stack([packed(dgin0, d0, out0, mixed0), p1])
    p = p + swap_section(p)
    p, back_g, own_x1, own_o0, away_o0 = sums.end((p, back_g, own_x1, own_o0, away_o0))

    sums.finish([z0])
    sums.begin()
    own_z0 = exchange(sums.values[z0])
    away_x1 = hand_over(own_x1, 1)
    m = 1
    while m < n:
        p = p + move_fsdp(p, m)
        m *= 2
    away_z0 = hand_over(own_z0, 0)
    p, back_g, own_z0, away_z0, own_x1, away_x1 = sums.end(
        (p, back_g, own_z0, away_z0, own_x1, away_x1)
    )
    sums.finish([x0])
    own_x0 = sums.values[x0]
    away_x0 = hand_over(own_x0, 0)
    back_g = in_group(back_g)
    p = p + move_seq(p, 1)

    held = [
        [(own_z0, own_x0, own_o0), (own_z1, own_x1, own_o1)],
        [(away_z0, away_x0, away_o0), (away_z1, away_x1, away_o1)],
    ]

    def both_halves(a, b):
        return jnp.stack([pick(a, b), pick(b, a)], axis=1)

    rows_of = GROUP // n // 2, HEADS // n // 2
    narrow = [pick(side[0][1], side[1][1])[:, share : share + sum(rows_of)] for side in held]
    narrow = both_halves(*[v.astype(F32) for v in narrow])
    small_in = jnp.concatenate(
        [
            narrow[:, :, : rows_of[0]].reshape(GROUP, share),
            narrow[:, :, rows_of[0] :].reshape(HEADS, share),
        ]
    )
    g_w_in = []
    shape_in = (2 * INNER + GROUP + HEADS, share)
    for k, rows_of_small in ((0, None), (1, (2 * INNER, GROUP + HEADS))):
        if g_w_in:
            back_g, g_w_in, p = tie((back_g, g_w_in, p))
            back_g = exchange(back_g)
        arrays, plan = [], []
        for s in range(2):
            arrays += [held[s][0][k], held[s][1][k]]
            firsts = tuple(k * INNER + q * width for q in range(n))
            plan.append((len(arrays) - 2, len(arrays) - 1, s, firsts))
        g_w_in = [
            place_in(
                ids, arrays, tuple(plan), small_in, rows_of_small, g_w_in, shape_in, part_width
            )
        ]
    m = 2
    while m < nz:
        p = p + move_seq(p, m)
        m *= 2
    p = pick(p[0], p[1])
    g_w_in, back_g, p = tie((g_w_in, back_g, p))

    used = 0

    def part(size):
        nonlocal used
        used += size
        return p[used - size : used]

    mine_of = lambda v, size: lax.dynamic_slice_in_dim(v, f * size, size, v.ndim - 1)
    o_gain_in = mine_of(part(D), share)
    o_conv = mine_of(part(5 * CHANNELS).reshape(5, CHANNELS), CHANNELS // n)
    o_heads = mine_of(part(3 * HEADS).reshape(3, HEADS), heads)
    o_gain_out = mine_of(part(INNER), width)
    totals = part(3)
    act_rms = jnp.sqrt(totals[:2] / (totals[2] * D))[None]

    back = jnp.concatenate([back_h, joined(back_g)])
    halves_out = [pick(side[0][2], side[1][2]) for side in held]
    g_w_out = jnp.concatenate([pick(*halves_out), pick(*halves_out[::-1])]).astype(F32)

    back = back.reshape(2, 2, rows, D)
    kept_back = pick(back[:, 0], back[:, 1])
    other_back = swap_section(pick(back[:, 1], back[:, 0]))
    both_back = jnp.stack(
        [pick(kept_back, other_back), pick(other_back, kept_back)], axis=1
    )
    return (
        both_back[0][None, :, None],
        both_back[1].astype(F32)[None, :, None],
        o_gain_in[None],
        g_w_in[0].T[None],
        o_conv[None, :4],
        o_conv[None, 4],
        o_heads[None, 0],
        o_heads[None, 1],
        o_heads[None, 2],
        o_gain_out[None],
        g_w_out[None],
        act_rms,
    )


def solution(mesh):
    in_specs = (
        P(None, "fsdp", "seq", None),
        P(None, "fsdp", "seq", None),
        P(None, "fsdp"),
        P("section", "fsdp"),
        P("section", "fsdp", None),
        P("section", None, "fsdp"),
        P("section", "fsdp"),
        P("section", "fsdp"),
        P("section", "fsdp"),
        P("section", "fsdp"),
        P("section", "fsdp"),
        P("section", "fsdp", None),
    )
    out_specs = (
        P("section", None, "fsdp", "seq", None),
        P("section", None, "fsdp", "seq", None),
        P("section", "fsdp"),
        P("section", "fsdp", None),
        P("section", None, "fsdp"),
        P("section", "fsdp"),
        P("section", "fsdp"),
        P("section", "fsdp"),
        P("section", "fsdp"),
        P("section", "fsdp"),
        P("section", "fsdp", None),
        P("section", None),
    )
    return jax.shard_map(
        per_device, mesh=mesh, in_specs=in_specs, out_specs=out_specs, check_vma=False
    )
```
